32 devices in a mesh: grp: 2 (over x), ep: 16 (over z, y, core).
Axes of the slice: x: 2, y: 2, z: 4, core: 2. Of those that a mesh axis runs over, the one named last changes fastest.
Arguments:
- block_input: bfloat16 [4096, 2048], P(('grp', 'ep')), may hold values from -6 to 6
- cotangent: bfloat16 [4096, 2048], P(('grp', 'ep')), may hold values from -6 to 6
- routes: int32 [4096, 8], P(('grp', 'ep')), may hold values from 0 to 15, all different within a row; in each aligned block of 128 rows (0 to 127, 128 to 255, ...) at most 66 rows name the same one
- w_query: bfloat16 [2048, 2048], P(('grp', 'ep')), may hold values from -0.125 to 0.125
- w_key: bfloat16 [2048, 2048], P(('grp', 'ep')), may hold values from -0.125 to 0.125
- w_value: bfloat16 [2048, 2048], P(('grp', 'ep')), may hold values from -0.125 to 0.125
- w_output: bfloat16 [2048, 2048], P(('grp', 'ep')), may hold values from -1.5 to 1.5
- w_router: bfloat16 [2048, 16], P(('grp', 'ep')), may hold values from -0.0625 to 0.0625
- gain_attn: bfloat16 [2048], P(('grp', 'ep')), may hold values from 0.25 to 1.75
- gain_query: bfloat16 [2048], P(('grp', 'ep')), may hold values from 0.25 to 1.75
- gain_key: bfloat16 [2048], P(('grp', 'ep')), may hold values from 0.25 to 1.75
- gain_mlp: bfloat16 [2048], P(('grp', 'ep')), may hold values from 0.25 to 1.75
- w_gate: bfloat16 [16, 2048, 1024], P('ep'), may hold values from -0.125 to 0.125
- w_up: bfloat16 [16, 2048, 1024], P('ep'), may hold values from -0.125 to 0.125
- w_down: bfloat16 [16, 1024, 2048], P('ep'), may hold values from -1.5 to 1.5
Outputs:
- block_output: bfloat16 [4096, 2048], P(('grp', 'ep'))
- input_grad: float32 [4096, 2048], P(('grp', 'ep'))
- grad_query: float32 [2048, 2048], P(('grp', 'ep'))
- grad_key: float32 [2048, 2048], P(('grp', 'ep'))
- grad_value: float32 [2048, 2048], P(('grp', 'ep'))
- grad_output: float32 [2048, 2048], P(('grp', 'ep'))
- grad_router: float32 [2048, 16], P(('grp', 'ep'))
- grad_gain_attn: float32 [2048], P(('grp', 'ep'))
- grad_gain_query: float32 [2048], P(('grp', 'ep'))
- grad_gain_key: float32 [2048], P(('grp', 'ep'))
- grad_gain_mlp: float32 [2048], P(('grp', 'ep'))
- grad_gate: float32 [16, 2048, 1024], P('ep')
- grad_up: float32 [16, 2048, 1024], P('ep')
- grad_down: float32 [16, 1024, 2048], P('ep')
The draws below stay inside these ranges and needn't reach their ends.
Inputs may be any that keep to these rules, and one draw needn't show every extreme that they name: `routes`: each token names 8 different experts. Among the rows of one device (aligned blocks of 128 rows) no expert is named by more than 66 rows, a bound that some block reaches.
All inputs are finite; a program needn't handle non-finite values.
Results may differ from the reference program's by a relative error of at most 0.02.
Values may be sent and summed in bfloat16 or wider, within the bound.
A program may use at most 320 MiB of HBM per device.

```python
import math
import jax
import jax.numpy as jnp
import numpy as np
from jax import lax

D = 2048
HEADS = 16
HEAD_DIM = 128
FF = 1024
TOP = 8
ROWS = 128
EXPERTS = 16
CAP = 66
PROMPT = 1024
TOKENS = 4096
N_EP = 16


def block_scale(key, shape, split, least, top_value):
    factor_of = 1.0
    for axis_at, shards_of in split:
        steps = jax.random.uniform(jax.random.fold_in(jax.random.fold_in(key, 6), axis_at), (shards_of,), jnp.float32, least / len(split), top_value / len(split))
        factor_of = factor_of * jnp.repeat(jnp.exp(steps), shape[axis_at] // shards_of).reshape((-1,) + (1,) * (len(shape) - 1 - axis_at))
    return factor_of


def routed_block(stream_key, own, number, rows, count, top, bound, skew):
    ranking = jax.random.permutation(stream_key, count)
    packed, ordinary = shares(count, rows * top, bound, skew, True), shares(count, rows * top, bound, skew, False)
    places = jnp.arange(count)

    def named(sizes, rotation):
        used = int((sizes > 0).sum())
        fixed = max(1, used // 4)
        moved = fixed + (places - fixed + rotation * (used - fixed)) % max(1, count - fixed)
        return jnp.zeros((count,), jnp.int32).at[ranking[jnp.where(places < fixed, places, moved)]].set(jnp.asarray(sizes, jnp.int32))

    sizes = jnp.where(number % 4 == 0, named(packed, number // 4), named(ordinary, number - number // 4 - 1))
    mixed = jax.random.permutation(jax.random.fold_in(own, 3), count)
    giver, receiver = mixed[0:count // 2 * 2:2], mixed[1:count // 2 * 2:2]
    margin = jnp.minimum(sizes[giver] - 1, bound - sizes[receiver]) // 2
    margin = jnp.where((giver == ranking[0]) | (receiver == ranking[0]) | (sizes[receiver] == 0), 0, jnp.maximum(margin, 0))
    moved = jax.random.randint(jax.random.fold_in(own, 4), (count // 2,), 0, 1 << 20) % (margin + 1)
    sizes = sizes.at[giver].add(-moved).at[receiver].add(moved)
    items = jnp.searchsorted(jnp.cumsum(sizes), jnp.arange(rows * top), side="right").astype(jnp.int32)
    listing = items.reshape(top, rows).T
    listing = listing[jax.random.permutation(jax.random.fold_in(own, 1), rows)]
    rotation = jax.random.randint(jax.random.fold_in(own, 2), (rows, 1), 0, top)
    return jnp.take_along_axis(listing, (jnp.arange(top)[None, :] + rotation) % top, axis=1)


def shares(amount, total, most, lean, full):
    portions = [(1 << 20) // math.isqrt(grade ** lean) + 1 for grade in range(1, amount + 1)]
    largest = most if full else min(most, max(-(-total // amount), total * portions[0] // sum(portions)))
    least = 1 if total - largest >= amount - 1 else 0
    counts, surplus = [largest] + [least] * (amount - 1), total - largest - least * (amount - 1)
    while surplus > 0:
        candidates = [i for i in range(1, amount) if counts[i] < largest] or [i for i in range(1, amount) if counts[i] < most]
        mass, budget = sum([portions[i] for i in candidates]), surplus
        for i in candidates:
            addition = min(most - counts[i], max(1, budget * portions[i] // mass), surplus)
            counts[i] = counts[i] + addition
            surplus = surplus - addition
    return np.array(counts)


def bell_draw(rng, extent, width, bound, split=(), kind=jnp.bfloat16):
    array = width * jax.random.normal(rng, extent, jnp.float32)
    if split:
        array = array * block_scale(rng, extent, split, -0.22, 0.18)
    return jnp.clip(array, -bound, bound).astype(kind)


def setup_inputs(seed: int = 0) -> dict:
    seeds = jax.random.split(jax.random.key(seed), 16)
    block_input = bell_draw(seeds[0], (TOKENS, D), 1.0, 6.0, ((0, 32),))
    cotangent = bell_draw(seeds[1], (TOKENS, D), 1.0, 6.0, ((0, 32),))
    routes_keys = jax.random.split(jax.random.fold_in(seeds[2], 1), TOKENS // ROWS)
    routes_turns = jax.random.permutation(jax.random.fold_in(seeds[2], 3), TOKENS // ROWS)
    routes = jax.vmap(lambda own, number: routed_block(jax.random.fold_in(seeds[2], 2), own, number, ROWS, EXPERTS, TOP, CAP, 1))(routes_keys, routes_turns).reshape((TOKENS, TOP))
    w_query = bell_draw(seeds[3], (D, D), D ** -0.5, 0.125, ((0, 32),))
    w_key = bell_draw(seeds[4], (D, D), D ** -0.5, 0.125, ((0, 32),))
    w_value = bell_draw(seeds[5], (D, D), D ** -0.5, 0.125, ((0, 32),))
    w_output = bell_draw(seeds[6], (D, D), (D // 128) ** -0.5, 1.5, ((0, 32),))
    w_router = bell_draw(seeds[7], (D, EXPERTS), (4 * D) ** -0.5, 0.0625, ((0, 32),))
    gain_attn = jnp.clip(1.0 + 0.15 * jax.random.normal(seeds[8], (D,), jnp.float32), 0.25, 1.75).astype(jnp.bfloat16)
    gain_query = jnp.clip(1.0 + 0.15 * jax.random.normal(seeds[9], (D,), jnp.float32), 0.25, 1.75).astype(jnp.bfloat16)
    gain_key = jnp.clip(1.0 + 0.15 * jax.random.normal(seeds[10], (D,), jnp.float32), 0.25, 1.75).astype(jnp.bfloat16)
    gain_mlp = jnp.clip(1.0 + 0.15 * jax.random.normal(seeds[11], (D,), jnp.float32), 0.25, 1.75).astype(jnp.bfloat16)
    w_gate = bell_draw(seeds[12], (EXPERTS, D, FF), D ** -0.5, 0.125, ((0, 16),))
    w_up = bell_draw(seeds[13], (EXPERTS, D, FF), D ** -0.5, 0.125, ((0, 16),))
    w_down = bell_draw(seeds[14], (EXPERTS, FF, D), (FF // 64) ** -0.5, 1.5, ((0, 16),))
    return {"block_input": block_input, "cotangent": cotangent, "routes": routes, "w_query": w_query, "w_key": w_key, "w_value": w_value, "w_output": w_output, "w_router": w_router, "gain_attn": gain_attn, "gain_query": gain_query, "gain_key": gain_key, "gain_mlp": gain_mlp, "w_gate": w_gate, "w_up": w_up, "w_down": w_down}


@jax.custom_vjp
def low(v):
    return lax.optimization_barrier(v.astype(jnp.bfloat16)).astype(jnp.float32)

@jax.custom_vjp
def low_back(v):
    return v

def low_keep(v):
    return (low(v), None)

def low_pass(kept, grad):
    return (grad,)

def back_keep(v):
    return (v, None)

def back_low(kept, grad):
    return (low(grad),)
low.defvjp(low_keep, low_pass)
low_back.defvjp(back_keep, back_low)
eps = 1e-05
theta_base = 10000.0

def exact_dot(matrix_a, matrix_b):
    return jnp.dot(matrix_a, matrix_b, precision=lax.Precision.HIGHEST, preferred_element_type=jnp.float32)

def rms_scale(values, gain_vec):
    return values * lax.rsqrt(lax.optimization_barrier(jnp.mean(values * values, axis=-1, keepdims=True)) + eps) * gain_vec

def rotate(values, position):
    token_count = values.shape[0]
    by_head = values.reshape(token_count, -1, HEAD_DIM)
    half_dim = HEAD_DIM // 2
    frequency = theta_base ** (-2.0 * jnp.arange(half_dim, dtype=jnp.float32) / HEAD_DIM)
    angles = position.astype(jnp.float32)[:, None] * frequency[None, :]
    cosine = jnp.cos(angles)[:, None, :]
    sine_part = jnp.sin(angles)[:, None, :]
    former = by_head[..., :half_dim]
    latter = by_head[..., half_dim:]
    turned = jnp.concatenate([former * cosine - latter * sine_part, latter * cosine + former * sine_part], axis=-1)
    return turned.reshape(token_count, -1)

def group_layer(params, group_input, selected):
    w_query, w_key, w_value, w_output, w_router, gain_attn, gain_query, gain_key, gain_mlp, w_gate, w_up, w_down = params
    token_count = group_input.shape[0]
    prompt_len = PROMPT
    indices = jnp.arange(token_count, dtype=jnp.int32)
    in_prompt = indices < prompt_len
    position = jnp.where(in_prompt, indices, prompt_len + (indices - prompt_len) % ROWS)
    series = jnp.where(in_prompt, -1, (indices - prompt_len) // ROWS)
    allowed = (position[None, :] <= position[:, None]) & (in_prompt[None, :] | (series[None, :] == series[:, None]))
    normed = low(rms_scale(group_input, gain_attn))
    query_lin = low_back(exact_dot(normed, w_query))
    key_lin = low_back(exact_dot(normed, w_key))
    value_lin = low_back(exact_dot(normed, w_value))
    query_rot = low(rotate(rms_scale(query_lin, gain_query), position))
    key_rot = low(rotate(rms_scale(key_lin, gain_key), position))
    value_low = low(value_lin)
    scale = HEAD_DIM ** (-0.5)

    def one_head(pieces):
        head_query, head_key, head_value = pieces
        scores = low_back(exact_dot(head_query, head_key.T) * scale)
        scores = jnp.where(allowed, scores, -1e+30)
        weights = low(jax.nn.softmax(scores, axis=-1))
        return exact_dot(weights, head_value)

    def split_heads(values):
        return values.reshape(token_count, HEADS, HEAD_DIM).transpose(1, 0, 2)
    mixed = lax.map(jax.checkpoint(one_head), (split_heads(query_rot), split_heads(key_rot), split_heads(value_low)))
    attended = low(low_back(mixed.transpose(1, 0, 2).reshape(token_count, D)))
    residual = group_input + low_back(exact_dot(attended, w_output))
    normed_mlp = low(rms_scale(residual, gain_mlp))
    logits = low_back(exact_dot(normed_mlp, w_router))
    gates = jax.nn.softmax(logits, axis=-1) * selected

    def one_expert(summed, pieces):
        gate_w, up_w, down_w, column = pieces
        rows_in = low_back(normed_mlp)
        gate_pre = low_back(exact_dot(rows_in, gate_w))
        up_pre = low_back(exact_dot(rows_in, up_w))
        hidden = low(jax.nn.silu(gate_pre) * up_pre)
        result = low(low_back(exact_dot(hidden, down_w)))
        return (summed + column[:, None] * result, None)
    mixture, unused = lax.scan(jax.checkpoint(one_expert), jnp.zeros_like(residual), (w_gate, w_up, w_down, gates.T))
    return residual + mixture

def reference(block_input, cotangent, routes, w_query, w_key, w_value, w_output, w_router, gain_attn, gain_query, gain_key, gain_mlp, w_gate, w_up, w_down):
    params = tuple((weight_arr.astype(jnp.float32) for weight_arr in (w_query, w_key, w_value, w_output, w_router, gain_attn, gain_query, gain_key, gain_mlp, w_gate, w_up, w_down)))
    group_size = ROWS * N_EP
    groups = block_input.shape[0] // group_size
    inputs = block_input.astype(jnp.float32).reshape(groups, group_size, D)
    selected = lax.optimization_barrier(jnp.sum((routes[:, :, None] == jnp.arange(EXPERTS, dtype=jnp.int32)[None, None, :]).astype(jnp.float32), axis=1))
    selected = selected.reshape(groups, group_size, EXPERTS)

    def whole(params, inputs):

        def one_group(pieces):
            return group_layer(params, pieces[0], pieces[1])
        return lax.map(jax.checkpoint(one_group), (inputs, selected))
    outputs, pullback = jax.vjp(whole, params, inputs)
    param_grads, input_grad = pullback(cotangent.astype(jnp.float32).reshape(groups, group_size, D))
    return (outputs.reshape(-1, D).astype(jnp.bfloat16), input_grad.reshape(-1, D), param_grads[0], param_grads[1], param_grads[2], param_grads[3], param_grads[4], param_grads[5], param_grads[6], param_grads[7], param_grads[8], param_grads[9], param_grads[10], param_grads[11])
```

```python
import math

import jax
import jax.numpy as jnp
from jax import lax
from jax.experimental import pallas as pl
from jax.experimental.pallas import tpu as pltpu
from jax.sharding import PartitionSpec as P

HEAD_DIM = 128
MESH = pl.DeviceIdType.MESH
BF = jnp.bfloat16
F32 = jnp.float32


eps = 1e-05
theta_base = 10000.0


def mm(a, b):
    return jnp.dot(a, b, preferred_element_type=F32)


def mm_nt(a, b):
    return lax.dot_general(a, b, (((1,), (1,)), ((), ())), preferred_element_type=F32)


def mm_tn(a, b):
    return lax.dot_general(a, b, (((0,), (0,)), ((), ())), preferred_element_type=F32)


class Place:
    def __init__(self, ep_count):
        self.grp = lax.axis_index("grp")
        self.ep = lax.axis_index("ep")
        self.count = ep_count
        self.ring = ep_count // 2
        self.half = self.ring // 2
        self.core = self.ep % 2
        y = (self.ep // 2) % 2
        z = self.ep // 4
        self.place = z + y * (self.ring - 1 - 2 * z)

    def index(self, place, core):
        y = place // self.half
        z = place + y * (self.ring - 1 - 2 * place)
        return (z * 2 + y) * 2 + core

    def at(self, offset):
        return (self.place + offset + self.ring) % self.ring

    def chip(self, offset):
        return self.index(self.at(offset), self.core)

    def right(self):
        return (self.grp, self.chip(1))

    def left(self):
        return (self.grp, self.chip(-1))

    def sibling(self):
        return (self.grp, self.index(self.place, 1 - self.core))

    def across(self):
        return (1 - self.grp, self.ep)

    def peer(self, offset):
        return (self.grp, (self.ep + offset + self.count) % self.count)


def greet(devices):
    barrier = pltpu.get_barrier_semaphore()
    for device in devices:
        pl.semaphore_signal(barrier, inc=1, device_id=device, device_id_type=MESH)
    pl.semaphore_wait(barrier, len(devices))


def remote(src, dst, send, recv, device):
    return pltpu.make_async_remote_copy(
        src_ref=src, dst_ref=dst, send_sem=send, recv_sem=recv, device_id=device, device_id_type=MESH
    )


class Gather:
    def __init__(self, here, src, dst, sems):
        self.here, self.src, self.dst = here, src, dst
        self.ring_send, self.ring_recv, self.side_send, self.side_recv, self.own_sem = sems
        self.rows = dst.shape[1] // 2
        self.far = here.ring // 2
        self.started = []

    @staticmethod
    def scratch(ep_count):
        far = ep_count // 4
        ring = pltpu.SemaphoreType.DMA((2, far, 2))
        side = pltpu.SemaphoreType.DMA((2, far + 1, 2))
        return [ring, ring, side, side, pltpu.SemaphoreType.DMA]

    def block(self, index, part):
        return self.dst.at[index, pl.ds(part * self.rows, self.rows)]

    def go(self, copy):
        copy.start()
        self.started.append(copy)

    def hops(self, way, part):
        return self.far if way == part else self.far - 1

    def ring_copy(self, way, step, part, src, index):
        device = self.here.right() if way == 0 else self.here.left()
        return remote(
            src, self.block(index, part), self.ring_send.at[way, step, part], self.ring_recv.at[way, step, part], device
        )

    def side_copy(self, way, step, part, src, index):
        return remote(
            src,
            self.block(index, part),
            self.side_send.at[way, step, part],
            self.side_recv.at[way, step, part],
            self.here.sibling(),
        )

    def start(self):
        here = self.here
        for part in range(2):
            src = self.src.at[pl.ds(part * self.rows, self.rows)]
            for way in range(2):
                if self.hops(way, part) > 0:
                    self.go(self.ring_copy(way, 0, part, src, here.ep))
            self.go(self.side_copy(0, 0, part, src, here.ep))
        self.own = pltpu.make_async_copy(self.src, self.dst.at[here.ep], self.own_sem)
        self.own.start()

    def step(self, step):
        here = self.here
        for part in range(2):
            for way in range(2):
                if step < self.hops(way, part):
                    index = here.chip(-1 - step if way == 0 else 1 + step)
                    src = self.block(index, part)
                    self.ring_copy(way, step, part, src, index).wait_recv()
                    if step + 1 < self.hops(way, part):
                        self.go(self.ring_copy(way, step + 1, part, src, index))
                    self.go(self.side_copy(way, step + 1, part, src, index))

    def side(self, step):
        here = self.here
        for part in range(2):
            for way in range(2):
                if (step < 0 and way == 0) or (0 <= step < self.hops(way, part)):
                    offset = 0 if step < 0 else (-1 - step if way == 0 else 1 + step)
                    index = here.index(here.at(offset), 1 - here.core)
                    self.side_copy(way, step + 1, part, self.block(index, part), index).wait_recv()

    def finish(self):
        self.own.wait()
        for copy in self.started:
            copy.wait_send()


class Exchange:
    def __init__(self, here, src, dst, sems):
        self.here, self.src, self.dst = here, src, dst
        self.send, self.recv, self.own_sem = sems

    @staticmethod
    def scratch(ep_count):
        return [
            pltpu.SemaphoreType.DMA((ep_count,)),
            pltpu.SemaphoreType.DMA((ep_count,)),
            pltpu.SemaphoreType.DMA,
        ]

    def start(self):
        here = self.here
        self.own = pltpu.make_async_copy(self.src(here.ep), self.dst(here.ep), self.own_sem)
        self.own.start()
        self.copies = []
        for offset in range(1, here.count):
            device = here.peer(offset)
            copy = remote(self.src(device[1]), self.dst(here.ep), self.send.at[offset], self.recv.at[offset], device)
            copy.start()
            self.copies.append(copy)

    def arrive(self):
        here = self.here
        self.own.wait()
        for offset in range(1, here.count):
            source = here.peer(-offset)[1]
            remote(
                self.dst(source), self.dst(source), self.send.at[offset], self.recv.at[offset], here.peer(offset)
            ).wait_recv()

    def finish(self):
        for copy in self.copies:
            copy.wait_send()


def ring_devices(here):
    return [here.right(), here.left(), here.sibling()]


def plane_devices(here):
    return [here.peer(offset) for offset in range(1, here.count)]


def comm_call(kernel, out_shape, scratch, name, collective_id, operands, vmem=False):
    space = pltpu.VMEM if vmem else pl.ANY
    spec = pl.BlockSpec(memory_space=space)
    out_spec = [spec] * len(out_shape) if isinstance(out_shape, (list, tuple)) else spec
    return pl.pallas_call(
        kernel,
        out_shape=out_shape,
        in_specs=[spec] * len(operands),
        out_specs=out_spec,
        scratch_shapes=scratch,
        compiler_params=pltpu.CompilerParams(
            collective_id=collective_id, has_side_effects=True, vmem_limit_bytes=56 << 20
        ),
        name=name,
    )(*operands)


def split(refs, *sizes):
    groups, start = [], 0
    for size in sizes:
        groups.append(refs[start : start + size])
        start += size
    return groups


def gather_inputs(ep_count, rows_block, weights, small):
    rows, width = rows_block.shape
    kinds, depth, columns = weights.shape
    mine = columns // ep_count
    small_rows = small.shape[0]

    def kernel(x_ref, w_ref, s_ref, x_out, w_out, s_out, *scratch):
        gather_sems, w_sems, s_sems, cross = split(scratch, 5, 3, 3, 4)
        here = Place(ep_count)
        greet(plane_devices(here) + [here.across()])
        first = pltpu.make_async_copy(s_ref, s_out.at[here.grp, here.ep], cross[0].at[2])
        first.start()
        swap = remote(s_ref, s_out.at[here.grp, here.ep], cross[1].at[0], cross[2].at[0], here.across())
        swap.start()
        gather = Gather(here, x_ref, x_out, gather_sems)
        gather.start()
        columns_of = Exchange(
            here,
            lambda e: w_ref.at[:, :, pl.ds(pl.multiple_of(e * mine, mine), mine)],
            lambda e: w_out.at[here.grp, e],
            w_sems,
        )
        columns_of.start()
        first.wait()
        remote(
            s_ref, s_out.at[1 - here.grp, here.ep], cross[1].at[0], cross[2].at[0], here.across()
        ).wait_recv()
        swap.wait_send()
        spread = Exchange(here, lambda e: s_out.at[:, here.ep], lambda e: s_out.at[:, e], s_sems)
        copies = []
        for offset in range(1, here.count):
            copy = remote(
                s_out.at[:, here.ep], s_out.at[:, here.ep], s_sems[0].at[offset], s_sems[1].at[offset], here.peer(offset)
            )
            copy.start()
            copies.append(copy)
        gather.step(0)
        columns_of.arrive()
        over = remote(w_out.at[here.grp], w_out.at[here.grp], cross[1].at[1], cross[2].at[1], here.across())
        over.start()
        for step in range(1, gather.far):
            gather.step(step)
        for offset in range(1, here.count):
            source = here.peer(-offset)[1]
            remote(
                s_out.at[:, source], s_out.at[:, source], s_sems[0].at[offset], s_sems[1].at[offset], here.peer(offset)
            ).wait_recv()
        for step in range(-1, gather.far):
            gather.side(step)
        remote(
            w_out.at[1 - here.grp], w_out.at[1 - here.grp], cross[1].at[1], cross[2].at[1], here.across()
        ).wait_recv()
        gather.finish()
        columns_of.finish()
        over.wait_send()
        for copy in copies:
            copy.wait_send()

    dma = pltpu.SemaphoreType.DMA
    return comm_call(
        kernel,
        [
            jax.ShapeDtypeStruct((ep_count, rows, width), rows_block.dtype),
            jax.ShapeDtypeStruct((2, ep_count, kinds, depth, mine), weights.dtype),
            jax.ShapeDtypeStruct((2, ep_count, small_rows, small.shape[1]), small.dtype),
        ],
        Gather.scratch(ep_count)
        + Exchange.scratch(ep_count)
        + Exchange.scratch(ep_count)
        + [dma((3,)), dma((2,)), dma((2,)), dma((1,))],
        "gather_inputs",
        1,
        [rows_block, weights, small],
    )


def gather_both(ep_count, block, name, collective_id):
    rows, width = block.shape

    def kernel(x_ref, own_ref, other_ref, *scratch):
        gather_sems, cross = split(scratch, 5, 4)
        across_send, across_recv, hand_send, hand_recv = cross
        here = Place(ep_count)
        greet(ring_devices(here) + [here.across()])
        gather = Gather(here, x_ref, own_ref, gather_sems)
        gather.start()
        sent = []
        places = [0]

        def cross_copy(slot, index, src):
            return remote(src, other_ref.at[index], across_send.at[slot], across_recv.at[slot], here.across())

        def hand_copy(slot, index):
            return remote(
                other_ref.at[index], other_ref.at[index], hand_send.at[slot], hand_recv.at[slot], here.sibling()
            )

        def start(copy):
            copy.start()
            sent.append(copy)

        start(cross_copy(0, here.ep, x_ref))
        slots = [(0, 0)]
        for step in range(gather.far):
            gather.step(step)
            for way in range(2):
                if step < gather.far - 1 or way == 0:
                    offset = -1 - step if way == 0 else 1 + step
                    slots.append((len(slots), offset))
                    index = here.chip(offset)
                    start(cross_copy(slots[-1][0], index, own_ref.at[index]))
        for step in range(-1, gather.far):
            gather.side(step)
        for slot, offset in slots:
            index = here.chip(offset)
            cross_copy(slot, index, other_ref.at[index]).wait_recv()
            start(hand_copy(slot, index))
        for slot, offset in slots:
            hand_copy(slot, here.index(here.at(offset), 1 - here.core)).wait_recv()
        gather.finish()
        for copy in sent:
            copy.wait_send()

    dma = pltpu.SemaphoreType.DMA
    shape = jax.ShapeDtypeStruct((ep_count, rows, width), block.dtype)
    slots = dma((ep_count // 2,))
    return comm_call(
        kernel, [shape, shape], Gather.scratch(ep_count) + [slots] * 4, name, collective_id, [block]
    )


def exchange(ep_count, tiles, name, collective_id):
    def kernel(src, dst, *sems):
        here = Place(ep_count)
        greet(plane_devices(here))
        swap = Exchange(here, lambda e: src.at[e], lambda e: dst.at[e], sems)
        swap.start()
        swap.arrive()
        swap.finish()

    return comm_call(
        kernel,
        jax.ShapeDtypeStruct(tiles.shape, tiles.dtype),
        Exchange.scratch(ep_count),
        name,
        collective_id,
        [tiles],
    )


def spread(ep_count, tile, name, collective_id):
    def kernel(src, dst, *sems):
        here = Place(ep_count)
        greet(plane_devices(here))
        swap = Exchange(here, lambda e: src, lambda e: dst.at[e], sems)
        swap.start()
        swap.arrive()
        swap.finish()

    return comm_call(
        kernel,
        jax.ShapeDtypeStruct((ep_count,) + tile.shape, tile.dtype),
        Exchange.scratch(ep_count),
        name,
        collective_id,
        [tile],
    )


def scatter_sum(ep_count, blocks, name, collective_id):
    rows, width = blocks.shape[1:]
    part_rows = rows // 2
    far = ep_count // 4

    def hops(way, part):
        return far if way == part else far - 1

    def kernel(src, out, joint, travel, landed, side_send, side_recv, ring_send, ring_recv):
        here = Place(ep_count)
        greet(ring_devices(here))
        offsets = [far] + [sign * k for k in range(far - 1, 0, -1) for sign in (1, -1)] + [0]
        sides = []
        for slot, offset in enumerate(offsets):
            index = here.index(here.at(offset), 1 - here.core)
            copy = remote(src.at[index], joint.at[slot], side_send.at[slot], side_recv.at[slot], here.sibling())
            copy.start()
            sides.append(copy)
        waited = set()

        def term(offset, part):
            offset = far if offset == -far else offset
            slot = offsets.index(offset)
            if slot not in waited:
                waited.add(slot)
                sides[slot].wait_recv()
            index = here.chip(offset)
            at = pl.ds(part * part_rows, part_rows)
            return src[index, at].astype(F32) + joint[slot, at].astype(F32)

        sends = []

        def ring_copy(way, step, part):
            at = pl.ds(part * part_rows, part_rows)
            return remote(
                travel.at[way, step, at],
                landed.at[way, step, at],
                ring_send.at[way, step, part],
                ring_recv.at[way, step, part],
                here.right() if way == 0 else here.left(),
            )

        for step in range(far):
            for part in range(2):
                for way in range(2):
                    count = hops(way, part)
                    if step < count:
                        distance = count - step
                        value = term(distance if way == 0 else -distance, part)
                        at = pl.ds(part * part_rows, part_rows)
                        if step > 0:
                            ring_copy(way, step - 1, part).wait_recv()
                            value = value + landed[way, step - 1, at].astype(F32)
                        travel[way, step, at] = value.astype(travel.dtype)
                        copy = ring_copy(way, step, part)
                        copy.start()
                        sends.append(copy)
        for part in range(2):
            value = term(0, part)
            at = pl.ds(part * part_rows, part_rows)
            for way in range(2):
                count = hops(way, part)
                ring_copy(way, count - 1, part).wait_recv()
                value = value + landed[way, count - 1, at].astype(F32)
            out[at] = value
        for copy in sides + sends:
            copy.wait_send()

    dma = pltpu.SemaphoreType.DMA
    ring = ep_count // 2
    return comm_call(
        kernel,
        jax.ShapeDtypeStruct((rows, width), F32),
        [
            pltpu.VMEM((ring, rows, width), blocks.dtype),
            pltpu.VMEM((2, far, rows, width), blocks.dtype),
            pltpu.VMEM((2, far, rows, width), blocks.dtype),
            dma((ring,)),
            dma((ring,)),
            dma((2, far, 2)),
            dma((2, far, 2)),
        ],
        name,
        collective_id,
        [blocks],
        vmem=True,
    )


def rms_scale(values, gain_vec):
    return values * lax.rsqrt(jnp.mean(values * values, axis=-1, keepdims=True) + eps) * gain_vec


def angles_of(position):
    half_dim = HEAD_DIM // 2
    frequency = theta_base ** (-2.0 * jnp.arange(half_dim, dtype=F32) / HEAD_DIM)
    angles = position.astype(F32)[:, None] * frequency[None, :]
    return jnp.cos(angles), jnp.sin(angles)


def turn(values, cosine, sine):
    half_dim = HEAD_DIM // 2
    former, latter = values[:, :half_dim], values[:, half_dim:]
    return jnp.concatenate([former * cosine - latter * sine, latter * cosine + former * sine], axis=-1)


def attend(query, key, value, prompt_len, length, scale):
    causal = jnp.tril(jnp.ones((prompt_len, prompt_len), jnp.bool_))
    small_causal = jnp.tril(jnp.ones((length, length), jnp.bool_))
    q_p, k_p, v_p = query[:prompt_len], key[:prompt_len], value[:prompt_len]
    q_c, k_c, v_c = query[prompt_len:], key[prompt_len:], value[prompt_len:]
    s_p = jnp.where(causal, mm_nt(q_p, k_p) * scale, -1e30)
    top = jnp.max(s_p, axis=-1, keepdims=True)
    e_p = jnp.exp(s_p - top)
    total = jnp.sum(e_p, axis=-1, keepdims=True)
    out_p = mm((e_p / total).astype(BF), v_p)
    log_p = top + jnp.log(total)
    shape = (-1, length, query.shape[1])
    s_c = mm_nt(q_c, k_p) * scale
    s_o = jnp.einsum("nqd,nkd->nqk", q_c.reshape(shape), k_c.reshape(shape), preferred_element_type=F32) * scale
    s_o = jnp.where(small_causal, s_o, -1e30).reshape(-1, length)
    top = jnp.maximum(jnp.max(s_c, axis=-1, keepdims=True), jnp.max(s_o, axis=-1, keepdims=True))
    e_c = jnp.exp(s_c - top)
    e_o = jnp.exp(s_o - top)
    total = jnp.sum(e_c, axis=-1, keepdims=True) + jnp.sum(e_o, axis=-1, keepdims=True)
    out_c = mm((e_c / total).astype(BF), v_p)
    own = jnp.einsum(
        "nqk,nkd->nqd",
        (e_o / total).astype(BF).reshape(-1, length, length),
        v_c.reshape(shape),
        preferred_element_type=F32,
    )
    out_c = out_c + own.reshape(out_c.shape)
    log_c = top + jnp.log(total)
    return jnp.concatenate([out_p, out_c]), jnp.concatenate([log_p, log_c])


def attend_back(query, key, value, grad, logs, prompt_len, length, scale):
    causal = jnp.tril(jnp.ones((prompt_len, prompt_len), jnp.bool_))
    small_causal = jnp.tril(jnp.ones((length, length), jnp.bool_))
    q_p, k_p, v_p, g_p, l_p = (a[:prompt_len] for a in (query, key, value, grad, logs))
    q_c, k_c, v_c, g_c, l_c = (a[prompt_len:] for a in (query, key, value, grad, logs))
    shape = (-1, length, query.shape[1])
    w_p = jnp.where(causal, jnp.exp(mm_nt(q_p, k_p) * scale - l_p), 0.0)
    d_p = mm_nt(g_p, v_p)
    ds_p = (w_p * (d_p - jnp.sum(w_p * d_p, axis=-1, keepdims=True))).astype(BF)
    w_c = jnp.exp(mm_nt(q_c, k_p) * scale - l_c)
    d_c = mm_nt(g_c, v_p)
    q_n, k_n, v_n, g_n = (a.reshape(shape) for a in (q_c, k_c, v_c, g_c))
    s_o = jnp.einsum("nqd,nkd->nqk", q_n, k_n, preferred_element_type=F32) * scale
    w_o = jnp.where(small_causal, jnp.exp(s_o - l_c.reshape(-1, length, 1)), 0.0)
    d_o = jnp.einsum("nqd,nkd->nqk", g_n, v_n, preferred_element_type=F32)
    inner = jnp.sum(w_c * d_c, axis=-1, keepdims=True) + jnp.sum(w_o * d_o, axis=-1).reshape(-1, 1)
    ds_c = (w_c * (d_c - inner)).astype(BF)
    ds_o = (w_o * (d_o - inner.reshape(-1, length, 1))).astype(BF)

    def over(eq, a, b):
        return jnp.einsum(eq, a, b, preferred_element_type=F32)

    dq_p = mm(ds_p, k_p)
    dq_c = mm(ds_c, k_p) + over("nqk,nkd->nqd", ds_o, k_n).reshape(q_c.shape)
    dk_p = mm_tn(ds_p, q_p) + mm_tn(ds_c, q_c)
    dk_c = over("nqk,nqd->nkd", ds_o, q_n).reshape(q_c.shape)
    dv_p = mm_tn(w_p.astype(BF), g_p) + mm_tn(w_c.astype(BF), g_c)
    dv_c = over("nqk,nqd->nkd", w_o.astype(BF), g_n).reshape(q_c.shape)
    return (
        jnp.concatenate([dq_p, dq_c]) * scale,
        jnp.concatenate([dk_p, dk_c]) * scale,
        jnp.concatenate([dv_p, dv_c]),
    )


def per_device(
    block_input,
    cotangent,
    routes,
    w_query,
    w_key,
    w_value,
    w_output,
    w_router,
    gain_attn,
    gain_query,
    gain_key,
    gain_mlp,
    w_gate,
    w_up,
    w_down,
):
    rows, width = block_input.shape
    top_count = routes.shape[1]
    ep_count = lax.axis_size("ep")
    grp_count = lax.axis_size("grp")
    me = lax.axis_index("ep")
    my_group = lax.axis_index("grp")
    tokens = rows * ep_count
    prompt_len = tokens // 2
    capacity = min(rows, rows * top_count * 33 // (32 * ep_count))
    cols = width // ep_count
    scale = HEAD_DIM ** (-0.5)
    depth = w_query.shape[0]

    chosen = jnp.any(routes[:, :, None] == jnp.arange(ep_count, dtype=jnp.int32), axis=1)
    per_row = 128
    router_rows = depth * ep_count // per_row
    gains = jnp.concatenate([gain_attn, gain_query, gain_key, gain_mlp])
    gain_rows = gains.shape[0] // per_row
    small = jnp.concatenate(
        [
            w_router.reshape(router_rows, per_row),
            gains.reshape(gain_rows, per_row),
            jnp.zeros((16 - router_rows - gain_rows, per_row), BF),
            chosen.T.astype(BF),
        ]
    )
    weights = jnp.stack([w_query, w_key, w_value])
    full_output = lax.all_gather(w_output, ("grp", "ep"), axis=0, tiled=True)
    cot_both = lax.all_gather(cotangent, ("grp", "ep"), axis=0, tiled=True)

    x_all, w_cols, smalls = gather_inputs(ep_count, block_input, weights, small)
    x_all = x_all.reshape(tokens, width)
    w_q, w_k, w_v = (w_cols[:, :, i].reshape(width, cols) for i in range(3))
    smalls = smalls.reshape(grp_count * ep_count, small.shape[0], per_row)
    full_router = smalls[:, :router_rows].reshape(width, ep_count)
    gains = smalls[:, router_rows : router_rows + gain_rows].reshape(-1, 4, depth).transpose(1, 0, 2).reshape(4, width)
    gain_first, gain_qnorm, gain_knorm, gain_second = (gains[i].astype(F32) for i in range(4))
    chosen_all = smalls[:, 16:].reshape(grp_count, ep_count, ep_count, rows)

    token = jnp.arange(tokens, dtype=jnp.int32)
    position = jnp.where(token < prompt_len, token, prompt_len + (token - prompt_len) % rows)
    cosine, sine = angles_of(position)
    x_wide = x_all.astype(F32)
    normed_all = rms_scale(x_wide, gain_first).astype(BF)
    q_lin = mm(normed_all, w_q)
    k_lin = mm(normed_all, w_k)
    value = mm(normed_all, w_v).astype(BF)
    squares = jnp.stack([jnp.sum(q_lin * q_lin, axis=-1), jnp.sum(k_lin * k_lin, axis=-1)])
    squares = jnp.sum(spread(ep_count, squares.reshape(-1, per_row), "spread_squares", 2), axis=0).reshape(2, tokens)
    r_q, r_k = (lax.rsqrt(squares[i] / width + eps)[:, None] for i in range(2))
    gain_q = lax.dynamic_slice(gain_qnorm, (me * cols,), (cols,))
    gain_k = lax.dynamic_slice(gain_knorm, (me * cols,), (cols,))
    n_q, n_k = q_lin * r_q, k_lin * r_k
    query = turn(n_q * gain_q, cosine, sine).astype(BF)
    key = turn(n_k * gain_k, cosine, sine).astype(BF)
    attended, logs = attend(query, key, value, prompt_len, rows, scale)
    tiles = exchange(ep_count, attended.astype(BF).reshape(ep_count, rows, cols), "exchange_attended", 3)
    att_loc = tiles.transpose(1, 0, 2).reshape(rows, width)

    inputs = block_input.astype(F32)
    residual = inputs + mm(att_loc, full_output)
    r_m = lax.rsqrt(jnp.mean(residual * residual, axis=-1, keepdims=True) + eps)
    n_m = residual * r_m
    normed_mlp = (n_m * gain_second).astype(BF)
    own_rows, other_rows = gather_both(ep_count, normed_mlp, "gather_normed", 4)

    pair = 2 * rows
    slots = -(-2 * capacity // 16) * 16
    chips = ep_count // 2

    def picks(group):
        mine = lax.dynamic_index_in_dim(chosen_all, group, 0, keepdims=False)[:, me]
        mine = mine.reshape(chips, pair)
        slot = jnp.cumsum(mine.astype(jnp.int32), axis=1) - 1
        hot = (slot[:, None, :] == jnp.arange(slots, dtype=jnp.int32)[None, :, None]) & (mine[:, None, :] > 0)
        return hot

    def gate_of(normed_rows):
        probs = jax.nn.softmax(mm(normed_rows, full_router), axis=-1)
        return lax.dynamic_index_in_dim(probs, me, 1, keepdims=False)

    def take(hot, values):
        return jnp.einsum(
            "csp,cpd->csd", hot, values.reshape(chips, pair, width), preferred_element_type=F32
        ).astype(BF).reshape(-1, width)

    def give(hot, values):
        return jnp.einsum(
            "csp,csd->cpd", hot, values.reshape(chips, slots, width), preferred_element_type=F32
        ).reshape(tokens, width)

    gate_w, up_w, down_w = w_gate[0], w_up[0], w_down[0]
    cot_both = cot_both.reshape(grp_count, tokens, width)

    def expert(normed_rows, cot_rows, group):
        hot = picks(group)
        hot_low = hot.astype(BF)
        gate = gate_of(normed_rows)
        gate_rows = jnp.sum(jnp.where(hot, gate.reshape(chips, 1, pair), 0.0), axis=2).reshape(-1, 1)
        units = take(hot_low, normed_rows)
        cot_units = take(hot_low, cot_rows).astype(F32)
        grad_out = (gate_rows * cot_units).astype(BF)
        gate_pre = mm(units, gate_w)
        up_pre = mm(units, up_w)
        sigma = jax.nn.sigmoid(gate_pre)
        hidden = (gate_pre * sigma * up_pre).astype(BF)
        grad_hidden = mm_nt(grad_out, down_w)
        grad_gate_pre = (grad_hidden * up_pre * sigma * (1.0 + gate_pre * (1.0 - sigma))).astype(BF)
        grad_up_pre = (grad_hidden * gate_pre * sigma).astype(BF)
        return hot, hot_low, gate, units, cot_units, grad_out, hidden, grad_gate_pre, grad_up_pre

    own_rows = own_rows.reshape(tokens, width)
    cot_own = lax.dynamic_index_in_dim(cot_both, my_group, 0, keepdims=False)
    hot, hot_low, gate, units, cot_units, grad_out, hidden, grad_gate_pre, grad_up_pre = expert(
        own_rows, cot_own, my_group
    )
    result = mm(hidden, down_w).astype(BF)
    gate_grad_rows = jnp.sum(cot_units * result.astype(F32), axis=-1).reshape(chips, slots, 1)
    gate_grad = jnp.sum(jnp.where(hot, gate_grad_rows, 0.0), axis=1).reshape(ep_count, 1, rows)
    grad_units = (mm_nt(grad_gate_pre, gate_w) + mm_nt(grad_up_pre, up_w)).astype(BF)
    partial_units = give(hot_low, grad_units).astype(BF).reshape(ep_count, rows, width)
    partial_result = (gate[:, None] * give(hot_low, result)).astype(BF)
    mixture = lax.psum_scatter(partial_result, "ep", scatter_dimension=0, tiled=True).astype(F32)
    block_output = (residual + mixture).astype(BF)
    d_normed_mlp = scatter_sum(ep_count, partial_units, "scatter_units", 5)
    gate_grads = exchange(
        ep_count, jnp.broadcast_to(gate_grad, (ep_count, 8, rows)), "exchange_gate_grads", 6
    )[:, 0]

    _, _, _, units_2, _, grad_out_2, hidden_2, grad_gate_pre_2, grad_up_pre_2 = expert(
        other_rows.reshape(tokens, width),
        lax.dynamic_index_in_dim(cot_both, 1 - my_group, 0, keepdims=False),
        1 - my_group,
    )
    grad_gate = (mm_tn(units, grad_gate_pre) + mm_tn(units_2, grad_gate_pre_2))[None]
    grad_up = (mm_tn(units, grad_up_pre) + mm_tn(units_2, grad_up_pre_2))[None]
    grad_down = (mm_tn(hidden, grad_out) + mm_tn(hidden_2, grad_out_2))[None]

    probs = jax.nn.softmax(mm(normed_mlp, full_router), axis=-1)
    d_probs = gate_grads.T
    d_logits = (probs * (d_probs - jnp.sum(probs * d_probs, axis=-1, keepdims=True))).astype(BF)
    local_router = mm_tn(normed_mlp, d_logits)
    d_normed_mlp = d_normed_mlp + mm_nt(d_logits, full_router)
    local_gain_mlp = jnp.sum(d_normed_mlp * n_m, axis=0)
    d_n = d_normed_mlp * gain_second
    d_residual = cotangent.astype(F32) + r_m * (d_n - n_m * jnp.mean(n_m * d_n, axis=-1, keepdims=True))
    d_proj = d_residual.astype(BF)
    d_attended = mm_nt(d_proj, full_output).astype(BF)
    local_output = mm_tn(att_loc, d_proj).astype(BF)
    grad_output = lax.psum_scatter(local_output, ("grp", "ep"), scatter_dimension=0, tiled=True).astype(F32)
    d_attended = exchange(
        ep_count, d_attended.reshape(rows, ep_count, cols).transpose(1, 0, 2), "exchange_d_attended", 7
    ).reshape(tokens, cols)

    d_query, d_key, d_value = attend_back(query, key, value, d_attended, logs, prompt_len, rows, scale)
    d_query = turn(d_query, cosine, -sine)
    d_key = turn(d_key, cosine, -sine)
    gain_grad_q = jnp.sum(d_query * n_q, axis=0)
    gain_grad_k = jnp.sum(d_key * n_k, axis=0)
    d_nq, d_nk = d_query * gain_q, d_key * gain_k
    dots = jnp.stack([jnp.sum(d_nq * n_q, axis=-1), jnp.sum(d_nk * n_k, axis=-1)])
    dots = jnp.sum(spread(ep_count, dots.reshape(-1, per_row), "spread_dots", 8), axis=0).reshape(2, tokens) / width
    d_q_lin = (r_q * (d_nq - n_q * dots[0][:, None])).astype(BF)
    d_k_lin = (r_k * (d_nk - n_k * dots[1][:, None])).astype(BF)
    d_v_lin = d_value.astype(BF)
    d_lin = jnp.concatenate([d_q_lin, d_k_lin, d_v_lin], axis=1)
    w_all = jnp.concatenate([w_q, w_k, w_v], axis=1)
    partial_normed = mm_nt(d_lin, w_all).astype(BF).reshape(ep_count, rows, width)
    d_normed = scatter_sum(ep_count, partial_normed, "scatter_normed", 9)
    r_a = lax.rsqrt(jnp.mean(inputs * inputs, axis=-1, keepdims=True) + eps)
    n_a = inputs * r_a
    local_gain_attn = jnp.sum(d_normed * n_a, axis=0)
    d_n = d_normed * gain_first
    input_grad = d_residual + r_a * (d_n - n_a * jnp.mean(n_a * d_n, axis=-1, keepdims=True))

    grad_w = mm_tn(normed_all, d_lin).astype(BF)
    grad_w = lax.psum_scatter(
        grad_w.reshape(grp_count, ep_count * depth, 3 * cols), "grp", scatter_dimension=0, tiled=True
    )
    grad_w = exchange(ep_count, grad_w.reshape(ep_count, depth, 3 * cols), "exchange_grad_w", 10)
    grad_w = grad_w.reshape(ep_count, depth, 3, cols).transpose(2, 1, 0, 3).reshape(3, depth, width).astype(F32)
    grad_router = lax.psum_scatter(local_router, ("grp", "ep"), scatter_dimension=0, tiled=True)
    zeros = jnp.zeros((width,), F32)
    gain_sums = jnp.stack(
        [
            local_gain_attn,
            lax.dynamic_update_slice(zeros, gain_grad_q, (me * cols,)),
            lax.dynamic_update_slice(zeros, gain_grad_k, (me * cols,)),
            local_gain_mlp,
        ]
    )
    gain_sums = lax.psum(gain_sums, ("grp", "ep"))
    gain_sums = lax.dynamic_slice(gain_sums, (0, (my_group * ep_count + me) * depth), (4, depth))
    return (
        block_output,
        input_grad,
        grad_w[0],
        grad_w[1],
        grad_w[2],
        grad_output,
        grad_router,
        gain_sums[0],
        gain_sums[1],
        gain_sums[2],
        gain_sums[3],
        grad_gate,
        grad_up,
        grad_down,
    )


def plain_scale(values, gain_vec):
    return values * lax.rsqrt(jnp.mean(values * values, axis=-1, keepdims=True) + eps) * gain_vec


def rotate(values, position):
    token_count = values.shape[0]
    by_head = values.reshape(token_count, -1, HEAD_DIM)
    half_dim = HEAD_DIM // 2
    frequency = theta_base ** (-2.0 * jnp.arange(half_dim, dtype=jnp.float32) / HEAD_DIM)
    angles = position.astype(jnp.float32)[:, None] * frequency[None, :]
    cosine = jnp.cos(angles)[:, None, :]
    sine_part = jnp.sin(angles)[:, None, :]
    former = by_head[..., :half_dim]
    latter = by_head[..., half_dim:]
    turned = jnp.concatenate(
        [former * cosine - latter * sine_part, latter * cosine + former * sine_part], axis=-1
    )
    return turned.reshape(token_count, -1)


def masked_scores(query, keys, allowed, scale):
    raw_scores = jnp.einsum("qhd,khd->hqk", query, keys, preferred_element_type=jnp.float32) * scale
    return jnp.where(allowed[None], raw_scores, -1e30)


def plain_attend(query, keys, values, allowed, scale, head_group):
    outputs = []
    log_totals = []
    for head_start in range(0, query.shape[1], head_group):
        head_slice = slice(head_start, head_start + head_group)
        scores = masked_scores(query[:, head_slice], keys[:, head_slice], allowed, scale)
        largest = jnp.max(scores, axis=-1, keepdims=True)
        exponent = jnp.exp(scores - largest)
        summed = jnp.sum(exponent, axis=-1, keepdims=True)
        weights = (exponent / summed).astype(jnp.bfloat16)
        outputs.append(
            jnp.einsum(
                "hqk,khd->qhd", weights, values[:, head_slice], preferred_element_type=jnp.float32
            )
        )
        log_totals.append(largest + jnp.log(summed))
    return (jnp.concatenate(outputs, axis=1), jnp.concatenate(log_totals, axis=0))


def plain_attend_back(query, keys, values, grad_out, log_totals, allowed, scale, head_group):
    query_grads = []
    key_grads = []
    value_grads = []
    for head_start in range(0, query.shape[1], head_group):
        head_slice = slice(head_start, head_start + head_group)
        query_part = query[:, head_slice]
        keys_part = keys[:, head_slice]
        grad_part = grad_out[:, head_slice]
        scores = masked_scores(query_part, keys_part, allowed, scale)
        weights = jnp.where(allowed[None], jnp.exp(scores - log_totals[head_slice]), 0.0)
        grad_weights = jnp.einsum(
            "qhd,khd->hqk", grad_part, values[:, head_slice], preferred_element_type=jnp.float32
        )
        inner = jnp.sum(weights * grad_weights, axis=-1, keepdims=True)
        grad_scores = (weights * (grad_weights - inner)).astype(jnp.bfloat16)
        query_grads.append(
            jnp.einsum("hqk,khd->qhd", grad_scores, keys_part, preferred_element_type=jnp.float32)
            * scale
        )
        key_grads.append(
            jnp.einsum("hqk,qhd->khd", grad_scores, query_part, preferred_element_type=jnp.float32)
            * scale
        )
        value_grads.append(
            jnp.einsum(
                "hqk,qhd->khd",
                weights.astype(jnp.bfloat16),
                grad_part,
                preferred_element_type=jnp.float32,
            )
        )
    return (
        jnp.concatenate(query_grads, axis=1),
        jnp.concatenate(key_grads, axis=1),
        jnp.concatenate(value_grads, axis=1),
    )


def per_device_plain(
    block_input,
    cotangent,
    routes,
    w_query,
    w_key,
    w_value,
    w_output,
    w_router,
    gain_attn,
    gain_query,
    gain_key,
    gain_mlp,
    w_gate,
    w_up,
    w_down,
):
    row_count, model_width = block_input.shape
    top_count = routes.shape[1]
    ep_count = lax.axis_size("ep")
    my_index = lax.axis_index("ep")
    half_count = ep_count // 2
    prompt_len = row_count * half_count
    capacity = min(row_count, row_count * top_count * 33 // (32 * ep_count))
    head_count = model_width // HEAD_DIM
    head_group = math.gcd(4, head_count)
    scale = HEAD_DIM ** (-0.5)
    gathered = (
        lax.all_gather(w_query, ("grp", "ep"), axis=0, tiled=True),
        lax.all_gather(w_key, ("grp", "ep"), axis=0, tiled=True),
        lax.all_gather(w_value, ("grp", "ep"), axis=0, tiled=True),
        lax.all_gather(w_output, ("grp", "ep"), axis=0, tiled=True),
        lax.all_gather(w_router, ("grp", "ep"), axis=0, tiled=True),
        lax.all_gather(gain_attn, ("grp", "ep"), axis=0, tiled=True),
        lax.all_gather(gain_query, ("grp", "ep"), axis=0, tiled=True),
        lax.all_gather(gain_key, ("grp", "ep"), axis=0, tiled=True),
        lax.all_gather(gain_mlp, ("grp", "ep"), axis=0, tiled=True),
    )
    full_query, full_key, full_value, full_output, full_router = (
        gathered[0],
        gathered[1],
        gathered[2],
        gathered[3],
        gathered[4],
    )
    gain_first = gathered[5].astype(jnp.float32)
    gain_qnorm = gathered[6].astype(jnp.float32)
    gain_knorm = gathered[7].astype(jnp.float32)
    gain_second = gathered[8].astype(jnp.float32)
    offsets = jnp.arange(row_count, dtype=jnp.int32)
    in_prompt = my_index < half_count
    position = jnp.where(in_prompt, my_index * row_count + offsets, prompt_len + offsets)
    key_position = jnp.concatenate([jnp.arange(prompt_len, dtype=jnp.int32), prompt_len + offsets])
    from_prompt = jnp.arange(prompt_len + row_count, dtype=jnp.int32) < prompt_len
    allowed = (key_position[None, :] <= position[:, None]) & (
        from_prompt[None, :] | jnp.logical_not(in_prompt)
    )

    def prepare(linear, gain_vec):
        return rotate(plain_scale(linear, gain_vec), position)

    inputs = block_input.astype(jnp.float32)
    normed = plain_scale(inputs, gain_first).astype(jnp.bfloat16)
    query_lin = jnp.dot(normed, full_query, preferred_element_type=jnp.float32)
    key_lin = jnp.dot(normed, full_key, preferred_element_type=jnp.float32)
    value_lin = jnp.dot(normed, full_value, preferred_element_type=jnp.float32)
    query_low = prepare(query_lin, gain_qnorm).astype(jnp.bfloat16)
    key_low = prepare(key_lin, gain_knorm).astype(jnp.bfloat16)
    value_low = value_lin.astype(jnp.bfloat16)
    shared = (
        lax.all_gather(key_low, "ep", axis=0, tiled=True),
        lax.all_gather(value_low, "ep", axis=0, tiled=True),
    )
    keys = jnp.concatenate([shared[0][:prompt_len], key_low]).reshape(-1, head_count, HEAD_DIM)
    values = jnp.concatenate([shared[1][:prompt_len], value_low]).reshape(-1, head_count, HEAD_DIM)
    query = query_low.reshape(row_count, head_count, HEAD_DIM)
    attn_out, log_totals = plain_attend(query, keys, values, allowed, scale, head_group)
    attended = attn_out.reshape(row_count, model_width).astype(jnp.bfloat16)
    residual = inputs + jnp.dot(attended, full_output, preferred_element_type=jnp.float32)
    normed_mlp = plain_scale(residual, gain_second).astype(jnp.bfloat16)
    logits = jnp.dot(normed_mlp, full_router, preferred_element_type=jnp.float32)
    probs = jax.nn.softmax(logits, axis=-1)
    picks = routes[:, :, None] == jnp.arange(ep_count, dtype=jnp.int32)[None, None, :]
    gates = jnp.sum(jnp.where(picks, probs[:, None, :], 0.0), axis=-1)
    hot_table = picks.reshape(-1, ep_count).astype(jnp.int32)
    before = jnp.cumsum(hot_table, axis=0) - hot_table
    slot_index = jnp.sum(before * hot_table, axis=1)
    target = routes.reshape(-1) * capacity + slot_index
    sentinel = row_count * top_count
    source = (
        jnp.full((ep_count * capacity,), sentinel, jnp.int32)
        .at[target]
        .set(jnp.arange(sentinel, dtype=jnp.int32))
    )
    token_of = source // top_count
    padded_rows = jnp.concatenate([normed_mlp, jnp.zeros((1, model_width), jnp.bfloat16)])
    outgoing = padded_rows[token_of].reshape(ep_count, capacity, model_width)
    arrived = lax.all_to_all(outgoing, "ep", split_axis=0, concat_axis=0, tiled=True)
    units = arrived.reshape(-1, model_width)
    gate_w = w_gate[0]
    up_w = w_up[0]
    down_w = w_down[0]
    gate_pre = jnp.dot(units, gate_w, preferred_element_type=jnp.float32)
    up_pre = jnp.dot(units, up_w, preferred_element_type=jnp.float32)
    hidden = (jax.nn.silu(gate_pre) * up_pre).astype(jnp.bfloat16)
    expert_result = jnp.dot(hidden, down_w, preferred_element_type=jnp.float32).astype(jnp.bfloat16)
    returned = lax.all_to_all(
        expert_result.reshape(ep_count, capacity, model_width),
        "ep",
        split_axis=0,
        concat_axis=0,
        tiled=True,
    )
    picked = (
        returned.reshape(-1, model_width)[target]
        .reshape(row_count, top_count, model_width)
        .astype(jnp.float32)
    )
    output_full = residual + jnp.sum(gates[:, :, None] * picked, axis=1)
    block_output = output_full.astype(jnp.bfloat16)
    back_query, back_key, back_value, back_output, back_router = (
        full_query,
        full_key,
        full_value,
        full_output,
        full_router,
    )
    grad_top = cotangent.astype(jnp.float32)
    grad_gates = jnp.sum(grad_top[:, None, :] * picked, axis=-1)
    grad_expert = (
        (gates[:, :, None] * grad_top[:, None, :]).astype(jnp.bfloat16).reshape(-1, model_width)
    )
    padded_grads = jnp.concatenate([grad_expert, jnp.zeros((1, model_width), jnp.bfloat16)])
    grad_outgoing = padded_grads[source].reshape(ep_count, capacity, model_width)
    grad_arrived = lax.all_to_all(
        grad_outgoing, "ep", split_axis=0, concat_axis=0, tiled=True
    ).reshape(-1, model_width)
    grad_hidden = jnp.einsum("nd,fd->nf", grad_arrived, down_w, preferred_element_type=jnp.float32)
    sigma = jax.nn.sigmoid(gate_pre)
    grad_gate_pre = (grad_hidden * up_pre * sigma * (1.0 + gate_pre * (1.0 - sigma))).astype(
        jnp.bfloat16
    )
    grad_up_pre = (grad_hidden * gate_pre * sigma).astype(jnp.bfloat16)
    local_down = jnp.einsum("nf,nd->fd", hidden, grad_arrived, preferred_element_type=jnp.float32)
    local_gate = jnp.einsum("nd,nf->df", units, grad_gate_pre, preferred_element_type=jnp.float32)
    local_up = jnp.einsum("nd,nf->df", units, grad_up_pre, preferred_element_type=jnp.float32)
    grad_units = jnp.einsum("nf,df->nd", grad_gate_pre, gate_w, preferred_element_type=jnp.float32)
    grad_units = grad_units + jnp.einsum(
        "nf,df->nd", grad_up_pre, up_w, preferred_element_type=jnp.float32
    )
    grad_units = grad_units.astype(jnp.bfloat16).reshape(ep_count, capacity, model_width)
    grad_returned = lax.all_to_all(
        grad_units, "ep", split_axis=0, concat_axis=0, tiled=True
    ).reshape(-1, model_width)
    grad_normed_mlp = jnp.sum(
        grad_returned[target].reshape(row_count, top_count, model_width).astype(jnp.float32), axis=1
    )
    expert_sums = (
        lax.psum(local_gate[None].astype(jnp.bfloat16), "grp").astype(jnp.float32),
        lax.psum(local_up[None].astype(jnp.bfloat16), "grp").astype(jnp.float32),
        lax.psum(local_down[None].astype(jnp.bfloat16), "grp").astype(jnp.float32),
    )
    grad_probs = jnp.sum(jnp.where(picks, grad_gates[:, :, None], 0.0), axis=1)
    grad_logits = (
        probs * (grad_probs - jnp.sum(probs * grad_probs, axis=-1, keepdims=True))
    ).astype(jnp.bfloat16)
    local_router = jnp.einsum(
        "rd,re->de", normed_mlp, grad_logits, preferred_element_type=jnp.float32
    )
    grad_normed_mlp = grad_normed_mlp + jnp.einsum(
        "re,de->rd", grad_logits, back_router, preferred_element_type=jnp.float32
    )
    unused_mlp, second_back = jax.vjp(plain_scale, residual, gain_second)
    grad_from_mlp, local_gain_mlp = second_back(grad_normed_mlp)
    grad_residual = grad_top + grad_from_mlp
    grad_proj = grad_residual.astype(jnp.bfloat16)
    local_output = jnp.einsum("rd,re->de", attended, grad_proj, preferred_element_type=jnp.float32)
    grad_attended = jnp.einsum(
        "re,de->rd", grad_proj, back_output, preferred_element_type=jnp.float32
    )
    grad_attended = grad_attended.astype(jnp.bfloat16).reshape(row_count, head_count, HEAD_DIM)
    grad_query_rot, grad_keys, grad_values = plain_attend_back(
        query, keys, values, grad_attended, log_totals, allowed, scale, head_group
    )
    grad_keys = grad_keys.reshape(-1, model_width)
    grad_values = grad_values.reshape(-1, model_width)
    padding = jnp.zeros((ep_count * row_count - prompt_len, model_width), jnp.float32)
    key_share, value_share = (
        lax.psum_scatter(
            jnp.concatenate([grad_keys[:prompt_len], padding]).astype(jnp.bfloat16),
            "ep",
            scatter_dimension=0,
            tiled=True,
        ).astype(jnp.float32),
        lax.psum_scatter(
            jnp.concatenate([grad_values[:prompt_len], padding]).astype(jnp.bfloat16),
            "ep",
            scatter_dimension=0,
            tiled=True,
        ).astype(jnp.float32),
    )
    grad_key_rot = key_share + grad_keys[prompt_len:]
    grad_value_lin = (value_share + grad_values[prompt_len:]).astype(jnp.bfloat16)
    unused_query, query_back = jax.vjp(prepare, query_lin, gain_qnorm)
    grad_query_lin, local_gain_query = query_back(grad_query_rot.reshape(row_count, model_width))
    unused_key, key_back = jax.vjp(prepare, key_lin, gain_knorm)
    grad_key_lin, local_gain_key = key_back(grad_key_rot)
    grad_query_low = grad_query_lin.astype(jnp.bfloat16)
    grad_key_low = grad_key_lin.astype(jnp.bfloat16)
    local_query = jnp.einsum(
        "rd,re->de", normed, grad_query_low, preferred_element_type=jnp.float32
    )
    local_key = jnp.einsum("rd,re->de", normed, grad_key_low, preferred_element_type=jnp.float32)
    local_value = jnp.einsum(
        "rd,re->de", normed, grad_value_lin, preferred_element_type=jnp.float32
    )
    grad_normed = jnp.einsum(
        "re,de->rd", grad_query_low, back_query, preferred_element_type=jnp.float32
    )
    grad_normed = grad_normed + jnp.einsum(
        "re,de->rd", grad_key_low, back_key, preferred_element_type=jnp.float32
    )
    grad_normed = grad_normed + jnp.einsum(
        "re,de->rd", grad_value_lin, back_value, preferred_element_type=jnp.float32
    )
    unused_first, first_back = jax.vjp(plain_scale, inputs, gain_first)
    grad_from_attn, local_gain_attn = first_back(grad_normed)
    input_grad = grad_residual + grad_from_attn
    summed_grads = (
        lax.psum_scatter(local_query, ("grp", "ep"), scatter_dimension=0, tiled=True),
        lax.psum_scatter(local_key, ("grp", "ep"), scatter_dimension=0, tiled=True),
        lax.psum_scatter(local_value, ("grp", "ep"), scatter_dimension=0, tiled=True),
        lax.psum_scatter(local_output, ("grp", "ep"), scatter_dimension=0, tiled=True),
        lax.psum_scatter(local_router, ("grp", "ep"), scatter_dimension=0, tiled=True),
        lax.psum_scatter(local_gain_attn, ("grp", "ep"), scatter_dimension=0, tiled=True),
        lax.psum_scatter(local_gain_query, ("grp", "ep"), scatter_dimension=0, tiled=True),
        lax.psum_scatter(local_gain_key, ("grp", "ep"), scatter_dimension=0, tiled=True),
        lax.psum_scatter(local_gain_mlp, ("grp", "ep"), scatter_dimension=0, tiled=True),
    )
    return (
        block_output,
        input_grad,
        summed_grads[0],
        summed_grads[1],
        summed_grads[2],
        summed_grads[3],
        summed_grads[4],
        summed_grads[5],
        summed_grads[6],
        summed_grads[7],
        summed_grads[8],
        expert_sums[0],
        expert_sums[1],
        expert_sums[2],
    )


def solution(mesh):
    both = ("grp", "ep")
    return jax.shard_map(
        per_device if mesh.shape["grp"] == 2 else per_device_plain,
        mesh=mesh,
        in_specs=(P(both, None),) * 8 + (P(both),) * 4 + (P("ep", None, None),) * 3,
        out_specs=(P(both, None),) * 7 + (P(both),) * 4 + (P("ep", None, None),) * 3,
        check_vma=False,
    )
```

```python
import math

import jax
import jax.numpy as jnp
from jax import lax
from jax.experimental import pallas as pl
from jax.experimental.pallas import tpu as pltpu
from jax.sharding import PartitionSpec as P

HEAD_DIM = 128
MESH = pl.DeviceIdType.MESH
BF = jnp.bfloat16
F32 = jnp.float32


eps = 1e-05
theta_base = 10000.0


def mm(a, b):
    return jnp.dot(a, b, preferred_element_type=F32)


def mm_nt(a, b):
    return lax.dot_general(a, b, (((1,), (1,)), ((), ())), preferred_element_type=F32)


def mm_tn(a, b):
    return lax.dot_general(a, b, (((0,), (0,)), ((), ())), preferred_element_type=F32)


class Place:
    def __init__(self, ep_count):
        self.grp = lax.axis_index("grp")
        self.ep = lax.axis_index("ep")
        self.count = ep_count
        self.ring = ep_count // 2
        self.half = self.ring // 2
        self.core = self.ep % 2
        y = (self.ep // 2) % 2
        z = self.ep // 4
        self.place = z + y * (self.ring - 1 - 2 * z)

    def index(self, place, core):
        y = place // self.half
        z = place + y * (self.ring - 1 - 2 * place)
        return (z * 2 + y) * 2 + core

    def at(self, offset):
        return (self.place + offset + self.ring) % self.ring

    def chip(self, offset):
        return self.index(self.at(offset), self.core)

    def right(self):
        return (self.grp, self.chip(1))

    def left(self):
        return (self.grp, self.chip(-1))

    def sibling(self):
        return (self.grp, self.index(self.place, 1 - self.core))

    def across(self):
        return (1 - self.grp, self.ep)

    def peer(self, offset):
        return (self.grp, (self.ep + offset + self.count) % self.count)


def greet(devices):
    barrier = pltpu.get_barrier_semaphore()
    for device in devices:
        pl.semaphore_signal(barrier, inc=1, device_id=device, device_id_type=MESH)
    pl.semaphore_wait(barrier, len(devices))


def remote(src, dst, send, recv, device):
    return pltpu.make_async_remote_copy(
        src_ref=src, dst_ref=dst, send_sem=send, recv_sem=recv, device_id=device, device_id_type=MESH
    )


class Gather:
    def __init__(self, here, src, dst, sems):
        self.here, self.src, self.dst = here, src, dst
        self.ring_send, self.ring_recv, self.side_send, self.side_recv, self.own_sem = sems
        self.rows = dst.shape[1] // 2
        self.far = here.ring // 2
        self.started = []

    @staticmethod
    def scratch(ep_count):
        far = ep_count // 4
        ring = pltpu.SemaphoreType.DMA((2, far, 2))
        side = pltpu.SemaphoreType.DMA((2, far + 1, 2))
        return [ring, ring, side, side, pltpu.SemaphoreType.DMA]

    def block(self, index, part):
        return self.dst.at[index, pl.ds(part * self.rows, self.rows)]

    def go(self, copy):
        copy.start()
        self.started.append(copy)

    def hops(self, way, part):
        return self.far if way == part else self.far - 1

    def ring_copy(self, way, step, part, src, index):
        device = self.here.right() if way == 0 else self.here.left()
        return remote(
            src, self.block(index, part), self.ring_send.at[way, step, part], self.ring_recv.at[way, step, part], device
        )

    def side_copy(self, way, step, part, src, index):
        return remote(
            src,
            self.block(index, part),
            self.side_send.at[way, step, part],
            self.side_recv.at[way, step, part],
            self.here.sibling(),
        )

    def start(self):
        here = self.here
        for part in range(2):
            src = self.src.at[pl.ds(part * self.rows, self.rows)]
            for way in range(2):
                if self.hops(way, part) > 0:
                    self.go(self.ring_copy(way, 0, part, src, here.ep))
            self.go(self.side_copy(0, 0, part, src, here.ep))
        self.own = pltpu.make_async_copy(self.src, self.dst.at[here.ep], self.own_sem)
        self.own.start()

    def step(self, step):
        here = self.here
        for part in range(2):
            for way in range(2):
                if step < self.hops(way, part):
                    index = here.chip(-1 - step if way == 0 else 1 + step)
                    src = self.block(index, part)
                    self.ring_copy(way, step, part, src, index).wait_recv()
                    if step + 1 < self.hops(way, part):
                        self.go(self.ring_copy(way, step + 1, part, src, index))
                    self.go(self.side_copy(way, step + 1, part, src, index))

    def side(self, step):
        here = self.here
        for part in range(2):
            for way in range(2):
                if (step < 0 and way == 0) or (0 <= step < self.hops(way, part)):
                    offset = 0 if step < 0 else (-1 - step if way == 0 else 1 + step)
                    index = here.index(here.at(offset), 1 - here.core)
                    self.side_copy(way, step + 1, part, self.block(index, part), index).wait_recv()

    def settle(self):
        self.own.wait()

    def finish(self):
        for copy in self.started:
            copy.wait_send()


class Exchange:
    def __init__(self, here, src, dst, sems):
        self.here, self.src, self.dst = here, src, dst
        self.send, self.recv, self.own_sem = sems

    @staticmethod
    def scratch(ep_count):
        return [
            pltpu.SemaphoreType.DMA((ep_count,)),
            pltpu.SemaphoreType.DMA((ep_count,)),
            pltpu.SemaphoreType.DMA,
        ]

    def start(self):
        here = self.here
        self.own = pltpu.make_async_copy(self.src(here.ep), self.dst(here.ep), self.own_sem)
        self.own.start()
        self.copies = []
        for offset in range(1, here.count):
            device = here.peer(offset)
            copy = remote(self.src(device[1]), self.dst(here.ep), self.send.at[offset], self.recv.at[offset], device)
            copy.start()
            self.copies.append(copy)

    def arrive(self):
        here = self.here
        self.own.wait()
        for offset in range(1, here.count):
            source = here.peer(-offset)[1]
            remote(
                self.dst(source), self.dst(source), self.send.at[offset], self.recv.at[offset], here.peer(offset)
            ).wait_recv()

    def finish(self):
        for copy in self.copies:
            copy.wait_send()


def far_devices(here):
    return [(1 - here.grp, (here.ep + offset) % here.count) for offset in range(here.count)]


def ring_devices(here):
    return [here.right(), here.left(), here.sibling()]


def plane_devices(here):
    return [here.peer(offset) for offset in range(1, here.count)]


def comm_call(kernel, out_shape, scratch, name, collective_id, operands, vmem=False):
    space = pltpu.VMEM if vmem else pl.ANY
    spec = pl.BlockSpec(memory_space=space)
    out_spec = [spec] * len(out_shape) if isinstance(out_shape, (list, tuple)) else spec
    return pl.pallas_call(
        kernel,
        out_shape=out_shape,
        in_specs=[spec] * len(operands),
        out_specs=out_spec,
        scratch_shapes=scratch,
        compiler_params=pltpu.CompilerParams(
            collective_id=collective_id, has_side_effects=True, vmem_limit_bytes=56 << 20
        ),
        name=name,
    )(*operands)


def split(refs, *sizes):
    groups, start = [], 0
    for size in sizes:
        groups.append(refs[start : start + size])
        start += size
    return groups


def gather_inputs(ep_count, rows_block, weights, small):
    rows, width = rows_block.shape
    kinds, depth, columns = weights.shape
    mine = columns // ep_count
    small_rows = small.shape[0]

    def kernel(x_ref, w_ref, s_ref, x_out, w_out, s_out, *scratch):
        gather_sems, w_sems, s_sems, cross = split(scratch, 5, 3, 3, 4)
        here = Place(ep_count)
        greet(plane_devices(here) + [here.across()])
        first = pltpu.make_async_copy(s_ref, s_out.at[here.grp, here.ep], cross[0].at[2])
        first.start()
        swap = remote(s_ref, s_out.at[here.grp, here.ep], cross[1].at[0], cross[2].at[0], here.across())
        swap.start()
        gather = Gather(here, x_ref, x_out, gather_sems)
        gather.start()
        columns_of = Exchange(
            here,
            lambda e: w_ref.at[:, :, pl.ds(pl.multiple_of(e * mine, mine), mine)],
            lambda e: w_out.at[here.grp, e],
            w_sems,
        )
        columns_of.start()
        first.wait()
        remote(
            s_ref, s_out.at[1 - here.grp, here.ep], cross[1].at[0], cross[2].at[0], here.across()
        ).wait_recv()
        swap.wait_send()
        spread = Exchange(here, lambda e: s_out.at[:, here.ep], lambda e: s_out.at[:, e], s_sems)
        copies = []
        for offset in range(1, here.count):
            copy = remote(
                s_out.at[:, here.ep], s_out.at[:, here.ep], s_sems[0].at[offset], s_sems[1].at[offset], here.peer(offset)
            )
            copy.start()
            copies.append(copy)
        gather.step(0)
        columns_of.arrive()
        over = remote(w_out.at[here.grp], w_out.at[here.grp], cross[1].at[1], cross[2].at[1], here.across())
        over.start()
        for step in range(1, gather.far):
            gather.step(step)
        for offset in range(1, here.count):
            source = here.peer(-offset)[1]
            remote(
                s_out.at[:, source], s_out.at[:, source], s_sems[0].at[offset], s_sems[1].at[offset], here.peer(offset)
            ).wait_recv()
        for step in range(-1, gather.far):
            gather.side(step)
        remote(
            w_out.at[1 - here.grp], w_out.at[1 - here.grp], cross[1].at[1], cross[2].at[1], here.across()
        ).wait_recv()
        gather.settle()
        gather.finish()
        columns_of.finish()
        over.wait_send()
        for copy in copies:
            copy.wait_send()

    dma = pltpu.SemaphoreType.DMA
    return comm_call(
        kernel,
        [
            jax.ShapeDtypeStruct((ep_count, rows, width), rows_block.dtype),
            jax.ShapeDtypeStruct((2, ep_count, kinds, depth, mine), weights.dtype),
            jax.ShapeDtypeStruct((2, ep_count, small_rows, small.shape[1]), small.dtype),
        ],
        Gather.scratch(ep_count)
        + Exchange.scratch(ep_count)
        + Exchange.scratch(ep_count)
        + [dma((3,)), dma((2,)), dma((2,)), dma((1,))],
        "gather_inputs",
        1,
        [rows_block, weights, small],
    )


def gather_both(ep_count, block, name, collective_id):
    rows, width = block.shape

    def kernel(x_ref, own_ref, other_ref, *scratch):
        gather_sems, cross = split(scratch, 5, 4)
        across_send, across_recv, hand_send, hand_recv = cross
        here = Place(ep_count)
        greet(ring_devices(here) + [here.across()])
        gather = Gather(here, x_ref, own_ref, gather_sems)
        gather.start()
        sent = []
        places = [0]

        def cross_copy(slot, index, src):
            return remote(src, other_ref.at[index], across_send.at[slot], across_recv.at[slot], here.across())

        def hand_copy(slot, index):
            return remote(
                other_ref.at[index], other_ref.at[index], hand_send.at[slot], hand_recv.at[slot], here.sibling()
            )

        def start(copy):
            copy.start()
            sent.append(copy)

        start(cross_copy(0, here.ep, x_ref))
        slots = [(0, 0)]
        for step in range(gather.far):
            gather.step(step)
            for way in range(2):
                if step < gather.far - 1 or way == 0:
                    offset = -1 - step if way == 0 else 1 + step
                    slots.append((len(slots), offset))
                    index = here.chip(offset)
                    start(cross_copy(slots[-1][0], index, own_ref.at[index]))
        for step in range(-1, gather.far):
            gather.side(step)
        for slot, offset in slots:
            index = here.chip(offset)
            cross_copy(slot, index, other_ref.at[index]).wait_recv()
            start(hand_copy(slot, index))
        for slot, offset in slots:
            hand_copy(slot, here.index(here.at(offset), 1 - here.core)).wait_recv()
        gather.settle()
        gather.finish()
        for copy in sent:
            copy.wait_send()

    dma = pltpu.SemaphoreType.DMA
    shape = jax.ShapeDtypeStruct((ep_count, rows, width), block.dtype)
    slots = dma((ep_count // 2,))
    return comm_call(
        kernel, [shape, shape], Gather.scratch(ep_count) + [slots] * 4, name, collective_id, [block]
    )


def exchange(ep_count, tiles, name, collective_id):
    def kernel(src, dst, *sems):
        here = Place(ep_count)
        greet(plane_devices(here))
        swap = Exchange(here, lambda e: src.at[e], lambda e: dst.at[e], sems)
        swap.start()
        swap.arrive()
        swap.finish()

    return comm_call(
        kernel,
        jax.ShapeDtypeStruct(tiles.shape, tiles.dtype),
        Exchange.scratch(ep_count),
        name,
        collective_id,
        [tiles],
    )


def spread(ep_count, tile, name, collective_id):
    def kernel(src, dst, *sems):
        here = Place(ep_count)
        greet(plane_devices(here))
        swap = Exchange(here, lambda e: src, lambda e: dst.at[e], sems)
        swap.start()
        swap.arrive()
        swap.finish()

    return comm_call(
        kernel,
        jax.ShapeDtypeStruct((ep_count,) + tile.shape, tile.dtype),
        Exchange.scratch(ep_count),
        name,
        collective_id,
        [tile],
    )


def scatter_sum(ep_count, blocks, name, collective_id):
    rows, width = blocks.shape[1:]
    part_rows = rows // 2
    far = ep_count // 4

    def hops(way, part):
        return far if way == part else far - 1

    def kernel(src, out, joint, travel, landed, side_send, side_recv, ring_send, ring_recv):
        here = Place(ep_count)
        greet(ring_devices(here))
        offsets = [far] + [sign * k for k in range(far - 1, 0, -1) for sign in (1, -1)] + [0]
        sides = []
        for slot, offset in enumerate(offsets):
            index = here.index(here.at(offset), 1 - here.core)
            copy = remote(src.at[index], joint.at[slot], side_send.at[slot], side_recv.at[slot], here.sibling())
            copy.start()
            sides.append(copy)
        waited = set()

        def term(offset, part):
            offset = far if offset == -far else offset
            slot = offsets.index(offset)
            if slot not in waited:
                waited.add(slot)
                sides[slot].wait_recv()
            index = here.chip(offset)
            at = pl.ds(part * part_rows, part_rows)
            return src[index, at].astype(F32) + joint[slot, at].astype(F32)

        sends = []

        def ring_copy(way, step, part):
            at = pl.ds(part * part_rows, part_rows)
            return remote(
                travel.at[way, step, at],
                landed.at[way, step, at],
                ring_send.at[way, step, part],
                ring_recv.at[way, step, part],
                here.right() if way == 0 else here.left(),
            )

        for step in range(far):
            for part in range(2):
                for way in range(2):
                    count = hops(way, part)
                    if step < count:
                        distance = count - step
                        value = term(distance if way == 0 else -distance, part)
                        at = pl.ds(part * part_rows, part_rows)
                        if step > 0:
                            ring_copy(way, step - 1, part).wait_recv()
                            value = value + landed[way, step - 1, at].astype(F32)
                        travel[way, step, at] = value.astype(travel.dtype)
                        copy = ring_copy(way, step, part)
                        copy.start()
                        sends.append(copy)
        for part in range(2):
            value = term(0, part)
            at = pl.ds(part * part_rows, part_rows)
            for way in range(2):
                count = hops(way, part)
                ring_copy(way, count - 1, part).wait_recv()
                value = value + landed[way, count - 1, at].astype(F32)
            out[at] = value
        for copy in sides + sends:
            copy.wait_send()

    dma = pltpu.SemaphoreType.DMA
    ring = ep_count // 2
    return comm_call(
        kernel,
        jax.ShapeDtypeStruct((rows, width), F32),
        [
            pltpu.VMEM((ring, rows, width), blocks.dtype),
            pltpu.VMEM((2, far, rows, width), blocks.dtype),
            pltpu.VMEM((2, far, rows, width), blocks.dtype),
            dma((ring,)),
            dma((ring,)),
            dma((2, far, 2)),
            dma((2, far, 2)),
        ],
        name,
        collective_id,
        [blocks],
        vmem=True,
    )


class Sums:
    def __init__(self, here, buffers, sems):
        self.here = here
        self.mine, self.theirs, self.joint, self.first, self.landed = buffers
        self.side_send, self.side_recv, self.ring_send, self.ring_recv = sems
        self.far = here.ring // 2
        self.offsets = ring_offsets(here.ring)
        self.part_rows = self.mine.shape[1] // 2
        self.waited, self.copies = set(), []

    @staticmethod
    def scratch(ep_count, rows, width, dtype=BF):
        ring, far = ep_count // 2, ep_count // 4
        dma = pltpu.SemaphoreType.DMA
        buffers = [pltpu.VMEM((ring, rows, width), dtype) for _ in range(3)]
        buffers += [pltpu.VMEM((2, rows, width), dtype), pltpu.VMEM((2, far, rows, width), dtype)]
        return buffers, [dma((ring,)), dma((ring,)), dma((2, far, 2)), dma((2, far, 2))]

    def side_copy(self, slot):
        return remote(
            self.theirs.at[slot],
            self.joint.at[slot],
            self.side_send.at[slot],
            self.side_recv.at[slot],
            self.here.sibling(),
        )

    def give(self, slot):
        copy = self.side_copy(slot)
        copy.start()
        self.copies.append(copy)

    def hops(self, way, part):
        return self.far if way == part else self.far - 1

    def rows(self, part):
        return pl.ds(part * self.part_rows, self.part_rows)

    def term(self, offset, part):
        slot = self.offsets.index(self.far if offset == -self.far else offset)
        if slot not in self.waited:
            self.waited.add(slot)
            self.side_copy(slot).wait_recv()
        at = self.rows(part)
        return self.mine[slot, at].astype(F32) + self.joint[slot, at].astype(F32)

    def ring_copy(self, way, step, part):
        at = self.rows(part)
        src = self.first.at[way, at] if step == 0 else self.landed.at[way, step - 1, at]
        return remote(
            src,
            self.landed.at[way, step, at],
            self.ring_send.at[way, step, part],
            self.ring_recv.at[way, step, part],
            self.here.right() if way == 0 else self.here.left(),
        )

    def step(self, step):
        for part in range(2):
            for way in range(2):
                count = self.hops(way, part)
                if step < count:
                    distance = count - step
                    value = self.term(distance if way == 0 else -distance, part)
                    at = self.rows(part)
                    if step == 0:
                        self.first[way, at] = value.astype(self.first.dtype)
                    else:
                        self.ring_copy(way, step - 1, part).wait_recv()
                        value = value + self.landed[way, step - 1, at].astype(F32)
                        self.landed[way, step - 1, at] = value.astype(self.landed.dtype)
                    copy = self.ring_copy(way, step, part)
                    copy.start()
                    self.copies.append(copy)

    def finish(self, put):
        for part in range(2):
            value = self.term(0, part)
            at = self.rows(part)
            for way in range(2):
                count = self.hops(way, part)
                self.ring_copy(way, count - 1, part).wait_recv()
                value = value + self.landed[way, count - 1, at].astype(F32)
            put(at, value)
        for copy in self.copies:
            copy.wait_send()


def ring_offsets(ring):
    far = ring // 2
    return [0] + [sign * k for k in range(1, far) for sign in (1, -1)] + [far]


def experts(ep_count, block, cots, hots, hots_t, router, gate_w, up_w, down_w, name, collective_id):
    rows, width = block.shape
    hidden_width = gate_w.shape[1]
    slots = hots.shape[2]
    pair = 2 * rows
    ring = ep_count // 2
    offsets = ring_offsets(ring)
    batches = [[0]] + [[2 * k - 1, 2 * k] for k in range(1, ring // 2)] + [[ring - 1]]
    tile, wide = 512, 1024
    far = ring // 2

    def kernel(*refs):
        ins, outs, scratch = split(refs, 8, 10, len(refs) - 18)
        block_ref, cot_ref, hot_ref, hot_t_ref, router_ref, gate_ref, up_ref, down_ref = ins
        own_ref, other_ref, u_out, e_out, h_out, g_out, p_out, r_out, sum_out, dot_out = outs
        gather_sems, cross, bufs, stage, sum_bufs, sum_sems, dot_sems, load_sems = split(scratch, 5, 4, 5, 9, 5, 4, 3, 4)
        across_send, across_recv, hand_send, hand_recv = cross
        gate_v, up_v, down_v, rows_v, cot_v = bufs
        u_s, e_s, h_s, g_s, p_s, r_s, dx_s, dot_s, line_s = stage
        dot_send, dot_recv, dot_own = dot_sems
        weight_sem, rows_sem, cot_sem, stage_sem = load_sems
        here = Place(ep_count)
        sums = Sums(here, sum_bufs, sum_sems)
        weights = []
        for i, (src, dst) in enumerate(((gate_ref, gate_v), (up_ref, up_v), (down_ref, down_v))):
            copy = pltpu.make_async_copy(src, dst, weight_sem.at[i])
            copy.start()
            weights.append(copy)
        greet(plane_devices(here) + [here.across()])
        gather = Gather(here, block_ref, own_ref, gather_sems)
        gather.start()
        sent = []

        def start(copy):
            copy.start()
            sent.append(copy)

        def cross_copy(slot, src):
            index = here.chip(offsets[slot])
            return remote(src, other_ref.at[index], across_send.at[slot], across_recv.at[slot], here.across())

        def hand_copy(slot, core):
            index = here.index(here.at(offsets[slot]), core)
            return remote(
                other_ref.at[index], other_ref.at[index], hand_send.at[slot], hand_recv.at[slot], here.sibling()
            )

        start(cross_copy(0, block_ref))

        def chip_of(slot):
            return here.index(here.at(offsets[slot]), 0) // 2

        def group_of(which):
            return here.grp if which == 0 else 1 - here.grp

        def cot_copy(which, slot, buffer):
            return pltpu.make_async_copy(
                cot_ref.at[group_of(which), chip_of(slot)], cot_v.at[buffer], cot_sem.at[buffer]
            )

        def rows_copy(src, slot, buffer):
            return pltpu.make_async_copy(
                src.at[pl.ds(2 * chip_of(slot), 2)], rows_v.at[buffer], rows_sem.at[buffer]
            )

        pending = {}
        stages = {"u": (u_s, u_out), "e": (e_s, e_out), "h": (h_s, h_out), "g": (g_s, g_out), "p": (p_s, p_out), "r": (r_s, r_out)}

        def settle(keys):
            for key in keys:
                for copy in pending.pop(key, []):
                    copy.wait()

        def store(key, which, batch):
            src, dst = stages[key]
            sem = list(stages).index(key)
            count = len(batch) * slots
            if key == "r":
                pending[key] = [
                    pltpu.make_async_copy(src.at[pl.ds(i * slots, slots)], dst.at[chip_of(slot)], stage_sem.at[sem + i])
                    for i, slot in enumerate(batch)
                ]
            else:
                target = dst.at[which, pl.ds(batch[0] * slots, count)]
                pending[key] = [pltpu.make_async_copy(src.at[pl.ds(0, count)], target, stage_sem.at[sem])]
            for copy in pending[key]:
                copy.start()

        def loop(extent, tile, body):
            def run(i, carry):
                body(pl.ds(pl.multiple_of(i * tile, tile), tile))
                return carry

            lax.fori_loop(0, extent // tile, run, 0)

        def prefetch(which, batch, parity):
            for i, slot in enumerate(batch):
                cot_copy(which, slot, 2 * parity + i).start()

        def work(which, batch, parity):
            count = len(batch) * slots
            every = pl.ds(0, count)
            src = own_ref if which == 0 else other_ref
            for i, slot in enumerate(batch):
                rows_copy(src, slot, i).start()
            for i, slot in enumerate(batch):
                rows_copy(src, slot, i).wait()
                cot_copy(which, slot, 2 * parity + i).wait()
            settle("u")
            for i, slot in enumerate(batch):
                hot = hot_ref[which, chip_of(slot)]

                def pick_rows(at, i=i, hot=hot):
                    picked = mm(hot, rows_v[i, :, :, at].reshape(pair, wide))
                    u_s[pl.ds(i * slots, slots), at] = picked.astype(BF)

                loop(width, wide, pick_rows)
            store("u", which, batch)
            logits = mm(u_s[every], router_ref[...])
            lane = lax.broadcasted_iota(jnp.int32, logits.shape, 1)
            logits = jnp.where(lane < ep_count, logits, -1e30)
            powers = jnp.exp(logits - jnp.max(logits, axis=-1, keepdims=True))
            gate = jnp.sum(jnp.where(lane == here.ep, powers, 0.0), axis=-1, keepdims=True)
            gate = gate / jnp.sum(powers, axis=-1, keepdims=True)
            settle("er")
            for i, slot in enumerate(batch):
                hot = hot_ref[which, chip_of(slot)]

                def pick_cots(at, i=i, hot=hot):
                    part = pl.ds(i * slots, slots)
                    picked = mm(hot, cot_v[2 * parity + i, :, at])
                    e_s[part, at] = (gate[i * slots : (i + 1) * slots] * picked).astype(BF)
                    if which == 0:
                        r_s[part, at] = picked.astype(BF)

                loop(width, wide, pick_cots)
            store("e", which, batch)
            settle("hgp")

            def inner(at):
                gate_pre = mm(u_s[every], gate_v[:, at])
                up_pre = mm(u_s[every], up_v[:, at])
                grad = mm_nt(e_s[every], down_v[at, :])
                sigma = 1.0 / (1.0 + jnp.exp(-gate_pre))
                swish = gate_pre * sigma
                h_s[every, at] = (swish * up_pre).astype(BF)
                g_s[every, at] = (grad * up_pre * sigma * (1.0 + gate_pre * (1.0 - sigma))).astype(BF)
                p_s[every, at] = (grad * swish).astype(BF)

            loop(hidden_width, tile, inner)
            for key in "hgp":
                store(key, which, batch)
            if which == 1:
                return
            dot_s[...] = jnp.zeros_like(dot_s)

            def outer(at):
                result = mm(h_s[every], down_v[:, at]).astype(BF).astype(F32)
                dot_s[every] += jnp.sum(result * r_s[every, at].astype(F32), axis=-1, keepdims=True)
                r_s[every, at] = (gate * result).astype(BF)

            loop(width, wide, outer)
            store("r", which, batch)

            def back(at):
                grad = mm_nt(g_s[every], gate_v[at, :]) + mm_nt(p_s[every], up_v[at, :])
                dx_s[every, at] = grad.astype(BF)

            loop(width, tile, back)
            for i, slot in enumerate(batch):
                part = pl.ds(i * slots, slots)
                chip = chip_of(slot)

                def put(at, slot=slot, part=part, chip=chip):
                    grads = dx_s[part, at]
                    for buffer, core in ((sums.mine, here.core), (sums.theirs, 1 - here.core)):
                        turned = hot_t_ref[which, chip, pl.ds(pl.multiple_of(core * rows, rows), rows)]
                        buffer[slot, :, at] = mm(turned, grads).astype(BF)

                loop(width, wide, put)
                sums.give(slot)
                line = jnp.sum(hot_ref[which, chip].astype(F32) * dot_s[part], axis=0, keepdims=True)
                for core in range(2):
                    line_s[slot, core] = jnp.broadcast_to(line[:, core * rows : (core + 1) * rows], (8, rows))

        prefetch(0, batches[0], 0)
        for copy in weights:
            copy.wait()
        for number, batch in enumerate(batches):
            if number == 0:
                gather.settle()
            else:
                gather.step(number - 1)
                for slot in batch:
                    start(cross_copy(slot, own_ref.at[here.chip(offsets[slot])]))
            gather.side(number - 1)
            if number + 1 < len(batches):
                prefetch(0, batches[number + 1], (number + 1) % 2)
            else:
                prefetch(1, batches[0], (number + 1) % 2)
            work(0, batch, number % 2)

        def dot_copy(slot, core, sender_core, source, target):
            return remote(
                line_s.at[slot, core], dot_out.at[source], dot_send.at[slot, core], dot_recv.at[slot, sender_core], (here.grp, target)
            )

        own_dots = pltpu.make_async_copy(line_s.at[0, here.core], dot_out.at[here.ep], dot_own)
        own_dots.start()
        start(dot_copy(0, 1 - here.core, here.core, here.ep, here.sibling()[1]))
        for slot in range(1, ring):
            for core in range(2):
                target = here.index(here.at(offsets[slot]), core)
                start(dot_copy(slot, core, here.core, here.ep, target))
        count = len(batches)

        def put_sum(at, value):
            sum_out[at] = value

        for number, batch in enumerate(batches):
            for slot in batch:
                index = here.chip(offsets[slot])
                cross_copy(slot, other_ref.at[index]).wait_recv()
                start(hand_copy(slot, here.core))
            if number < far:
                sums.step(number)
            else:
                sums.finish(put_sum)
            for slot in batch:
                hand_copy(slot, 1 - here.core).wait_recv()
            parity = (count + number) % 2
            if number + 1 < count:
                prefetch(1, batches[number + 1], 1 - parity)
            work(1, batch, parity)
        own_dots.wait()
        dot_copy(0, 0, 1 - here.core, here.sibling()[1], here.sibling()[1]).wait_recv()
        for slot in range(1, ring):
            for core in range(2):
                source = here.index(here.at(-offsets[slot]), core)
                dot_copy(slot, 0, core, source, source).wait_recv()
        gather.finish()
        for copy in sent:
            copy.wait_send()
        settle("uehgp")

    dma = pltpu.SemaphoreType.DMA
    total = ring * slots
    most = max(len(batch) for batch in batches) * slots
    sum_buffers, sum_sems = Sums.scratch(ep_count, rows, width)
    hbm = pl.BlockSpec(memory_space=pl.ANY)
    vmem = pl.BlockSpec(memory_space=pltpu.VMEM)

    def low(*shape):
        return jax.ShapeDtypeStruct(shape, BF)

    def keep(*shape):
        return pltpu.VMEM(shape, BF)

    return pl.pallas_call(
        kernel,
        out_shape=[
            low(ep_count, rows, width),
            low(ep_count, rows, width),
            low(2, total, width),
            low(2, total, width),
            low(2, total, hidden_width),
            low(2, total, hidden_width),
            low(2, total, hidden_width),
            low(ring, slots, width),
            jax.ShapeDtypeStruct((rows, width), F32),
            jax.ShapeDtypeStruct((ep_count, 8, rows), F32),
        ],
        in_specs=[hbm, hbm, vmem, vmem, vmem, hbm, hbm, hbm],
        out_specs=[hbm] * 8 + [vmem, hbm],
        scratch_shapes=Gather.scratch(ep_count)
        + [dma((ring,))] * 4
        + [keep(*gate_w.shape), keep(*up_w.shape), keep(*down_w.shape), keep(2, 2, rows, width), keep(4, pair, width)]
        + [keep(most, width), keep(most, width)]
        + [keep(most, hidden_width)] * 3
        + [keep(most, width), keep(most, width), pltpu.VMEM((most, 1), F32), pltpu.VMEM((ring, 2, 8, rows), F32)]
        + sum_buffers
        + sum_sems
        + [dma((ring, 2)), dma((ring, 2)), dma]
        + [dma((3,)), dma((2,)), dma((4,)), dma((7,))],
        compiler_params=pltpu.CompilerParams(
            collective_id=collective_id, has_side_effects=True, vmem_limit_bytes=60 << 20
        ),
        name=name,
    )(block, cots, hots, hots_t, router, gate_w, up_w, down_w)


class RingSum:
    def __init__(self, here, term, buffers, sems, more=None):
        self.here, self.term, self.more = here, term, more
        self.joint, self.first, self.landed, self.stage = buffers
        self.side_send, self.side_recv, self.ring_send, self.ring_recv, self.stage_sem = sems
        self.far = here.ring // 2
        self.offsets = ring_offsets(here.ring)
        self.part_rows = self.stage.shape[2]
        self.waited, self.copies = set(), []

    @staticmethod
    def scratch(ep_count, rows, width, dtype=BF):
        ring, far = ep_count // 2, ep_count // 4
        dma = pltpu.SemaphoreType.DMA
        shapes = [(ring, rows, width), (2, rows, width), (2, far, rows, width), (2, 2, rows // 2, width)]
        buffers = [pltpu.VMEM(shape, dtype) for shape in shapes]
        return buffers + [dma((ring,)), dma((ring,)), dma((2, far, 2)), dma((2, far, 2)), dma((2, 2))]

    def hops(self, way, part):
        return self.far if way == part else self.far - 1

    def rows(self, part):
        return pl.ds(part * self.part_rows, self.part_rows)

    def distance(self, way, part, step):
        distance = max(self.hops(way, part) - step, 0)
        return distance if way == 0 else -distance

    def load(self, way, part, step):
        index = self.here.chip(self.distance(way, part, step))
        return pltpu.make_async_copy(
            self.term(index).at[self.rows(part)], self.stage.at[way, part], self.stage_sem.at[way, part]
        )

    def side_copy(self, slot):
        here = self.here
        index = here.index(here.at(self.offsets[slot]), 1 - here.core)
        return remote(
            self.term(index), self.joint.at[slot], self.side_send.at[slot], self.side_recv.at[slot], here.sibling()
        )

    def start(self):
        for way in range(2):
            for part in range(2):
                self.load(way, part, 0).start()
        for slot in reversed(range(len(self.offsets))):
            copy = self.side_copy(slot)
            copy.start()
            self.copies.append(copy)

    def value(self, way, part, step):
        offset = self.distance(way, part, step)
        slot = self.offsets.index(self.far if offset == -self.far else offset)
        if slot not in self.waited:
            self.waited.add(slot)
            self.side_copy(slot).wait_recv()
        self.load(way, part, step).wait()
        value = self.stage[way, part].astype(F32) + self.joint[slot, self.rows(part)].astype(F32)
        if self.more is not None:
            value = value + self.more(offset, self.rows(part))
        return value

    def ring_copy(self, way, step, part):
        at = self.rows(part)
        src = self.first.at[way, at] if step == 0 else self.landed.at[way, step - 1, at]
        return remote(
            src,
            self.landed.at[way, step, at],
            self.ring_send.at[way, step, part],
            self.ring_recv.at[way, step, part],
            self.here.right() if way == 0 else self.here.left(),
        )

    def step(self, step):
        for part in range(2):
            for way in range(2):
                if step < self.hops(way, part):
                    value = self.value(way, part, step)
                    at = self.rows(part)
                    if step == 0:
                        self.first[way, at] = value.astype(self.first.dtype)
                    else:
                        self.ring_copy(way, step - 1, part).wait_recv()
                        value = value + self.landed[way, step - 1, at].astype(F32)
                        self.landed[way, step - 1, at] = value.astype(self.landed.dtype)
                    copy = self.ring_copy(way, step, part)
                    copy.start()
                    self.copies.append(copy)
                    if step + 1 < self.hops(way, part) or way == 0:
                        self.load(way, part, step + 1).start()

    def finish(self, put):
        for part in range(2):
            value = self.value(0, part, self.hops(0, part))
            at = self.rows(part)
            for way in range(2):
                count = self.hops(way, part)
                self.ring_copy(way, count - 1, part).wait_recv()
                value = value + self.landed[way, count - 1, at].astype(F32)
            put(at, value)
        for copy in self.copies:
            copy.wait_send()


def sum_all(ep_count, normed_terms, result_terms, output_terms, weight_terms, tiles, expert_rows, name, collective_id):
    rows, width = normed_terms.shape[1:]
    units, grads, hidden, gate_grads, up_grads = expert_rows
    depth_rows, hidden_width = hidden.shape
    ring = ep_count // 2
    far = ring // 2
    out_rows = output_terms.shape[3]
    weight_rows, weight_cols = weight_terms.shape[2:]
    slab, wide = 256, 1024
    dma = pltpu.SemaphoreType.DMA

    def kernel(*refs):
        ins, outs, scratch = split(refs, 10, 8, len(refs) - 18)
        dn_ref, eo_ref, go_ref, gw_ref, tile_ref, u_ref, e_ref, h_ref, g_ref, p_ref = ins
        dn_out, eo_out, go_out, gw_out, tile_out, gate_out, up_out, down_out = outs
        dn_s, eo_s, go_s, go_more, gw_s, tile_s, work_s = split(scratch, 9, 9, 9, 6, 9, 3, 6)
        here = Place(ep_count)
        greet(plane_devices(here) + far_devices(here))
        sent = []

        def start(copy):
            copy.start()
            sent.append(copy)

        tile_send, tile_recv, tile_own = tile_s
        me = here.grp * ep_count + here.ep
        own_tile = pltpu.make_async_copy(tile_ref.at[me], tile_out.at[me], tile_own)
        own_tile.start()

        def tile_copy(turn, offset, source):
            group = (here.grp + turn) % 2
            target = (here.ep + offset) % ep_count
            slot = turn * ep_count + offset
            return remote(
                tile_ref.at[group * ep_count + target],
                tile_out.at[source],
                tile_send.at[slot],
                tile_recv.at[slot],
                (group, target),
            )

        (gw_x, gw_own, gw_sum, gw_x_send, gw_x_recv, gw_sem), gw_swap = gw_s[:6], gw_s[6:]
        over = remote(gw_ref.at[1 - here.grp], gw_x, gw_x_send, gw_x_recv, here.across())
        start(over)
        gw_load = pltpu.make_async_copy(gw_ref.at[here.grp], gw_own, gw_sem)
        gw_load.start()

        x_own, x_joint, x_in, go_own_sem, go_send, go_recv = go_more
        go_load = pltpu.make_async_copy(go_ref.at[1 - here.grp, :, here.core], x_own, go_own_sem)
        go_load.start()
        go_side = remote(go_ref.at[1 - here.grp, :, 1 - here.core], x_joint, go_send.at[0], go_recv.at[0], here.sibling())
        start(go_side)
        go_over = remote(x_own, x_in, go_send.at[1], go_recv.at[1], here.across())
        normed = RingSum(here, lambda e: dn_ref.at[e], dn_s[:4], dn_s[4:])
        normed.start()
        result = RingSum(here, lambda e: eo_ref.at[e], eo_s[:4], eo_s[4:])
        result.start()
        arrived = []

        def from_across(offset, at):
            if not arrived:
                arrived.append(True)
                go_over.wait_recv()
            chip = here.chip(offset) // 2
            return x_in[chip, at].astype(F32)

        output = RingSum(here, lambda e: go_ref.at[here.grp, e // 2, e % 2], go_s[:4], go_s[4:], from_across)
        output.start()

        left, right, sheet, left_sem, right_sem, sheet_sem = work_s
        parts = [
            (u_ref, g_ref, 0, gate_out, width),
            (u_ref, p_ref, 0, up_out, width),
            (h_ref, e_ref, 0, down_out, hidden_width),
            (h_ref, e_ref, 1, down_out, hidden_width),
        ]

        def task(number, begin, end):
            lhs, rhs, column, out, _ = parts[number]

            def left_copy(i):
                at = pl.ds(pl.multiple_of(i * slab, slab), slab)
                return pltpu.make_async_copy(lhs.at[:, at], left.at[i % 2], left_sem.at[i % 2])

            def sheet_copy(i):
                at = pl.ds(pl.multiple_of(i * slab, slab), slab)
                return pltpu.make_async_copy(
                    sheet.at[i % 2], out.at[at, pl.ds(column * wide, wide)], sheet_sem.at[i % 2]
                )

            if begin == 0:
                load = pltpu.make_async_copy(rhs.at[:, pl.ds(column * wide, wide)], right, right_sem)
                load.start()
            left_copy(begin).start()
            if begin == 0:
                load.wait()

            def run(i, carry):
                left_copy(i).wait()

                @pl.when(i + 1 < end)
                def _():
                    left_copy(i + 1).start()

                @pl.when(i >= begin + 2)
                def _():
                    sheet_copy(i - 2).wait()

                sheet[i % 2] = mm_tn(left[i % 2], right[...]).astype(sheet.dtype)
                sheet_copy(i).start()
                return carry

            lax.fori_loop(begin, end, run, 0)
            for i in range(max(begin, end - 2), end):
                sheet_copy(i).wait()

        count, less = width // slab, hidden_width // slab
        normed.step(0)
        result.step(0)
        for turn in range(2):
            for offset in range(ep_count):
                if turn + offset > 0:
                    start(tile_copy(turn, offset, me))
        go_load.wait()
        go_side.wait_recv()
        for chip in range(ring):
            x_own[chip] = (x_own[chip].astype(F32) + x_joint[chip].astype(F32)).astype(BF)
        start(go_over)
        task(0, 0, count // 2)
        gw_load.wait()
        over.wait_recv()
        for e in range(ep_count):
            gw_sum[e] = (gw_own[e].astype(F32) + gw_x[e].astype(F32)).astype(BF)
        swap = Exchange(here, lambda e: gw_sum.at[e], lambda e: gw_out.at[e], gw_swap)
        swap.start()
        normed.step(1)
        result.step(1)
        task(0, count // 2, count)
        task(1, 0, count // 2)
        normed.step(2)
        result.step(2)
        task(1, count // 2, count)
        output.step(0)
        normed.step(3)
        result.step(3)
        for step in range(4, far):
            normed.step(step)
            result.step(step)
        task(2, 0, less)
        output.step(1)
        task(3, 0, less // 2)
        output.step(2)
        task(3, less // 2, less)
        for step in range(3, far):
            output.step(step)

        def put(out):
            def store(at, value):
                out[at] = value

            return store

        normed.finish(put(dn_out))
        result.finish(put(eo_out))
        output.finish(put(go_out))
        own_tile.wait()
        for turn in range(2):
            for offset in range(ep_count):
                if turn + offset > 0:
                    source = ((here.grp + turn) % 2) * ep_count + (here.ep + ep_count - offset) % ep_count
                    tile_copy(turn, offset, source).wait_recv()
        swap.arrive()
        swap.finish()
        for copy in sent:
            copy.wait_send()

    hbm = pl.BlockSpec(memory_space=pl.ANY)
    vmem = pl.BlockSpec(memory_space=pltpu.VMEM)

    def keep(*shape):
        return pltpu.VMEM(shape, BF)

    return pl.pallas_call(
        kernel,
        out_shape=[
            jax.ShapeDtypeStruct((rows, width), F32),
            jax.ShapeDtypeStruct((rows, width), F32),
            jax.ShapeDtypeStruct((out_rows, width), F32),
            jax.ShapeDtypeStruct((ep_count, weight_rows, weight_cols), BF),
            jax.ShapeDtypeStruct(tiles.shape, tiles.dtype),
            jax.ShapeDtypeStruct((width, hidden_width), BF),
            jax.ShapeDtypeStruct((width, hidden_width), BF),
            jax.ShapeDtypeStruct((hidden_width, width), BF),
        ],
        in_specs=[hbm] * 10,
        out_specs=[vmem] * 3 + [hbm] * 5,
        scratch_shapes=RingSum.scratch(ep_count, rows, width)
        + RingSum.scratch(ep_count, rows, width)
        + RingSum.scratch(ep_count, out_rows, width)
        + [keep(ring, out_rows, width)] * 3
        + [dma, dma((2,)), dma((2,))]
        + [keep(ep_count, weight_rows, weight_cols)] * 3
        + [dma, dma, dma]
        + Exchange.scratch(ep_count)
        + [dma((2 * ep_count,)), dma((2 * ep_count,)), dma]
        + [keep(2, depth_rows, slab), keep(depth_rows, wide), keep(2, slab, wide), dma((2,)), dma, dma((2,))],
        compiler_params=pltpu.CompilerParams(
            collective_id=collective_id, has_side_effects=True, vmem_limit_bytes=60 << 20
        ),
        name=name,
    )(normed_terms, result_terms, output_terms, weight_terms, tiles, units, grads, hidden, gate_grads, up_grads)


def rms_scale(values, gain_vec):
    return values * lax.rsqrt(jnp.mean(values * values, axis=-1, keepdims=True) + eps) * gain_vec


def angles_of(position):
    half_dim = HEAD_DIM // 2
    frequency = theta_base ** (-2.0 * jnp.arange(half_dim, dtype=F32) / HEAD_DIM)
    angles = position.astype(F32)[:, None] * frequency[None, :]
    return jnp.cos(angles), jnp.sin(angles)


def turn(values, cosine, sine):
    half_dim = HEAD_DIM // 2
    former, latter = values[:, :half_dim], values[:, half_dim:]
    return jnp.concatenate([former * cosine - latter * sine, latter * cosine + former * sine], axis=-1)


def attend(query, key, value, prompt_len, length, scale):
    causal = jnp.tril(jnp.ones((prompt_len, prompt_len), jnp.bool_))
    small_causal = jnp.tril(jnp.ones((length, length), jnp.bool_))
    q_p, k_p, v_p = query[:prompt_len], key[:prompt_len], value[:prompt_len]
    q_c, k_c, v_c = query[prompt_len:], key[prompt_len:], value[prompt_len:]
    s_p = jnp.where(causal, mm_nt(q_p, k_p) * scale, -1e30)
    top = jnp.max(s_p, axis=-1, keepdims=True)
    e_p = jnp.exp(s_p - top)
    total = jnp.sum(e_p, axis=-1, keepdims=True)
    out_p = mm((e_p / total).astype(BF), v_p)
    log_p = top + jnp.log(total)
    shape = (-1, length, query.shape[1])
    s_c = mm_nt(q_c, k_p) * scale
    s_o = jnp.einsum("nqd,nkd->nqk", q_c.reshape(shape), k_c.reshape(shape), preferred_element_type=F32) * scale
    s_o = jnp.where(small_causal, s_o, -1e30).reshape(-1, length)
    top = jnp.maximum(jnp.max(s_c, axis=-1, keepdims=True), jnp.max(s_o, axis=-1, keepdims=True))
    e_c = jnp.exp(s_c - top)
    e_o = jnp.exp(s_o - top)
    total = jnp.sum(e_c, axis=-1, keepdims=True) + jnp.sum(e_o, axis=-1, keepdims=True)
    out_c = mm((e_c / total).astype(BF), v_p)
    own = jnp.einsum(
        "nqk,nkd->nqd",
        (e_o / total).astype(BF).reshape(-1, length, length),
        v_c.reshape(shape),
        preferred_element_type=F32,
    )
    out_c = out_c + own.reshape(out_c.shape)
    log_c = top + jnp.log(total)
    return jnp.concatenate([out_p, out_c]), jnp.concatenate([log_p, log_c])


def attend_back(query, key, value, grad, logs, prompt_len, length, scale):
    causal = jnp.tril(jnp.ones((prompt_len, prompt_len), jnp.bool_))
    small_causal = jnp.tril(jnp.ones((length, length), jnp.bool_))
    q_p, k_p, v_p, g_p, l_p = (a[:prompt_len] for a in (query, key, value, grad, logs))
    q_c, k_c, v_c, g_c, l_c = (a[prompt_len:] for a in (query, key, value, grad, logs))
    shape = (-1, length, query.shape[1])
    w_p = jnp.where(causal, jnp.exp(mm_nt(q_p, k_p) * scale - l_p), 0.0)
    d_p = mm_nt(g_p, v_p)
    ds_p = (w_p * (d_p - jnp.sum(w_p * d_p, axis=-1, keepdims=True))).astype(BF)
    w_c = jnp.exp(mm_nt(q_c, k_p) * scale - l_c)
    d_c = mm_nt(g_c, v_p)
    q_n, k_n, v_n, g_n = (a.reshape(shape) for a in (q_c, k_c, v_c, g_c))
    s_o = jnp.einsum("nqd,nkd->nqk", q_n, k_n, preferred_element_type=F32) * scale
    w_o = jnp.where(small_causal, jnp.exp(s_o - l_c.reshape(-1, length, 1)), 0.0)
    d_o = jnp.einsum("nqd,nkd->nqk", g_n, v_n, preferred_element_type=F32)
    inner = jnp.sum(w_c * d_c, axis=-1, keepdims=True) + jnp.sum(w_o * d_o, axis=-1).reshape(-1, 1)
    ds_c = (w_c * (d_c - inner)).astype(BF)
    ds_o = (w_o * (d_o - inner.reshape(-1, length, 1))).astype(BF)

    def over(eq, a, b):
        return jnp.einsum(eq, a, b, preferred_element_type=F32)

    dq_p = mm(ds_p, k_p)
    dq_c = mm(ds_c, k_p) + over("nqk,nkd->nqd", ds_o, k_n).reshape(q_c.shape)
    dk_p = mm_tn(ds_p, q_p) + mm_tn(ds_c, q_c)
    dk_c = over("nqk,nqd->nkd", ds_o, q_n).reshape(q_c.shape)
    dv_p = mm_tn(w_p.astype(BF), g_p) + mm_tn(w_c.astype(BF), g_c)
    dv_c = over("nqk,nqd->nkd", w_o.astype(BF), g_n).reshape(q_c.shape)
    return (
        jnp.concatenate([dq_p, dq_c]) * scale,
        jnp.concatenate([dk_p, dk_c]) * scale,
        jnp.concatenate([dv_p, dv_c]),
    )


def per_device(
    block_input,
    cotangent,
    routes,
    w_query,
    w_key,
    w_value,
    w_output,
    w_router,
    gain_attn,
    gain_query,
    gain_key,
    gain_mlp,
    w_gate,
    w_up,
    w_down,
):
    rows, width = block_input.shape
    top_count = routes.shape[1]
    ep_count = lax.axis_size("ep")
    grp_count = lax.axis_size("grp")
    me = lax.axis_index("ep")
    my_group = lax.axis_index("grp")
    tokens = rows * ep_count
    prompt_len = tokens // 2
    capacity = min(rows, rows * top_count * 33 // (32 * ep_count))
    cols = width // ep_count
    scale = HEAD_DIM ** (-0.5)
    depth = w_query.shape[0]

    chosen = jnp.any(routes[:, :, None] == jnp.arange(ep_count, dtype=jnp.int32), axis=1)
    per_row = 128
    router_rows = depth * ep_count // per_row
    gains = jnp.concatenate([gain_attn, gain_query, gain_key, gain_mlp])
    gain_rows = gains.shape[0] // per_row
    small = jnp.concatenate(
        [
            w_router.reshape(router_rows, per_row),
            gains.reshape(gain_rows, per_row),
            jnp.zeros((16 - router_rows - gain_rows, per_row), BF),
            chosen.T.astype(BF),
        ]
    )
    weights = jnp.stack([w_query, w_key, w_value])
    full_output = lax.all_gather(w_output, ("grp", "ep"), axis=0, tiled=True)
    cot_both = lax.all_gather(cotangent, ("grp", "ep"), axis=0, tiled=True)

    x_all, w_cols, smalls = gather_inputs(ep_count, block_input, weights, small)
    x_all = x_all.reshape(tokens, width)
    w_q, w_k, w_v = (w_cols[:, :, i].reshape(width, cols) for i in range(3))
    smalls = smalls.reshape(grp_count * ep_count, small.shape[0], per_row)
    full_router = smalls[:, :router_rows].reshape(width, ep_count)
    gains = smalls[:, router_rows : router_rows + gain_rows].reshape(-1, 4, depth).transpose(1, 0, 2).reshape(4, width)
    gain_first, gain_qnorm, gain_knorm, gain_second = (gains[i].astype(F32) for i in range(4))
    chosen_all = smalls[:, 16:].reshape(grp_count, ep_count, ep_count, rows)

    token = jnp.arange(tokens, dtype=jnp.int32)
    position = jnp.where(token < prompt_len, token, prompt_len + (token - prompt_len) % rows)
    cosine, sine = angles_of(position)
    x_wide = x_all.astype(F32)
    normed_all = rms_scale(x_wide, gain_first).astype(BF)
    q_lin = mm(normed_all, w_q)
    k_lin = mm(normed_all, w_k)
    value = mm(normed_all, w_v).astype(BF)
    squares = jnp.stack([jnp.sum(q_lin * q_lin, axis=-1), jnp.sum(k_lin * k_lin, axis=-1)])
    squares = jnp.sum(spread(ep_count, squares.reshape(-1, per_row), "spread_squares", 2), axis=0).reshape(2, tokens)
    r_q, r_k = (lax.rsqrt(squares[i] / width + eps)[:, None] for i in range(2))
    gain_q = lax.dynamic_slice(gain_qnorm, (me * cols,), (cols,))
    gain_k = lax.dynamic_slice(gain_knorm, (me * cols,), (cols,))
    n_q, n_k = q_lin * r_q, k_lin * r_k
    query = turn(n_q * gain_q, cosine, sine).astype(BF)
    key = turn(n_k * gain_k, cosine, sine).astype(BF)
    attended, logs = attend(query, key, value, prompt_len, rows, scale)
    tiles = exchange(ep_count, attended.astype(BF).reshape(ep_count, rows, cols), "exchange_attended", 3)
    att_loc = tiles.transpose(1, 0, 2).reshape(rows, width)

    inputs = block_input.astype(F32)
    residual = inputs + mm(att_loc, full_output)
    r_m = lax.rsqrt(jnp.mean(residual * residual, axis=-1, keepdims=True) + eps)
    n_m = residual * r_m
    normed_mlp = (n_m * gain_second).astype(BF)
    pair = 2 * rows
    slots = -(-2 * capacity // 16) * 16
    chips = ep_count // 2
    groups = jnp.stack([my_group, 1 - my_group])
    mine = lax.dynamic_index_in_dim(chosen_all, me, 2, keepdims=False)[groups].reshape(2, chips, pair)
    slot = jnp.cumsum(mine.astype(jnp.int32), axis=-1) - 1
    places = jnp.arange(slots, dtype=jnp.int32)
    hots = ((slot[:, :, None, :] == places[:, None]) & (mine[:, :, None, :] > 0)).astype(BF)
    hots_t = ((slot[:, :, :, None] == places) & (mine[:, :, :, None] > 0)).astype(BF)
    router = jnp.pad(full_router, ((0, 0), (0, per_row - ep_count)))
    gate_w, up_w, down_w = w_gate[0], w_up[0], w_down[0]
    cots = cot_both.reshape(grp_count, chips, pair, width)
    _, _, units, grad_out, hidden, grad_gate_pre, grad_up_pre, result, d_normed_mlp, gate_grads = experts(
        ep_count, normed_mlp, cots, hots, hots_t, router, gate_w, up_w, down_w, "experts", 4
    )
    gate_grads = gate_grads[:, 0]
    result_terms = jnp.einsum("cps,csd->cpd", hots_t[0], result, preferred_element_type=F32).astype(BF)

    probs = jax.nn.softmax(mm(normed_mlp, full_router), axis=-1)
    d_probs = gate_grads.T
    d_logits = (probs * (d_probs - jnp.sum(probs * d_probs, axis=-1, keepdims=True))).astype(BF)
    local_router = mm_tn(normed_mlp, d_logits)
    d_normed_mlp = d_normed_mlp + mm_nt(d_logits, full_router)
    local_gain_mlp = jnp.sum(d_normed_mlp * n_m, axis=0)
    d_n = d_normed_mlp * gain_second
    d_residual = cotangent.astype(F32) + r_m * (d_n - n_m * jnp.mean(n_m * d_n, axis=-1, keepdims=True))
    d_proj = d_residual.astype(BF)
    d_attended = mm_nt(d_proj, full_output).astype(BF)
    local_output = mm_tn(att_loc, d_proj).astype(BF)
    d_attended = exchange(
        ep_count, d_attended.reshape(rows, ep_count, cols).transpose(1, 0, 2), "exchange_d_attended", 7
    ).reshape(tokens, cols)

    d_query, d_key, d_value = attend_back(query, key, value, d_attended, logs, prompt_len, rows, scale)
    d_query = turn(d_query, cosine, -sine)
    d_key = turn(d_key, cosine, -sine)
    gain_grad_q = jnp.sum(d_query * n_q, axis=0)
    gain_grad_k = jnp.sum(d_key * n_k, axis=0)
    d_nq, d_nk = d_query * gain_q, d_key * gain_k
    dots = jnp.stack([jnp.sum(d_nq * n_q, axis=-1), jnp.sum(d_nk * n_k, axis=-1)])
    dots = jnp.sum(spread(ep_count, dots.reshape(-1, per_row), "spread_dots", 8), axis=0).reshape(2, tokens) / width
    d_q_lin = (r_q * (d_nq - n_q * dots[0][:, None])).astype(BF)
    d_k_lin = (r_k * (d_nk - n_k * dots[1][:, None])).astype(BF)
    d_v_lin = d_value.astype(BF)
    d_lin = jnp.concatenate([d_q_lin, d_k_lin, d_v_lin], axis=1)
    w_all = jnp.concatenate([w_q, w_k, w_v], axis=1)
    partial_normed = mm_nt(d_lin, w_all).astype(BF).reshape(ep_count, rows, width)
    local_w = mm_tn(normed_all, d_lin)
    local_gain_attn = jnp.sum(local_w * w_all.astype(F32), axis=-1) / gain_first
    owners = grp_count * ep_count
    heads_own = (jnp.arange(owners) * depth // cols == me)[:, None]
    tiles = jnp.concatenate(
        [
            local_router.reshape(owners, router_rows, per_row),
            jnp.concatenate([local_gain_attn.reshape(owners, depth), local_gain_mlp.reshape(owners, depth)], axis=1)[:, None],
            jnp.concatenate(
                [
                    jnp.where(heads_own, jnp.tile(grad.reshape(-1, depth), (owners * depth // cols, 1)), 0.0)
                    for grad in (gain_grad_q, gain_grad_k)
                ],
                axis=1,
            )[:, None],
            jnp.zeros((owners, 16 - router_rows - 2, per_row), F32),
        ],
        axis=1,
    )
    d_normed, mixture, grad_output, grad_w, tiles, grad_gate, grad_up, grad_down = sum_all(
        ep_count,
        partial_normed,
        result_terms.reshape(ep_count, rows, width),
        local_output.reshape(grp_count, chips, 2, depth, width),
        local_w.astype(BF).reshape(grp_count, ep_count, depth, 3 * cols),
        tiles,
        [a.reshape(-1, a.shape[-1]) for a in (units, grad_out, hidden, grad_gate_pre, grad_up_pre)],
        "sum_all",
        9,
    )
    block_output = (residual + mixture).astype(BF)
    r_a = lax.rsqrt(jnp.mean(inputs * inputs, axis=-1, keepdims=True) + eps)
    n_a = inputs * r_a
    d_n = d_normed * gain_first
    input_grad = d_residual + r_a * (d_n - n_a * jnp.mean(n_a * d_n, axis=-1, keepdims=True))
    grad_w = grad_w.reshape(ep_count, depth, 3, cols).transpose(2, 1, 0, 3).reshape(3, depth, width).astype(F32)
    sums = jnp.sum(tiles, axis=0)
    grad_router = sums[:router_rows].reshape(depth, ep_count)
    gain_sums = [sums[router_rows, :depth], sums[router_rows + 1, :depth], sums[router_rows + 1, depth:], sums[router_rows, depth:]]
    grad_gate, grad_up, grad_down = (grad.astype(F32)[None] for grad in (grad_gate, grad_up, grad_down))
    return (
        block_output,
        input_grad,
        grad_w[0],
        grad_w[1],
        grad_w[2],
        grad_output,
        grad_router,
        gain_sums[0],
        gain_sums[1],
        gain_sums[2],
        gain_sums[3],
        grad_gate,
        grad_up,
        grad_down,
    )


def plain_scale(values, gain_vec):
    return values * lax.rsqrt(jnp.mean(values * values, axis=-1, keepdims=True) + eps) * gain_vec


def rotate(values, position):
    token_count = values.shape[0]
    by_head = values.reshape(token_count, -1, HEAD_DIM)
    half_dim = HEAD_DIM // 2
    frequency = theta_base ** (-2.0 * jnp.arange(half_dim, dtype=jnp.float32) / HEAD_DIM)
    angles = position.astype(jnp.float32)[:, None] * frequency[None, :]
    cosine = jnp.cos(angles)[:, None, :]
    sine_part = jnp.sin(angles)[:, None, :]
    former = by_head[..., :half_dim]
    latter = by_head[..., half_dim:]
    turned = jnp.concatenate(
        [former * cosine - latter * sine_part, latter * cosine + former * sine_part], axis=-1
    )
    return turned.reshape(token_count, -1)


def masked_scores(query, keys, allowed, scale):
    raw_scores = jnp.einsum("qhd,khd->hqk", query, keys, preferred_element_type=jnp.float32) * scale
    return jnp.where(allowed[None], raw_scores, -1e30)


def plain_attend(query, keys, values, allowed, scale, head_group):
    outputs = []
    log_totals = []
    for head_start in range(0, query.shape[1], head_group):
        head_slice = slice(head_start, head_start + head_group)
        scores = masked_scores(query[:, head_slice], keys[:, head_slice], allowed, scale)
        largest = jnp.max(scores, axis=-1, keepdims=True)
        exponent = jnp.exp(scores - largest)
        summed = jnp.sum(exponent, axis=-1, keepdims=True)
        weights = (exponent / summed).astype(jnp.bfloat16)
        outputs.append(
            jnp.einsum(
                "hqk,khd->qhd", weights, values[:, head_slice], preferred_element_type=jnp.float32
            )
        )
        log_totals.append(largest + jnp.log(summed))
    return (jnp.concatenate(outputs, axis=1), jnp.concatenate(log_totals, axis=0))


def plain_attend_back(query, keys, values, grad_out, log_totals, allowed, scale, head_group):
    query_grads = []
    key_grads = []
    value_grads = []
    for head_start in range(0, query.shape[1], head_group):
        head_slice = slice(head_start, head_start + head_group)
        query_part = query[:, head_slice]
        keys_part = keys[:, head_slice]
        grad_part = grad_out[:, head_slice]
        scores = masked_scores(query_part, keys_part, allowed, scale)
        weights = jnp.where(allowed[None], jnp.exp(scores - log_totals[head_slice]), 0.0)
        grad_weights = jnp.einsum(
            "qhd,khd->hqk", grad_part, values[:, head_slice], preferred_element_type=jnp.float32
        )
        inner = jnp.sum(weights * grad_weights, axis=-1, keepdims=True)
        grad_scores = (weights * (grad_weights - inner)).astype(jnp.bfloat16)
        query_grads.append(
            jnp.einsum("hqk,khd->qhd", grad_scores, keys_part, preferred_element_type=jnp.float32)
            * scale
        )
        key_grads.append(
            jnp.einsum("hqk,qhd->khd", grad_scores, query_part, preferred_element_type=jnp.float32)
            * scale
        )
        value_grads.append(
            jnp.einsum(
                "hqk,qhd->khd",
                weights.astype(jnp.bfloat16),
                grad_part,
                preferred_element_type=jnp.float32,
            )
        )
    return (
        jnp.concatenate(query_grads, axis=1),
        jnp.concatenate(key_grads, axis=1),
        jnp.concatenate(value_grads, axis=1),
    )


def per_device_plain(
    block_input,
    cotangent,
    routes,
    w_query,
    w_key,
    w_value,
    w_output,
    w_router,
    gain_attn,
    gain_query,
    gain_key,
    gain_mlp,
    w_gate,
    w_up,
    w_down,
):
    row_count, model_width = block_input.shape
    top_count = routes.shape[1]
    ep_count = lax.axis_size("ep")
    my_index = lax.axis_index("ep")
    half_count = ep_count // 2
    prompt_len = row_count * half_count
    capacity = min(row_count, row_count * top_count * 33 // (32 * ep_count))
    head_count = model_width // HEAD_DIM
    head_group = math.gcd(4, head_count)
    scale = HEAD_DIM ** (-0.5)
    gathered = (
        lax.all_gather(w_query, ("grp", "ep"), axis=0, tiled=True),
        lax.all_gather(w_key, ("grp", "ep"), axis=0, tiled=True),
        lax.all_gather(w_value, ("grp", "ep"), axis=0, tiled=True),
        lax.all_gather(w_output, ("grp", "ep"), axis=0, tiled=True),
        lax.all_gather(w_router, ("grp", "ep"), axis=0, tiled=True),
        lax.all_gather(gain_attn, ("grp", "ep"), axis=0, tiled=True),
        lax.all_gather(gain_query, ("grp", "ep"), axis=0, tiled=True),
        lax.all_gather(gain_key, ("grp", "ep"), axis=0, tiled=True),
        lax.all_gather(gain_mlp, ("grp", "ep"), axis=0, tiled=True),
    )
    full_query, full_key, full_value, full_output, full_router = (
        gathered[0],
        gathered[1],
        gathered[2],
        gathered[3],
        gathered[4],
    )
    gain_first = gathered[5].astype(jnp.float32)
    gain_qnorm = gathered[6].astype(jnp.float32)
    gain_knorm = gathered[7].astype(jnp.float32)
    gain_second = gathered[8].astype(jnp.float32)
    offsets = jnp.arange(row_count, dtype=jnp.int32)
    in_prompt = my_index < half_count
    position = jnp.where(in_prompt, my_index * row_count + offsets, prompt_len + offsets)
    key_position = jnp.concatenate([jnp.arange(prompt_len, dtype=jnp.int32), prompt_len + offsets])
    from_prompt = jnp.arange(prompt_len + row_count, dtype=jnp.int32) < prompt_len
    allowed = (key_position[None, :] <= position[:, None]) & (
        from_prompt[None, :] | jnp.logical_not(in_prompt)
    )

    def prepare(linear, gain_vec):
        return rotate(plain_scale(linear, gain_vec), position)

    inputs = block_input.astype(jnp.float32)
    normed = plain_scale(inputs, gain_first).astype(jnp.bfloat16)
    query_lin = jnp.dot(normed, full_query, preferred_element_type=jnp.float32)
    key_lin = jnp.dot(normed, full_key, preferred_element_type=jnp.float32)
    value_lin = jnp.dot(normed, full_value, preferred_element_type=jnp.float32)
    query_low = prepare(query_lin, gain_qnorm).astype(jnp.bfloat16)
    key_low = prepare(key_lin, gain_knorm).astype(jnp.bfloat16)
    value_low = value_lin.astype(jnp.bfloat16)
    shared = (
        lax.all_gather(key_low, "ep", axis=0, tiled=True),
        lax.all_gather(value_low, "ep", axis=0, tiled=True),
    )
    keys = jnp.concatenate([shared[0][:prompt_len], key_low]).reshape(-1, head_count, HEAD_DIM)
    values = jnp.concatenate([shared[1][:prompt_len], value_low]).reshape(-1, head_count, HEAD_DIM)
    query = query_low.reshape(row_count, head_count, HEAD_DIM)
    attn_out, log_totals = plain_attend(query, keys, values, allowed, scale, head_group)
    attended = attn_out.reshape(row_count, model_width).astype(jnp.bfloat16)
    residual = inputs + jnp.dot(attended, full_output, preferred_element_type=jnp.float32)
    normed_mlp = plain_scale(residual, gain_second).astype(jnp.bfloat16)
    logits = jnp.dot(normed_mlp, full_router, preferred_element_type=jnp.float32)
    probs = jax.nn.softmax(logits, axis=-1)
    picks = routes[:, :, None] == jnp.arange(ep_count, dtype=jnp.int32)[None, None, :]
    gates = jnp.sum(jnp.where(picks, probs[:, None, :], 0.0), axis=-1)
    hot_table = picks.reshape(-1, ep_count).astype(jnp.int32)
    before = jnp.cumsum(hot_table, axis=0) - hot_table
    slot_index = jnp.sum(before * hot_table, axis=1)
    target = routes.reshape(-1) * capacity + slot_index
    sentinel = row_count * top_count
    source = (
        jnp.full((ep_count * capacity,), sentinel, jnp.int32)
        .at[target]
        .set(jnp.arange(sentinel, dtype=jnp.int32))
    )
    token_of = source // top_count
    padded_rows = jnp.concatenate([normed_mlp, jnp.zeros((1, model_width), jnp.bfloat16)])
    outgoing = padded_rows[token_of].reshape(ep_count, capacity, model_width)
    arrived = lax.all_to_all(outgoing, "ep", split_axis=0, concat_axis=0, tiled=True)
    units = arrived.reshape(-1, model_width)
    gate_w = w_gate[0]
    up_w = w_up[0]
    down_w = w_down[0]
    gate_pre = jnp.dot(units, gate_w, preferred_element_type=jnp.float32)
    up_pre = jnp.dot(units, up_w, preferred_element_type=jnp.float32)
    hidden = (jax.nn.silu(gate_pre) * up_pre).astype(jnp.bfloat16)
    expert_result = jnp.dot(hidden, down_w, preferred_element_type=jnp.float32).astype(jnp.bfloat16)
    returned = lax.all_to_all(
        expert_result.reshape(ep_count, capacity, model_width),
        "ep",
        split_axis=0,
        concat_axis=0,
        tiled=True,
    )
    picked = (
        returned.reshape(-1, model_width)[target]
        .reshape(row_count, top_count, model_width)
        .astype(jnp.float32)
    )
    output_full = residual + jnp.sum(gates[:, :, None] * picked, axis=1)
    block_output = output_full.astype(jnp.bfloat16)
    back_query, back_key, back_value, back_output, back_router = (
        full_query,
        full_key,
        full_value,
        full_output,
        full_router,
    )
    grad_top = cotangent.astype(jnp.float32)
    grad_gates = jnp.sum(grad_top[:, None, :] * picked, axis=-1)
    grad_expert = (
        (gates[:, :, None] * grad_top[:, None, :]).astype(jnp.bfloat16).reshape(-1, model_width)
    )
    padded_grads = jnp.concatenate([grad_expert, jnp.zeros((1, model_width), jnp.bfloat16)])
    grad_outgoing = padded_grads[source].reshape(ep_count, capacity, model_width)
    grad_arrived = lax.all_to_all(
        grad_outgoing, "ep", split_axis=0, concat_axis=0, tiled=True
    ).reshape(-1, model_width)
    grad_hidden = jnp.einsum("nd,fd->nf", grad_arrived, down_w, preferred_element_type=jnp.float32)
    sigma = jax.nn.sigmoid(gate_pre)
    grad_gate_pre = (grad_hidden * up_pre * sigma * (1.0 + gate_pre * (1.0 - sigma))).astype(
        jnp.bfloat16
    )
    grad_up_pre = (grad_hidden * gate_pre * sigma).astype(jnp.bfloat16)
    local_down = jnp.einsum("nf,nd->fd", hidden, grad_arrived, preferred_element_type=jnp.float32)
    local_gate = jnp.einsum("nd,nf->df", units, grad_gate_pre, preferred_element_type=jnp.float32)
    local_up = jnp.einsum("nd,nf->df", units, grad_up_pre, preferred_element_type=jnp.float32)
    grad_units = jnp.einsum("nf,df->nd", grad_gate_pre, gate_w, preferred_element_type=jnp.float32)
    grad_units = grad_units + jnp.einsum(
        "nf,df->nd", grad_up_pre, up_w, preferred_element_type=jnp.float32
    )
    grad_units = grad_units.astype(jnp.bfloat16).reshape(ep_count, capacity, model_width)
    grad_returned = lax.all_to_all(
        grad_units, "ep", split_axis=0, concat_axis=0, tiled=True
    ).reshape(-1, model_width)
    grad_normed_mlp = jnp.sum(
        grad_returned[target].reshape(row_count, top_count, model_width).astype(jnp.float32), axis=1
    )
    expert_sums = (
        lax.psum(local_gate[None].astype(jnp.bfloat16), "grp").astype(jnp.float32),
        lax.psum(local_up[None].astype(jnp.bfloat16), "grp").astype(jnp.float32),
        lax.psum(local_down[None].astype(jnp.bfloat16), "grp").astype(jnp.float32),
    )
    grad_probs = jnp.sum(jnp.where(picks, grad_gates[:, :, None], 0.0), axis=1)
    grad_logits = (
        probs * (grad_probs - jnp.sum(probs * grad_probs, axis=-1, keepdims=True))
    ).astype(jnp.bfloat16)
    local_router = jnp.einsum(
        "rd,re->de", normed_mlp, grad_logits, preferred_element_type=jnp.float32
    )
    grad_normed_mlp = grad_normed_mlp + jnp.einsum(
        "re,de->rd", grad_logits, back_router, preferred_element_type=jnp.float32
    )
    unused_mlp, second_back = jax.vjp(plain_scale, residual, gain_second)
    grad_from_mlp, local_gain_mlp = second_back(grad_normed_mlp)
    grad_residual = grad_top + grad_from_mlp
    grad_proj = grad_residual.astype(jnp.bfloat16)
    local_output = jnp.einsum("rd,re->de", attended, grad_proj, preferred_element_type=jnp.float32)
    grad_attended = jnp.einsum(
        "re,de->rd", grad_proj, back_output, preferred_element_type=jnp.float32
    )
    grad_attended = grad_attended.astype(jnp.bfloat16).reshape(row_count, head_count, HEAD_DIM)
    grad_query_rot, grad_keys, grad_values = plain_attend_back(
        query, keys, values, grad_attended, log_totals, allowed, scale, head_group
    )
    grad_keys = grad_keys.reshape(-1, model_width)
    grad_values = grad_values.reshape(-1, model_width)
    padding = jnp.zeros((ep_count * row_count - prompt_len, model_width), jnp.float32)
    key_share, value_share = (
        lax.psum_scatter(
            jnp.concatenate([grad_keys[:prompt_len], padding]).astype(jnp.bfloat16),
            "ep",
            scatter_dimension=0,
            tiled=True,
        ).astype(jnp.float32),
        lax.psum_scatter(
            jnp.concatenate([grad_values[:prompt_len], padding]).astype(jnp.bfloat16),
            "ep",
            scatter_dimension=0,
            tiled=True,
        ).astype(jnp.float32),
    )
    grad_key_rot = key_share + grad_keys[prompt_len:]
    grad_value_lin = (value_share + grad_values[prompt_len:]).astype(jnp.bfloat16)
    unused_query, query_back = jax.vjp(prepare, query_lin, gain_qnorm)
    grad_query_lin, local_gain_query = query_back(grad_query_rot.reshape(row_count, model_width))
    unused_key, key_back = jax.vjp(prepare, key_lin, gain_knorm)
    grad_key_lin, local_gain_key = key_back(grad_key_rot)
    grad_query_low = grad_query_lin.astype(jnp.bfloat16)
    grad_key_low = grad_key_lin.astype(jnp.bfloat16)
    local_query = jnp.einsum(
        "rd,re->de", normed, grad_query_low, preferred_element_type=jnp.float32
    )
    local_key = jnp.einsum("rd,re->de", normed, grad_key_low, preferred_element_type=jnp.float32)
    local_value = jnp.einsum(
        "rd,re->de", normed, grad_value_lin, preferred_element_type=jnp.float32
    )
    grad_normed = jnp.einsum(
        "re,de->rd", grad_query_low, back_query, preferred_element_type=jnp.float32
    )
    grad_normed = grad_normed + jnp.einsum(
        "re,de->rd", grad_key_low, back_key, preferred_element_type=jnp.float32
    )
    grad_normed = grad_normed + jnp.einsum(
        "re,de->rd", grad_value_lin, back_value, preferred_element_type=jnp.float32
    )
    unused_first, first_back = jax.vjp(plain_scale, inputs, gain_first)
    grad_from_attn, local_gain_attn = first_back(grad_normed)
    input_grad = grad_residual + grad_from_attn
    summed_grads = (
        lax.psum_scatter(local_query, ("grp", "ep"), scatter_dimension=0, tiled=True),
        lax.psum_scatter(local_key, ("grp", "ep"), scatter_dimension=0, tiled=True),
        lax.psum_scatter(local_value, ("grp", "ep"), scatter_dimension=0, tiled=True),
        lax.psum_scatter(local_output, ("grp", "ep"), scatter_dimension=0, tiled=True),
        lax.psum_scatter(local_router, ("grp", "ep"), scatter_dimension=0, tiled=True),
        lax.psum_scatter(local_gain_attn, ("grp", "ep"), scatter_dimension=0, tiled=True),
        lax.psum_scatter(local_gain_query, ("grp", "ep"), scatter_dimension=0, tiled=True),
        lax.psum_scatter(local_gain_key, ("grp", "ep"), scatter_dimension=0, tiled=True),
        lax.psum_scatter(local_gain_mlp, ("grp", "ep"), scatter_dimension=0, tiled=True),
    )
    return (
        block_output,
        input_grad,
        summed_grads[0],
        summed_grads[1],
        summed_grads[2],
        summed_grads[3],
        summed_grads[4],
        summed_grads[5],
        summed_grads[6],
        summed_grads[7],
        summed_grads[8],
        expert_sums[0],
        expert_sums[1],
        expert_sums[2],
    )


def solution(mesh):
    both = ("grp", "ep")
    return jax.shard_map(
        per_device if mesh.shape["grp"] == 2 else per_device_plain,
        mesh=mesh,
        in_specs=(P(both, None),) * 8 + (P(both),) * 4 + (P("ep", None, None),) * 3,
        out_specs=(P(both, None),) * 7 + (P(both),) * 4 + (P("ep", None, None),) * 3,
        check_vma=False,
    )
```

```python
import math

import jax
import jax.numpy as jnp
from jax import lax
from jax.experimental import pallas as pl
from jax.experimental.pallas import tpu as pltpu
from jax.sharding import PartitionSpec as P

HEAD_DIM = 128
MESH = pl.DeviceIdType.MESH
BF = jnp.bfloat16
F32 = jnp.float32


eps = 1e-05
theta_base = 10000.0


def mm(a, b):
    return jnp.dot(a, b, preferred_element_type=F32)


def mm_nt(a, b):
    return lax.dot_general(a, b, (((1,), (1,)), ((), ())), preferred_element_type=F32)


def mm_tn(a, b):
    return lax.dot_general(a, b, (((0,), (0,)), ((), ())), preferred_element_type=F32)


class Place:
    def __init__(self, ep_count):
        self.grp = lax.axis_index("grp")
        self.ep = lax.axis_index("ep")
        self.count = ep_count
        self.ring = ep_count // 2
        self.half = self.ring // 2
        self.core = self.ep % 2
        y = (self.ep // 2) % 2
        z = self.ep // 4
        self.place = z + y * (self.ring - 1 - 2 * z)

    def index(self, place, core):
        y = place // self.half
        z = place + y * (self.ring - 1 - 2 * place)
        return (z * 2 + y) * 2 + core

    def at(self, offset):
        return (self.place + offset + self.ring) % self.ring

    def chip(self, offset):
        return self.index(self.at(offset), self.core)

    def right(self):
        return (self.grp, self.chip(1))

    def left(self):
        return (self.grp, self.chip(-1))

    def sibling(self):
        return (self.grp, self.index(self.place, 1 - self.core))

    def across(self):
        return (1 - self.grp, self.ep)

    def peer(self, offset):
        return (self.grp, (self.ep + offset + self.count) % self.count)


def greet(devices):
    barrier = pltpu.get_barrier_semaphore()
    for device in devices:
        pl.semaphore_signal(barrier, inc=1, device_id=device, device_id_type=MESH)
    pl.semaphore_wait(barrier, len(devices))


def remote(src, dst, send, recv, device):
    return pltpu.make_async_remote_copy(
        src_ref=src, dst_ref=dst, send_sem=send, recv_sem=recv, device_id=device, device_id_type=MESH
    )


class Gather:
    def __init__(self, here, src, dst, sems):
        self.here, self.src, self.dst = here, src, dst
        self.ring_send, self.ring_recv, self.side_send, self.side_recv, self.own_sem = sems
        self.rows = dst.shape[1] // 2
        self.far = here.ring // 2
        self.started = []

    @staticmethod
    def scratch(ep_count):
        far = ep_count // 4
        ring = pltpu.SemaphoreType.DMA((2, far, 2))
        side = pltpu.SemaphoreType.DMA((2, far + 1, 2))
        return [ring, ring, side, side, pltpu.SemaphoreType.DMA]

    def block(self, index, part):
        return self.dst.at[index, pl.ds(part * self.rows, self.rows)]

    def go(self, copy):
        copy.start()
        self.started.append(copy)

    def hops(self, way, part):
        return self.far if way == part else self.far - 1

    def ring_copy(self, way, step, part, src, index):
        device = self.here.right() if way == 0 else self.here.left()
        return remote(
            src, self.block(index, part), self.ring_send.at[way, step, part], self.ring_recv.at[way, step, part], device
        )

    def side_copy(self, way, step, part, src, index):
        return remote(
            src,
            self.block(index, part),
            self.side_send.at[way, step, part],
            self.side_recv.at[way, step, part],
            self.here.sibling(),
        )

    def start(self):
        here = self.here
        for part in range(2):
            src = self.src.at[pl.ds(part * self.rows, self.rows)]
            for way in range(2):
                if self.hops(way, part) > 0:
                    self.go(self.ring_copy(way, 0, part, src, here.ep))
            self.go(self.side_copy(0, 0, part, src, here.ep))
        self.own = pltpu.make_async_copy(self.src, self.dst.at[here.ep], self.own_sem)
        self.own.start()

    def step(self, step):
        here = self.here
        for part in range(2):
            for way in range(2):
                if step < self.hops(way, part):
                    index = here.chip(-1 - step if way == 0 else 1 + step)
                    src = self.block(index, part)
                    self.ring_copy(way, step, part, src, index).wait_recv()
                    if step + 1 < self.hops(way, part):
                        self.go(self.ring_copy(way, step + 1, part, src, index))
                    self.go(self.side_copy(way, step + 1, part, src, index))

    def side(self, step):
        here = self.here
        for part in range(2):
            for way in range(2):
                if (step < 0 and way == 0) or (0 <= step < self.hops(way, part)):
                    offset = 0 if step < 0 else (-1 - step if way == 0 else 1 + step)
                    index = here.index(here.at(offset), 1 - here.core)
                    self.side_copy(way, step + 1, part, self.block(index, part), index).wait_recv()

    def settle(self):
        self.own.wait()

    def finish(self):
        for copy in self.started:
            copy.wait_send()


class Exchange:
    def __init__(self, here, src, dst, sems):
        self.here, self.src, self.dst = here, src, dst
        self.send, self.recv, self.own_sem = sems

    @staticmethod
    def scratch(ep_count):
        return [
            pltpu.SemaphoreType.DMA((ep_count,)),
            pltpu.SemaphoreType.DMA((ep_count,)),
            pltpu.SemaphoreType.DMA,
        ]

    def start(self):
        here = self.here
        self.own = pltpu.make_async_copy(self.src(here.ep), self.dst(here.ep), self.own_sem)
        self.own.start()
        self.copies = []
        for offset in range(1, here.count):
            device = here.peer(offset)
            copy = remote(self.src(device[1]), self.dst(here.ep), self.send.at[offset], self.recv.at[offset], device)
            copy.start()
            self.copies.append(copy)

    def arrive(self):
        here = self.here
        self.own.wait()
        for offset in range(1, here.count):
            source = here.peer(-offset)[1]
            remote(
                self.dst(source), self.dst(source), self.send.at[offset], self.recv.at[offset], here.peer(offset)
            ).wait_recv()

    def finish(self):
        for copy in self.copies:
            copy.wait_send()


def far_devices(here):
    return [(1 - here.grp, (here.ep + offset) % here.count) for offset in range(here.count)]


def plane_devices(here):
    return [here.peer(offset) for offset in range(1, here.count)]


def split(refs, *sizes):
    groups, start = [], 0
    for size in sizes:
        groups.append(refs[start : start + size])
        start += size
    return groups


def ring_offsets(ring):
    far = ring // 2
    return [0] + [sign * k for k in range(1, far) for sign in (1, -1)] + [far]


def experts(
    ep_count, block, cot_own, cot_other, early, hots, hots_t, router, gate_w, up_w, down_w, name, collective_id
):
    rows, width = block.shape
    hidden_width = gate_w.shape[1]
    slots = hots.shape[2]
    pair = 2 * rows
    ring = ep_count // 2
    offsets = ring_offsets(ring)
    batches = [[0]] + [[2 * k - 1, 2 * k] for k in range(1, ring // 2)] + [[ring - 1]]
    tile, wide = 512, 1024
    far = ring // 2

    def kernel(*refs):
        ins, outs, scratch = split(refs, 9, 13, len(refs) - 22)
        block_ref, cot_ref, cot_far, hot_ref, hot_t_ref, router_ref, gate_ref, up_ref, down_ref = ins
        own_ref, other_ref, u_out, e_out, h_out, g_out, p_out, du_terms, eo_terms, du_joint, sum_out, dot_out, cot_late = outs
        gather_sems, cross, cot_cross, bufs, stage, du_s, dot_sems, load_sems = split(scratch, 5, 4, 4, 5, 11, 8, 3, 5)
        across_send, across_recv, hand_send, hand_recv = cross
        gate_v, up_v, down_v, rows_v, cot_v = bufs
        u_s, e_s, h_s, g_s, p_s, r_s, dx_s, gate_s, dot_s, line_s, term_v = stage
        dot_send, dot_recv, dot_own = dot_sems
        weight_sem, rows_sem, cot_sem, stage_sem, term_sem = load_sems
        here = Place(ep_count)
        sums = RingSum(here, lambda e: du_terms.at[e], du_joint, du_s[:3], du_s[3:])
        weights = []
        for i, (src, dst) in enumerate(((gate_ref, gate_v), (up_ref, up_v), (down_ref, down_v))):
            copy = pltpu.make_async_copy(src, dst, weight_sem.at[i])
            copy.start()
            weights.append(copy)
        greet(plane_devices(here) + [here.across()])
        gather = Gather(here, block_ref, own_ref, gather_sems)
        gather.start()
        sent = []

        def start(copy):
            copy.start()
            sent.append(copy)

        def cross_copy(slot, src):
            index = here.chip(offsets[slot])
            return remote(src, other_ref.at[index], across_send.at[slot], across_recv.at[slot], here.across())

        def hand_copy(slot, core):
            index = here.index(here.at(offsets[slot]), core)
            return remote(
                other_ref.at[index], other_ref.at[index], hand_send.at[slot], hand_recv.at[slot], here.sibling()
            )

        start(cross_copy(0, block_ref))
        cot_over = Crossing(here, lambda e: cot_late.at[e], lambda e: cot_late.at[e], cot_cross)
        for slot in range(early, ring):
            cot_over.send(slot, cot_ref.at[here.chip(offsets[slot])])

        def chip_of(slot):
            return here.index(here.at(offsets[slot]), 0) // 2

        def cot_copy(which, slot, buffer):
            src = cot_ref if which == 0 else (cot_far if slot < early else cot_late)
            return pltpu.make_async_copy(src.at[pl.ds(2 * chip_of(slot), 2)], cot_v.at[buffer], cot_sem.at[buffer])

        def rows_copy(src, slot, buffer):
            return pltpu.make_async_copy(
                src.at[pl.ds(2 * chip_of(slot), 2)], rows_v.at[buffer], rows_sem.at[buffer]
            )

        pending = {}
        stages = {"u": (u_s, u_out), "e": (e_s, e_out), "g": (g_s, g_out), "p": (p_s, p_out)}

        def settle(keys):
            for key in keys:
                for copy in pending.pop(key, []):
                    copy.wait()

        def store(key, which, batch):
            src, dst = stages[key]
            sem = list(stages).index(key)
            count = len(batch) * slots
            at = pl.ds(batch[0] * slots, count)
            target = dst.at[which, at]
            pending[key] = [pltpu.make_async_copy(src.at[pl.ds(0, count)], target, stage_sem.at[sem])]
            for copy in pending[key]:
                copy.start()

        def loop(extent, tile, body):
            def run(i, carry):
                body(pl.ds(pl.multiple_of(i * tile, tile), tile))
                return carry

            lax.fori_loop(0, extent // tile, run, 0)

        def prefetch(which, batch, parity):
            for i, slot in enumerate(batch):
                cot_copy(which, slot, 2 * parity + i).start()

        hidden_copies = {}

        def store_hidden(which, batch):
            at = pl.ds(batch[0] * slots, len(batch) * slots)
            sem = weight_sem.at[3 + batches.index(batch)]
            hidden_copies[batch[0]] = pltpu.make_async_copy(h_s.at[at], h_out.at[which, at], sem)
            hidden_copies[batch[0]].start()

        given = []

        def give(src, first, chip, terms):
            buffer = len(given) % 2
            if len(given) > 1:
                given[-2].wait()

            def put(at):
                spread_rows = mm(hot_t_ref[0, chip], src[pl.ds(first, slots), at]).astype(BF)
                term_v[buffer, :, :, at] = spread_rows.reshape(2, rows, width)

            loop(width, width, put)
            copy = pltpu.make_async_copy(term_v.at[buffer], terms.at[pl.ds(2 * chip, 2)], term_sem.at[buffer])
            copy.start()
            given.append(copy)

        def settle_given():
            for copy in given[-2:]:
                copy.wait()
            given.clear()

        def work(which, batch, parity):
            count = len(batch) * slots
            every = pl.ds(0, count)
            src = own_ref if which == 0 else other_ref
            for i, slot in enumerate(batch):
                rows_copy(src, slot, i).start()
            for i, slot in enumerate(batch):
                rows_copy(src, slot, i).wait()
                cot_copy(which, slot, 2 * parity + i).wait()
            settle("u")
            for i, slot in enumerate(batch):
                hot = hot_ref[which, chip_of(slot)]

                def pick_rows(at, i=i, hot=hot):
                    picked = mm(hot, rows_v[i, :, :, at].reshape(pair, width))
                    u_s[pl.ds(i * slots, slots), at] = picked.astype(BF)

                loop(width, width, pick_rows)
            store("u", which, batch)
            logits = mm(u_s[every], router_ref[...])
            lane = lax.broadcasted_iota(jnp.int32, logits.shape, 1)
            logits = jnp.where(lane < ep_count, logits, -1e30)
            powers = jnp.exp(logits - jnp.max(logits, axis=-1, keepdims=True))
            gate = jnp.sum(jnp.where(lane == here.ep, powers, 0.0), axis=-1, keepdims=True)
            gate = gate / jnp.sum(powers, axis=-1, keepdims=True)
            settle("e")
            for i, slot in enumerate(batch):
                hot = hot_ref[which, chip_of(slot)]

                def pick_cots(at, i=i, hot=hot):
                    part = pl.ds(i * slots, slots)
                    picked = mm(hot, cot_v[2 * parity + i, :, :, at].reshape(pair, width))
                    e_s[part, at] = (gate[i * slots : (i + 1) * slots] * picked).astype(BF)
                    if which == 0:
                        r_s[pl.ds((batch[0] + i) * slots, slots), at] = picked.astype(BF)

                loop(width, width, pick_cots)
            store("e", which, batch)
            settle("gp")
            held = pl.ds(batch[0] * slots, count)
            if batch[0] in hidden_copies:
                hidden_copies.pop(batch[0]).wait()
            gate_s[held] = gate

            def inner(at):
                gate_pre = mm(u_s[every], gate_v[:, at])
                up_pre = mm(u_s[every], up_v[:, at])
                grad = mm_nt(e_s[every], down_v[at, :])
                sigma = 1.0 / (1.0 + jnp.exp(-gate_pre))
                swish = gate_pre * sigma
                h_s[held, at] = (swish * up_pre).astype(BF)
                g_s[every, at] = (grad * up_pre * sigma * (1.0 + gate_pre * (1.0 - sigma))).astype(BF)
                p_s[every, at] = (grad * swish).astype(BF)

            loop(hidden_width, tile, inner)
            for key in "gp":
                store(key, which, batch)
            store_hidden(which, batch)
            if which == 1:
                return None
            return lambda: work_back(batch, every)

        def work_back(batch, every):
            def back(at):
                grad = mm_nt(g_s[every], gate_v[at, :]) + mm_nt(p_s[every], up_v[at, :])
                dx_s[every, at] = grad.astype(BF)

            loop(width, wide, back)
            for i, slot in enumerate(batch):
                part = pl.ds(i * slots, slots)
                give(dx_s, i * slots, chip_of(slot), du_terms)

        def results():
            dot_s[...] = jnp.zeros_like(dot_s)

            def outer(at):
                result = mm(h_s[...], down_v[:, at]).astype(BF).astype(F32)
                dot_s[...] += jnp.sum(result * r_s[:, at].astype(F32), axis=-1, keepdims=True)
                r_s[:, at] = (gate_s[...] * result).astype(BF)

            loop(width, tile, outer)
            for slot in range(ring):
                part = pl.ds(slot * slots, slots)
                line = jnp.sum(hot_ref[0, chip_of(slot)].astype(F32) * dot_s[part], axis=0, keepdims=True)
                for core in range(2):
                    line_s[slot, core] = jnp.broadcast_to(line[:, core * rows : (core + 1) * rows], (8, rows))

        prefetch(0, batches[0], 0)
        for copy in weights:
            copy.wait()
        gather.settle()
        for number, batch in enumerate(batches):
            gather.side(number - 1)
            if number + 1 < len(batches):
                prefetch(0, batches[number + 1], (number + 1) % 2)
            else:
                prefetch(1, batches[0], (number + 1) % 2)
            rest = work(0, batch, number % 2)
            if number < far:
                gather.step(number)
                for slot in batches[number + 1]:
                    start(cross_copy(slot, own_ref.at[here.chip(offsets[slot])]))
            rest()
        def dot_copy(slot, core, sender_core, source, target):
            return remote(
                line_s.at[slot, core],
                dot_out.at[source],
                dot_send.at[slot, core],
                dot_recv.at[slot, sender_core],
                (here.grp, target),
            )

        settle_given()
        sums.start()
        sums.step(0)
        results()
        own_dots = pltpu.make_async_copy(line_s.at[0, here.core], dot_out.at[here.ep], dot_own)
        own_dots.start()

        start(dot_copy(0, 1 - here.core, here.core, here.ep, here.sibling()[1]))
        for slot in range(1, ring):
            for core in range(2):
                target = here.index(here.at(offsets[slot]), core)
                start(dot_copy(slot, core, here.core, here.ep, target))
        count = len(batches)

        def put(out):
            def keep_sum(at, value):
                out[at] = value

            return keep_sum

        for number, batch in enumerate(batches):
            for slot in batch:
                index = here.chip(offsets[slot])
                cross_copy(slot, other_ref.at[index]).wait_recv()
                start(hand_copy(slot, here.core))
            if 0 < number < far:
                sums.step(number)
            if number == 1:
                for slot in range(ring):
                    give(r_s, slot * slots, chip_of(slot), eo_terms)
                settle_given()
            if number == far:
                sums.finish(put(sum_out))
            for slot in batch:
                hand_copy(slot, 1 - here.core).wait_recv()
            parity = (count + number) % 2
            if number + 1 < count:
                late = [slot for slot in batches[number + 1] if slot >= early]
                for slot in late:
                    cot_over.take(slot)
                for slot in late:
                    cot_over.settle(slot)
                prefetch(1, batches[number + 1], 1 - parity)
            work(1, batch, parity)
        own_dots.wait()
        dot_copy(0, 0, 1 - here.core, here.sibling()[1], here.sibling()[1]).wait_recv()
        for slot in range(1, ring):
            for core in range(2):
                source = here.index(here.at(-offsets[slot]), core)
                dot_copy(slot, 0, core, source, source).wait_recv()
        gather.finish()
        cot_over.finish()
        for copy in sent:
            copy.wait_send()
        settle("uegp")
        for copy in hidden_copies.values():
            copy.wait()

    dma = pltpu.SemaphoreType.DMA
    total = ring * slots
    most = max(len(batch) for batch in batches) * slots
    hbm = pl.BlockSpec(memory_space=pl.ANY)
    vmem = pl.BlockSpec(memory_space=pltpu.VMEM)

    def low(*shape):
        return jax.ShapeDtypeStruct(shape, BF)

    def keep(*shape):
        return pltpu.VMEM(shape, BF)

    return pl.pallas_call(
        kernel,
        out_shape=[
            low(ep_count, rows, width),
            low(ep_count, rows, width),
            low(2, total, width),
            low(2, total, width),
            low(2, total, hidden_width),
            low(2, total, hidden_width),
            low(2, total, hidden_width),
            low(ep_count, rows, width),
            low(ep_count, rows, width),
            low(ring, rows, width),
            jax.ShapeDtypeStruct((rows, width), F32),
            jax.ShapeDtypeStruct((ep_count, 8, rows), F32),
            low(ep_count, rows, width),
        ],
        in_specs=[hbm, hbm, hbm, vmem, vmem, vmem, hbm, hbm, hbm],
        out_specs=[hbm] * 10 + [vmem, hbm, hbm],
        scratch_shapes=Gather.scratch(ep_count)
        + [dma((ring,))] * 4
        + Crossing.scratch(ep_count)
        + [keep(*gate_w.shape), keep(*up_w.shape), keep(*down_w.shape), keep(2, 2, rows, width), keep(4, 2, rows, width)]
        + [keep(most, width), keep(most, width), keep(total, hidden_width)]
        + [keep(most, hidden_width)] * 2
        + [keep(total, width), keep(most, width)]
        + [pltpu.VMEM((total, 1), F32), pltpu.VMEM((total, 1), F32), pltpu.VMEM((ring, 2, 8, rows), F32)]
        + [keep(2, 2, rows, width)]
        + RingSum.scratch(ep_count, rows, width)
        + [dma((ring, 2)), dma((ring, 2)), dma]
        + [dma((3 + len(batches),)), dma((2,)), dma((4,)), dma((4,)), dma((2,))],
        compiler_params=pltpu.CompilerParams(
            collective_id=collective_id, has_side_effects=True, vmem_limit_bytes=62 << 20
        ),
        name=name,
    )(block, cot_own, cot_other, hots, hots_t, router, gate_w, up_w, down_w)


class RingSum:
    def __init__(self, here, term, joint, buffers, sems, more=None):
        self.here, self.term, self.joint, self.more = here, term, joint, more
        self.first, self.landed, self.stage = buffers
        self.side_send, self.side_recv, self.ring_send, self.ring_recv, self.stage_sem = sems
        self.far = here.ring // 2
        self.offsets = ring_offsets(here.ring)
        self.part_rows = self.stage.shape[3]
        self.waited, self.copies = set(), []

    @staticmethod
    def scratch(ep_count, rows, width, dtype=BF):
        ring, far = ep_count // 2, ep_count // 4
        dma = pltpu.SemaphoreType.DMA
        shapes = [(2, rows, width), (2, far, rows, width), (2, 2, 2, rows // 2, width)]
        buffers = [pltpu.VMEM(shape, dtype) for shape in shapes]
        return buffers + [dma((ring,)), dma((ring,)), dma((2, far, 2)), dma((2, far, 2)), dma((2, 2, 2))]

    def hops(self, way, part):
        return self.far if way == part else self.far - 1

    def rows(self, part):
        return pl.ds(part * self.part_rows, self.part_rows)

    def distance(self, way, part, step):
        distance = max(self.hops(way, part) - step, 0)
        return distance if way == 0 else -distance

    def slot(self, way, part, step):
        offset = self.distance(way, part, step)
        return self.offsets.index(self.far if offset == -self.far else offset)

    def loads(self, way, part, step):
        index = self.here.chip(self.distance(way, part, step))
        sources = (self.term(index), self.joint.at[self.slot(way, part, step)])
        return [
            pltpu.make_async_copy(
                source.at[self.rows(part)], self.stage.at[way, part, i], self.stage_sem.at[way, part, i]
            )
            for i, source in enumerate(sources)
        ]

    def load(self, way, part, step):
        slot = self.slot(way, part, step)
        if slot not in self.waited:
            self.waited.add(slot)
            self.side_copy(slot).wait_recv()
        for copy in self.loads(way, part, step):
            copy.start()

    def side_copy(self, slot):
        here = self.here
        index = here.index(here.at(self.offsets[slot]), 1 - here.core)
        return remote(
            self.term(index), self.joint.at[slot], self.side_send.at[slot], self.side_recv.at[slot], here.sibling()
        )

    def start(self):
        for slot in reversed(range(len(self.offsets))):
            copy = self.side_copy(slot)
            copy.start()
            self.copies.append(copy)
        for part in range(2):
            for way in range(2):
                self.load(way, part, 0)

    def value(self, way, part, step):
        for copy in self.loads(way, part, step):
            copy.wait()
        value = self.stage[way, part, 0].astype(F32) + self.stage[way, part, 1].astype(F32)
        if self.more is not None:
            value = value + self.more(self.distance(way, part, step), self.rows(part))
        return value

    def ring_copy(self, way, step, part):
        at = self.rows(part)
        src = self.first.at[way, at] if step == 0 else self.landed.at[way, step - 1, at]
        return remote(
            src,
            self.landed.at[way, step, at],
            self.ring_send.at[way, step, part],
            self.ring_recv.at[way, step, part],
            self.here.right() if way == 0 else self.here.left(),
        )

    def step(self, step):
        for part in range(2):
            for way in range(2):
                if step < self.hops(way, part):
                    value = self.value(way, part, step)
                    at = self.rows(part)
                    if step == 0:
                        self.first[way, at] = value.astype(self.first.dtype)
                    else:
                        self.ring_copy(way, step - 1, part).wait_recv()
                        value = value + self.landed[way, step - 1, at].astype(F32)
                        self.landed[way, step - 1, at] = value.astype(self.landed.dtype)
                    copy = self.ring_copy(way, step, part)
                    copy.start()
                    self.copies.append(copy)
                    if step + 1 < self.hops(way, part) or way == 0:
                        self.load(way, part, step + 1)

    def finish(self, put):
        for part in range(2):
            value = self.value(0, part, self.hops(0, part))
            at = self.rows(part)
            for way in range(2):
                count = self.hops(way, part)
                self.ring_copy(way, count - 1, part).wait_recv()
                value = value + self.landed[way, count - 1, at].astype(F32)
            put(at, value)
        for copy in self.copies:
            copy.wait_send()


def rolled(values):
    return pltpu.roll(values, HEAD_DIM // 2, 1)


def as_rows(columns, count):
    shape = (columns[0].shape[0], 128)
    lane = lax.broadcasted_iota(jnp.int32, shape, 1)
    packed = jnp.zeros(shape, F32)
    for i, column in enumerate(columns):
        packed = jnp.where(lane == i, column, packed)
    return packed.T[:count]


def as_columns(tile):
    padded = jnp.concatenate([tile, jnp.zeros((128 - tile.shape[0], tile.shape[1]), F32)], axis=0)
    return padded.T


def backward(
    ep_count, d_att, head, columns, tables, gains, w_all, normed, output_terms, result_terms, tiles, expert_rows, name, collective_id
):
    rows = d_att.shape[1]
    query, key, value, norm_q, norm_k = head
    tokens, cols = query.shape
    width = w_all.shape[0]
    prompt_len = tokens // 2
    units, grads, hidden, gate_grads, up_grads = expert_rows
    depth_rows, hidden_width = hidden.shape
    ring = ep_count // 2
    far = ring // 2
    out_rows = output_terms.shape[3]
    slab, wide, block = 256, 512, 256
    segment = 512
    pieces = tokens // segment
    scale = HEAD_DIM ** (-0.5)
    dma = pltpu.SemaphoreType.DMA

    def kernel(*refs):
        ins, outs, scratch = split(refs, 20, 13, len(refs) - 33)
        (att_ref, q_ref, k_ref, v_ref, nq_ref, nk_ref, col_ref, cos_ref, sin_ref, gain_ref, w_ref, normed_ref) = ins[:12]
        go_ref, eo_ref, tile_ref, u_ref, e_ref, h_ref, g_ref, p_ref = ins[12:]
        dn_out, go_out, eo_out, gw_out, tile_out, late_out, gate_out, up_out, down_out = outs[:9]
        dn_terms, dn_joint, go_joint, eo_joint = outs[9:]
        dn_s, go_s, eo_s, go_more, gw_s, tile_s, late_s, work_s, att_s, dots_s, own_s = split(
            scratch, 8, 8, 8, 6, 7, 3, 4, 6, 8, 5, 5
        )
        here = Place(ep_count)
        greet(plane_devices(here) + far_devices(here))
        sent = []

        def start(copy):
            copy.start()
            sent.append(copy)

        (att_v, dq_s, dk_s, dv_s, lin_s), att_sems = att_s[:5], att_s[5:]
        attended = Exchange(here, lambda e: att_ref.at[e], lambda e: att_v.at[e], att_sems)
        attended.start()

        me = here.grp * ep_count + here.ep

        def tile_copy(turn, offset, source, src, dst, sems):
            group = (here.grp + turn) % 2
            target = (here.ep + offset) % ep_count
            slot = turn * ep_count + offset
            return remote(src(group * ep_count + target), dst.at[source], sems[0].at[slot], sems[1].at[slot], (group, target))

        others = [(turn, offset) for turn in range(2) for offset in range(ep_count) if turn + offset > 0]

        def send_tiles(src, dst, sems):
            own = pltpu.make_async_copy(src(me), dst.at[me], sems[2])
            own.start()
            for turn, offset in others:
                start(tile_copy(turn, offset, me, src, dst, sems))
            return own

        def take_tiles(own, src, dst, sems):
            own.wait()
            for turn, offset in others:
                source = ((here.grp + turn) % 2) * ep_count + (here.ep + ep_count - offset) % ep_count
                tile_copy(turn, offset, source, src, dst, sems).wait_recv()

        x_own, x_joint, x_in, go_own_sem, go_send, go_recv = go_more
        go_load = pltpu.make_async_copy(go_ref.at[1 - here.grp, :, here.core], x_own, go_own_sem)
        go_load.start()
        go_side = remote(go_ref.at[1 - here.grp, :, 1 - here.core], x_joint, go_send.at[0], go_recv.at[0], here.sibling())
        start(go_side)

        def go_over(part):
            at = pl.ds(part * (ring // 2), ring // 2)
            return remote(x_own.at[at], x_in.at[at], go_send.at[1 + part], go_recv.at[1 + part], here.across())

        arrived = []

        def from_across(offset, at):
            if not arrived:
                arrived.append(True)
                for half in range(2):
                    go_over(half).wait_recv()
            return x_in[here.chip(offset) // 2, at].astype(F32)

        output = RingSum(
            here, lambda e: go_ref.at[here.grp, e // 2, e % 2], go_joint, go_s[:3], go_s[3:], from_across
        )
        result = RingSum(here, lambda e: eo_ref.at[e], eo_joint, eo_s[:3], eo_s[3:])

        left, right, sheet, left_sem, right_sem, sheet_sem = work_s
        parts = [(u_ref, g_ref, i, gate_out, width) for i in range(hidden_width // wide)]
        parts += [(u_ref, p_ref, i, up_out, width) for i in range(hidden_width // wide)]
        parts += [(h_ref, e_ref, i, down_out, hidden_width) for i in range(width // wide)]

        def task(lhs, rhs, column, out, end):
            def left_copy(i):
                at = pl.ds(pl.multiple_of(i * slab, slab), slab)
                return pltpu.make_async_copy(lhs.at[:, at], left.at[lax.rem(i, 2)], left_sem.at[lax.rem(i, 2)])

            def sheet_copy(i):
                at = pl.ds(pl.multiple_of(i * slab, slab), slab)
                return pltpu.make_async_copy(
                    sheet.at[lax.rem(i, 2)], out.at[at, pl.ds(column * wide, wide)], sheet_sem.at[lax.rem(i, 2)]
                )

            load = pltpu.make_async_copy(rhs.at[:, pl.ds(column * wide, wide)], right, right_sem)
            load.start()
            left_copy(jnp.int32(0)).start()
            load.wait()

            def run(i, carry):
                left_copy(i).wait()

                @pl.when(i + 1 < end)
                def _():
                    left_copy(i + 1).start()

                @pl.when(i >= 2)
                def _():
                    sheet_copy(i - 2).wait()

                sheet[lax.rem(i, 2)] = mm_tn(left[lax.rem(i, 2)], right[...]).astype(sheet.dtype)
                sheet_copy(i).start()
                return carry

            lax.fori_loop(0, end, run, 0)
            for i in range(max(0, end - 2), end):
                sheet_copy(jnp.int32(i)).wait()

        def tasks(count):
            for _ in range(min(count, len(parts))):
                lhs, rhs, column, out, extent = parts.pop(0)
                task(lhs, rhs, column, out, extent // slab)

        result.start()
        result.step(0)
        own_tiles = send_tiles(lambda i: tile_ref.at[i], tile_out, tile_s)
        go_load.wait()
        go_side.wait_recv()
        for chip in range(ring):
            x_own[chip] = (x_own[chip].astype(F32) + x_joint[chip].astype(F32)).astype(BF)
        start(go_over(0))
        tasks(1)
        attended.arrive()

        dk_s[...] = jnp.zeros_like(dk_s)
        dv_s[...] = jnp.zeros_like(dv_s)
        per = block // rows
        line = lax.broadcasted_iota(jnp.int32, (block, block), 0)
        column_at = lax.broadcasted_iota(jnp.int32, (block, block), 1)
        causal = line >= column_at
        same = causal & (line // rows == column_at // rows)

        def grads_of(first, spans):
            at = pl.ds(first, block)
            q = q_ref[at]
            g = att_v[pl.ds(first // rows, per)].reshape(block, cols)
            log = col_ref[at, 0:1]
            kept = []
            inner = jnp.zeros((block, 1), F32)
            for begin, length, mask in spans:
                keys = pl.ds(begin, length)
                weight = jnp.exp(mm_nt(q, k_ref[keys]) * scale - log)
                if mask is not None:
                    weight = jnp.where(mask, weight, 0.0)
                d_weight = mm_nt(g, v_ref[keys])
                inner = inner + jnp.sum(weight * d_weight, axis=-1, keepdims=True)
                kept.append((keys, weight, d_weight))
            dq = jnp.zeros((block, cols), F32)
            for keys, weight, d_weight in kept:
                d_score = (weight * (d_weight - inner)).astype(BF)
                dq = dq + mm(d_score, k_ref[keys])
                dk_s[keys] += mm_tn(d_score, q)
                dv_s[keys] += mm_tn(weight.astype(BF), g)
            dq_s[at] = dq * scale

        for number in range(prompt_len // block):
            spans = [(0, number * block, None)] if number else []
            grads_of(number * block, spans + [(number * block, block, causal)])

        def later(number, carry):
            first = pl.multiple_of(prompt_len + number * block, block)
            grads_of(first, [(0, prompt_len, None), (first, block, same)])
            return carry

        lax.fori_loop(0, (tokens - prompt_len) // block, later, 0)
        result.step(1)

        dots_v, dots_all, dots_sems = dots_s[0], dots_s[1], dots_s[2:]
        late_v, late_sems = late_s[0], late_s[1:]
        gain_sums = [jnp.zeros((1, cols), F32), jnp.zeros((1, cols), F32)]
        stats = []
        for piece in range(pieces):
            at = pl.ds(piece * segment, segment)
            for kind, (ref, n_ref, factor) in enumerate(((dq_s, nq_ref, 1.0), (dk_s, nk_ref, scale))):
                turned = ref[at] * factor
                turned = turned * cos_ref[at] - rolled(turned) * sin_ref[at]
                gain_sums[kind] = gain_sums[kind] + jnp.sum(turned * n_ref[at], axis=0, keepdims=True)
                turned = turned * gain_ref[kind : kind + 1]
                ref[at] = turned
                stats.append(jnp.sum(turned * n_ref[at], axis=-1, keepdims=True))
        dots_v[...] = as_rows(stats, dots_v.shape[0])
        spread_dots = Exchange(here, lambda e: dots_v, lambda e: dots_all.at[e], dots_sems)
        spread_dots.start()
        gain_tile = jnp.concatenate(gain_sums + [jnp.zeros((6, cols), F32)], axis=0)
        for piece in range(pieces):
            at = pl.ds(piece * segment, segment)
            lin_s[at, 2 * cols : 3 * cols] = dv_s[at].astype(BF)
        slab_v, slab_sem, term_v, term_sem, gw_v = own_s
        slabs = width // slab
        half = slabs // 2

        def slab_at(turn):
            return lax.rem((1 - here.grp) * half + turn, slabs) * slab

        def slab_copy(turn):
            at = pl.ds(pl.multiple_of(slab_at(turn), slab), slab)
            return pltpu.make_async_copy(normed_ref.at[:, at], slab_v.at[turn % 2], slab_sem.at[turn % 2])

        slab_copy(0).start()
        slab_copy(1).start()
        spread_dots.arrive()
        total = dots_all[0]
        for e in range(1, ep_count):
            total = total + dots_all[e]
        total = as_columns(total / width)
        for piece in range(pieces):
            at = pl.ds(piece * segment, segment)
            for kind, (ref, n_ref) in enumerate(((dq_s, nq_ref), (dk_s, nk_ref))):
                lane = 2 * piece + kind
                grad = col_ref[at, 1 + kind : 2 + kind] * (ref[at] - n_ref[at] * total[:, lane : lane + 1])
                lin_s[at, kind * cols : (kind + 1) * cols] = grad.astype(BF)

        (gw_x, gw_sum, gw_x_send, gw_x_recv), gw_swap = gw_s[:4], gw_s[4:]
        per_slab = slab // out_rows
        gain_lines = []

        def projections(turn):
            slab_copy(turn).wait()
            first = slab_at(turn)
            grad = mm_tn(slab_v[turn % 2], lin_s[...])
            if turn + 2 < slabs:
                slab_copy(turn + 2).start()
            weight = w_ref[pl.ds(pl.multiple_of(first, slab), slab)].astype(F32)
            line = as_rows([jnp.sum(grad * weight, axis=-1, keepdims=True)], 8)[0:1]
            owner = first // out_rows
            gw_v[pl.ds(owner, per_slab)] = grad.astype(BF).reshape(per_slab, out_rows, 3 * cols)
            for i in range(per_slab):
                part = line[:, i * out_rows : (i + 1) * out_rows]
                part = jnp.concatenate([part, jnp.zeros((1, cols - out_rows), F32)], axis=1)
                late_v[owner + i] = jnp.concatenate([gain_tile[0:2], part, gain_tile[3:]], axis=0)
            return owner

        def over_copy(turn, owner):
            at = pl.ds(owner - (1 - here.grp) * ep_count, per_slab)
            return remote(gw_v.at[pl.ds(owner, per_slab)], gw_x.at[at], gw_x_send.at[turn], gw_x_recv.at[turn], here.across())

        for turn in range(half):
            start(over_copy(turn, projections(turn)))
        start(go_over(1))
        output.start()

        normed_sum = RingSum(here, lambda e: dn_terms.at[e], dn_joint, dn_s[:3], dn_s[3:])
        offsets = ring_offsets(ring)
        stores = {}
        for turn, slot in enumerate(reversed(range(ring))):
            chip = here.index(here.at(offsets[slot]), 0) // 2
            if turn >= 2:
                stores.pop(turn - 2).wait()
            at = pl.ds(pl.multiple_of(chip * 2 * rows, 2 * rows), 2 * rows)

            def fill(i, carry, at=at, turn=turn):
                wide_at = pl.ds(pl.multiple_of(i * 1024, 1024), 1024)
                part = mm_nt(lin_s[at], w_ref[wide_at]).astype(BF)
                term_v[turn % 2, :, :, wide_at] = part.reshape(2, rows, 1024)
                return carry

            lax.fori_loop(0, width // 1024, fill, 0)
            stores[turn] = pltpu.make_async_copy(
                term_v.at[turn % 2], dn_terms.at[pl.ds(chip * 2, 2)], term_sem.at[turn % 2]
            )
            stores[turn].start()
        for turn in sorted(stores):
            stores[turn].wait()
        normed_sum.start()
        normed_sum.step(0)
        result.step(2)
        for turn in range(half, slabs):
            projections(turn)
        own_late = send_tiles(lambda i: late_v.at[i], late_out, late_sems)
        tasks(1)
        for turn in range(half):
            over_copy(turn, (1 - here.grp) * ep_count + turn * per_slab).wait_recv()
        for e in range(ep_count):
            gw_sum[e] = (gw_v[here.grp * ep_count + e].astype(F32) + gw_x[e].astype(F32)).astype(BF)
        swap = Exchange(here, lambda e: gw_sum.at[e], lambda e: gw_out.at[e], gw_swap)
        swap.start()
        normed_sum.step(1)
        for step in range(3, far):
            result.step(step)
        tasks(2)
        normed_sum.step(2)
        tasks(2)
        for step in range(3, far):
            normed_sum.step(step)
        output.step(0)
        tasks(1)
        output.step(1)
        tasks(1)
        output.step(2)
        for step in range(3, far):
            output.step(step)

        def put(out):
            def store(at, value):
                out[at] = value

            return store

        normed_sum.finish(put(dn_out))
        tasks(len(parts))
        result.finish(put(eo_out))
        output.finish(put(go_out))
        take_tiles(own_tiles, lambda i: tile_ref.at[i], tile_out, tile_s)
        take_tiles(own_late, lambda i: late_v.at[i], late_out, late_sems)
        attended.finish()
        spread_dots.finish()
        swap.arrive()
        swap.finish()
        for copy in sent:
            copy.wait_send()

    hbm = pl.BlockSpec(memory_space=pl.ANY)
    vmem = pl.BlockSpec(memory_space=pltpu.VMEM)
    group_rows = 2 * ep_count

    def keep(*shape):
        return pltpu.VMEM(shape, BF)

    def wide_keep(*shape):
        return pltpu.VMEM(shape, F32)

    return pl.pallas_call(
        kernel,
        out_shape=[
            jax.ShapeDtypeStruct((rows, width), F32),
            jax.ShapeDtypeStruct((out_rows, width), F32),
            jax.ShapeDtypeStruct((rows, width), F32),
            jax.ShapeDtypeStruct((ep_count, out_rows, 3 * cols), BF),
            jax.ShapeDtypeStruct(tiles.shape, F32),
            jax.ShapeDtypeStruct((group_rows, 8, cols), F32),
            jax.ShapeDtypeStruct((width, hidden_width), BF),
            jax.ShapeDtypeStruct((width, hidden_width), BF),
            jax.ShapeDtypeStruct((hidden_width, width), BF),
            jax.ShapeDtypeStruct((ep_count, rows, width), BF),
            jax.ShapeDtypeStruct((ring, rows, width), BF),
            jax.ShapeDtypeStruct((ring, out_rows, width), BF),
            jax.ShapeDtypeStruct((ring, rows, width), BF),
        ],
        in_specs=[hbm] + [vmem] * 10 + [hbm] * 9,
        out_specs=[vmem] * 3 + [hbm] * 10,
        scratch_shapes=RingSum.scratch(ep_count, rows, width)
        + RingSum.scratch(ep_count, out_rows, width)
        + RingSum.scratch(ep_count, rows, width)
        + [keep(ring, out_rows, width)] * 3
        + [dma, dma((3,)), dma((3,))]
        + [keep(ep_count, out_rows, 3 * cols)] * 2
        + [dma((ring,)), dma((ring,))]
        + Exchange.scratch(ep_count)
        + [dma((group_rows,)), dma((group_rows,)), dma]
        + [wide_keep(group_rows, 8, cols), dma((group_rows,)), dma((group_rows,)), dma]
        + [keep(2, depth_rows, slab), keep(depth_rows, wide), keep(2, slab, wide), dma((2,)), dma, dma((2,))]
        + [keep(ep_count, rows, cols)]
        + [wide_keep(tokens, cols)] * 3
        + [keep(tokens, 3 * cols)]
        + Exchange.scratch(ep_count)
        + [wide_keep(8, segment), wide_keep(ep_count, 8, segment)]
        + Exchange.scratch(ep_count)
        + [keep(2, tokens, slab), dma((2,)), keep(2, 2, rows, width), dma((2,))]
        + [keep(group_rows, out_rows, 3 * cols)],
        compiler_params=pltpu.CompilerParams(
            collective_id=collective_id, has_side_effects=True, vmem_limit_bytes=62 << 20
        ),
        name=name,
    )(d_att, query, key, value, norm_q, norm_k, columns, *tables, gains, w_all, normed, output_terms, result_terms, tiles, *expert_rows)


class Crossing:
    def __init__(self, here, out, into, sems):
        self.here, self.out, self.into = here, out, into
        self.across_send, self.across_recv, self.hand_send, self.hand_recv = sems
        self.offsets = ring_offsets(here.ring)
        self.copies = []

    @staticmethod
    def scratch(ep_count):
        return [pltpu.SemaphoreType.DMA((ep_count // 2,))] * 4

    def go(self, copy):
        copy.start()
        self.copies.append(copy)

    def across(self, slot, src, dst):
        return remote(src, dst, self.across_send.at[slot], self.across_recv.at[slot], self.here.across())

    def hand(self, slot, core):
        block = self.into(self.here.index(self.here.at(self.offsets[slot]), core))
        return remote(block, block, self.hand_send.at[slot], self.hand_recv.at[slot], self.here.sibling())

    def send(self, slot, src):
        self.go(self.across(slot, src, self.out(self.here.chip(self.offsets[slot]))))

    def take(self, slot):
        block = self.into(self.here.chip(self.offsets[slot]))
        self.across(slot, block, block).wait_recv()
        self.go(self.hand(slot, self.here.core))

    def settle(self, slot):
        self.hand(slot, 1 - self.here.core).wait_recv()

    def finish(self):
        for copy in self.copies:
            copy.wait_send()


def attention(ep_count, x, weights, small, w_out, cot, tables, early, name, collective_id):
    rows, width = x.shape
    kinds, depth, _ = weights.shape
    cols = width // ep_count
    tokens = rows * ep_count
    prompt_len = tokens // 2
    ring = ep_count // 2
    far = ring // 2
    offsets = ring_offsets(ring)
    batches = [[0]] + [[2 * k - 1, 2 * k] for k in range(1, far)] + [[ring - 1]]
    gain_row = depth * ep_count // 128
    block, segment, chunk = 256, 512, 64
    pieces = tokens // segment
    scale = HEAD_DIM ** (-0.5)
    dma = pltpu.SemaphoreType.DMA

    def kernel(*refs):
        ins, outs, scratch = split(refs, 7, 14, len(refs) - 21)
        x_ref, weights_ref, small_ref, w_ref, cot_ref, cos_ref, sin_ref = ins
        normed_out, w_all, s_out, full_out, cot_out, cot_other = outs[:6]
        q_out, k_out, v_out, nq_out, nk_out, col_out, att_out, x_land = outs[6:]
        x_s, w_s, s_s, cross, w_ring, cot_ring, w_cross, cot_cross, bufs, loads, dots_s, att_s = split(
            scratch, 5, 3, 2, 3, 5, 5, 4, 4, 5, 2, 5, 4
        )
        rows_v, normed_v, columns_v, gain_v, lin_v = bufs
        rows_sem, normed_sem = loads
        here = Place(ep_count)
        greet(plane_devices(here) + [here.across()])

        cross_own, cross_send, cross_recv = cross
        first = pltpu.make_async_copy(small_ref, s_out.at[here.grp, here.ep], cross_own)
        first.start()

        def small_over(group):
            return remote(
                small_ref, s_out.at[group, here.ep], cross_send.at[0], cross_recv.at[0], here.across()
            )

        small_over(here.grp).start()
        gather = Gather(here, x_ref, x_land, x_s)
        gather.start()
        columns_of = Exchange(
            here,
            lambda e: weights_ref.at[:, :, pl.ds(pl.multiple_of(e * cols, cols), cols)],
            lambda e: columns_v.at[here.grp, e],
            w_s,
        )
        columns_of.start()
        full = Gather(here, w_ref, full_out.at[here.grp], w_ring)
        full_over = Crossing(
            here, lambda e: full_out.at[here.grp, e], lambda e: full_out.at[1 - here.grp, e], w_cross
        )
        cots = Gather(here, cot_ref, cot_out, cot_ring)
        cots_over = Crossing(here, lambda e: cot_other.at[e], lambda e: cot_other.at[e], cot_cross)
        full_over.send(0, w_ref)
        cots_over.send(0, cot_ref)

        first.wait()
        small_over(1 - here.grp).wait_recv()
        small_over(here.grp).wait_send()
        small_copies = []
        for offset in range(1, here.count):
            mine = s_out.at[:, here.ep]
            copy = remote(mine, mine, s_s[0].at[offset], s_s[1].at[offset], here.peer(offset))
            copy.start()
            small_copies.append(copy)
        for offset in range(1, here.count):
            source = s_out.at[:, here.peer(-offset)[1]]
            remote(source, source, s_s[0].at[offset], s_s[1].at[offset], here.peer(offset)).wait_recv()

        def gains(row, half, owner):
            lines = []
            for i in range(2):
                tile = s_out[(owner + i) // ep_count, (owner + i) % ep_count, pl.ds(0, 16)].astype(F32)
                lines.append(tile[row : row + 1, half * depth : (half + 1) * depth])
            return jnp.concatenate(lines, axis=1)

        for i in range(width // 128):
            gain_v[:, i * 128 : (i + 1) * 128] = gains(gain_row, 0, 2 * i)
        gain_q, gain_k = gains(gain_row, 1, 2 * here.ep), gains(gain_row + 1, 0, 2 * here.ep)

        def chip_of(slot):
            return here.index(here.at(offsets[slot]), 0) // 2

        stores = []

        def norm(batch):
            loaded = []
            for i, slot in enumerate(batch):
                loaded.append(pltpu.make_async_copy(x_land.at[pl.ds(2 * chip_of(slot), 2)], rows_v.at[i], rows_sem.at[i]))
                loaded[-1].start()
            for i, slot in enumerate(batch):
                loaded[i].wait()
                chip = chip_of(slot)
                for core in range(2):

                    def run(j, carry, i=i, core=core, chip=chip):
                        at = pl.ds(pl.multiple_of(j * chunk, chunk), chunk)
                        wide = rows_v[i, core, at].astype(F32)
                        r = lax.rsqrt(jnp.mean(wide * wide, axis=-1, keepdims=True) + eps)
                        normed_v[2 * chip + core, at] = (wide * r * gain_v[...]).astype(BF)
                        return carry

                    lax.fori_loop(0, rows // chunk, run, 0)
                at = pl.ds(2 * chip, 2)
                stores.append(pltpu.make_async_copy(normed_v.at[at], normed_out.at[at], normed_sem.at[slot]))
                stores[-1].start()

        def project(batch):
            for slot in batch:
                chip = chip_of(slot)
                lin = mm(normed_v[pl.ds(2 * chip, 2)].reshape(2 * rows, width), w_all[...])
                at = pl.ds(pl.multiple_of(chip * 2 * rows, 2 * rows), 2 * rows)
                lin_v[0, at] = lin[:, :cols]
                lin_v[1, at] = lin[:, cols : 2 * cols]
                v_out[at] = lin[:, 2 * cols :].astype(BF)

        over = remote(columns_v.at[here.grp], columns_v.at[here.grp], cross_send.at[1], cross_recv.at[1], here.across())
        gather.settle()
        for number, batch in enumerate(batches):
            gather.side(number - 1)
            norm(batch)
            if number < far:
                gather.step(number)
            if number == 1:
                columns_of.arrive()
                over.start()
            if number == far - 1:
                cots.start()
                full.start()
                remote(
                    columns_v.at[1 - here.grp],
                    columns_v.at[1 - here.grp],
                    cross_send.at[1],
                    cross_recv.at[1],
                    here.across(),
                ).wait_recv()
                for owner in range(2 * ep_count):
                    for kind in range(kinds):
                        w_all[owner * depth : (owner + 1) * depth, kind * cols : (kind + 1) * cols] = columns_v[
                            owner // ep_count, owner % ep_count, kind
                        ]
                for earlier in batches[:number]:
                    project(earlier)
            if number >= far - 1:
                project(batch)

        def pass_on(ring_gather, crossing, step, count):
            ring_gather.step(step)
            for slot in batches[step + 1]:
                if slot < count:
                    crossing.send(slot, ring_gather.dst.at[here.chip(offsets[slot])])

        dots_v, dots_all, dots_sems = dots_s[0], dots_s[1], dots_s[2:]
        stats = []
        for piece in range(pieces):
            at = pl.ds(piece * segment, segment)
            for kind in range(2):
                lin = lin_v[kind, at]
                stats.append(jnp.sum(lin * lin, axis=-1, keepdims=True))
        dots_v[...] = as_rows(stats, dots_v.shape[0])
        spread_dots = Exchange(here, lambda e: dots_v, lambda e: dots_all.at[e], dots_sems)
        spread_dots.start()
        pass_on(full, full_over, 0, ring)
        pass_on(cots, cots_over, 0, early)
        spread_dots.arrive()
        total = dots_all[0]
        for e in range(1, ep_count):
            total = total + dots_all[e]
        r_all = as_columns(lax.rsqrt(total / width + eps))
        lane = lax.broadcasted_iota(jnp.int32, (segment, 128), 1)
        for piece in range(pieces):
            at = pl.ds(piece * segment, segment)
            kept = jnp.zeros((segment, 128), F32)
            for kind, (gain, n_out, out) in enumerate(((gain_q, nq_out, q_out), (gain_k, nk_out, k_out))):
                r = r_all[:, 2 * piece + kind : 2 * piece + kind + 1]
                n = lin_v[kind, at] * r
                n_out[at] = n
                n = n * gain
                out[at] = (n * cos_ref[at] + rolled(n) * sin_ref[at]).astype(BF)
                kept = jnp.where(lane == 1 + kind, r, kept)
            col_out[at] = kept

        att_v, att_sems = att_s[0], att_s[1:]
        per = block // rows
        line = lax.broadcasted_iota(jnp.int32, (block, block), 0)
        column_at = lax.broadcasted_iota(jnp.int32, (block, block), 1)
        causal = line >= column_at
        same = causal & (line // rows == column_at // rows)
        block_lane = lax.broadcasted_iota(jnp.int32, (block, 128), 1)

        def attend(first, spans):
            at = pl.ds(first, block)
            q = q_out[at]
            scores = []
            for begin, length, mask in spans:
                score = mm_nt(q, k_out[pl.ds(begin, length)]) * scale
                scores.append(score if mask is None else jnp.where(mask, score, -1e30))
            top = jnp.max(scores[0], axis=-1, keepdims=True)
            for score in scores[1:]:
                top = jnp.maximum(top, jnp.max(score, axis=-1, keepdims=True))
            powers = [jnp.exp(score - top) for score in scores]
            summed = sum(jnp.sum(power, axis=-1, keepdims=True) for power in powers)
            out = jnp.zeros((block, cols), F32)
            for (begin, length, _), power in zip(spans, powers):
                out = out + mm((power / summed).astype(BF), v_out[pl.ds(begin, length)])
            att_v[pl.ds(first // rows, per)] = out.astype(BF).reshape(per, rows, cols)
            col_out[at] = jnp.where(block_lane == 0, top + jnp.log(summed), col_out[at])

        for number in range(prompt_len // block):
            spans = [(0, number * block, None)] if number else []
            attend(number * block, spans + [(number * block, block, causal)])
        pass_on(full, full_over, 1, ring)
        pass_on(cots, cots_over, 1, early)

        def later(number, carry):
            first = pl.multiple_of(prompt_len + number * block, block)
            attend(first, [(0, prompt_len, None), (first, block, same)])
            return carry

        lax.fori_loop(0, (tokens - prompt_len) // block, later, 0)
        attended = Exchange(here, lambda e: att_v.at[e], lambda e: att_out.at[e], att_sems)
        attended.start()
        for step in range(2, far):
            pass_on(full, full_over, step, ring)
            pass_on(cots, cots_over, step, early)
        attended.arrive()
        for step in range(-1, far):
            full.side(step)
            cots.side(step)
        for slot in range(ring):
            full_over.take(slot)
            if slot < early:
                cots_over.take(slot)
        for slot in range(ring):
            full_over.settle(slot)
            if slot < early:
                cots_over.settle(slot)
        full.settle()
        cots.settle()
        for part in (gather, full, cots, full_over, cots_over, columns_of, spread_dots, attended):
            part.finish()
        over.wait_send()
        for copy in small_copies:
            copy.wait_send()
        for copy in stores:
            copy.wait()

    hbm = pl.BlockSpec(memory_space=pl.ANY)
    vmem = pl.BlockSpec(memory_space=pltpu.VMEM)

    def low(*shape):
        return jax.ShapeDtypeStruct(shape, BF)

    def wide(*shape):
        return jax.ShapeDtypeStruct(shape, F32)

    outs = pl.pallas_call(
        kernel,
        out_shape=[
            low(ep_count, rows, width),
            low(width, kinds * cols),
            low(2, ep_count, *small.shape),
            low(2, ep_count, *w_out.shape),
            low(ep_count, rows, width),
            low(ep_count, rows, width),
            low(tokens, cols),
            low(tokens, cols),
            low(tokens, cols),
            wide(tokens, cols),
            wide(tokens, cols),
            wide(tokens, 128),
            low(ep_count, rows, cols),
            low(ep_count, rows, width),
        ],
        in_specs=[hbm, hbm, hbm, hbm, hbm, vmem, vmem],
        out_specs=[hbm, vmem, vmem, hbm, hbm, hbm] + [vmem] * 6 + [hbm, hbm],
        scratch_shapes=Gather.scratch(ep_count)
        + Exchange.scratch(ep_count)
        + [dma((ep_count,)), dma((ep_count,))]
        + [dma, dma((2,)), dma((2,))]
        + Gather.scratch(ep_count)
        + Gather.scratch(ep_count)
        + Crossing.scratch(ep_count)
        + Crossing.scratch(ep_count)
        + [
            pltpu.VMEM((2, 2, rows, width), BF),
            pltpu.VMEM((ep_count, rows, width), BF),
            pltpu.VMEM((2, ep_count, kinds, depth, cols), BF),
            pltpu.VMEM((1, width), F32),
            pltpu.VMEM((2, tokens, cols), F32),
        ]
        + [dma((2,)), dma((ring,))]
        + [pltpu.VMEM((8, segment), F32), pltpu.VMEM((ep_count, 8, segment), F32)]
        + Exchange.scratch(ep_count)
        + [pltpu.VMEM((ep_count, rows, cols), BF)]
        + Exchange.scratch(ep_count),
        compiler_params=pltpu.CompilerParams(
            collective_id=collective_id, has_side_effects=True, vmem_limit_bytes=56 << 20
        ),
        name=name,
    )(x, weights, small, w_out, cot, *tables)
    return outs[:-1]


def angles_of(position):
    half_dim = HEAD_DIM // 2
    frequency = theta_base ** (-2.0 * jnp.arange(half_dim, dtype=F32) / HEAD_DIM)
    angles = position.astype(F32)[:, None] * frequency[None, :]
    return jnp.cos(angles), jnp.sin(angles)


def per_device(
    block_input,
    cotangent,
    routes,
    w_query,
    w_key,
    w_value,
    w_output,
    w_router,
    gain_attn,
    gain_query,
    gain_key,
    gain_mlp,
    w_gate,
    w_up,
    w_down,
):
    rows, width = block_input.shape
    top_count = routes.shape[1]
    ep_count = lax.axis_size("ep")
    grp_count = lax.axis_size("grp")
    me = lax.axis_index("ep")
    my_group = lax.axis_index("grp")
    tokens = rows * ep_count
    prompt_len = tokens // 2
    capacity = min(rows, rows * top_count * 33 // (32 * ep_count))
    cols = width // ep_count
    scale = HEAD_DIM ** (-0.5)
    depth = w_query.shape[0]

    chosen = jnp.any(routes[:, :, None] == jnp.arange(ep_count, dtype=jnp.int32), axis=1)
    per_row = 128
    router_rows = depth * ep_count // per_row
    gains = jnp.concatenate([gain_attn, gain_query, gain_key, gain_mlp])
    gain_rows = gains.shape[0] // per_row
    small = jnp.concatenate(
        [
            w_router.reshape(router_rows, per_row),
            gains.reshape(gain_rows, per_row),
            jnp.zeros((16 - router_rows - gain_rows, per_row), BF),
            chosen.T.astype(BF),
        ]
    )
    weights = jnp.stack([w_query, w_key, w_value])
    token = jnp.arange(tokens, dtype=jnp.int32)
    position = jnp.where(token < prompt_len, token, prompt_len + (token - prompt_len) % rows)
    cosine, sine = angles_of(position)
    tables = (jnp.concatenate([cosine, cosine], axis=1), jnp.concatenate([-sine, sine], axis=1))
    early = ep_count // 4
    normed_all, w_all, smalls, full_output, cot_own, cot_other, query, key, value, n_q, n_k, columns, tiles = attention(
        ep_count, block_input, weights, small, w_output, cotangent, tables, early, "attention", 1
    )
    normed_all = normed_all.reshape(tokens, width)
    full_output = full_output.reshape(width, width)
    smalls = smalls.reshape(grp_count * ep_count, small.shape[0], per_row)
    full_router = smalls[:, :router_rows].reshape(width, ep_count)
    gains = smalls[:, router_rows : router_rows + gain_rows].reshape(-1, 4, depth).transpose(1, 0, 2).reshape(4, width)
    gain_first, gain_qnorm, gain_knorm, gain_second = (gains[i].astype(F32) for i in range(4))
    chosen_all = smalls[:, 16:].reshape(grp_count, ep_count, ep_count, rows)

    gain_q = lax.dynamic_slice(gain_qnorm, (me * cols,), (cols,))
    gain_k = lax.dynamic_slice(gain_knorm, (me * cols,), (cols,))
    att_loc = tiles.transpose(1, 0, 2).reshape(rows, width)

    inputs = block_input.astype(F32)
    residual = inputs + mm(att_loc, full_output)
    r_m = lax.rsqrt(jnp.mean(residual * residual, axis=-1, keepdims=True) + eps)
    n_m = residual * r_m
    normed_mlp = (n_m * gain_second).astype(BF)
    pair = 2 * rows
    slots = -(-2 * capacity // 16) * 16
    chips = ep_count // 2
    groups = jnp.stack([my_group, 1 - my_group])
    mine = lax.dynamic_index_in_dim(chosen_all, me, 2, keepdims=False)[groups].reshape(2, chips, pair)
    slot = jnp.cumsum(mine.astype(jnp.int32), axis=-1) - 1
    places = jnp.arange(slots, dtype=jnp.int32)
    hots = ((slot[:, :, None, :] == places[:, None]) & (mine[:, :, None, :] > 0)).astype(BF)
    hots_t = ((slot[:, :, :, None] == places) & (mine[:, :, :, None] > 0)).astype(BF)
    router = jnp.pad(full_router, ((0, 0), (0, per_row - ep_count)))
    gate_w, up_w, down_w = w_gate[0], w_up[0], w_down[0]
    _, _, units, grad_out, hidden, grad_gate_pre, grad_up_pre, _, result_terms, _, d_normed_mlp, gate_grads, _ = experts(
        ep_count, normed_mlp, cot_own, cot_other, early, hots, hots_t, router, gate_w, up_w, down_w, "experts", 4
    )
    gate_grads = gate_grads[:, 0]

    probs = jax.nn.softmax(mm(normed_mlp, full_router), axis=-1)
    d_probs = gate_grads.T
    d_logits = (probs * (d_probs - jnp.sum(probs * d_probs, axis=-1, keepdims=True))).astype(BF)
    local_router = mm_tn(normed_mlp, d_logits)
    d_normed_mlp = d_normed_mlp + mm_nt(d_logits, full_router)
    local_gain_mlp = jnp.sum(d_normed_mlp * n_m, axis=0)
    d_n = d_normed_mlp * gain_second
    d_residual = cotangent.astype(F32) + r_m * (d_n - n_m * jnp.mean(n_m * d_n, axis=-1, keepdims=True))
    d_proj = d_residual.astype(BF)
    d_attended = mm_nt(d_proj, full_output).astype(BF)
    local_output = mm_tn(att_loc, d_proj).astype(BF)
    d_attended = d_attended.reshape(rows, ep_count, cols).transpose(1, 0, 2)

    gain_rows_own = jnp.stack([gain_q, gain_k])
    owners = grp_count * ep_count
    tiles = jnp.concatenate(
        [
            local_router.reshape(owners, router_rows, per_row),
            jnp.pad(local_gain_mlp.reshape(owners, 1, depth), ((0, 0), (0, 16 - router_rows - 1), (0, per_row - depth))),
        ],
        axis=1,
    )
    d_normed, grad_output, mixture, grad_w, tiles, late, grad_gate, grad_up, grad_down = backward(
        ep_count,
        d_attended,
        (query, key, value, n_q, n_k),
        columns,
        tables,
        gain_rows_own,
        w_all,
        normed_all,
        local_output.reshape(grp_count, chips, 2, depth, width),
        result_terms,
        tiles,
        [a.reshape(-1, a.shape[-1]) for a in (units, grad_out, hidden, grad_gate_pre, grad_up_pre)],
        "backward",
        9,
    )[:9]
    block_output = (residual + mixture).astype(BF)
    r_a = lax.rsqrt(jnp.mean(inputs * inputs, axis=-1, keepdims=True) + eps)
    n_a = inputs * r_a
    d_n = d_normed * gain_first
    input_grad = d_residual + r_a * (d_n - n_a * jnp.mean(n_a * d_n, axis=-1, keepdims=True))
    my_rows = my_group * ep_count + me
    grad_w = grad_w.reshape(ep_count, depth, 3, cols).transpose(2, 1, 0, 3).reshape(3, depth, width).astype(F32)
    sums = jnp.sum(tiles, axis=0)
    grad_router = sums[:router_rows].reshape(depth, ep_count)
    gain_part = jnp.sum(late[:, 2, :depth], axis=0) / lax.dynamic_slice(gain_first, (my_rows * depth,), (depth,))
    late = jnp.sum(late.reshape(grp_count, ep_count, 8, cols), axis=0)[:, :2].transpose(1, 0, 2).reshape(2, width)
    late = lax.dynamic_slice(late, (0, my_rows * depth), (2, depth))
    gain_sums = [gain_part, late[0], late[1], sums[router_rows, :depth]]
    grad_gate, grad_up, grad_down = (grad.astype(F32)[None] for grad in (grad_gate, grad_up, grad_down))
    return (
        block_output,
        input_grad,
        grad_w[0],
        grad_w[1],
        grad_w[2],
        grad_output,
        grad_router,
        gain_sums[0],
        gain_sums[1],
        gain_sums[2],
        gain_sums[3],
        grad_gate,
        grad_up,
        grad_down,
    )


def plain_scale(values, gain_vec):
    return values * lax.rsqrt(jnp.mean(values * values, axis=-1, keepdims=True) + eps) * gain_vec


def rotate(values, position):
    token_count = values.shape[0]
    by_head = values.reshape(token_count, -1, HEAD_DIM)
    half_dim = HEAD_DIM // 2
    frequency = theta_base ** (-2.0 * jnp.arange(half_dim, dtype=jnp.float32) / HEAD_DIM)
    angles = position.astype(jnp.float32)[:, None] * frequency[None, :]
    cosine = jnp.cos(angles)[:, None, :]
    sine_part = jnp.sin(angles)[:, None, :]
    former = by_head[..., :half_dim]
    latter = by_head[..., half_dim:]
    turned = jnp.concatenate(
        [former * cosine - latter * sine_part, latter * cosine + former * sine_part], axis=-1
    )
    return turned.reshape(token_count, -1)


def masked_scores(query, keys, allowed, scale):
    raw_scores = jnp.einsum("qhd,khd->hqk", query, keys, preferred_element_type=jnp.float32) * scale
    return jnp.where(allowed[None], raw_scores, -1e30)


def plain_attend(query, keys, values, allowed, scale, head_group):
    outputs = []
    log_totals = []
    for head_start in range(0, query.shape[1], head_group):
        head_slice = slice(head_start, head_start + head_group)
        scores = masked_scores(query[:, head_slice], keys[:, head_slice], allowed, scale)
        largest = jnp.max(scores, axis=-1, keepdims=True)
        exponent = jnp.exp(scores - largest)
        summed = jnp.sum(exponent, axis=-1, keepdims=True)
        weights = (exponent / summed).astype(jnp.bfloat16)
        outputs.append(
            jnp.einsum(
                "hqk,khd->qhd", weights, values[:, head_slice], preferred_element_type=jnp.float32
            )
        )
        log_totals.append(largest + jnp.log(summed))
    return (jnp.concatenate(outputs, axis=1), jnp.concatenate(log_totals, axis=0))


def plain_attend_back(query, keys, values, grad_out, log_totals, allowed, scale, head_group):
    query_grads = []
    key_grads = []
    value_grads = []
    for head_start in range(0, query.shape[1], head_group):
        head_slice = slice(head_start, head_start + head_group)
        query_part = query[:, head_slice]
        keys_part = keys[:, head_slice]
        grad_part = grad_out[:, head_slice]
        scores = masked_scores(query_part, keys_part, allowed, scale)
        weights = jnp.where(allowed[None], jnp.exp(scores - log_totals[head_slice]), 0.0)
        grad_weights = jnp.einsum(
            "qhd,khd->hqk", grad_part, values[:, head_slice], preferred_element_type=jnp.float32
        )
        inner = jnp.sum(weights * grad_weights, axis=-1, keepdims=True)
        grad_scores = (weights * (grad_weights - inner)).astype(jnp.bfloat16)
        query_grads.append(
            jnp.einsum("hqk,khd->qhd", grad_scores, keys_part, preferred_element_type=jnp.float32)
            * scale
        )
        key_grads.append(
            jnp.einsum("hqk,qhd->khd", grad_scores, query_part, preferred_element_type=jnp.float32)
            * scale
        )
        value_grads.append(
            jnp.einsum(
                "hqk,qhd->khd",
                weights.astype(jnp.bfloat16),
                grad_part,
                preferred_element_type=jnp.float32,
            )
        )
    return (
        jnp.concatenate(query_grads, axis=1),
        jnp.concatenate(key_grads, axis=1),
        jnp.concatenate(value_grads, axis=1),
    )


def per_device_plain(
    block_input,
    cotangent,
    routes,
    w_query,
    w_key,
    w_value,
    w_output,
    w_router,
    gain_attn,
    gain_query,
    gain_key,
    gain_mlp,
    w_gate,
    w_up,
    w_down,
):
    row_count, model_width = block_input.shape
    top_count = routes.shape[1]
    ep_count = lax.axis_size("ep")
    my_index = lax.axis_index("ep")
    half_count = ep_count // 2
    prompt_len = row_count * half_count
    capacity = min(row_count, row_count * top_count * 33 // (32 * ep_count))
    head_count = model_width // HEAD_DIM
    head_group = math.gcd(4, head_count)
    scale = HEAD_DIM ** (-0.5)
    gathered = (
        lax.all_gather(w_query, ("grp", "ep"), axis=0, tiled=True),
        lax.all_gather(w_key, ("grp", "ep"), axis=0, tiled=True),
        lax.all_gather(w_value, ("grp", "ep"), axis=0, tiled=True),
        lax.all_gather(w_output, ("grp", "ep"), axis=0, tiled=True),
        lax.all_gather(w_router, ("grp", "ep"), axis=0, tiled=True),
        lax.all_gather(gain_attn, ("grp", "ep"), axis=0, tiled=True),
        lax.all_gather(gain_query, ("grp", "ep"), axis=0, tiled=True),
        lax.all_gather(gain_key, ("grp", "ep"), axis=0, tiled=True),
        lax.all_gather(gain_mlp, ("grp", "ep"), axis=0, tiled=True),
    )
    full_query, full_key, full_value, full_output, full_router = (
        gathered[0],
        gathered[1],
        gathered[2],
        gathered[3],
        gathered[4],
    )
    gain_first = gathered[5].astype(jnp.float32)
    gain_qnorm = gathered[6].astype(jnp.float32)
    gain_knorm = gathered[7].astype(jnp.float32)
    gain_second = gathered[8].astype(jnp.float32)
    offsets = jnp.arange(row_count, dtype=jnp.int32)
    in_prompt = my_index < half_count
    position = jnp.where(in_prompt, my_index * row_count + offsets, prompt_len + offsets)
    key_position = jnp.concatenate([jnp.arange(prompt_len, dtype=jnp.int32), prompt_len + offsets])
    from_prompt = jnp.arange(prompt_len + row_count, dtype=jnp.int32) < prompt_len
    allowed = (key_position[None, :] <= position[:, None]) & (
        from_prompt[None, :] | jnp.logical_not(in_prompt)
    )

    def prepare(linear, gain_vec):
        return rotate(plain_scale(linear, gain_vec), position)

    inputs = block_input.astype(jnp.float32)
    normed = plain_scale(inputs, gain_first).astype(jnp.bfloat16)
    query_lin = jnp.dot(normed, full_query, preferred_element_type=jnp.float32)
    key_lin = jnp.dot(normed, full_key, preferred_element_type=jnp.float32)
    value_lin = jnp.dot(normed, full_value, preferred_element_type=jnp.float32)
    query_low = prepare(query_lin, gain_qnorm).astype(jnp.bfloat16)
    key_low = prepare(key_lin, gain_knorm).astype(jnp.bfloat16)
    value_low = value_lin.astype(jnp.bfloat16)
    shared = (
        lax.all_gather(key_low, "ep", axis=0, tiled=True),
        lax.all_gather(value_low, "ep", axis=0, tiled=True),
    )
    keys = jnp.concatenate([shared[0][:prompt_len], key_low]).reshape(-1, head_count, HEAD_DIM)
    values = jnp.concatenate([shared[1][:prompt_len], value_low]).reshape(-1, head_count, HEAD_DIM)
    query = query_low.reshape(row_count, head_count, HEAD_DIM)
    attn_out, log_totals = plain_attend(query, keys, values, allowed, scale, head_group)
    attended = attn_out.reshape(row_count, model_width).astype(jnp.bfloat16)
    residual = inputs + jnp.dot(attended, full_output, preferred_element_type=jnp.float32)
    normed_mlp = plain_scale(residual, gain_second).astype(jnp.bfloat16)
    logits = jnp.dot(normed_mlp, full_router, preferred_element_type=jnp.float32)
    probs = jax.nn.softmax(logits, axis=-1)
    picks = routes[:, :, None] == jnp.arange(ep_count, dtype=jnp.int32)[None, None, :]
    gates = jnp.sum(jnp.where(picks, probs[:, None, :], 0.0), axis=-1)
    hot_table = picks.reshape(-1, ep_count).astype(jnp.int32)
    before = jnp.cumsum(hot_table, axis=0) - hot_table
    slot_index = jnp.sum(before * hot_table, axis=1)
    target = routes.reshape(-1) * capacity + slot_index
    sentinel = row_count * top_count
    source = (
        jnp.full((ep_count * capacity,), sentinel, jnp.int32)
        .at[target]
        .set(jnp.arange(sentinel, dtype=jnp.int32))
    )
    token_of = source // top_count
    padded_rows = jnp.concatenate([normed_mlp, jnp.zeros((1, model_width), jnp.bfloat16)])
    outgoing = padded_rows[token_of].reshape(ep_count, capacity, model_width)
    arrived = lax.all_to_all(outgoing, "ep", split_axis=0, concat_axis=0, tiled=True)
    units = arrived.reshape(-1, model_width)
    gate_w = w_gate[0]
    up_w = w_up[0]
    down_w = w_down[0]
    gate_pre = jnp.dot(units, gate_w, preferred_element_type=jnp.float32)
    up_pre = jnp.dot(units, up_w, preferred_element_type=jnp.float32)
    hidden = (jax.nn.silu(gate_pre) * up_pre).astype(jnp.bfloat16)
    expert_result = jnp.dot(hidden, down_w, preferred_element_type=jnp.float32).astype(jnp.bfloat16)
    returned = lax.all_to_all(
        expert_result.reshape(ep_count, capacity, model_width),
        "ep",
        split_axis=0,
        concat_axis=0,
        tiled=True,
    )
    picked = (
        returned.reshape(-1, model_width)[target]
        .reshape(row_count, top_count, model_width)
        .astype(jnp.float32)
    )
    output_full = residual + jnp.sum(gates[:, :, None] * picked, axis=1)
    block_output = output_full.astype(jnp.bfloat16)
    back_query, back_key, back_value, back_output, back_router = (
        full_query,
        full_key,
        full_value,
        full_output,
        full_router,
    )
    grad_top = cotangent.astype(jnp.float32)
    grad_gates = jnp.sum(grad_top[:, None, :] * picked, axis=-1)
    grad_expert = (
        (gates[:, :, None] * grad_top[:, None, :]).astype(jnp.bfloat16).reshape(-1, model_width)
    )
    padded_grads = jnp.concatenate([grad_expert, jnp.zeros((1, model_width), jnp.bfloat16)])
    grad_outgoing = padded_grads[source].reshape(ep_count, capacity, model_width)
    grad_arrived = lax.all_to_all(
        grad_outgoing, "ep", split_axis=0, concat_axis=0, tiled=True
    ).reshape(-1, model_width)
    grad_hidden = jnp.einsum("nd,fd->nf", grad_arrived, down_w, preferred_element_type=jnp.float32)
    sigma = jax.nn.sigmoid(gate_pre)
    grad_gate_pre = (grad_hidden * up_pre * sigma * (1.0 + gate_pre * (1.0 - sigma))).astype(
        jnp.bfloat16
    )
    grad_up_pre = (grad_hidden * gate_pre * sigma).astype(jnp.bfloat16)
    local_down = jnp.einsum("nf,nd->fd", hidden, grad_arrived, preferred_element_type=jnp.float32)
    local_gate = jnp.einsum("nd,nf->df", units, grad_gate_pre, preferred_element_type=jnp.float32)
    local_up = jnp.einsum("nd,nf->df", units, grad_up_pre, preferred_element_type=jnp.float32)
    grad_units = jnp.einsum("nf,df->nd", grad_gate_pre, gate_w, preferred_element_type=jnp.float32)
    grad_units = grad_units + jnp.einsum(
        "nf,df->nd", grad_up_pre, up_w, preferred_element_type=jnp.float32
    )
    grad_units = grad_units.astype(jnp.bfloat16).reshape(ep_count, capacity, model_width)
    grad_returned = lax.all_to_all(
        grad_units, "ep", split_axis=0, concat_axis=0, tiled=True
    ).reshape(-1, model_width)
    grad_normed_mlp = jnp.sum(
        grad_returned[target].reshape(row_count, top_count, model_width).astype(jnp.float32), axis=1
    )
    expert_sums = (
        lax.psum(local_gate[None].astype(jnp.bfloat16), "grp").astype(jnp.float32),
        lax.psum(local_up[None].astype(jnp.bfloat16), "grp").astype(jnp.float32),
        lax.psum(local_down[None].astype(jnp.bfloat16), "grp").astype(jnp.float32),
    )
    grad_probs = jnp.sum(jnp.where(picks, grad_gates[:, :, None], 0.0), axis=1)
    grad_logits = (
        probs * (grad_probs - jnp.sum(probs * grad_probs, axis=-1, keepdims=True))
    ).astype(jnp.bfloat16)
    local_router = jnp.einsum(
        "rd,re->de", normed_mlp, grad_logits, preferred_element_type=jnp.float32
    )
    grad_normed_mlp = grad_normed_mlp + jnp.einsum(
        "re,de->rd", grad_logits, back_router, preferred_element_type=jnp.float32
    )
    unused_mlp, second_back = jax.vjp(plain_scale, residual, gain_second)
    grad_from_mlp, local_gain_mlp = second_back(grad_normed_mlp)
    grad_residual = grad_top + grad_from_mlp
    grad_proj = grad_residual.astype(jnp.bfloat16)
    local_output = jnp.einsum("rd,re->de", attended, grad_proj, preferred_element_type=jnp.float32)
    grad_attended = jnp.einsum(
        "re,de->rd", grad_proj, back_output, preferred_element_type=jnp.float32
    )
    grad_attended = grad_attended.astype(jnp.bfloat16).reshape(row_count, head_count, HEAD_DIM)
    grad_query_rot, grad_keys, grad_values = plain_attend_back(
        query, keys, values, grad_attended, log_totals, allowed, scale, head_group
    )
    grad_keys = grad_keys.reshape(-1, model_width)
    grad_values = grad_values.reshape(-1, model_width)
    padding = jnp.zeros((ep_count * row_count - prompt_len, model_width), jnp.float32)
    key_share, value_share = (
        lax.psum_scatter(
            jnp.concatenate([grad_keys[:prompt_len], padding]).astype(jnp.bfloat16),
            "ep",
            scatter_dimension=0,
            tiled=True,
        ).astype(jnp.float32),
        lax.psum_scatter(
            jnp.concatenate([grad_values[:prompt_len], padding]).astype(jnp.bfloat16),
            "ep",
            scatter_dimension=0,
            tiled=True,
        ).astype(jnp.float32),
    )
    grad_key_rot = key_share + grad_keys[prompt_len:]
    grad_value_lin = (value_share + grad_values[prompt_len:]).astype(jnp.bfloat16)
    unused_query, query_back = jax.vjp(prepare, query_lin, gain_qnorm)
    grad_query_lin, local_gain_query = query_back(grad_query_rot.reshape(row_count, model_width))
    unused_key, key_back = jax.vjp(prepare, key_lin, gain_knorm)
    grad_key_lin, local_gain_key = key_back(grad_key_rot)
    grad_query_low = grad_query_lin.astype(jnp.bfloat16)
    grad_key_low = grad_key_lin.astype(jnp.bfloat16)
    local_query = jnp.einsum(
        "rd,re->de", normed, grad_query_low, preferred_element_type=jnp.float32
    )
    local_key = jnp.einsum("rd,re->de", normed, grad_key_low, preferred_element_type=jnp.float32)
    local_value = jnp.einsum(
        "rd,re->de", normed, grad_value_lin, preferred_element_type=jnp.float32
    )
    grad_normed = jnp.einsum(
        "re,de->rd", grad_query_low, back_query, preferred_element_type=jnp.float32
    )
    grad_normed = grad_normed + jnp.einsum(
        "re,de->rd", grad_key_low, back_key, preferred_element_type=jnp.float32
    )
    grad_normed = grad_normed + jnp.einsum(
        "re,de->rd", grad_value_lin, back_value, preferred_element_type=jnp.float32
    )
    unused_first, first_back = jax.vjp(plain_scale, inputs, gain_first)
    grad_from_attn, local_gain_attn = first_back(grad_normed)
    input_grad = grad_residual + grad_from_attn
    summed_grads = (
        lax.psum_scatter(local_query, ("grp", "ep"), scatter_dimension=0, tiled=True),
        lax.psum_scatter(local_key, ("grp", "ep"), scatter_dimension=0, tiled=True),
        lax.psum_scatter(local_value, ("grp", "ep"), scatter_dimension=0, tiled=True),
        lax.psum_scatter(local_output, ("grp", "ep"), scatter_dimension=0, tiled=True),
        lax.psum_scatter(local_router, ("grp", "ep"), scatter_dimension=0, tiled=True),
        lax.psum_scatter(local_gain_attn, ("grp", "ep"), scatter_dimension=0, tiled=True),
        lax.psum_scatter(local_gain_query, ("grp", "ep"), scatter_dimension=0, tiled=True),
        lax.psum_scatter(local_gain_key, ("grp", "ep"), scatter_dimension=0, tiled=True),
        lax.psum_scatter(local_gain_mlp, ("grp", "ep"), scatter_dimension=0, tiled=True),
    )
    return (
        block_output,
        input_grad,
        summed_grads[0],
        summed_grads[1],
        summed_grads[2],
        summed_grads[3],
        summed_grads[4],
        summed_grads[5],
        summed_grads[6],
        summed_grads[7],
        summed_grads[8],
        expert_sums[0],
        expert_sums[1],
        expert_sums[2],
    )


def solution(mesh):
    both = ("grp", "ep")
    return jax.shard_map(
        per_device if mesh.shape["grp"] == 2 else per_device_plain,
        mesh=mesh,
        in_specs=(P(both, None),) * 8 + (P(both),) * 4 + (P("ep", None, None),) * 3,
        out_specs=(P(both, None),) * 7 + (P(both),) * 4 + (P("ep", None, None),) * 3,
        check_vma=False,
    )
```

```python
import math

import jax
import jax.numpy as jnp
import numpy as np
from jax import lax
from jax.experimental import pallas as pl
from jax.experimental.pallas import tpu as pltpu
from jax.sharding import PartitionSpec as P

HEAD_DIM = 128
MESH = pl.DeviceIdType.MESH
BF = jnp.bfloat16
F32 = jnp.float32


eps = 1e-05
theta_base = 10000.0


def mm(a, b):
    return jnp.dot(a, b, preferred_element_type=F32)


def mm_nt(a, b):
    return lax.dot_general(a, b, (((1,), (1,)), ((), ())), preferred_element_type=F32)


def mm_tn(a, b):
    return lax.dot_general(a, b, (((0,), (0,)), ((), ())), preferred_element_type=F32)


class Place:
    def __init__(self, ep_count):
        self.grp = lax.axis_index("grp")
        self.ep = lax.axis_index("ep")
        self.count = ep_count
        self.ring = ep_count // 2
        self.half = self.ring // 2
        self.core = self.ep % 2
        y = (self.ep // 2) % 2
        z = self.ep // 4
        self.place = z + y * (self.ring - 1 - 2 * z)

    def index(self, place, core):
        y = place // self.half
        z = place + y * (self.ring - 1 - 2 * place)
        return (z * 2 + y) * 2 + core

    def at(self, offset):
        return (self.place + offset + self.ring) % self.ring

    def chip(self, offset):
        return self.index(self.at(offset), self.core)

    def right(self):
        return (self.grp, self.chip(1))

    def left(self):
        return (self.grp, self.chip(-1))

    def sibling(self):
        return (self.grp, self.index(self.place, 1 - self.core))

    def across(self):
        return (1 - self.grp, self.ep)

    def peer(self, offset):
        return (self.grp, (self.ep + offset + self.count) % self.count)


def greet(devices):
    barrier = pltpu.get_barrier_semaphore()
    for device in devices:
        pl.semaphore_signal(barrier, inc=1, device_id=device, device_id_type=MESH)
    pl.semaphore_wait(barrier, len(devices))


def remote(src, dst, send, recv, device):
    return pltpu.make_async_remote_copy(
        src_ref=src, dst_ref=dst, send_sem=send, recv_sem=recv, device_id=device, device_id_type=MESH
    )


class Gather:
    def __init__(self, here, src, dst, sems, reach=None):
        self.here, self.src, self.dst, self.reach = here, src, dst, reach
        self.ring_send, self.ring_recv, self.side_send, self.side_recv, self.own_sem = sems
        self.rows = dst.shape[1] // 2
        self.far = here.ring // 2
        self.started = []

    @staticmethod
    def scratch(ep_count):
        far = ep_count // 4
        ring = pltpu.SemaphoreType.DMA((2, far, 2))
        side = pltpu.SemaphoreType.DMA((2, far + 1, 2))
        return [ring, ring, side, side, pltpu.SemaphoreType.DMA]

    def block(self, index, part):
        return self.dst.at[index, pl.ds(part * self.rows, self.rows)]

    def go(self, copy):
        copy.start()
        self.started.append(copy)

    def hops(self, way, part):
        if self.reach is not None:
            return self.reach
        return self.far if way == part else self.far - 1

    def ring_copy(self, way, step, part, src, index):
        device = self.here.right() if way == 0 else self.here.left()
        return remote(
            src, self.block(index, part), self.ring_send.at[way, step, part], self.ring_recv.at[way, step, part], device
        )

    def side_copy(self, way, step, part, src, index):
        return remote(
            src,
            self.block(index, part),
            self.side_send.at[way, step, part],
            self.side_recv.at[way, step, part],
            self.here.sibling(),
        )

    def start(self):
        here = self.here
        for part in range(2):
            src = self.src.at[pl.ds(part * self.rows, self.rows)]
            for way in range(2):
                if self.hops(way, part) > 0:
                    self.go(self.ring_copy(way, 0, part, src, here.ep))
            self.go(self.side_copy(0, 0, part, src, here.ep))
        if self.reach is not None:
            return
        self.own = pltpu.make_async_copy(self.src, self.dst.at[here.ep], self.own_sem)
        self.own.start()

    def step(self, step):
        here = self.here
        for part in range(2):
            for way in range(2):
                if step < self.hops(way, part):
                    index = here.chip(-1 - step if way == 0 else 1 + step)
                    src = self.block(index, part)
                    self.ring_copy(way, step, part, src, index).wait_recv()
                    if step + 1 < self.hops(way, part):
                        self.go(self.ring_copy(way, step + 1, part, src, index))
                    self.go(self.side_copy(way, step + 1, part, src, index))

    def side(self, step):
        here = self.here
        for part in range(2):
            for way in range(2):
                if (step < 0 and way == 0) or (0 <= step < self.hops(way, part)):
                    offset = 0 if step < 0 else (-1 - step if way == 0 else 1 + step)
                    index = here.index(here.at(offset), 1 - here.core)
                    self.side_copy(way, step + 1, part, self.block(index, part), index).wait_recv()

    def settle(self):
        self.own.wait()

    def finish(self):
        for copy in self.started:
            copy.wait_send()


class Exchange:
    def __init__(self, here, src, dst, sems):
        self.here, self.src, self.dst = here, src, dst
        self.send, self.recv, self.own_sem = sems

    @staticmethod
    def scratch(ep_count):
        return [
            pltpu.SemaphoreType.DMA((ep_count,)),
            pltpu.SemaphoreType.DMA((ep_count,)),
            pltpu.SemaphoreType.DMA,
        ]

    def start(self):
        here = self.here
        self.own = pltpu.make_async_copy(self.src(here.ep), self.dst(here.ep), self.own_sem)
        self.own.start()
        self.copies = []
        for offset in range(1, here.count):
            device = here.peer(offset)
            copy = remote(self.src(device[1]), self.dst(here.ep), self.send.at[offset], self.recv.at[offset], device)
            copy.start()
            self.copies.append(copy)

    def arrive(self):
        here = self.here
        self.own.wait()
        for offset in range(1, here.count):
            source = here.peer(-offset)[1]
            remote(
                self.dst(source), self.dst(source), self.send.at[offset], self.recv.at[offset], here.peer(offset)
            ).wait_recv()

    def finish(self):
        for copy in self.copies:
            copy.wait_send()


def far_devices(here):
    return [(1 - here.grp, (here.ep + offset) % here.count) for offset in range(here.count)]


def plane_devices(here):
    return [here.peer(offset) for offset in range(1, here.count)]


def split(refs, *sizes):
    groups, start = [], 0
    for size in sizes:
        groups.append(refs[start : start + size])
        start += size
    return groups


def ring_offsets(ring):
    far = ring // 2
    return [0] + [sign * k for k in range(1, far) for sign in (1, -1)] + [far]


def experts(
    ep_count, block, cot_own, cot_other, early, mine, slots, router, gate_w, up_w, down_w, name, collective_id
):
    rows, width = block.shape
    hidden_width = gate_w.shape[1]
    pair = 2 * rows
    ring = ep_count // 2
    offsets = ring_offsets(ring)
    batches = [[0]] + [[2 * k - 1, 2 * k] for k in range(1, ring // 2)] + [[ring - 1]]
    tile, wide = 512, 1024
    far = ring // 2
    reach = far // 2

    def kernel(*refs):
        ins, outs, scratch = split(refs, 8, 12, len(refs) - 20)
        block_ref, cot_ref, cot_far, mine_ref, router_ref, gate_ref, up_ref, down_ref = ins
        other_ref, u_out, e_out, h_out, g_out, p_out, du_terms, eo_terms, du_joint, sum_out, dot_out, cot_late = outs
        gather_sems, near_sems, cross, cot_cross, bufs, stage, du_s, dot_sems, load_sems = split(scratch, 5, 5, 4, 4, 6, 12, 8, 3, 5)
        across_send, across_recv, hand_send, hand_recv = cross
        gate_v, up_v, down_v, rows_v, cot_v, own_ref = bufs
        u_s, e_s, h_s, g_s, p_s, r_s, dx_s, gate_s, dot_s, line_s, term_v, hot_ref = stage
        dot_send, dot_recv, dot_own = dot_sems
        weight_sem, rows_sem, cot_sem, stage_sem, term_sem = load_sems
        here = Place(ep_count)
        sums = RingSum(here, lambda e: du_terms.at[e], du_joint, du_s[:3], du_s[3:])
        weights = []
        for i, (src, dst) in enumerate(((gate_ref, gate_v), (up_ref, up_v), (down_ref, down_v))):
            copy = pltpu.make_async_copy(src, dst, weight_sem.at[i])
            copy.start()
            weights.append(copy)
        greet(plane_devices(here) + [here.across()])
        gather = Gather(here, block_ref, own_ref, gather_sems)
        gather.start()
        sent = []

        def start(copy):
            copy.start()
            sent.append(copy)

        def cross_copy(slot, src):
            index = here.chip(offsets[slot])
            return remote(src, other_ref.at[index], across_send.at[slot], across_recv.at[slot], here.across())

        def hand_copy(slot, core):
            index = here.index(here.at(offsets[slot]), core)
            return remote(
                other_ref.at[index], other_ref.at[index], hand_send.at[slot], hand_recv.at[slot], here.sibling()
            )

        start(cross_copy(0, block_ref))
        near = Gather(here, other_ref.at[here.ep], other_ref, near_sems, reach)
        straight = 2 * reach + 1
        cot_over = Crossing(here, lambda e: cot_late.at[e], lambda e: cot_late.at[e], cot_cross)
        for slot in range(early, ring):
            cot_over.send(slot, cot_ref.at[here.chip(offsets[slot])])

        def chip_of(slot):
            return here.index(here.at(offsets[slot]), 0) // 2

        def cot_copy(which, slot, buffer):
            src = cot_ref if which == 0 else (cot_far if slot < early else cot_late)
            return pltpu.make_async_copy(src.at[pl.ds(2 * chip_of(slot), 2)], cot_v.at[buffer], cot_sem.at[buffer])

        def rows_copy(src, slot, buffer):
            return pltpu.make_async_copy(
                src.at[pl.ds(2 * chip_of(slot), 2)], rows_v.at[buffer], rows_sem.at[buffer]
            )

        pending = {}
        stages = {"u": (u_s, u_out), "e": (e_s, e_out), "g": (g_s, g_out), "p": (p_s, p_out)}

        def settle(keys):
            for key in keys:
                for copy in pending.pop(key, []):
                    copy.wait()

        def store(key, which, batch):
            src, dst = stages[key]
            sem = list(stages).index(key)
            count = len(batch) * slots
            at = pl.ds(batch[0] * slots, count)
            target = dst.at[which, at]
            pending[key] = [pltpu.make_async_copy(src.at[pl.ds(0, count)], target, stage_sem.at[sem])]
            for copy in pending[key]:
                copy.start()

        def loop(extent, tile, body):
            def run(i, carry):
                body(pl.ds(pl.multiple_of(i * tile, tile), tile))
                return carry

            lax.fori_loop(0, extent // tile, run, 0)

        def prefetch(which, batch, parity):
            for i, slot in enumerate(batch):
                cot_copy(which, slot, 2 * parity + i).start()

        hidden_copies = {}

        def store_hidden(which, batch):
            at = pl.ds(batch[0] * slots, len(batch) * slots)
            sem = weight_sem.at[3 + batches.index(batch)]
            hidden_copies[batch[0]] = pltpu.make_async_copy(h_s.at[at], h_out.at[which, at], sem)
            hidden_copies[batch[0]].start()

        given = []

        def give(src, first, chip, terms):
            buffer = len(given) % 2
            if len(given) > 1:
                given[-2].wait()

            def put(at):
                spread_rows = mm_tn(hot_ref[0, chip], src[pl.ds(first, slots), at]).astype(BF)
                term_v[buffer, :, :, at] = spread_rows.reshape(2, rows, width)

            loop(width, width, put)
            copy = pltpu.make_async_copy(term_v.at[buffer], terms.at[pl.ds(2 * chip, 2)], term_sem.at[buffer])
            copy.start()
            given.append(copy)

        def settle_given():
            for copy in given[-2:]:
                copy.wait()
            given.clear()

        def work(which, batch, parity):
            count = len(batch) * slots
            every = pl.ds(0, count)
            if which == 1:
                for i, slot in enumerate(batch):
                    rows_copy(other_ref, slot, i).start()
                for i, slot in enumerate(batch):
                    rows_copy(other_ref, slot, i).wait()
            for i, slot in enumerate(batch):
                cot_copy(which, slot, 2 * parity + i).wait()
            settle("u")
            for i, slot in enumerate(batch):
                hot = hot_ref[which, chip_of(slot)]

                def pick_rows(at, i=i, hot=hot):
                    if which == 0:
                        taken = own_ref[pl.ds(2 * chip_of(batch[i]), 2), :, at]
                    else:
                        taken = rows_v[i, :, :, at]
                    picked = mm(hot, taken.reshape(pair, width))
                    u_s[pl.ds(i * slots, slots), at] = picked.astype(BF)

                loop(width, width, pick_rows)
            store("u", which, batch)
            logits = mm(u_s[every], router_ref[...])
            lane = lax.broadcasted_iota(jnp.int32, logits.shape, 1)
            logits = jnp.where(lane < ep_count, logits, -1e30)
            powers = jnp.exp(logits - jnp.max(logits, axis=-1, keepdims=True))
            gate = jnp.sum(jnp.where(lane == here.ep, powers, 0.0), axis=-1, keepdims=True)
            gate = gate / jnp.sum(powers, axis=-1, keepdims=True)
            settle("e")
            for i, slot in enumerate(batch):
                hot = hot_ref[which, chip_of(slot)]

                def pick_cots(at, i=i, hot=hot):
                    part = pl.ds(i * slots, slots)
                    picked = mm(hot, cot_v[2 * parity + i, :, :, at].reshape(pair, width))
                    e_s[part, at] = (gate[i * slots : (i + 1) * slots] * picked).astype(BF)
                    if which == 0:
                        r_s[pl.ds((batch[0] + i) * slots, slots), at] = picked.astype(BF)

                loop(width, width, pick_cots)
            store("e", which, batch)
            settle("gp")
            held = pl.ds(batch[0] * slots, count)
            if batch[0] in hidden_copies:
                hidden_copies.pop(batch[0]).wait()
            gate_s[held] = gate

            def inner(at):
                gate_pre = mm(u_s[every], gate_v[:, at])
                up_pre = mm(u_s[every], up_v[:, at])
                grad = mm_nt(e_s[every], down_v[at, :])
                sigma = 1.0 / (1.0 + jnp.exp(-gate_pre))
                swish = gate_pre * sigma
                h_s[held, at] = (swish * up_pre).astype(BF)
                g_s[every, at] = (grad * up_pre * sigma * (1.0 + gate_pre * (1.0 - sigma))).astype(BF)
                p_s[every, at] = (grad * swish).astype(BF)

            loop(hidden_width, tile, inner)
            for key in "gp":
                store(key, which, batch)
            store_hidden(which, batch)
            if which == 1:
                return None
            return lambda: work_back(batch, every)

        def work_back(batch, every):
            def back(at):
                grad = mm_nt(g_s[every], gate_v[at, :]) + mm_nt(p_s[every], up_v[at, :])
                dx_s[every, at] = grad.astype(BF)

            loop(width, wide, back)
            for i, slot in enumerate(batch):
                part = pl.ds(i * slots, slots)
                give(dx_s, i * slots, chip_of(slot), du_terms)

        def results():
            dot_s[...] = jnp.zeros_like(dot_s)

            def outer(at):
                result = mm(h_s[...], down_v[:, at]).astype(BF).astype(F32)
                dot_s[...] += jnp.sum(result * r_s[:, at].astype(F32), axis=-1, keepdims=True)
                r_s[:, at] = (gate_s[...] * result).astype(BF)

            loop(width, tile, outer)
            for slot in range(ring):
                part = pl.ds(slot * slots, slots)
                line = jnp.sum(hot_ref[0, chip_of(slot)].astype(F32) * dot_s[part], axis=0, keepdims=True)
                for core in range(2):
                    line_s[slot, core] = jnp.broadcast_to(line[:, core * rows : (core + 1) * rows], (8, rows))

        prefetch(0, batches[0], 0)
        upto = lax.broadcasted_iota(jnp.int32, (pair, pair), 0) <= lax.broadcasted_iota(jnp.int32, (pair, pair), 1)
        mine_all = mine_ref[...]
        order = mm(mine_all.astype(BF), upto.astype(BF))
        order = jnp.where(mine_all > 0, order - 1.0, -1.0)
        place = lax.broadcasted_iota(jnp.int32, (slots, pair), 0).astype(F32)
        for which in range(2):
            for chip in range(ring):
                line = order[which * ring + chip : which * ring + chip + 1]
                hot_ref[which, chip] = jnp.where(place == line, 1.0, 0.0).astype(BF)
        for copy in weights:
            copy.wait()
        gather.settle()
        for number, batch in enumerate(batches):
            gather.side(number - 1)
            if number + 1 < len(batches):
                prefetch(0, batches[number + 1], (number + 1) % 2)
            else:
                prefetch(1, batches[0], (number + 1) % 2)
            rest = work(0, batch, number % 2)
            if number < far:
                gather.step(number)
                for slot in batches[number + 1]:
                    if slot >= straight:
                        start(cross_copy(slot, own_ref.at[here.chip(offsets[slot])]))
                if number == 1:
                    cross_copy(0, other_ref.at[here.ep]).wait_recv()
                    near.start()
                elif number > 2:
                    near.step(number - 3)
            rest()
        def dot_copy(slot, core, sender_core, source, target):
            return remote(
                line_s.at[slot, core],
                dot_out.at[source],
                dot_send.at[slot, core],
                dot_recv.at[slot, sender_core],
                (here.grp, target),
            )

        settle_given()
        sums.start()
        sums.step(0)
        results()
        own_dots = pltpu.make_async_copy(line_s.at[0, here.core], dot_out.at[here.ep], dot_own)
        own_dots.start()

        start(dot_copy(0, 1 - here.core, here.core, here.ep, here.sibling()[1]))
        for slot in range(1, ring):
            for core in range(2):
                target = here.index(here.at(offsets[slot]), core)
                start(dot_copy(slot, core, here.core, here.ep, target))
        count = len(batches)

        def put(out):
            def keep_sum(at, value):
                out[at] = value

            return keep_sum

        for number, batch in enumerate(batches):
            far_slots = [slot for slot in batch if slot >= straight]
            for slot in far_slots:
                index = here.chip(offsets[slot])
                cross_copy(slot, other_ref.at[index]).wait_recv()
                start(hand_copy(slot, here.core))
            if 0 < number < reach:
                near.step(number)
            if 0 < number < far:
                sums.step(number)
            if number == 1:
                for slot in range(ring):
                    give(r_s, slot * slots, chip_of(slot), eo_terms)
                settle_given()
            if number == far:
                sums.finish(put(sum_out))
            for slot in far_slots:
                hand_copy(slot, 1 - here.core).wait_recv()
            if number <= reach:
                near.side(number - 1)
            parity = (count + number) % 2
            if number + 1 < count:
                late = [slot for slot in batches[number + 1] if slot >= early]
                for slot in late:
                    cot_over.take(slot)
                for slot in late:
                    cot_over.settle(slot)
                prefetch(1, batches[number + 1], 1 - parity)
            work(1, batch, parity)
        own_dots.wait()
        dot_copy(0, 0, 1 - here.core, here.sibling()[1], here.sibling()[1]).wait_recv()
        for slot in range(1, ring):
            for core in range(2):
                source = here.index(here.at(-offsets[slot]), core)
                dot_copy(slot, 0, core, source, source).wait_recv()
        gather.finish()
        near.finish()
        cot_over.finish()
        for copy in sent:
            copy.wait_send()
        settle("uegp")
        for copy in hidden_copies.values():
            copy.wait()

    dma = pltpu.SemaphoreType.DMA
    total = ring * slots
    most = max(len(batch) for batch in batches) * slots
    hbm = pl.BlockSpec(memory_space=pl.ANY)
    vmem = pl.BlockSpec(memory_space=pltpu.VMEM)

    def low(*shape):
        return jax.ShapeDtypeStruct(shape, BF)

    def keep(*shape):
        return pltpu.VMEM(shape, BF)

    return pl.pallas_call(
        kernel,
        out_shape=[
            low(ep_count, rows, width),
            low(2, total, width),
            low(2, total, width),
            low(2, total, hidden_width),
            low(2, total, hidden_width),
            low(2, total, hidden_width),
            low(ep_count, rows, width),
            low(ep_count, rows, width),
            low(ring, rows, width),
            jax.ShapeDtypeStruct((rows, width), F32),
            jax.ShapeDtypeStruct((ep_count, 8, rows), F32),
            low(ep_count, rows, width),
        ],
        in_specs=[hbm, hbm, hbm, vmem, vmem, hbm, hbm, hbm],
        out_specs=[hbm] * 9 + [vmem, hbm, hbm],
        scratch_shapes=Gather.scratch(ep_count)
        + Gather.scratch(ep_count)
        + [dma((ring,))] * 4
        + Crossing.scratch(ep_count)
        + [keep(*gate_w.shape), keep(*up_w.shape), keep(*down_w.shape), keep(2, 2, rows, width), keep(4, 2, rows, width), keep(ep_count, rows, width)]
        + [keep(most, width), keep(most, width), keep(total, hidden_width)]
        + [keep(most, hidden_width)] * 2
        + [keep(total, width), keep(most, width)]
        + [pltpu.VMEM((total, 1), F32), pltpu.VMEM((total, 1), F32), pltpu.VMEM((ring, 2, 8, rows), F32)]
        + [keep(2, 2, rows, width), keep(2, ring, slots, pair)]
        + RingSum.scratch(ep_count, rows, width)
        + [dma((ring, 2)), dma((ring, 2)), dma]
        + [dma((3 + len(batches),)), dma((2,)), dma((4,)), dma((4,)), dma((2,))],
        compiler_params=pltpu.CompilerParams(
            collective_id=collective_id, has_side_effects=True, vmem_limit_bytes=62 << 20
        ),
        name=name,
    )(block, cot_own, cot_other, mine, router, gate_w, up_w, down_w)


class RingSum:
    def __init__(self, here, term, joint, buffers, sems, more=None):
        self.here, self.term, self.joint, self.more = here, term, joint, more
        self.first, self.landed, self.stage = buffers
        self.side_send, self.side_recv, self.ring_send, self.ring_recv, self.stage_sem = sems
        self.far = here.ring // 2
        self.offsets = ring_offsets(here.ring)
        self.part_rows = self.stage.shape[3]
        self.waited, self.copies = set(), []

    @staticmethod
    def scratch(ep_count, rows, width, summands=2, dtype=BF):
        ring, far = ep_count // 2, ep_count // 4
        dma = pltpu.SemaphoreType.DMA
        shapes = [(2, rows, width), (2, far, rows, width), (2, 2, summands, rows // 2, width)]
        buffers = [pltpu.VMEM(shape, dtype) for shape in shapes]
        return buffers + [dma((ring,)), dma((ring,)), dma((2, far, 2)), dma((2, far, 2)), dma((2, 2, summands))]

    def hops(self, way, part):
        return self.far if way == part else self.far - 1

    def rows(self, part):
        return pl.ds(part * self.part_rows, self.part_rows)

    def distance(self, way, part, step):
        distance = max(self.hops(way, part) - step, 0)
        return distance if way == 0 else -distance

    def slot(self, way, part, step):
        offset = self.distance(way, part, step)
        return self.offsets.index(self.far if offset == -self.far else offset)

    def loads(self, way, part, step):
        index = self.here.chip(self.distance(way, part, step))
        sources = [self.term(index), self.joint.at[self.slot(way, part, step)]]
        if self.more is not None:
            sources.append(self.more(index))
        return [
            pltpu.make_async_copy(
                source.at[self.rows(part)], self.stage.at[way, part, i], self.stage_sem.at[way, part, i]
            )
            for i, source in enumerate(sources)
        ]

    def load(self, way, part, step):
        slot = self.slot(way, part, step)
        if slot not in self.waited:
            self.waited.add(slot)
            self.side_copy(slot).wait_recv()
        for copy in self.loads(way, part, step):
            copy.start()

    def side_copy(self, slot):
        here = self.here
        index = here.index(here.at(self.offsets[slot]), 1 - here.core)
        return remote(
            self.term(index), self.joint.at[slot], self.side_send.at[slot], self.side_recv.at[slot], here.sibling()
        )

    def start(self):
        self.trade()
        self.begin()

    def trade(self):
        for slot in reversed(range(len(self.offsets))):
            copy = self.side_copy(slot)
            copy.start()
            self.copies.append(copy)

    def begin(self):
        for part in range(2):
            for way in range(2):
                self.load(way, part, 0)

    def value(self, way, part, step):
        for copy in self.loads(way, part, step):
            copy.wait()
        return sum(self.stage[way, part, i].astype(F32) for i in range(self.stage.shape[2]))

    def ring_copy(self, way, step, part):
        at = self.rows(part)
        src = self.first.at[way, at] if step == 0 else self.landed.at[way, step - 1, at]
        return remote(
            src,
            self.landed.at[way, step, at],
            self.ring_send.at[way, step, part],
            self.ring_recv.at[way, step, part],
            self.here.right() if way == 0 else self.here.left(),
        )

    def step(self, step):
        for part in range(2):
            for way in range(2):
                if step < self.hops(way, part):
                    value = self.value(way, part, step)
                    at = self.rows(part)
                    if step == 0:
                        self.first[way, at] = value.astype(self.first.dtype)
                    else:
                        self.ring_copy(way, step - 1, part).wait_recv()
                        value = value + self.landed[way, step - 1, at].astype(F32)
                        self.landed[way, step - 1, at] = value.astype(self.landed.dtype)
                    copy = self.ring_copy(way, step, part)
                    copy.start()
                    self.copies.append(copy)
                    if step + 1 < self.hops(way, part) or way == 0:
                        self.load(way, part, step + 1)

    def finish(self, put):
        for part in range(2):
            value = self.value(0, part, self.hops(0, part))
            at = self.rows(part)
            for way in range(2):
                count = self.hops(way, part)
                self.ring_copy(way, count - 1, part).wait_recv()
                value = value + self.landed[way, count - 1, at].astype(F32)
            put(at, value)
        for copy in self.copies:
            copy.wait_send()


def rolled(values):
    return pltpu.roll(values, HEAD_DIM // 2, 1)


def turns(table):
    other = rolled(table)
    first = lax.broadcasted_iota(jnp.int32, table.shape, 1) < HEAD_DIM // 2
    return jnp.where(first, table, other), jnp.where(first, -other, table)


def as_rows(columns, count):
    shape = (columns[0].shape[0], 128)
    lane = lax.broadcasted_iota(jnp.int32, shape, 1)
    packed = jnp.zeros(shape, F32)
    for i, column in enumerate(columns):
        packed = jnp.where(lane == i, column, packed)
    return packed.T[:count]


def as_columns(tile):
    padded = jnp.concatenate([tile, jnp.zeros((128 - tile.shape[0], tile.shape[1]), F32)], axis=0)
    return padded.T


BACKWARD_STEPS = {
    "sent": (("x", 0), ("x", 1), ("t", 2)),
    "attended": (("e", 1),),
    "scores": (("t", 2),),
    "dots": (("t", 2), ("e", 2)),
    "columns": (("t", 1),),
    "terms": (("e", 3),),
    "swap": (
        ("d", 1),
        ("t", 1),
        ("g", 0),
        ("t", 1),
        ("d", 2),
        ("g", 1),
        ("t", 1),
        ("d", 3),
        ("g", 2),
        ("t", 1),
        ("g", 3),
        ("t", 1),
    ),
}


def backward(
    ep_count, d_proj, att_loc, w_out, head, columns, table, gains, w_all, normed, result_terms, tiles, expert_rows, name, collective_id
):
    rows = d_proj.shape[0]
    query, key, value, norm_q, norm_k = head
    tokens, cols = query.shape
    width = w_all.shape[0]
    prompt_len = tokens // 2
    units, grads, hidden, gate_grads, up_grads = expert_rows
    depth_rows, hidden_width = hidden.shape
    ring = ep_count // 2
    far = ring // 2
    out_rows = w_out.shape[1]
    slab, wide, block = 256, 1024, 256
    segment = 512
    pieces = tokens // segment
    scale = HEAD_DIM ** (-0.5)
    dma = pltpu.SemaphoreType.DMA

    def kernel(*refs):
        ins, outs, scratch = split(refs, 20, 16, len(refs) - 36)
        (proj_ref, att_ref, q_ref, k_ref, v_ref, nq_ref, nk_ref, col_ref, table_ref, gain_ref, w_ref) = ins[:11]
        full_ref, normed_ref, eo_ref, tile_ref, u_ref, e_ref, h_ref, g_ref, p_ref = ins[11:]
        dn_out, go_out, eo_out, gw_out, tile_out, late_out, gate_out, up_out, down_out = outs[:9]
        dn_terms, dn_joint, go_joint, eo_joint, go_mine, go_theirs, x_in = outs[9:]
        dn_s, go_s, eo_s, go_more, gw_s, tile_s, late_s, work_s, att_s, dots_s, own_s = split(
            scratch, 8, 8, 8, 5, 6, 3, 4, 6, 9, 5, 5
        )
        here = Place(ep_count)
        greet(plane_devices(here) + far_devices(here))
        sent = []

        def start(copy):
            copy.start()
            sent.append(copy)

        (att_v, tile_v, dq_s, dk_s, dv_s, lin_s), att_sems = att_s[:6], att_s[6:]
        slab_v, slab_sem, term_v, term_sem, gw_v = own_s

        def full_copy(number):
            return pltpu.make_async_copy(
                full_ref.at[pl.ds(2 * number, 2)], term_v.at[number % 2], term_sem.at[number % 2]
            )

        for number in range(2):
            full_copy(number).start()
        for number in range(ring):
            full_copy(number).wait()
            for i in range(2):
                tile_v[2 * number + i] = mm_nt(proj_ref[...], term_v[number % 2, i]).astype(BF)
            if number + 2 < ring:
                full_copy(number + 2).start()
        attended = Exchange(here, lambda e: tile_v.at[e], lambda e: att_v.at[e], att_sems)
        attended.start()

        me = here.grp * ep_count + here.ep

        def tile_copy(turn, offset, source, src, dst, sems):
            group = (here.grp + turn) % 2
            target = (here.ep + offset) % ep_count
            slot = turn * ep_count + offset
            return remote(src(group * ep_count + target), dst.at[source], sems[0].at[slot], sems[1].at[slot], (group, target))

        others = [(turn, offset) for turn in range(2) for offset in range(ep_count) if turn + offset > 0]

        def send_tiles(src, dst, sems):
            own = pltpu.make_async_copy(src(me), dst.at[me], sems[2])
            own.start()
            for turn, offset in others:
                start(tile_copy(turn, offset, me, src, dst, sems))
            return own

        def take_tiles(own, src, dst, sems):
            own.wait()
            for turn, offset in others:
                source = ((here.grp + turn) % 2) * ep_count + (here.ep + ep_count - offset) % ep_count
                tile_copy(turn, offset, source, src, dst, sems).wait_recv()

        x_own, x_joint, go_own_sem, go_send, go_recv = go_more
        go_load = pltpu.make_async_copy(go_theirs.at[:, here.core], x_own, go_own_sem)
        go_side = remote(go_theirs.at[:, 1 - here.core], x_joint, go_send.at[0], go_recv.at[0], here.sibling())

        def go_over(part):
            at = pl.ds(part * (ring // 2), ring // 2)
            return remote(x_own.at[at], x_in.at[at], go_send.at[1 + part], go_recv.at[1 + part], here.across())

        output = RingSum(
            here, lambda e: go_mine.at[e // 2, e % 2], go_joint, go_s[:3], go_s[3:], lambda e: x_in.at[e // 2]
        )
        result = RingSum(here, lambda e: eo_ref.at[e], eo_joint, eo_s[:3], eo_s[3:])

        left, right, sheet, left_sem, right_sem, sheet_sem = work_s
        units = [(u_ref, i) for i in range(width // slab)] + [(h_ref, i) for i in range(hidden_width // slab)]
        turning = width // slab
        done = []

        def right_copies(late):
            if late:
                return [pltpu.make_async_copy(e_ref, right, right_sem.at[0])]
            return [
                pltpu.make_async_copy(src, right.at[:, pl.ds(i * hidden_width, hidden_width)], right_sem.at[i])
                for i, src in enumerate((g_ref, p_ref))
            ]

        def left_copy(number):
            src, i = units[number]
            return pltpu.make_async_copy(src.at[:, pl.ds(i * slab, slab)], left.at[number % 2], left_sem.at[number % 2])

        def sheet_copies(number):
            src, i = units[number]
            at = pl.ds(i * slab, slab)
            if number >= turning:
                return [pltpu.make_async_copy(sheet.at[number % 2], down_out.at[at], sheet_sem.at[number % 2, 0, 0])]
            return [
                pltpu.make_async_copy(
                    sheet.at[number % 2, :, pl.ds(j * hidden_width, hidden_width)], out.at[at], sheet_sem.at[number % 2, 0, j]
                )
                for j, out in enumerate((gate_out, up_out))
            ]

        def unit(number):
            if number in (0, turning):
                for copy in right_copies(number > 0):
                    copy.wait()
            left_copy(number).wait()
            if number + 1 < len(units):
                left_copy(number + 1).start()
            if number >= 2:
                for copy in sheet_copies(number - 2):
                    copy.wait()

            def run(i, carry):
                at = pl.ds(pl.multiple_of(i * wide, wide), wide)
                sheet[number % 2, :, at] = mm_tn(left[number % 2], right[:, at]).astype(sheet.dtype)
                return carry

            lax.fori_loop(0, width // wide, run, 0)
            for copy in sheet_copies(number):
                copy.start()
            if number + 1 == turning:
                for copy in right_copies(True):
                    copy.start()

        def tasks(count):
            for _ in range(min(count, len(units) - len(done))):
                unit(len(done))
                done.append(True)

        for copy in right_copies(False):
            copy.start()
        left_copy(0).start()
        term_copies = []

        def poll(point):
            for kind, number in BACKWARD_STEPS.get(point, ()):
                if kind == "t":
                    tasks(number)
                elif kind == "e":
                    result.step(number)
                elif kind == "d":
                    normed_sum.step(number)
                elif kind == "g":
                    if number == 0:
                        for half in range(2):
                            go_over(half).wait_recv()
                        output.begin()
                    output.step(number)
                elif kind == "x":
                    start(go_over(number))

        own_tiles = send_tiles(lambda i: tile_ref.at[i], tile_out, tile_s)
        result.start()
        result.step(0)
        for number in range(2 * ring):
            first = lax.rem((1 - here.grp) * ring + number, 2 * ring) * cols
            turned = mm_tn(att_ref[:, pl.ds(pl.multiple_of(first, cols), cols)], proj_ref[...]).astype(BF)
            buffer, at = number // 2 % 2, number % 2
            terms = go_theirs if number < ring else go_mine
            chip = number % ring
            if at == 0 and number >= 4:
                for copy in term_copies.pop(0):
                    copy.wait()
            sheet[buffer, pl.ds(at * cols, cols)] = turned
            if at == 1:
                copies = [
                    pltpu.make_async_copy(
                        sheet.at[buffer, pl.ds((2 * i + j) * out_rows, out_rows)],
                        terms.at[chip - 1 + i, j],
                        sheet_sem.at[buffer, i, j],
                    )
                    for i in range(2)
                    for j in range(2)
                ]
                for copy in copies:
                    copy.start()
                term_copies.append(copies)
            if number == ring + 2:
                go_load.start()
                start(go_side)
        for copies in term_copies:
            for copy in copies:
                copy.wait()
        go_load.wait()
        go_side.wait_recv()
        for chip in range(ring):
            x_own[chip] = (x_own[chip].astype(F32) + x_joint[chip].astype(F32)).astype(BF)
        poll("sent")
        attended.arrive()
        poll("attended")

        dk_s[...] = jnp.zeros_like(dk_s)
        dv_s[...] = jnp.zeros_like(dv_s)
        per = block // rows
        line = lax.broadcasted_iota(jnp.int32, (block, block), 0)
        column_at = lax.broadcasted_iota(jnp.int32, (block, block), 1)
        causal = line >= column_at
        same = causal & (line // rows == column_at // rows)

        def grads_of(first, spans):
            at = pl.ds(first, block)
            q = q_ref[at]
            g = att_v[pl.ds(first // rows, per)].reshape(block, cols)
            log = col_ref[at, 0:1]
            kept = []
            inner = jnp.zeros((block, 1), F32)
            for begin, length, mask in spans:
                keys = pl.ds(begin, length)
                weight = jnp.exp(mm_nt(q, k_ref[keys]) * scale - log)
                if mask is not None:
                    weight = jnp.where(mask, weight, 0.0)
                d_weight = mm_nt(g, v_ref[keys])
                inner = inner + jnp.sum(weight * d_weight, axis=-1, keepdims=True)
                kept.append((keys, weight, d_weight))
            dq = jnp.zeros((block, cols), F32)
            for keys, weight, d_weight in kept:
                d_score = (weight * (d_weight - inner)).astype(BF)
                dq = dq + mm(d_score, k_ref[keys])
                dk_s[keys] += mm_tn(d_score, q)
                dv_s[keys] += mm_tn(weight.astype(BF), g)
            dq_s[at] = dq * scale

        for number in range(prompt_len // block):
            spans = [(0, number * block, None)] if number else []
            grads_of(number * block, spans + [(number * block, block, causal)])

        def later(number, carry):
            first = pl.multiple_of(prompt_len + number * block, block)
            grads_of(first, [(0, prompt_len, None), (first, block, same)])
            return carry

        poll("prompt")
        lax.fori_loop(0, (tokens - prompt_len) // block, later, 0)
        poll("scores")

        dots_v, dots_all, dots_sems = dots_s[0], dots_s[1], dots_s[2:]
        late_v, late_sems = late_s[0], late_s[1:]
        gain_sums = [jnp.zeros((1, cols), F32), jnp.zeros((1, cols), F32)]
        stats = []
        for piece in range(pieces):
            at = pl.ds(piece * segment, segment)
            cosine, sine = turns(table_ref[at])
            for kind, (ref, n_ref, factor) in enumerate(((dq_s, nq_ref, 1.0), (dk_s, nk_ref, scale))):
                turned = ref[at] * factor
                turned = turned * cosine - rolled(turned) * sine
                gain_sums[kind] = gain_sums[kind] + jnp.sum(turned * n_ref[at].astype(F32), axis=0, keepdims=True)
                turned = turned * gain_ref[kind : kind + 1]
                ref[at] = turned
                stats.append(jnp.sum(turned * n_ref[at].astype(F32), axis=-1, keepdims=True))
        dots_v[...] = as_rows(stats, dots_v.shape[0])
        spread_dots = Exchange(here, lambda e: dots_v, lambda e: dots_all.at[e], dots_sems)
        spread_dots.start()
        gain_tile = jnp.concatenate(gain_sums + [jnp.zeros((6, cols), F32)], axis=0)
        for piece in range(pieces):
            at = pl.ds(piece * segment, segment)
            lin_s[at, 2 * cols : 3 * cols] = dv_s[at].astype(BF)
        slabs = width // slab
        half = slabs // 2

        def slab_at(turn):
            return lax.rem((1 - here.grp) * half + turn, slabs) * slab

        def slab_copy(turn):
            at = pl.ds(pl.multiple_of(slab_at(turn), slab), slab)
            return pltpu.make_async_copy(normed_ref.at[:, at], slab_v.at[turn % 2], slab_sem.at[turn % 2])

        slab_copy(0).start()
        slab_copy(1).start()
        poll("dots")
        spread_dots.arrive()
        total = dots_all[0]
        for e in range(1, ep_count):
            total = total + dots_all[e]
        total = as_columns(total / width)
        for piece in range(pieces):
            at = pl.ds(piece * segment, segment)
            for kind, (ref, n_ref) in enumerate(((dq_s, nq_ref), (dk_s, nk_ref))):
                lane = 2 * piece + kind
                grad = col_ref[at, 1 + kind : 2 + kind] * (ref[at] - n_ref[at].astype(F32) * total[:, lane : lane + 1])
                lin_s[at, kind * cols : (kind + 1) * cols] = grad.astype(BF)

        (gw_x, gw_x_send, gw_x_recv), gw_swap = gw_s[:3], gw_s[3:]
        per_slab = slab // out_rows
        gain_lines = []

        def projections(turn):
            slab_copy(turn).wait()
            first = slab_at(turn)
            grad = mm_tn(slab_v[turn % 2], lin_s[...])
            if turn + 2 < slabs:
                slab_copy(turn + 2).start()
            weight = w_ref[pl.ds(pl.multiple_of(first, slab), slab)].astype(F32)
            line = as_rows([jnp.sum(grad * weight, axis=-1, keepdims=True)], 8)[0:1]
            owner = first // out_rows
            for kind in range(3):
                part = grad[:, kind * cols : (kind + 1) * cols].astype(BF)
                gw_v[pl.ds(owner, per_slab), kind] = part.reshape(per_slab, out_rows, cols)
            for i in range(per_slab):
                part = line[:, i * out_rows : (i + 1) * out_rows]
                part = jnp.concatenate([part, jnp.zeros((1, cols - out_rows), F32)], axis=1)
                late_v[owner + i] = jnp.concatenate([gain_tile[0:2], part, gain_tile[3:]], axis=0)
            return owner

        def over_copy(turn, owner):
            at = pl.ds(owner - (1 - here.grp) * ep_count, per_slab)
            return remote(gw_v.at[pl.ds(owner, per_slab)], gw_x.at[at], gw_x_send.at[turn], gw_x_recv.at[turn], here.across())

        for turn in range(half):
            start(over_copy(turn, projections(turn)))
        poll("columns")
        output.trade()

        normed_sum = RingSum(here, lambda e: dn_terms.at[e], dn_joint, dn_s[:3], dn_s[3:])
        offsets = ring_offsets(ring)
        stores = {}
        for turn, slot in enumerate(reversed(range(ring))):
            chip = here.index(here.at(offsets[slot]), 0) // 2
            if turn >= 2:
                stores.pop(turn - 2).wait()
            at = pl.ds(pl.multiple_of(chip * 2 * rows, 2 * rows), 2 * rows)

            def fill(i, carry, at=at, turn=turn):
                wide_at = pl.ds(pl.multiple_of(i * 1024, 1024), 1024)
                part = mm_nt(lin_s[at], w_ref[wide_at]).astype(BF)
                term_v[turn % 2, :, :, wide_at] = part.reshape(2, rows, 1024)
                return carry

            lax.fori_loop(0, width // 1024, fill, 0)
            stores[turn] = pltpu.make_async_copy(
                term_v.at[turn % 2], dn_terms.at[pl.ds(chip * 2, 2)], term_sem.at[turn % 2]
            )
            stores[turn].start()
        for turn in sorted(stores):
            stores[turn].wait()
        normed_sum.start()
        normed_sum.step(0)
        poll("terms")
        for turn in range(half, slabs):
            projections(turn)
        own_late = send_tiles(lambda i: late_v.at[i], late_out, late_sems)
        poll("columns_2")
        for turn in range(half):
            over_copy(turn, (1 - here.grp) * ep_count + turn * per_slab).wait_recv()
        for e in range(ep_count):
            gw_x[e] = (gw_v[here.grp * ep_count + e].astype(F32) + gw_x[e].astype(F32)).astype(BF)
        swap = Exchange(here, lambda e: gw_x.at[e], lambda e: gw_out.at[:, :, pl.ds(pl.multiple_of(e * cols, cols), cols)], gw_swap)
        swap.start()
        poll("swap")

        def put(out):
            def store(at, value):
                out[at] = value

            return store

        normed_sum.finish(put(dn_out))
        tasks(len(units))
        for number in range(len(units) - 2, len(units)):
            for copy in sheet_copies(number):
                copy.wait()
        result.finish(put(eo_out))
        output.finish(put(go_out))
        take_tiles(own_tiles, lambda i: tile_ref.at[i], tile_out, tile_s)
        take_tiles(own_late, lambda i: late_v.at[i], late_out, late_sems)
        attended.finish()
        spread_dots.finish()
        swap.arrive()
        swap.finish()
        for copy in sent:
            copy.wait_send()

    hbm = pl.BlockSpec(memory_space=pl.ANY)
    vmem = pl.BlockSpec(memory_space=pltpu.VMEM)
    group_rows = 2 * ep_count

    def keep(*shape):
        return pltpu.VMEM(shape, BF)

    def wide_keep(*shape):
        return pltpu.VMEM(shape, F32)

    return pl.pallas_call(
        kernel,
        out_shape=[
            jax.ShapeDtypeStruct((rows, width), F32),
            jax.ShapeDtypeStruct((out_rows, width), F32),
            jax.ShapeDtypeStruct((rows, width), F32),
            jax.ShapeDtypeStruct((3, out_rows, width), BF),
            jax.ShapeDtypeStruct(tiles.shape, F32),
            jax.ShapeDtypeStruct((group_rows, 8, cols), F32),
            jax.ShapeDtypeStruct((width, hidden_width), BF),
            jax.ShapeDtypeStruct((width, hidden_width), BF),
            jax.ShapeDtypeStruct((hidden_width, width), BF),
            jax.ShapeDtypeStruct((ep_count, rows, width), BF),
            jax.ShapeDtypeStruct((ring, rows, width), BF),
            jax.ShapeDtypeStruct((ring, out_rows, width), BF),
            jax.ShapeDtypeStruct((ring, rows, width), BF),
            jax.ShapeDtypeStruct((ring, 2, out_rows, width), BF),
            jax.ShapeDtypeStruct((ring, 2, out_rows, width), BF),
            jax.ShapeDtypeStruct((ring, out_rows, width), BF),
        ],
        in_specs=[vmem] * 11 + [hbm] * 9,
        out_specs=[vmem] * 3 + [hbm] * 13,
        scratch_shapes=RingSum.scratch(ep_count, rows, width)
        + RingSum.scratch(ep_count, out_rows, width, 3)
        + RingSum.scratch(ep_count, rows, width)
        + [keep(ring, out_rows, width)] * 2
        + [dma, dma((3,)), dma((3,))]
        + [keep(ep_count, 3, out_rows, cols)]
        + [dma((ring,)), dma((ring,))]
        + Exchange.scratch(ep_count)
        + [dma((group_rows,)), dma((group_rows,)), dma]
        + [wide_keep(group_rows, 8, cols), dma((group_rows,)), dma((group_rows,)), dma]
        + [keep(2, depth_rows, slab), keep(depth_rows, width), keep(2, slab, width), dma((2,)), dma((2,)), dma((2, 2, 2))]
        + [keep(ep_count, rows, cols)] * 2
        + [wide_keep(tokens, cols)] * 3
        + [keep(tokens, 3 * cols)]
        + Exchange.scratch(ep_count)
        + [wide_keep(8, segment), wide_keep(ep_count, 8, segment)]
        + Exchange.scratch(ep_count)
        + [keep(2, tokens, slab), dma((2,)), keep(2, 2, rows, width), dma((2,))]
        + [keep(group_rows, 3, out_rows, cols)],
        compiler_params=pltpu.CompilerParams(
            collective_id=collective_id, has_side_effects=True, vmem_limit_bytes=63 << 20
        ),
        name=name,
    )(
        d_proj,
        att_loc,
        query,
        key,
        value,
        norm_q,
        norm_k,
        columns,
        table,
        gains,
        w_all,
        w_out.reshape(ep_count, cols, width),
        normed,
        result_terms,
        tiles,
        *expert_rows,
    )


class Crossing:
    def __init__(self, here, out, into, sems):
        self.here, self.out, self.into = here, out, into
        self.across_send, self.across_recv, self.hand_send, self.hand_recv = sems
        self.offsets = ring_offsets(here.ring)
        self.copies = []

    @staticmethod
    def scratch(ep_count):
        return [pltpu.SemaphoreType.DMA((ep_count // 2,))] * 4

    def go(self, copy):
        copy.start()
        self.copies.append(copy)

    def across(self, slot, src, dst):
        return remote(src, dst, self.across_send.at[slot], self.across_recv.at[slot], self.here.across())

    def hand(self, slot, core):
        block = self.into(self.here.index(self.here.at(self.offsets[slot]), core))
        return remote(block, block, self.hand_send.at[slot], self.hand_recv.at[slot], self.here.sibling())

    def send(self, slot, src):
        self.go(self.across(slot, src, self.out(self.here.chip(self.offsets[slot]))))

    def take(self, slot):
        block = self.into(self.here.chip(self.offsets[slot]))
        self.across(slot, block, block).wait_recv()
        self.go(self.hand(slot, self.here.core))

    def settle(self, slot):
        self.hand(slot, 1 - self.here.core).wait_recv()

    def finish(self):
        for copy in self.copies:
            copy.wait_send()


ATTENTION_STEPS = {
    ("x", 0): (("f", -1),),
    ("x", 1): (("f", 0),),
    ("x", 2): (("f", 1),),
    ("x", 3): (("f", 2), ("c", -1)),
    ("x", 4): (("f", 3),),
    "dots": (("c", 0),),
    "prompt": (("c", 1),),
    "sent": (("c", 2), ("c", 3)),
}


def attention(ep_count, x, weights, small, w_out, cot, table, early, name, collective_id):
    rows, width = x.shape
    kinds, depth, _ = weights.shape
    cols = width // ep_count
    tokens = rows * ep_count
    prompt_len = tokens // 2
    ring = ep_count // 2
    far = ring // 2
    offsets = ring_offsets(ring)
    batches = [[0]] + [[2 * k - 1, 2 * k] for k in range(1, far)] + [[ring - 1]]
    gain_row = depth * ep_count // 128
    block, segment, chunk = 256, 512, 64
    pieces = tokens // segment
    scale = HEAD_DIM ** (-0.5)
    dma = pltpu.SemaphoreType.DMA

    def kernel(*refs):
        ins, outs, scratch = split(refs, 6, 14, len(refs) - 20)
        x_ref, weights_ref, small_ref, w_ref, cot_ref, table_ref = ins
        normed_out, w_all, s_out, full_out, cot_out, cot_other = outs[:6]
        q_out, k_out, v_out, nq_out, nk_out, col_out, att_out, x_land = outs[6:]
        x_s, w_s, s_s, cross, w_ring, cot_ring, w_cross, cot_cross, bufs, loads, dots_s, att_s = split(
            scratch, 5, 3, 2, 3, 5, 5, 4, 4, 5, 2, 5, 4
        )
        rows_v, normed_v, columns_v, gain_v, lin_v = bufs
        rows_sem, normed_sem = loads
        here = Place(ep_count)
        greet(plane_devices(here) + [here.across()])

        cross_own, cross_send, cross_recv = cross
        first = pltpu.make_async_copy(small_ref, s_out.at[here.grp, here.ep], cross_own)
        first.start()

        def small_over(group):
            return remote(
                small_ref, s_out.at[group, here.ep], cross_send.at[0], cross_recv.at[0], here.across()
            )

        small_over(here.grp).start()
        gather = Gather(here, x_ref, x_land, x_s)
        gather.start()
        columns_of = Exchange(
            here,
            lambda e: weights_ref.at[:, :, pl.ds(pl.multiple_of(e * cols, cols), cols)],
            lambda e: columns_v.at[here.grp, e],
            w_s,
        )
        columns_of.start()
        full = Gather(here, w_ref, full_out.at[here.grp], w_ring)
        full_over = Crossing(
            here, lambda e: full_out.at[here.grp, e], lambda e: full_out.at[1 - here.grp, e], w_cross
        )
        cots = Gather(here, cot_ref, cot_out, cot_ring)
        cots_over = Crossing(here, lambda e: cot_other.at[e], lambda e: cot_other.at[e], cot_cross)
        full_over.send(0, w_ref)
        cots_over.send(0, cot_ref)

        first.wait()
        small_over(1 - here.grp).wait_recv()
        small_over(here.grp).wait_send()
        small_copies = []
        for offset in range(1, here.count):
            mine = s_out.at[:, here.ep]
            copy = remote(mine, mine, s_s[0].at[offset], s_s[1].at[offset], here.peer(offset))
            copy.start()
            small_copies.append(copy)
        for offset in range(1, here.count):
            source = s_out.at[:, here.peer(-offset)[1]]
            remote(source, source, s_s[0].at[offset], s_s[1].at[offset], here.peer(offset)).wait_recv()

        def gains(row, half, owner):
            lines = []
            for i in range(2):
                tile = s_out[(owner + i) // ep_count, (owner + i) % ep_count, pl.ds(0, 16)].astype(F32)
                lines.append(tile[row : row + 1, half * depth : (half + 1) * depth])
            return jnp.concatenate(lines, axis=1)

        for i in range(width // 128):
            gain_v[:, i * 128 : (i + 1) * 128] = gains(gain_row, 0, 2 * i)
        gain_q, gain_k = gains(gain_row, 1, 2 * here.ep), gains(gain_row + 1, 0, 2 * here.ep)

        def chip_of(slot):
            return here.index(here.at(offsets[slot]), 0) // 2

        stores = []

        def norm(batch):
            loaded = []
            for i, slot in enumerate(batch):
                loaded.append(pltpu.make_async_copy(x_land.at[pl.ds(2 * chip_of(slot), 2)], rows_v.at[i], rows_sem.at[i]))
                loaded[-1].start()
            for i, slot in enumerate(batch):
                loaded[i].wait()
                chip = chip_of(slot)
                for core in range(2):

                    def run(j, carry, i=i, core=core, chip=chip):
                        at = pl.ds(pl.multiple_of(j * chunk, chunk), chunk)
                        wide = rows_v[i, core, at].astype(F32)
                        r = lax.rsqrt(jnp.mean(wide * wide, axis=-1, keepdims=True) + eps)
                        normed_v[2 * chip + core, at] = (wide * r * gain_v[...]).astype(BF)
                        return carry

                    lax.fori_loop(0, rows // chunk, run, 0)
                at = pl.ds(2 * chip, 2)
                stores.append(pltpu.make_async_copy(normed_v.at[at], normed_out.at[at], normed_sem.at[slot]))
                stores[-1].start()

        def project(batch):
            for slot in batch:
                chip = chip_of(slot)
                lin = mm(normed_v[pl.ds(2 * chip, 2)].reshape(2 * rows, width), w_all[...])
                at = pl.ds(pl.multiple_of(chip * 2 * rows, 2 * rows), 2 * rows)
                lin_v[0, at] = lin[:, :cols]
                lin_v[1, at] = lin[:, cols : 2 * cols]
                v_out[at] = lin[:, 2 * cols :].astype(BF)

        def poll(point):
            for kind, step in ATTENTION_STEPS.get(point, ()):
                ring_gather, crossing, count = (full, full_over, ring) if kind == "f" else (cots, cots_over, early)
                if step < 0:
                    ring_gather.start()
                    continue
                ring_gather.step(step)
                for slot in batches[step + 1]:
                    if slot < count:
                        crossing.send(slot, ring_gather.dst.at[here.chip(offsets[slot])])

        over = remote(columns_v.at[here.grp], columns_v.at[here.grp], cross_send.at[1], cross_recv.at[1], here.across())
        gather.settle()
        for number, batch in enumerate(batches):
            gather.side(number - 1)
            norm(batch)
            if number < far:
                gather.step(number)
            poll(("x", number))
            if number == 1:
                columns_of.arrive()
                over.start()
            if number == far - 1:
                remote(
                    columns_v.at[1 - here.grp],
                    columns_v.at[1 - here.grp],
                    cross_send.at[1],
                    cross_recv.at[1],
                    here.across(),
                ).wait_recv()
                for owner in range(2 * ep_count):
                    for kind in range(kinds):
                        w_all[owner * depth : (owner + 1) * depth, kind * cols : (kind + 1) * cols] = columns_v[
                            owner // ep_count, owner % ep_count, kind
                        ]
                for earlier in batches[:number]:
                    project(earlier)
            if number >= far - 1:
                project(batch)

        dots_v, dots_all, dots_sems = dots_s[0], dots_s[1], dots_s[2:]
        stats = []
        for piece in range(pieces):
            at = pl.ds(piece * segment, segment)
            for kind in range(2):
                lin = lin_v[kind, at]
                stats.append(jnp.sum(lin * lin, axis=-1, keepdims=True))
        dots_v[...] = as_rows(stats, dots_v.shape[0])
        spread_dots = Exchange(here, lambda e: dots_v, lambda e: dots_all.at[e], dots_sems)
        spread_dots.start()
        poll("dots")
        spread_dots.arrive()
        total = dots_all[0]
        for e in range(1, ep_count):
            total = total + dots_all[e]
        r_all = as_columns(lax.rsqrt(total / width + eps))
        lane = lax.broadcasted_iota(jnp.int32, (segment, 128), 1)
        for piece in range(pieces):
            at = pl.ds(piece * segment, segment)
            kept = jnp.zeros((segment, 128), F32)
            cosine, sine = turns(table_ref[at])
            for kind, (gain, n_out, out) in enumerate(((gain_q, nq_out, q_out), (gain_k, nk_out, k_out))):
                r = r_all[:, 2 * piece + kind : 2 * piece + kind + 1]
                n = lin_v[kind, at] * r
                n_out[at] = n.astype(BF)
                n = n * gain
                out[at] = (n * cosine + rolled(n) * sine).astype(BF)
                kept = jnp.where(lane == 1 + kind, r, kept)
            col_out[at] = kept

        poll("turned")
        att_v, att_sems = att_s[0], att_s[1:]
        per = block // rows
        line = lax.broadcasted_iota(jnp.int32, (block, block), 0)
        column_at = lax.broadcasted_iota(jnp.int32, (block, block), 1)
        causal = line >= column_at
        same = causal & (line // rows == column_at // rows)
        block_lane = lax.broadcasted_iota(jnp.int32, (block, 128), 1)

        def attend(first, spans):
            at = pl.ds(first, block)
            q = q_out[at]
            scores = []
            for begin, length, mask in spans:
                score = mm_nt(q, k_out[pl.ds(begin, length)]) * scale
                scores.append(score if mask is None else jnp.where(mask, score, -1e30))
            top = jnp.max(scores[0], axis=-1, keepdims=True)
            for score in scores[1:]:
                top = jnp.maximum(top, jnp.max(score, axis=-1, keepdims=True))
            powers = [jnp.exp(score - top) for score in scores]
            summed = sum(jnp.sum(power, axis=-1, keepdims=True) for power in powers)
            out = jnp.zeros((block, cols), F32)
            for (begin, length, _), power in zip(spans, powers):
                out = out + mm((power / summed).astype(BF), v_out[pl.ds(begin, length)])
            att_v[pl.ds(first // rows, per)] = out.astype(BF).reshape(per, rows, cols)
            col_out[at] = jnp.where(block_lane == 0, top + jnp.log(summed), col_out[at])

        for number in range(prompt_len // block):
            spans = [(0, number * block, None)] if number else []
            attend(number * block, spans + [(number * block, block, causal)])
        poll("prompt")

        def later(number, carry):
            first = pl.multiple_of(prompt_len + number * block, block)
            attend(first, [(0, prompt_len, None), (first, block, same)])
            return carry

        lax.fori_loop(0, (tokens - prompt_len) // block, later, 0)
        attended = Exchange(here, lambda e: att_v.at[e], lambda e: att_out.at[e], att_sems)
        attended.start()
        poll("sent")
        attended.arrive()
        for step in range(-1, far):
            full.side(step)
            cots.side(step)
        for slot in range(ring):
            full_over.take(slot)
            if slot < early:
                cots_over.take(slot)
        for slot in range(ring):
            full_over.settle(slot)
            if slot < early:
                cots_over.settle(slot)
        full.settle()
        cots.settle()
        for part in (gather, full, cots, full_over, cots_over, columns_of, spread_dots, attended):
            part.finish()
        over.wait_send()
        for copy in small_copies:
            copy.wait_send()
        for copy in stores:
            copy.wait()

    hbm = pl.BlockSpec(memory_space=pl.ANY)
    vmem = pl.BlockSpec(memory_space=pltpu.VMEM)

    def low(*shape):
        return jax.ShapeDtypeStruct(shape, BF)

    def wide(*shape):
        return jax.ShapeDtypeStruct(shape, F32)

    outs = pl.pallas_call(
        kernel,
        out_shape=[
            low(ep_count, rows, width),
            low(width, kinds * cols),
            low(2, ep_count, *small.shape),
            low(2, ep_count, *w_out.shape),
            low(ep_count, rows, width),
            low(ep_count, rows, width),
            low(tokens, cols),
            low(tokens, cols),
            low(tokens, cols),
            low(tokens, cols),
            low(tokens, cols),
            wide(tokens, 128),
            low(ep_count, rows, cols),
            low(ep_count, rows, width),
        ],
        in_specs=[hbm, hbm, hbm, hbm, hbm, vmem],
        out_specs=[hbm, vmem, vmem, hbm, hbm, hbm] + [vmem] * 6 + [hbm, hbm],
        scratch_shapes=Gather.scratch(ep_count)
        + Exchange.scratch(ep_count)
        + [dma((ep_count,)), dma((ep_count,))]
        + [dma, dma((2,)), dma((2,))]
        + Gather.scratch(ep_count)
        + Gather.scratch(ep_count)
        + Crossing.scratch(ep_count)
        + Crossing.scratch(ep_count)
        + [
            pltpu.VMEM((2, 2, rows, width), BF),
            pltpu.VMEM((ep_count, rows, width), BF),
            pltpu.VMEM((2, ep_count, kinds, depth, cols), BF),
            pltpu.VMEM((1, width), F32),
            pltpu.VMEM((2, tokens, cols), F32),
        ]
        + [dma((2,)), dma((ring,))]
        + [pltpu.VMEM((8, segment), F32), pltpu.VMEM((ep_count, 8, segment), F32)]
        + Exchange.scratch(ep_count)
        + [pltpu.VMEM((ep_count, rows, cols), BF)]
        + Exchange.scratch(ep_count),
        compiler_params=pltpu.CompilerParams(
            collective_id=collective_id, has_side_effects=True, vmem_limit_bytes=56 << 20
        ),
        name=name,
    )(x, weights, small, w_out, cot, table)
    return outs[:-1]


def angles_of(position):
    half_dim = HEAD_DIM // 2
    frequency = np.float32(theta_base) ** (-2.0 * np.arange(half_dim, dtype=np.float32) / HEAD_DIM)
    angles = position.astype(np.float32)[:, None] * frequency.astype(np.float32)[None, :]
    return np.concatenate([np.cos(angles), np.sin(angles)], axis=1).astype(np.float32)


def per_device(
    block_input,
    cotangent,
    routes,
    w_query,
    w_key,
    w_value,
    w_output,
    w_router,
    gain_attn,
    gain_query,
    gain_key,
    gain_mlp,
    w_gate,
    w_up,
    w_down,
):
    rows, width = block_input.shape
    top_count = routes.shape[1]
    ep_count = lax.axis_size("ep")
    grp_count = lax.axis_size("grp")
    me = lax.axis_index("ep")
    my_group = lax.axis_index("grp")
    tokens = rows * ep_count
    prompt_len = tokens // 2
    capacity = min(rows, rows * top_count * 33 // (32 * ep_count))
    cols = width // ep_count
    scale = HEAD_DIM ** (-0.5)
    depth = w_query.shape[0]

    chosen = jnp.any(routes[:, :, None] == jnp.arange(ep_count, dtype=jnp.int32), axis=1)
    per_row = 128
    router_rows = depth * ep_count // per_row
    gains = jnp.concatenate([gain_attn, gain_query, gain_key, gain_mlp])
    gain_rows = gains.shape[0] // per_row
    small = jnp.concatenate(
        [
            w_router.reshape(router_rows, per_row),
            gains.reshape(gain_rows, per_row),
            jnp.zeros((16 - router_rows - gain_rows, per_row), BF),
            chosen.T.astype(BF),
        ]
    )
    weights = jnp.stack([w_query, w_key, w_value])
    token = np.arange(tokens)
    table = jnp.asarray(angles_of(np.where(token < prompt_len, token, prompt_len + (token - prompt_len) % rows)))
    early = ep_count // 4
    normed_all, w_all, smalls, full_output, cot_own, cot_other, query, key, value, n_q, n_k, columns, tiles = attention(
        ep_count, block_input, weights, small, w_output, cotangent, table, early, "attention", 1
    )
    normed_all = normed_all.reshape(tokens, width)
    full_rows = full_output.reshape(grp_count * ep_count, depth, width)
    full_output = full_output.reshape(width, width)
    smalls = smalls.reshape(grp_count * ep_count, small.shape[0], per_row)
    full_router = smalls[:, :router_rows].reshape(width, ep_count)
    gains = smalls[:, router_rows : router_rows + gain_rows].reshape(-1, 4, depth).transpose(1, 0, 2).reshape(4, width)
    gain_first, gain_qnorm, gain_knorm, gain_second = (gains[i].astype(F32) for i in range(4))
    chosen_all = smalls[:, 16:].reshape(grp_count, ep_count, ep_count, rows)

    gain_q = lax.dynamic_slice(gain_qnorm, (me * cols,), (cols,))
    gain_k = lax.dynamic_slice(gain_knorm, (me * cols,), (cols,))
    att_loc = tiles.transpose(1, 0, 2).reshape(rows, width)

    inputs = block_input.astype(F32)
    residual = inputs + mm(att_loc, full_output)
    r_m = lax.rsqrt(jnp.mean(residual * residual, axis=-1, keepdims=True) + eps)
    n_m = residual * r_m
    normed_mlp = (n_m * gain_second).astype(BF)
    pair = 2 * rows
    slots = -(-2 * capacity // 16) * 16
    chips = ep_count // 2
    mine = lax.dynamic_index_in_dim(chosen_all, me, 2, keepdims=False)
    mine = jnp.where(my_group == 0, mine, mine[::-1]).reshape(2 * chips, pair).astype(F32)
    router = jnp.pad(full_router, ((0, 0), (0, per_row - ep_count)))
    gate_w, up_w, down_w = w_gate[0], w_up[0], w_down[0]
    _, units, grad_out, hidden, grad_gate_pre, grad_up_pre, _, result_terms, _, d_normed_mlp, gate_grads, _ = experts(
        ep_count, normed_mlp, cot_own, cot_other, early, mine, slots, router, gate_w, up_w, down_w, "experts", 4
    )
    gate_grads = gate_grads[:, 0]

    probs = jax.nn.softmax(mm(normed_mlp, full_router), axis=-1)
    d_probs = gate_grads.T
    d_logits = (probs * (d_probs - jnp.sum(probs * d_probs, axis=-1, keepdims=True))).astype(BF)
    local_router = mm_tn(normed_mlp, d_logits)
    d_normed_mlp = d_normed_mlp + mm_nt(d_logits, full_router)
    local_gain_mlp = jnp.sum(d_normed_mlp * n_m, axis=0)
    d_n = d_normed_mlp * gain_second
    d_residual = cotangent.astype(F32) + r_m * (d_n - n_m * jnp.mean(n_m * d_n, axis=-1, keepdims=True))
    d_proj = d_residual.astype(BF)

    gain_rows_own = jnp.stack([gain_q, gain_k])
    owners = grp_count * ep_count
    tiles = jnp.concatenate(
        [
            local_router.reshape(owners, router_rows, per_row),
            jnp.pad(local_gain_mlp.reshape(owners, 1, depth), ((0, 0), (0, 16 - router_rows - 1), (0, per_row - depth))),
        ],
        axis=1,
    )
    d_normed, grad_output, mixture, grad_w, tiles, late, grad_gate, grad_up, grad_down = backward(
        ep_count,
        d_proj,
        att_loc,
        full_rows,
        (query, key, value, n_q, n_k),
        columns,
        table,
        gain_rows_own,
        w_all,
        normed_all,
        result_terms,
        tiles,
        [a.reshape(-1, a.shape[-1]) for a in (units, grad_out, hidden, grad_gate_pre, grad_up_pre)],
        "backward",
        9,
    )[:9]
    block_output = (residual + mixture).astype(BF)
    r_a = lax.rsqrt(jnp.mean(inputs * inputs, axis=-1, keepdims=True) + eps)
    n_a = inputs * r_a
    d_n = d_normed * gain_first
    input_grad = d_residual + r_a * (d_n - n_a * jnp.mean(n_a * d_n, axis=-1, keepdims=True))
    my_rows = my_group * ep_count + me
    grad_w = [grad_w[i].astype(F32) for i in range(3)]
    sums = jnp.sum(tiles, axis=0)
    grad_router = sums[:router_rows].reshape(depth, ep_count)
    gain_part = jnp.sum(late[:, 2, :depth], axis=0) / lax.dynamic_slice(gain_first, (my_rows * depth,), (depth,))
    late = jnp.sum(late.reshape(grp_count, ep_count, 8, cols), axis=0)[:, :2].transpose(1, 0, 2).reshape(2, width)
    late = lax.dynamic_slice(late, (0, my_rows * depth), (2, depth))
    gain_sums = [gain_part, late[0], late[1], sums[router_rows, :depth]]
    grad_gate, grad_up, grad_down = (grad.astype(F32)[None] for grad in (grad_gate, grad_up, grad_down))
    return (
        block_output,
        input_grad,
        grad_w[0],
        grad_w[1],
        grad_w[2],
        grad_output,
        grad_router,
        gain_sums[0],
        gain_sums[1],
        gain_sums[2],
        gain_sums[3],
        grad_gate,
        grad_up,
        grad_down,
    )


def plain_scale(values, gain_vec):
    return values * lax.rsqrt(jnp.mean(values * values, axis=-1, keepdims=True) + eps) * gain_vec


def rotate(values, position):
    token_count = values.shape[0]
    by_head = values.reshape(token_count, -1, HEAD_DIM)
    half_dim = HEAD_DIM // 2
    frequency = theta_base ** (-2.0 * jnp.arange(half_dim, dtype=jnp.float32) / HEAD_DIM)
    angles = position.astype(jnp.float32)[:, None] * frequency[None, :]
    cosine = jnp.cos(angles)[:, None, :]
    sine_part = jnp.sin(angles)[:, None, :]
    former = by_head[..., :half_dim]
    latter = by_head[..., half_dim:]
    turned = jnp.concatenate(
        [former * cosine - latter * sine_part, latter * cosine + former * sine_part], axis=-1
    )
    return turned.reshape(token_count, -1)


def masked_scores(query, keys, allowed, scale):
    raw_scores = jnp.einsum("qhd,khd->hqk", query, keys, preferred_element_type=jnp.float32) * scale
    return jnp.where(allowed[None], raw_scores, -1e30)


def plain_attend(query, keys, values, allowed, scale, head_group):
    outputs = []
    log_totals = []
    for head_start in range(0, query.shape[1], head_group):
        head_slice = slice(head_start, head_start + head_group)
        scores = masked_scores(query[:, head_slice], keys[:, head_slice], allowed, scale)
        largest = jnp.max(scores, axis=-1, keepdims=True)
        exponent = jnp.exp(scores - largest)
        summed = jnp.sum(exponent, axis=-1, keepdims=True)
        weights = (exponent / summed).astype(jnp.bfloat16)
        outputs.append(
            jnp.einsum(
                "hqk,khd->qhd", weights, values[:, head_slice], preferred_element_type=jnp.float32
            )
        )
        log_totals.append(largest + jnp.log(summed))
    return (jnp.concatenate(outputs, axis=1), jnp.concatenate(log_totals, axis=0))


def plain_attend_back(query, keys, values, grad_out, log_totals, allowed, scale, head_group):
    query_grads = []
    key_grads = []
    value_grads = []
    for head_start in range(0, query.shape[1], head_group):
        head_slice = slice(head_start, head_start + head_group)
        query_part = query[:, head_slice]
        keys_part = keys[:, head_slice]
        grad_part = grad_out[:, head_slice]
        scores = masked_scores(query_part, keys_part, allowed, scale)
        weights = jnp.where(allowed[None], jnp.exp(scores - log_totals[head_slice]), 0.0)
        grad_weights = jnp.einsum(
            "qhd,khd->hqk", grad_part, values[:, head_slice], preferred_element_type=jnp.float32
        )
        inner = jnp.sum(weights * grad_weights, axis=-1, keepdims=True)
        grad_scores = (weights * (grad_weights - inner)).astype(jnp.bfloat16)
        query_grads.append(
            jnp.einsum("hqk,khd->qhd", grad_scores, keys_part, preferred_element_type=jnp.float32)
            * scale
        )
        key_grads.append(
            jnp.einsum("hqk,qhd->khd", grad_scores, query_part, preferred_element_type=jnp.float32)
            * scale
        )
        value_grads.append(
            jnp.einsum(
                "hqk,qhd->khd",
                weights.astype(jnp.bfloat16),
                grad_part,
                preferred_element_type=jnp.float32,
            )
        )
    return (
        jnp.concatenate(query_grads, axis=1),
        jnp.concatenate(key_grads, axis=1),
        jnp.concatenate(value_grads, axis=1),
    )


def per_device_plain(
    block_input,
    cotangent,
    routes,
    w_query,
    w_key,
    w_value,
    w_output,
    w_router,
    gain_attn,
    gain_query,
    gain_key,
    gain_mlp,
    w_gate,
    w_up,
    w_down,
):
    row_count, model_width = block_input.shape
    top_count = routes.shape[1]
    ep_count = lax.axis_size("ep")
    my_index = lax.axis_index("ep")
    half_count = ep_count // 2
    prompt_len = row_count * half_count
    capacity = min(row_count, row_count * top_count * 33 // (32 * ep_count))
    head_count = model_width // HEAD_DIM
    head_group = math.gcd(4, head_count)
    scale = HEAD_DIM ** (-0.5)
    gathered = (
        lax.all_gather(w_query, ("grp", "ep"), axis=0, tiled=True),
        lax.all_gather(w_key, ("grp", "ep"), axis=0, tiled=True),
        lax.all_gather(w_value, ("grp", "ep"), axis=0, tiled=True),
        lax.all_gather(w_output, ("grp", "ep"), axis=0, tiled=True),
        lax.all_gather(w_router, ("grp", "ep"), axis=0, tiled=True),
        lax.all_gather(gain_attn, ("grp", "ep"), axis=0, tiled=True),
        lax.all_gather(gain_query, ("grp", "ep"), axis=0, tiled=True),
        lax.all_gather(gain_key, ("grp", "ep"), axis=0, tiled=True),
        lax.all_gather(gain_mlp, ("grp", "ep"), axis=0, tiled=True),
    )
    full_query, full_key, full_value, full_output, full_router = (
        gathered[0],
        gathered[1],
        gathered[2],
        gathered[3],
        gathered[4],
    )
    gain_first = gathered[5].astype(jnp.float32)
    gain_qnorm = gathered[6].astype(jnp.float32)
    gain_knorm = gathered[7].astype(jnp.float32)
    gain_second = gathered[8].astype(jnp.float32)
    offsets = jnp.arange(row_count, dtype=jnp.int32)
    in_prompt = my_index < half_count
    position = jnp.where(in_prompt, my_index * row_count + offsets, prompt_len + offsets)
    key_position = jnp.concatenate([jnp.arange(prompt_len, dtype=jnp.int32), prompt_len + offsets])
    from_prompt = jnp.arange(prompt_len + row_count, dtype=jnp.int32) < prompt_len
    allowed = (key_position[None, :] <= position[:, None]) & (
        from_prompt[None, :] | jnp.logical_not(in_prompt)
    )

    def prepare(linear, gain_vec):
        return rotate(plain_scale(linear, gain_vec), position)

    inputs = block_input.astype(jnp.float32)
    normed = plain_scale(inputs, gain_first).astype(jnp.bfloat16)
    query_lin = jnp.dot(normed, full_query, preferred_element_type=jnp.float32)
    key_lin = jnp.dot(normed, full_key, preferred_element_type=jnp.float32)
    value_lin = jnp.dot(normed, full_value, preferred_element_type=jnp.float32)
    query_low = prepare(query_lin, gain_qnorm).astype(jnp.bfloat16)
    key_low = prepare(key_lin, gain_knorm).astype(jnp.bfloat16)
    value_low = value_lin.astype(jnp.bfloat16)
    shared = (
        lax.all_gather(key_low, "ep", axis=0, tiled=True),
        lax.all_gather(value_low, "ep", axis=0, tiled=True),
    )
    keys = jnp.concatenate([shared[0][:prompt_len], key_low]).reshape(-1, head_count, HEAD_DIM)
    values = jnp.concatenate([shared[1][:prompt_len], value_low]).reshape(-1, head_count, HEAD_DIM)
    query = query_low.reshape(row_count, head_count, HEAD_DIM)
    attn_out, log_totals = plain_attend(query, keys, values, allowed, scale, head_group)
    attended = attn_out.reshape(row_count, model_width).astype(jnp.bfloat16)
    residual = inputs + jnp.dot(attended, full_output, preferred_element_type=jnp.float32)
    normed_mlp = plain_scale(residual, gain_second).astype(jnp.bfloat16)
    logits = jnp.dot(normed_mlp, full_router, preferred_element_type=jnp.float32)
    probs = jax.nn.softmax(logits, axis=-1)
    picks = routes[:, :, None] == jnp.arange(ep_count, dtype=jnp.int32)[None, None, :]
    gates = jnp.sum(jnp.where(picks, probs[:, None, :], 0.0), axis=-1)
    hot_table = picks.reshape(-1, ep_count).astype(jnp.int32)
    before = jnp.cumsum(hot_table, axis=0) - hot_table
    slot_index = jnp.sum(before * hot_table, axis=1)
    target = routes.reshape(-1) * capacity + slot_index
    sentinel = row_count * top_count
    source = (
        jnp.full((ep_count * capacity,), sentinel, jnp.int32)
        .at[target]
        .set(jnp.arange(sentinel, dtype=jnp.int32))
    )
    token_of = source // top_count
    padded_rows = jnp.concatenate([normed_mlp, jnp.zeros((1, model_width), jnp.bfloat16)])
    outgoing = padded_rows[token_of].reshape(ep_count, capacity, model_width)
    arrived = lax.all_to_all(outgoing, "ep", split_axis=0, concat_axis=0, tiled=True)
    units = arrived.reshape(-1, model_width)
    gate_w = w_gate[0]
    up_w = w_up[0]
    down_w = w_down[0]
    gate_pre = jnp.dot(units, gate_w, preferred_element_type=jnp.float32)
    up_pre = jnp.dot(units, up_w, preferred_element_type=jnp.float32)
    hidden = (jax.nn.silu(gate_pre) * up_pre).astype(jnp.bfloat16)
    expert_result = jnp.dot(hidden, down_w, preferred_element_type=jnp.float32).astype(jnp.bfloat16)
    returned = lax.all_to_all(
        expert_result.reshape(ep_count, capacity, model_width),
        "ep",
        split_axis=0,
        concat_axis=0,
        tiled=True,
    )
    picked = (
        returned.reshape(-1, model_width)[target]
        .reshape(row_count, top_count, model_width)
        .astype(jnp.float32)
    )
    output_full = residual + jnp.sum(gates[:, :, None] * picked, axis=1)
    block_output = output_full.astype(jnp.bfloat16)
    back_query, back_key, back_value, back_output, back_router = (
        full_query,
        full_key,
        full_value,
        full_output,
        full_router,
    )
    grad_top = cotangent.astype(jnp.float32)
    grad_gates = jnp.sum(grad_top[:, None, :] * picked, axis=-1)
    grad_expert = (
        (gates[:, :, None] * grad_top[:, None, :]).astype(jnp.bfloat16).reshape(-1, model_width)
    )
    padded_grads = jnp.concatenate([grad_expert, jnp.zeros((1, model_width), jnp.bfloat16)])
    grad_outgoing = padded_grads[source].reshape(ep_count, capacity, model_width)
    grad_arrived = lax.all_to_all(
        grad_outgoing, "ep", split_axis=0, concat_axis=0, tiled=True
    ).reshape(-1, model_width)
    grad_hidden = jnp.einsum("nd,fd->nf", grad_arrived, down_w, preferred_element_type=jnp.float32)
    sigma = jax.nn.sigmoid(gate_pre)
    grad_gate_pre = (grad_hidden * up_pre * sigma * (1.0 + gate_pre * (1.0 - sigma))).astype(
        jnp.bfloat16
    )
    grad_up_pre = (grad_hidden * gate_pre * sigma).astype(jnp.bfloat16)
    local_down = jnp.einsum("nf,nd->fd", hidden, grad_arrived, preferred_element_type=jnp.float32)
    local_gate = jnp.einsum("nd,nf->df", units, grad_gate_pre, preferred_element_type=jnp.float32)
    local_up = jnp.einsum("nd,nf->df", units, grad_up_pre, preferred_element_type=jnp.float32)
    grad_units = jnp.einsum("nf,df->nd", grad_gate_pre, gate_w, preferred_element_type=jnp.float32)
    grad_units = grad_units + jnp.einsum(
        "nf,df->nd", grad_up_pre, up_w, preferred_element_type=jnp.float32
    )
    grad_units = grad_units.astype(jnp.bfloat16).reshape(ep_count, capacity, model_width)
    grad_returned = lax.all_to_all(
        grad_units, "ep", split_axis=0, concat_axis=0, tiled=True
    ).reshape(-1, model_width)
    grad_normed_mlp = jnp.sum(
        grad_returned[target].reshape(row_count, top_count, model_width).astype(jnp.float32), axis=1
    )
    expert_sums = (
        lax.psum(local_gate[None].astype(jnp.bfloat16), "grp").astype(jnp.float32),
        lax.psum(local_up[None].astype(jnp.bfloat16), "grp").astype(jnp.float32),
        lax.psum(local_down[None].astype(jnp.bfloat16), "grp").astype(jnp.float32),
    )
    grad_probs = jnp.sum(jnp.where(picks, grad_gates[:, :, None], 0.0), axis=1)
    grad_logits = (
        probs * (grad_probs - jnp.sum(probs * grad_probs, axis=-1, keepdims=True))
    ).astype(jnp.bfloat16)
    local_router = jnp.einsum(
        "rd,re->de", normed_mlp, grad_logits, preferred_element_type=jnp.float32
    )
    grad_normed_mlp = grad_normed_mlp + jnp.einsum(
        "re,de->rd", grad_logits, back_router, preferred_element_type=jnp.float32
    )
    unused_mlp, second_back = jax.vjp(plain_scale, residual, gain_second)
    grad_from_mlp, local_gain_mlp = second_back(grad_normed_mlp)
    grad_residual = grad_top + grad_from_mlp
    grad_proj = grad_residual.astype(jnp.bfloat16)
    local_output = jnp.einsum("rd,re->de", attended, grad_proj, preferred_element_type=jnp.float32)
    grad_attended = jnp.einsum(
        "re,de->rd", grad_proj, back_output, preferred_element_type=jnp.float32
    )
    grad_attended = grad_attended.astype(jnp.bfloat16).reshape(row_count, head_count, HEAD_DIM)
    grad_query_rot, grad_keys, grad_values = plain_attend_back(
        query, keys, values, grad_attended, log_totals, allowed, scale, head_group
    )
    grad_keys = grad_keys.reshape(-1, model_width)
    grad_values = grad_values.reshape(-1, model_width)
    padding = jnp.zeros((ep_count * row_count - prompt_len, model_width), jnp.float32)
    key_share, value_share = (
        lax.psum_scatter(
            jnp.concatenate([grad_keys[:prompt_len], padding]).astype(jnp.bfloat16),
            "ep",
            scatter_dimension=0,
            tiled=True,
        ).astype(jnp.float32),
        lax.psum_scatter(
            jnp.concatenate([grad_values[:prompt_len], padding]).astype(jnp.bfloat16),
            "ep",
            scatter_dimension=0,
            tiled=True,
        ).astype(jnp.float32),
    )
    grad_key_rot = key_share + grad_keys[prompt_len:]
    grad_value_lin = (value_share + grad_values[prompt_len:]).astype(jnp.bfloat16)
    unused_query, query_back = jax.vjp(prepare, query_lin, gain_qnorm)
    grad_query_lin, local_gain_query = query_back(grad_query_rot.reshape(row_count, model_width))
    unused_key, key_back = jax.vjp(prepare, key_lin, gain_knorm)
    grad_key_lin, local_gain_key = key_back(grad_key_rot)
    grad_query_low = grad_query_lin.astype(jnp.bfloat16)
    grad_key_low = grad_key_lin.astype(jnp.bfloat16)
    local_query = jnp.einsum(
        "rd,re->de", normed, grad_query_low, preferred_element_type=jnp.float32
    )
    local_key = jnp.einsum("rd,re->de", normed, grad_key_low, preferred_element_type=jnp.float32)
    local_value = jnp.einsum(
        "rd,re->de", normed, grad_value_lin, preferred_element_type=jnp.float32
    )
    grad_normed = jnp.einsum(
        "re,de->rd", grad_query_low, back_query, preferred_element_type=jnp.float32
    )
    grad_normed = grad_normed + jnp.einsum(
        "re,de->rd", grad_key_low, back_key, preferred_element_type=jnp.float32
    )
    grad_normed = grad_normed + jnp.einsum(
        "re,de->rd", grad_value_lin, back_value, preferred_element_type=jnp.float32
    )
    unused_first, first_back = jax.vjp(plain_scale, inputs, gain_first)
    grad_from_attn, local_gain_attn = first_back(grad_normed)
    input_grad = grad_residual + grad_from_attn
    summed_grads = (
        lax.psum_scatter(local_query, ("grp", "ep"), scatter_dimension=0, tiled=True),
        lax.psum_scatter(local_key, ("grp", "ep"), scatter_dimension=0, tiled=True),
        lax.psum_scatter(local_value, ("grp", "ep"), scatter_dimension=0, tiled=True),
        lax.psum_scatter(local_output, ("grp", "ep"), scatter_dimension=0, tiled=True),
        lax.psum_scatter(local_router, ("grp", "ep"), scatter_dimension=0, tiled=True),
        lax.psum_scatter(local_gain_attn, ("grp", "ep"), scatter_dimension=0, tiled=True),
        lax.psum_scatter(local_gain_query, ("grp", "ep"), scatter_dimension=0, tiled=True),
        lax.psum_scatter(local_gain_key, ("grp", "ep"), scatter_dimension=0, tiled=True),
        lax.psum_scatter(local_gain_mlp, ("grp", "ep"), scatter_dimension=0, tiled=True),
    )
    return (
        block_output,
        input_grad,
        summed_grads[0],
        summed_grads[1],
        summed_grads[2],
        summed_grads[3],
        summed_grads[4],
        summed_grads[5],
        summed_grads[6],
        summed_grads[7],
        summed_grads[8],
        expert_sums[0],
        expert_sums[1],
        expert_sums[2],
    )


def solution(mesh):
    both = ("grp", "ep")
    return jax.shard_map(
        per_device if mesh.shape["grp"] == 2 else per_device_plain,
        mesh=mesh,
        in_specs=(P(both, None),) * 8 + (P(both),) * 4 + (P("ep", None, None),) * 3,
        out_specs=(P(both, None),) * 7 + (P(both),) * 4 + (P("ep", None, None),) * 3,
        check_vma=False,
    )
```

```python
import math

import jax
import jax.numpy as jnp
import numpy as np
from jax import lax
from jax.experimental import pallas as pl
from jax.experimental.pallas import tpu as pltpu
from jax.sharding import PartitionSpec as P

HEAD_DIM = 128
MESH = pl.DeviceIdType.MESH
BF = jnp.bfloat16
F32 = jnp.float32


eps = 1e-05
theta_base = 10000.0


def mm(a, b):
    return jnp.dot(a, b, preferred_element_type=F32)


def mm_nt(a, b):
    return lax.dot_general(a, b, (((1,), (1,)), ((), ())), preferred_element_type=F32)


def mm_tn(a, b):
    return lax.dot_general(a, b, (((0,), (0,)), ((), ())), preferred_element_type=F32)


class Place:
    def __init__(self, ep_count):
        self.grp = lax.axis_index("grp")
        self.ep = lax.axis_index("ep")
        self.count = ep_count
        self.ring = ep_count // 2
        self.half = self.ring // 2
        self.core = self.ep % 2
        y = (self.ep // 2) % 2
        z = self.ep // 4
        self.place = z + y * (self.ring - 1 - 2 * z)

    def index(self, place, core):
        y = place // self.half
        z = place + y * (self.ring - 1 - 2 * place)
        return (z * 2 + y) * 2 + core

    def at(self, offset):
        return (self.place + offset + self.ring) % self.ring

    def chip(self, offset):
        return self.index(self.at(offset), self.core)

    def right(self):
        return (self.grp, self.chip(1))

    def left(self):
        return (self.grp, self.chip(-1))

    def sibling(self):
        return (self.grp, self.index(self.place, 1 - self.core))

    def across(self):
        return (1 - self.grp, self.ep)

    def peer(self, offset):
        return (self.grp, (self.ep + offset + self.count) % self.count)


def greet(devices):
    barrier = pltpu.get_barrier_semaphore()
    for device in devices:
        pl.semaphore_signal(barrier, inc=1, device_id=device, device_id_type=MESH)
    pl.semaphore_wait(barrier, len(devices))


def remote(src, dst, send, recv, device):
    return pltpu.make_async_remote_copy(
        src_ref=src, dst_ref=dst, send_sem=send, recv_sem=recv, device_id=device, device_id_type=MESH
    )


class Gather:
    def __init__(self, here, src, dst, sems, reach=None):
        self.here, self.src, self.dst, self.reach = here, src, dst, reach
        self.ring_send, self.ring_recv, self.side_send, self.side_recv, self.own_sem = sems
        self.rows = dst.shape[1] // 2
        self.far = here.ring // 2
        self.started = []

    @staticmethod
    def scratch(ep_count):
        far = ep_count // 4
        ring = pltpu.SemaphoreType.DMA((2, far, 2))
        side = pltpu.SemaphoreType.DMA((2, far + 1, 2))
        return [ring, ring, side, side, pltpu.SemaphoreType.DMA]

    def block(self, index, part):
        return self.dst.at[index, pl.ds(part * self.rows, self.rows)]

    def go(self, copy):
        copy.start()
        self.started.append(copy)

    def hops(self, way, part):
        if self.reach is not None:
            return self.reach
        return self.far if way == part else self.far - 1

    def ring_copy(self, way, step, part, src, index):
        device = self.here.right() if way == 0 else self.here.left()
        return remote(
            src, self.block(index, part), self.ring_send.at[way, step, part], self.ring_recv.at[way, step, part], device
        )

    def side_copy(self, way, step, part, src, index):
        return remote(
            src,
            self.block(index, part),
            self.side_send.at[way, step, part],
            self.side_recv.at[way, step, part],
            self.here.sibling(),
        )

    def start(self):
        here = self.here
        for part in range(2):
            src = self.src.at[pl.ds(part * self.rows, self.rows)]
            for way in range(2):
                if self.hops(way, part) > 0:
                    self.go(self.ring_copy(way, 0, part, src, here.ep))
            self.go(self.side_copy(0, 0, part, src, here.ep))
        if self.reach is not None:
            return
        self.own = pltpu.make_async_copy(self.src, self.dst.at[here.ep], self.own_sem)
        self.own.start()

    def step(self, step):
        here = self.here
        for part in range(2):
            for way in range(2):
                if step < self.hops(way, part):
                    index = here.chip(-1 - step if way == 0 else 1 + step)
                    src = self.block(index, part)
                    self.ring_copy(way, step, part, src, index).wait_recv()
                    if step + 1 < self.hops(way, part):
                        self.go(self.ring_copy(way, step + 1, part, src, index))
                    self.go(self.side_copy(way, step + 1, part, src, index))

    def side(self, step):
        here = self.here
        for part in range(2):
            for way in range(2):
                if (step < 0 and way == 0) or (0 <= step < self.hops(way, part)):
                    offset = 0 if step < 0 else (-1 - step if way == 0 else 1 + step)
                    index = here.index(here.at(offset), 1 - here.core)
                    self.side_copy(way, step + 1, part, self.block(index, part), index).wait_recv()

    def settle(self):
        self.own.wait()

    def finish(self):
        for copy in self.started:
            copy.wait_send()


class Exchange:
    def __init__(self, here, src, dst, sems):
        self.here, self.src, self.dst = here, src, dst
        self.send, self.recv, self.own_sem = sems

    @staticmethod
    def scratch(ep_count):
        return [
            pltpu.SemaphoreType.DMA((ep_count,)),
            pltpu.SemaphoreType.DMA((ep_count,)),
            pltpu.SemaphoreType.DMA,
        ]

    def start(self):
        here = self.here
        self.own = pltpu.make_async_copy(self.src(here.ep), self.dst(here.ep), self.own_sem)
        self.own.start()
        self.copies = []
        for offset in range(1, here.count):
            device = here.peer(offset)
            copy = remote(self.src(device[1]), self.dst(here.ep), self.send.at[offset], self.recv.at[offset], device)
            copy.start()
            self.copies.append(copy)

    def arrive(self):
        here = self.here
        self.own.wait()
        for offset in range(1, here.count):
            source = here.peer(-offset)[1]
            remote(
                self.dst(source), self.dst(source), self.send.at[offset], self.recv.at[offset], here.peer(offset)
            ).wait_recv()

    def finish(self):
        for copy in self.copies:
            copy.wait_send()


def far_devices(here):
    return [(1 - here.grp, (here.ep + offset) % here.count) for offset in range(here.count)]


def plane_devices(here):
    return [here.peer(offset) for offset in range(1, here.count)]


def split(refs, *sizes):
    groups, start = [], 0
    for size in sizes:
        groups.append(refs[start : start + size])
        start += size
    return groups


def ring_offsets(ring):
    far = ring // 2
    return [0] + [sign * k for k in range(1, far) for sign in (1, -1)] + [far]


def experts(
    ep_count, block, cot_own, cot_other, early, mine, slots, router, gate_w, up_w, down_w, name, collective_id
):
    rows, width = block.shape
    hidden_width = gate_w.shape[1]
    pair = 2 * rows
    ring = ep_count // 2
    offsets = ring_offsets(ring)
    batches = [[0]] + [[2 * k - 1, 2 * k] for k in range(1, ring // 2)] + [[ring - 1]]
    tile, wide = 512, 1024
    far = ring // 2
    reach = far // 2

    def kernel(*refs):
        ins, outs, scratch = split(refs, 8, 12, len(refs) - 20)
        block_ref, cot_ref, cot_far, mine_ref, router_ref, gate_ref, up_ref, down_ref = ins
        other_ref, u_out, e_out, h_out, g_out, p_out, du_terms, eo_terms, du_joint, sum_out, dot_out, cot_late = outs
        gather_sems, near_sems, cross, cot_cross, bufs, stage, du_s, dot_sems, load_sems = split(scratch, 5, 5, 4, 4, 6, 12, 8, 3, 5)
        across_send, across_recv, hand_send, hand_recv = cross
        gate_v, up_v, down_v, rows_v, cot_v, own_ref = bufs
        u_s, e_s, h_s, g_s, p_s, r_s, dx_s, gate_s, dot_s, line_s, term_v, hot_ref = stage
        dot_send, dot_recv, dot_own = dot_sems
        weight_sem, rows_sem, cot_sem, stage_sem, term_sem = load_sems
        here = Place(ep_count)
        sums = RingSum(here, lambda e: du_terms.at[e], du_joint, du_s[:3], du_s[3:])
        weights = []
        for i, (src, dst) in enumerate(((gate_ref, gate_v), (up_ref, up_v), (down_ref, down_v))):
            copy = pltpu.make_async_copy(src, dst, weight_sem.at[i])
            copy.start()
            weights.append(copy)
        greet(plane_devices(here) + [here.across()])
        gather = Gather(here, block_ref, own_ref, gather_sems)
        gather.start()
        sent = []

        def start(copy):
            copy.start()
            sent.append(copy)

        def cross_copy(slot, src):
            index = here.chip(offsets[slot])
            return remote(src, other_ref.at[index], across_send.at[slot], across_recv.at[slot], here.across())

        def hand_copy(slot, core):
            index = here.index(here.at(offsets[slot]), core)
            return remote(
                other_ref.at[index], other_ref.at[index], hand_send.at[slot], hand_recv.at[slot], here.sibling()
            )

        start(cross_copy(0, block_ref))
        near = Gather(here, other_ref.at[here.ep], other_ref, near_sems, reach)
        straight = 2 * reach + 1
        cot_over = Crossing(here, lambda e: cot_late.at[e], lambda e: cot_late.at[e], cot_cross)
        for slot in range(early, ring):
            cot_over.send(slot, cot_ref.at[here.chip(offsets[slot])])

        def chip_of(slot):
            return here.index(here.at(offsets[slot]), 0) // 2

        def cot_copy(which, slot, buffer):
            src = cot_ref if which == 0 else (cot_far if slot < early else cot_late)
            return pltpu.make_async_copy(src.at[pl.ds(2 * chip_of(slot), 2)], cot_v.at[buffer], cot_sem.at[buffer])

        def rows_copy(src, slot, buffer):
            return pltpu.make_async_copy(
                src.at[pl.ds(2 * chip_of(slot), 2)], rows_v.at[buffer], rows_sem.at[buffer]
            )

        pending = {}
        stages = {"u": (u_s, u_out), "e": (e_s, e_out), "g": (g_s, g_out), "p": (p_s, p_out)}

        def settle(keys):
            for key in keys:
                for copy in pending.pop(key, []):
                    copy.wait()

        def store(key, which, batch):
            src, dst = stages[key]
            sem = list(stages).index(key)
            count = len(batch) * slots
            at = pl.ds(batch[0] * slots, count)
            target = dst.at[which, at]
            pending[key] = [pltpu.make_async_copy(src.at[pl.ds(0, count)], target, stage_sem.at[sem])]
            for copy in pending[key]:
                copy.start()

        def loop(extent, tile, body):
            def run(i, carry):
                body(pl.ds(pl.multiple_of(i * tile, tile), tile))
                return carry

            lax.fori_loop(0, extent // tile, run, 0)

        def prefetch(which, batch, parity):
            for i, slot in enumerate(batch):
                cot_copy(which, slot, 2 * parity + i).start()

        hidden_copies = {}

        def store_hidden(which, batch):
            at = pl.ds(batch[0] * slots, len(batch) * slots)
            sem = weight_sem.at[3 + batches.index(batch)]
            hidden_copies[batch[0]] = pltpu.make_async_copy(h_s.at[at], h_out.at[which, at], sem)
            hidden_copies[batch[0]].start()

        given = []

        def give(src, first, chip, terms):
            buffer = len(given) % 2
            if len(given) > 1:
                given[-2].wait()

            def put(at):
                spread_rows = mm_tn(hot_ref[0, chip], src[pl.ds(first, slots), at]).astype(BF)
                term_v[buffer, :, :, at] = spread_rows.reshape(2, rows, width)

            loop(width, width, put)
            copy = pltpu.make_async_copy(term_v.at[buffer], terms.at[pl.ds(2 * chip, 2)], term_sem.at[buffer])
            copy.start()
            given.append(copy)

        def settle_given():
            for copy in given[-2:]:
                copy.wait()
            given.clear()

        def work(which, batch, parity):
            count = len(batch) * slots
            every = pl.ds(0, count)
            if which == 1:
                for i, slot in enumerate(batch):
                    rows_copy(other_ref, slot, i).start()
                for i, slot in enumerate(batch):
                    rows_copy(other_ref, slot, i).wait()
            for i, slot in enumerate(batch):
                cot_copy(which, slot, 2 * parity + i).wait()
            settle("u")
            for i, slot in enumerate(batch):
                hot = hot_ref[which, chip_of(slot)]

                def pick_rows(at, i=i, hot=hot):
                    if which == 0:
                        taken = own_ref[pl.ds(2 * chip_of(batch[i]), 2), :, at]
                    else:
                        taken = rows_v[i, :, :, at]
                    picked = mm(hot, taken.reshape(pair, width))
                    u_s[pl.ds(i * slots, slots), at] = picked.astype(BF)

                loop(width, width, pick_rows)
            store("u", which, batch)
            logits = mm(u_s[every], router_ref[...])
            lane = lax.broadcasted_iota(jnp.int32, logits.shape, 1)
            powers = jnp.exp(logits - jnp.max(logits, axis=-1, keepdims=True))
            gate = jnp.sum(jnp.where(lane == here.ep, powers, 0.0), axis=-1, keepdims=True)
            gate = gate / jnp.sum(powers, axis=-1, keepdims=True)
            settle("e")
            for i, slot in enumerate(batch):
                hot = hot_ref[which, chip_of(slot)]

                def pick_cots(at, i=i, hot=hot):
                    part = pl.ds(i * slots, slots)
                    picked = mm(hot, cot_v[2 * parity + i, :, :, at].reshape(pair, width))
                    e_s[part, at] = (gate[i * slots : (i + 1) * slots] * picked).astype(BF)
                    if which == 0:
                        r_s[pl.ds((batch[0] + i) * slots, slots), at] = picked.astype(BF)

                loop(width, width, pick_cots)
            store("e", which, batch)
            settle("gp")
            held = pl.ds(batch[0] * slots, count)
            if batch[0] in hidden_copies:
                hidden_copies.pop(batch[0]).wait()
            gate_s[held] = gate

            def inner(at):
                gate_pre = mm(u_s[every], gate_v[:, at])
                up_pre = mm(u_s[every], up_v[:, at])
                grad = mm_nt(e_s[every], down_v[at, :])
                sigma = 1.0 / (1.0 + jnp.exp(-gate_pre))
                swish = gate_pre * sigma
                h_s[held, at] = (swish * up_pre).astype(BF)
                g_s[every, at] = (grad * up_pre * sigma * (1.0 + gate_pre * (1.0 - sigma))).astype(BF)
                p_s[every, at] = (grad * swish).astype(BF)

            loop(hidden_width, tile, inner)
            for key in "gp":
                store(key, which, batch)
            store_hidden(which, batch)
            if which == 1:
                return None
            return lambda: work_back(batch, every)

        def work_back(batch, every):
            def back(at):
                grad = mm_nt(g_s[every], gate_v[at, :]) + mm_nt(p_s[every], up_v[at, :])
                dx_s[every, at] = grad.astype(BF)

            loop(width, wide, back)
            for i, slot in enumerate(batch):
                part = pl.ds(i * slots, slots)
                give(dx_s, i * slots, chip_of(slot), du_terms)

        def results():
            dot_s[...] = jnp.zeros_like(dot_s)

            def outer(at):
                result = mm(h_s[...], down_v[:, at]).astype(BF).astype(F32)
                dot_s[...] += jnp.sum(result * r_s[:, at].astype(F32), axis=-1, keepdims=True)
                r_s[:, at] = (gate_s[...] * result).astype(BF)

            loop(width, tile, outer)
            for slot in range(ring):
                part = pl.ds(slot * slots, slots)
                line = jnp.sum(hot_ref[0, chip_of(slot)].astype(F32) * dot_s[part], axis=0, keepdims=True)
                for core in range(2):
                    line_s[slot, core] = jnp.broadcast_to(line[:, core * rows : (core + 1) * rows], (8, rows))

        prefetch(0, batches[0], 0)
        upto = lax.broadcasted_iota(jnp.int32, (pair, pair), 0) <= lax.broadcasted_iota(jnp.int32, (pair, pair), 1)
        mine_all = mine_ref[...]
        order = mm(mine_all.astype(BF), upto.astype(BF))
        order = jnp.where(mine_all > 0, order - 1.0, -1.0)
        place = lax.broadcasted_iota(jnp.int32, (slots, pair), 0).astype(F32)
        for which in range(2):
            for chip in range(ring):
                line = order[which * ring + chip : which * ring + chip + 1]
                hot_ref[which, chip] = jnp.where(place == line, 1.0, 0.0).astype(BF)
        for copy in weights:
            copy.wait()
        gather.settle()
        for number, batch in enumerate(batches):
            gather.side(number - 1)
            if number + 1 < len(batches):
                prefetch(0, batches[number + 1], (number + 1) % 2)
            else:
                prefetch(1, batches[0], (number + 1) % 2)
            rest = work(0, batch, number % 2)
            if number < far:
                gather.step(number)
                for slot in batches[number + 1]:
                    if slot >= straight:
                        start(cross_copy(slot, own_ref.at[here.chip(offsets[slot])]))
                if number == 1:
                    cross_copy(0, other_ref.at[here.ep]).wait_recv()
                    near.start()
                elif number > 2:
                    near.step(number - 3)
            rest()
        def dot_copy(slot, core, sender_core, source, target):
            return remote(
                line_s.at[slot, core],
                dot_out.at[source],
                dot_send.at[slot, core],
                dot_recv.at[slot, sender_core],
                (here.grp, target),
            )

        settle_given()
        sums.start()
        sums.step(0)
        results()
        own_dots = pltpu.make_async_copy(line_s.at[0, here.core], dot_out.at[here.ep], dot_own)
        own_dots.start()

        start(dot_copy(0, 1 - here.core, here.core, here.ep, here.sibling()[1]))
        for slot in range(1, ring):
            for core in range(2):
                target = here.index(here.at(offsets[slot]), core)
                start(dot_copy(slot, core, here.core, here.ep, target))
        count = len(batches)

        def put(out):
            def keep_sum(at, value):
                out[at] = value

            return keep_sum

        for number, batch in enumerate(batches):
            far_slots = [slot for slot in batch if slot >= straight]
            for slot in far_slots:
                index = here.chip(offsets[slot])
                cross_copy(slot, other_ref.at[index]).wait_recv()
                start(hand_copy(slot, here.core))
            if 0 < number < reach:
                near.step(number)
            if 0 < number < far:
                sums.step(number)
            if number == 1:
                for slot in range(ring):
                    give(r_s, slot * slots, chip_of(slot), eo_terms)
                settle_given()
            if number == far:
                sums.finish(put(sum_out))
            for slot in far_slots:
                hand_copy(slot, 1 - here.core).wait_recv()
            if number <= reach:
                near.side(number - 1)
            parity = (count + number) % 2
            if number + 1 < count:
                late = [slot for slot in batches[number + 1] if slot >= early]
                for slot in late:
                    cot_over.take(slot)
                for slot in late:
                    cot_over.settle(slot)
                prefetch(1, batches[number + 1], 1 - parity)
            work(1, batch, parity)
        own_dots.wait()
        dot_copy(0, 0, 1 - here.core, here.sibling()[1], here.sibling()[1]).wait_recv()
        for slot in range(1, ring):
            for core in range(2):
                source = here.index(here.at(-offsets[slot]), core)
                dot_copy(slot, 0, core, source, source).wait_recv()
        gather.finish()
        near.finish()
        cot_over.finish()
        for copy in sent:
            copy.wait_send()
        settle("uegp")
        for copy in hidden_copies.values():
            copy.wait()

    dma = pltpu.SemaphoreType.DMA
    total = ring * slots
    most = max(len(batch) for batch in batches) * slots
    hbm = pl.BlockSpec(memory_space=pl.ANY)
    vmem = pl.BlockSpec(memory_space=pltpu.VMEM)

    def low(*shape):
        return jax.ShapeDtypeStruct(shape, BF)

    def keep(*shape):
        return pltpu.VMEM(shape, BF)

    return pl.pallas_call(
        kernel,
        out_shape=[
            low(ep_count, rows, width),
            low(2, total, width),
            low(2, total, width),
            low(2, total, hidden_width),
            low(2, total, hidden_width),
            low(2, total, hidden_width),
            low(ep_count, rows, width),
            low(ep_count, rows, width),
            low(ring, rows, width),
            jax.ShapeDtypeStruct((rows, width), F32),
            jax.ShapeDtypeStruct((ep_count, 8, rows), F32),
            low(ep_count, rows, width),
        ],
        in_specs=[hbm, hbm, hbm, vmem, vmem, hbm, hbm, hbm],
        out_specs=[hbm] * 9 + [vmem, hbm, hbm],
        scratch_shapes=Gather.scratch(ep_count)
        + Gather.scratch(ep_count)
        + [dma((ring,))] * 4
        + Crossing.scratch(ep_count)
        + [keep(*gate_w.shape), keep(*up_w.shape), keep(*down_w.shape), keep(2, 2, rows, width), keep(4, 2, rows, width), keep(ep_count, rows, width)]
        + [keep(most, width), keep(most, width), keep(total, hidden_width)]
        + [keep(most, hidden_width)] * 2
        + [keep(total, width), keep(most, width)]
        + [pltpu.VMEM((total, 1), F32), pltpu.VMEM((total, 1), F32), pltpu.VMEM((ring, 2, 8, rows), F32)]
        + [keep(2, 2, rows, width), keep(2, ring, slots, pair)]
        + RingSum.scratch(ep_count, rows, width)
        + [dma((ring, 2)), dma((ring, 2)), dma]
        + [dma((3 + len(batches),)), dma((2,)), dma((4,)), dma((4,)), dma((2,))],
        compiler_params=pltpu.CompilerParams(
            collective_id=collective_id, has_side_effects=True, vmem_limit_bytes=62 << 20
        ),
        name=name,
    )(block, cot_own, cot_other, mine, router, gate_w, up_w, down_w)


class RingSum:
    def __init__(self, here, term, joint, buffers, sems, more=None):
        self.here, self.term, self.joint, self.more = here, term, joint, more
        self.first, self.landed, self.stage = buffers
        self.side_send, self.side_recv, self.ring_send, self.ring_recv, self.stage_sem = sems
        self.far = here.ring // 2
        self.offsets = ring_offsets(here.ring)
        self.part_rows = self.stage.shape[3]
        self.waited, self.copies = set(), []

    @staticmethod
    def scratch(ep_count, rows, width, summands=2, dtype=BF):
        ring, far = ep_count // 2, ep_count // 4
        dma = pltpu.SemaphoreType.DMA
        shapes = [(2, rows, width), (2, far, rows, width), (2, 2, summands, rows // 2, width)]
        buffers = [pltpu.VMEM(shape, dtype) for shape in shapes]
        return buffers + [dma((ring,)), dma((ring,)), dma((2, far, 2)), dma((2, far, 2)), dma((2, 2, summands))]

    def hops(self, way, part):
        return self.far if way == part else self.far - 1

    def rows(self, part):
        return pl.ds(part * self.part_rows, self.part_rows)

    def distance(self, way, part, step):
        distance = max(self.hops(way, part) - step, 0)
        return distance if way == 0 else -distance

    def slot(self, way, part, step):
        offset = self.distance(way, part, step)
        return self.offsets.index(self.far if offset == -self.far else offset)

    def loads(self, way, part, step):
        index = self.here.chip(self.distance(way, part, step))
        sources = [self.term(index), self.joint.at[self.slot(way, part, step)]]
        if self.more is not None:
            sources.append(self.more(index))
        return [
            pltpu.make_async_copy(
                source.at[self.rows(part)], self.stage.at[way, part, i], self.stage_sem.at[way, part, i]
            )
            for i, source in enumerate(sources)
        ]

    def load(self, way, part, step):
        slot = self.slot(way, part, step)
        if slot not in self.waited:
            self.waited.add(slot)
            self.side_copy(slot).wait_recv()
        for copy in self.loads(way, part, step):
            copy.start()

    def side_copy(self, slot):
        here = self.here
        index = here.index(here.at(self.offsets[slot]), 1 - here.core)
        return remote(
            self.term(index), self.joint.at[slot], self.side_send.at[slot], self.side_recv.at[slot], here.sibling()
        )

    def start(self):
        self.trade()
        self.begin()

    def trade(self):
        for slot in reversed(range(len(self.offsets))):
            copy = self.side_copy(slot)
            copy.start()
            self.copies.append(copy)

    def begin(self):
        for part in range(2):
            for way in range(2):
                self.load(way, part, 0)

    def value(self, way, part, step):
        for copy in self.loads(way, part, step):
            copy.wait()
        return sum(self.stage[way, part, i].astype(F32) for i in range(self.stage.shape[2]))

    def ring_copy(self, way, step, part):
        at = self.rows(part)
        src = self.first.at[way, at] if step == 0 else self.landed.at[way, step - 1, at]
        return remote(
            src,
            self.landed.at[way, step, at],
            self.ring_send.at[way, step, part],
            self.ring_recv.at[way, step, part],
            self.here.right() if way == 0 else self.here.left(),
        )

    def step(self, step):
        for part in range(2):
            for way in range(2):
                if step < self.hops(way, part):
                    value = self.value(way, part, step)
                    at = self.rows(part)
                    if step == 0:
                        self.first[way, at] = value.astype(self.first.dtype)
                    else:
                        self.ring_copy(way, step - 1, part).wait_recv()
                        value = value + self.landed[way, step - 1, at].astype(F32)
                        self.landed[way, step - 1, at] = value.astype(self.landed.dtype)
                    copy = self.ring_copy(way, step, part)
                    copy.start()
                    self.copies.append(copy)
                    if step + 1 < self.hops(way, part) or way == 0:
                        self.load(way, part, step + 1)

    def finish(self, put):
        for part in range(2):
            value = self.value(0, part, self.hops(0, part))
            at = self.rows(part)
            for way in range(2):
                count = self.hops(way, part)
                self.ring_copy(way, count - 1, part).wait_recv()
                value = value + self.landed[way, count - 1, at].astype(F32)
            put(at, value)
        for copy in self.copies:
            copy.wait_send()


def rolled(values):
    return pltpu.roll(values, HEAD_DIM // 2, 1)


def turns(table):
    other = rolled(table)
    first = lax.broadcasted_iota(jnp.int32, table.shape, 1) < HEAD_DIM // 2
    return jnp.where(first, table, other), jnp.where(first, -other, table)


def as_rows(columns, count):
    shape = (columns[0].shape[0], 128)
    lane = lax.broadcasted_iota(jnp.int32, shape, 1)
    packed = jnp.zeros(shape, F32)
    for i, column in enumerate(columns):
        packed = jnp.where(lane == i, column, packed)
    return packed.T[:count]


def as_columns(tile):
    padded = jnp.concatenate([tile, jnp.zeros((128 - tile.shape[0], tile.shape[1]), F32)], axis=0)
    return padded.T


BACKWARD_STEPS = {
    "sent": (("x", 0), ("x", 1), ("t", 1)),
    "attended": (("e", 2),),
    "scores": (("e", 3),),
    "dots": (("t", 2),),
    "columns": (("t", 1),),
    "columns_2": (("t", 1),),
    "swap": (
        ("d", 1),
        ("t", 1),
        ("g", 0),
        ("t", 1),
        ("d", 2),
        ("g", 1),
        ("t", 2),
        ("d", 3),
        ("g", 2),
        ("t", 2),
        ("g", 3),
        ("t", 1),
    ),
}


def backward(
    ep_count, d_proj, att_loc, w_out, head, columns, table, gains, w_all, normed, result_terms, tiles, expert_rows, name, collective_id
):
    rows = d_proj.shape[0]
    query, key, value, norm_q, norm_k = head
    tokens, cols = query.shape
    width = w_all.shape[0]
    prompt_len = tokens // 2
    units, grads, hidden, gate_grads, up_grads = expert_rows
    depth_rows, hidden_width = hidden.shape
    ring = ep_count // 2
    far = ring // 2
    out_rows = w_out.shape[1]
    slab, wide, block = 256, 1024, 256
    segment = 512
    pieces = tokens // segment
    scale = HEAD_DIM ** (-0.5)
    dma = pltpu.SemaphoreType.DMA

    def kernel(*refs):
        ins, outs, scratch = split(refs, 20, 16, len(refs) - 36)
        proj_ref, gain_ref = ins[0], ins[9]
        held = ins[1:9] + ins[10:11]
        full_ref, normed_ref, eo_ref, tile_ref, u_ref, e_ref, h_ref, g_ref, p_ref = ins[11:]
        dn_out, go_out, eo_out, gw_out, tile_out, late_out, gate_out, up_out, down_out = outs[:9]
        dn_terms, dn_joint, go_joint, eo_joint, go_mine, go_theirs, x_in = outs[9:]
        dn_s, go_s, eo_s, go_more, gw_s, tile_s, late_s, work_s, att_s, dots_s, own_s, held_s = split(
            scratch, 8, 8, 8, 5, 6, 3, 4, 6, 9, 5, 5, 10
        )
        att_ref, q_ref, k_ref, v_ref, nq_ref, nk_ref, col_ref, table_ref, w_ref = held_s[:9]
        held_copies = [
            pltpu.make_async_copy(src, dst, held_s[9].at[i]) for i, (src, dst) in enumerate(zip(held, held_s[:9]))
        ]
        for copy in held_copies:
            copy.start()
        here = Place(ep_count)
        greet(plane_devices(here) + far_devices(here))
        result = RingSum(here, lambda e: eo_ref.at[e], eo_joint, eo_s[:3], eo_s[3:])
        result.start()
        result.step(0)
        sent = []

        def start(copy):
            copy.start()
            sent.append(copy)

        (att_v, tile_v, dq_s, dk_s, dv_s, lin_s), att_sems = att_s[:6], att_s[6:]
        slab_v, slab_sem, term_v, term_sem, gw_v = own_s

        def full_copy(number):
            return pltpu.make_async_copy(
                full_ref.at[pl.ds(2 * number, 2)], term_v.at[number % 2], term_sem.at[number % 2]
            )

        for number in range(2):
            full_copy(number).start()
        for number in range(ring):
            full_copy(number).wait()
            both = mm_nt(proj_ref[...], term_v[number % 2].reshape(2 * cols, width)).astype(BF)
            for i in range(2):
                tile_v[2 * number + i] = both[:, i * cols : (i + 1) * cols]
            if number + 2 < ring:
                full_copy(number + 2).start()
        attended = Exchange(here, lambda e: tile_v.at[e], lambda e: att_v.at[e], att_sems)
        attended.start()
        result.step(1)

        me = here.grp * ep_count + here.ep

        def tile_copy(turn, offset, source, src, dst, sems):
            group = (here.grp + turn) % 2
            target = (here.ep + offset) % ep_count
            slot = turn * ep_count + offset
            return remote(src(group * ep_count + target), dst.at[source], sems[0].at[slot], sems[1].at[slot], (group, target))

        others = [(turn, offset) for turn in range(2) for offset in range(ep_count) if turn + offset > 0]

        def send_tiles(src, dst, sems):
            own = pltpu.make_async_copy(src(me), dst.at[me], sems[2])
            own.start()
            for turn, offset in others:
                start(tile_copy(turn, offset, me, src, dst, sems))
            return own

        def take_tiles(own, src, dst, sems):
            own.wait()
            for turn, offset in others:
                source = ((here.grp + turn) % 2) * ep_count + (here.ep + ep_count - offset) % ep_count
                tile_copy(turn, offset, source, src, dst, sems).wait_recv()

        x_own, x_joint, go_own_sem, go_send, go_recv = go_more
        go_load = pltpu.make_async_copy(go_theirs.at[:, here.core], x_own, go_own_sem)
        go_side = remote(go_theirs.at[:, 1 - here.core], x_joint, go_send.at[0], go_recv.at[0], here.sibling())

        def go_over(part):
            at = pl.ds(part * (ring // 2), ring // 2)
            return remote(x_own.at[at], x_in.at[at], go_send.at[1 + part], go_recv.at[1 + part], here.across())

        output = RingSum(
            here, lambda e: go_mine.at[e // 2, e % 2], go_joint, go_s[:3], go_s[3:], lambda e: x_in.at[e // 2]
        )

        left, right, sheet, left_sem, right_sem, sheet_sem = work_s
        units = [(u_ref, i) for i in range(width // slab)] + [(h_ref, i) for i in range(hidden_width // slab)]
        turning = width // slab
        done = []

        def right_copies(late):
            if late:
                return [pltpu.make_async_copy(e_ref, right, right_sem.at[0])]
            return [
                pltpu.make_async_copy(src, right.at[:, pl.ds(i * hidden_width, hidden_width)], right_sem.at[i])
                for i, src in enumerate((g_ref, p_ref))
            ]

        def left_copy(number):
            src, i = units[number]
            return pltpu.make_async_copy(src.at[:, pl.ds(i * slab, slab)], left.at[number % 2], left_sem.at[number % 2])

        def sheet_copies(number):
            src, i = units[number]
            at = pl.ds(i * slab, slab)
            if number >= turning:
                return [pltpu.make_async_copy(sheet.at[number % 2], down_out.at[at], sheet_sem.at[number % 2, 0, 0])]
            return [
                pltpu.make_async_copy(
                    sheet.at[number % 2, :, pl.ds(j * hidden_width, hidden_width)], out.at[at], sheet_sem.at[number % 2, 0, j]
                )
                for j, out in enumerate((gate_out, up_out))
            ]

        def unit(number):
            if number in (0, turning):
                for copy in right_copies(number > 0):
                    copy.wait()
            left_copy(number).wait()
            if number + 1 < len(units):
                left_copy(number + 1).start()
            if number >= 2:
                for copy in sheet_copies(number - 2):
                    copy.wait()

            def run(i, carry):
                at = pl.ds(pl.multiple_of(i * wide, wide), wide)
                sheet[number % 2, :, at] = mm_tn(left[number % 2], right[:, at]).astype(sheet.dtype)
                return carry

            lax.fori_loop(0, width // wide, run, 0)
            for copy in sheet_copies(number):
                copy.start()
            if number + 1 == turning:
                for copy in right_copies(True):
                    copy.start()

        def tasks(count):
            for _ in range(min(count, len(units) - len(done))):
                unit(len(done))
                done.append(True)

        for copy in right_copies(False):
            copy.start()
        left_copy(0).start()
        term_copies = []

        def poll(point):
            for kind, number in BACKWARD_STEPS.get(point, ()):
                if kind == "t":
                    tasks(number)
                elif kind == "e":
                    result.step(number)
                elif kind == "d":
                    normed_sum.step(number)
                elif kind == "g":
                    if number == 0:
                        for half in range(2):
                            go_over(half).wait_recv()
                        output.begin()
                    output.step(number)
                elif kind == "x":
                    start(go_over(number))

        for copy in held_copies:
            copy.wait()
        for number in range(ring):
            first = lax.rem((1 - here.grp) * ring + 2 * number, 2 * ring) * cols
            buffer, chip = number % 2, 2 * number % ring
            terms = go_theirs if number < ring // 2 else go_mine
            if number >= 2:
                for copy in term_copies.pop(0):
                    copy.wait()
            if number == ring // 2 + 1:
                go_load.start()
                start(go_side)
            turned = mm_tn(att_ref[:, pl.ds(pl.multiple_of(first, cols), 2 * cols)], proj_ref[...])
            sheet[buffer] = turned.astype(BF)
            copies = [
                pltpu.make_async_copy(
                    sheet.at[buffer, pl.ds((2 * i + j) * out_rows, out_rows)],
                    terms.at[chip + i, j],
                    sheet_sem.at[buffer, i, j],
                )
                for i in range(2)
                for j in range(2)
            ]
            for copy in copies:
                copy.start()
            term_copies.append(copies)
        for copies in term_copies:
            for copy in copies:
                copy.wait()
        go_load.wait()
        go_side.wait_recv()
        for chip in range(ring):
            x_own[chip] = (x_own[chip].astype(F32) + x_joint[chip].astype(F32)).astype(BF)
        poll("sent")
        attended.arrive()
        poll("attended")

        dk_s[...] = jnp.zeros_like(dk_s)
        dv_s[...] = jnp.zeros_like(dv_s)
        per = block // rows
        line = lax.broadcasted_iota(jnp.int32, (block, block), 0)
        column_at = lax.broadcasted_iota(jnp.int32, (block, block), 1)
        causal = line >= column_at
        same = causal & (line // rows == column_at // rows)

        def grads_of(first, spans):
            at = pl.ds(first, block)
            q = q_ref[at]
            g = att_v[pl.ds(first // rows, per)].reshape(block, cols)
            log = col_ref[at, 0:1]
            kept = []
            inner = jnp.zeros((block, 1), F32)
            for begin, length, mask in spans:
                keys = pl.ds(begin, length)
                weight = jnp.exp(mm_nt(q, k_ref[keys]) * scale - log)
                if mask is not None:
                    weight = jnp.where(mask, weight, 0.0)
                d_weight = mm_nt(g, v_ref[keys])
                inner = inner + jnp.sum(weight * d_weight, axis=-1, keepdims=True)
                kept.append((keys, weight, d_weight))
            dq = jnp.zeros((block, cols), F32)
            for keys, weight, d_weight in kept:
                d_score = (weight * (d_weight - inner)).astype(BF)
                dq = dq + mm(d_score, k_ref[keys])
                dk_s[keys] += mm_tn(d_score, q)
                dv_s[keys] += mm_tn(weight.astype(BF), g)
            dq_s[at] = dq * scale

        for number in range(prompt_len // block):
            spans = [(0, number * block, None)] if number else []
            grads_of(number * block, spans + [(number * block, block, causal)])

        def later(number, carry):
            first = pl.multiple_of(prompt_len + number * block, block)
            grads_of(first, [(0, prompt_len, None), (first, block, same)])
            return carry

        poll("prompt")
        lax.fori_loop(0, (tokens - prompt_len) // block, later, 0)
        poll("scores")

        dots_v, dots_all, dots_sems = dots_s[0], dots_s[1], dots_s[2:]
        late_v, late_sems = late_s[0], late_s[1:]
        gain_sums = [jnp.zeros((1, cols), F32), jnp.zeros((1, cols), F32)]
        stats = []
        for piece in range(pieces):
            at = pl.ds(piece * segment, segment)
            cosine, sine = turns(table_ref[at])
            for kind, (ref, n_ref, factor) in enumerate(((dq_s, nq_ref, 1.0), (dk_s, nk_ref, scale))):
                turned = ref[at] * factor
                turned = turned * cosine - rolled(turned) * sine
                gain_sums[kind] = gain_sums[kind] + jnp.sum(turned * n_ref[at].astype(F32), axis=0, keepdims=True)
                turned = turned * gain_ref[kind : kind + 1]
                ref[at] = turned
                stats.append(jnp.sum(turned * n_ref[at].astype(F32), axis=-1, keepdims=True))
        dots_v[...] = as_rows(stats, dots_v.shape[0])
        spread_dots = Exchange(here, lambda e: dots_v, lambda e: dots_all.at[e], dots_sems)
        spread_dots.start()
        gain_tile = jnp.concatenate(gain_sums + [jnp.zeros((6, cols), F32)], axis=0)
        for piece in range(pieces):
            at = pl.ds(piece * segment, segment)
            lin_s[at, 2 * cols : 3 * cols] = dv_s[at].astype(BF)
        slabs = width // slab
        half = slabs // 2

        def slab_at(turn):
            return lax.rem((1 - here.grp) * half + turn, slabs) * slab

        def slab_copy(turn):
            at = pl.ds(pl.multiple_of(slab_at(turn), slab), slab)
            return pltpu.make_async_copy(normed_ref.at[:, at], slab_v.at[turn % 2], slab_sem.at[turn % 2])

        slab_copy(0).start()
        slab_copy(1).start()
        poll("dots")
        spread_dots.arrive()
        total = dots_all[0]
        for e in range(1, ep_count):
            total = total + dots_all[e]
        total = as_columns(total / width)
        for piece in range(pieces):
            at = pl.ds(piece * segment, segment)
            for kind, (ref, n_ref) in enumerate(((dq_s, nq_ref), (dk_s, nk_ref))):
                lane = 2 * piece + kind
                grad = col_ref[at, 1 + kind : 2 + kind] * (ref[at] - n_ref[at].astype(F32) * total[:, lane : lane + 1])
                lin_s[at, kind * cols : (kind + 1) * cols] = grad.astype(BF)

        (gw_x, gw_x_send, gw_x_recv), gw_swap = gw_s[:3], gw_s[3:]
        per_slab = slab // out_rows
        gain_lines = []

        def projections(turn):
            slab_copy(turn).wait()
            first = slab_at(turn)
            grad = mm_tn(slab_v[turn % 2], lin_s[...])
            if turn + 2 < slabs:
                slab_copy(turn + 2).start()
            weight = w_ref[pl.ds(pl.multiple_of(first, slab), slab)].astype(F32)
            line = as_rows([jnp.sum(grad * weight, axis=-1, keepdims=True)], 8)[0:1]
            owner = first // out_rows
            for kind in range(3):
                part = grad[:, kind * cols : (kind + 1) * cols].astype(BF)
                gw_v[pl.ds(owner, per_slab), kind] = part.reshape(per_slab, out_rows, cols)
            for i in range(per_slab):
                part = line[:, i * out_rows : (i + 1) * out_rows]
                part = jnp.concatenate([part, jnp.zeros((1, cols - out_rows), F32)], axis=1)
                late_v[owner + i] = jnp.concatenate([gain_tile[0:2], part, gain_tile[3:]], axis=0)
            return owner

        def over_copy(turn, owner):
            at = pl.ds(owner - (1 - here.grp) * ep_count, per_slab)
            return remote(gw_v.at[pl.ds(owner, per_slab)], gw_x.at[at], gw_x_send.at[turn], gw_x_recv.at[turn], here.across())

        for turn in range(half):
            start(over_copy(turn, projections(turn)))
        poll("columns")
        output.trade()

        normed_sum = RingSum(here, lambda e: dn_terms.at[e], dn_joint, dn_s[:3], dn_s[3:])
        offsets = ring_offsets(ring)
        stores = {}
        for turn, slot in enumerate(reversed(range(ring))):
            chip = here.index(here.at(offsets[slot]), 0) // 2
            if turn >= 2:
                stores.pop(turn - 2).wait()
            at = pl.ds(pl.multiple_of(chip * 2 * rows, 2 * rows), 2 * rows)

            def fill(i, carry, at=at, turn=turn):
                wide_at = pl.ds(pl.multiple_of(i * 1024, 1024), 1024)
                part = mm_nt(lin_s[at], w_ref[wide_at]).astype(BF)
                term_v[turn % 2, :, :, wide_at] = part.reshape(2, rows, 1024)
                return carry

            lax.fori_loop(0, width // 1024, fill, 0)
            stores[turn] = pltpu.make_async_copy(
                term_v.at[turn % 2], dn_terms.at[pl.ds(chip * 2, 2)], term_sem.at[turn % 2]
            )
            stores[turn].start()
        for turn in sorted(stores):
            stores[turn].wait()
        normed_sum.start()
        normed_sum.step(0)
        own_tiles = send_tiles(lambda i: tile_ref.at[i], tile_out, tile_s)
        poll("terms")
        for turn in range(half, slabs):
            projections(turn)
        own_late = send_tiles(lambda i: late_v.at[i], late_out, late_sems)
        poll("columns_2")
        for turn in range(half):
            over_copy(turn, (1 - here.grp) * ep_count + turn * per_slab).wait_recv()
        for e in range(ep_count):
            gw_x[e] = (gw_v[here.grp * ep_count + e].astype(F32) + gw_x[e].astype(F32)).astype(BF)
        swap = Exchange(here, lambda e: gw_x.at[e], lambda e: gw_out.at[:, :, pl.ds(pl.multiple_of(e * cols, cols), cols)], gw_swap)
        swap.start()
        poll("swap")

        def put(out):
            def store(at, value):
                out[at] = value

            return store

        normed_sum.finish(put(dn_out))
        tasks(len(units))
        for number in range(len(units) - 2, len(units)):
            for copy in sheet_copies(number):
                copy.wait()
        result.finish(put(eo_out))
        output.finish(put(go_out))
        take_tiles(own_tiles, lambda i: tile_ref.at[i], tile_out, tile_s)
        take_tiles(own_late, lambda i: late_v.at[i], late_out, late_sems)
        attended.finish()
        spread_dots.finish()
        swap.arrive()
        swap.finish()
        for copy in sent:
            copy.wait_send()

    hbm = pl.BlockSpec(memory_space=pl.ANY)
    vmem = pl.BlockSpec(memory_space=pltpu.VMEM)
    group_rows = 2 * ep_count

    def keep(*shape):
        return pltpu.VMEM(shape, BF)

    def wide_keep(*shape):
        return pltpu.VMEM(shape, F32)

    return pl.pallas_call(
        kernel,
        out_shape=[
            jax.ShapeDtypeStruct((rows, width), F32),
            jax.ShapeDtypeStruct((out_rows, width), F32),
            jax.ShapeDtypeStruct((rows, width), F32),
            jax.ShapeDtypeStruct((3, out_rows, width), BF),
            jax.ShapeDtypeStruct(tiles.shape, F32),
            jax.ShapeDtypeStruct((group_rows, 8, cols), F32),
            jax.ShapeDtypeStruct((width, hidden_width), BF),
            jax.ShapeDtypeStruct((width, hidden_width), BF),
            jax.ShapeDtypeStruct((hidden_width, width), BF),
            jax.ShapeDtypeStruct((ep_count, rows, width), BF),
            jax.ShapeDtypeStruct((ring, rows, width), BF),
            jax.ShapeDtypeStruct((ring, out_rows, width), BF),
            jax.ShapeDtypeStruct((ring, rows, width), BF),
            jax.ShapeDtypeStruct((ring, 2, out_rows, width), BF),
            jax.ShapeDtypeStruct((ring, 2, out_rows, width), BF),
            jax.ShapeDtypeStruct((ring, out_rows, width), BF),
        ],
        in_specs=[vmem] + [hbm] * 8 + [vmem] + [hbm] * 10,
        out_specs=[vmem] * 3 + [hbm] * 13,
        scratch_shapes=RingSum.scratch(ep_count, rows, width)
        + RingSum.scratch(ep_count, out_rows, width, 3)
        + RingSum.scratch(ep_count, rows, width)
        + [keep(ring, out_rows, width)] * 2
        + [dma, dma((3,)), dma((3,))]
        + [keep(ep_count, 3, out_rows, cols)]
        + [dma((ring,)), dma((ring,))]
        + Exchange.scratch(ep_count)
        + [dma((group_rows,)), dma((group_rows,)), dma]
        + [wide_keep(group_rows, 8, cols), dma((group_rows,)), dma((group_rows,)), dma]
        + [keep(2, depth_rows, slab), keep(depth_rows, width), keep(2, slab, width), dma((2,)), dma((2,)), dma((2, 2, 2))]
        + [keep(ep_count, rows, cols)] * 2
        + [wide_keep(tokens, cols)] * 3
        + [keep(tokens, 3 * cols)]
        + Exchange.scratch(ep_count)
        + [wide_keep(8, segment), wide_keep(ep_count, 8, segment)]
        + Exchange.scratch(ep_count)
        + [keep(2, tokens, slab), dma((2,)), keep(2, 2, rows, width), dma((2,))]
        + [keep(group_rows, 3, out_rows, cols)]
        + [keep(rows, width)]
        + [keep(tokens, cols)] * 5
        + [wide_keep(tokens, cols)] * 2
        + [keep(width, 3 * cols), dma((9,))],
        compiler_params=pltpu.CompilerParams(
            collective_id=collective_id, has_side_effects=True, vmem_limit_bytes=63 << 20
        ),
        name=name,
    )(
        d_proj,
        att_loc,
        query,
        key,
        value,
        norm_q,
        norm_k,
        columns,
        table,
        gains,
        w_all,
        w_out.reshape(ep_count, cols, width),
        normed,
        result_terms,
        tiles,
        *expert_rows,
    )


class Crossing:
    def __init__(self, here, out, into, sems):
        self.here, self.out, self.into = here, out, into
        self.across_send, self.across_recv, self.hand_send, self.hand_recv = sems
        self.offsets = ring_offsets(here.ring)
        self.copies = []

    @staticmethod
    def scratch(ep_count):
        return [pltpu.SemaphoreType.DMA((ep_count // 2,))] * 4

    def go(self, copy):
        copy.start()
        self.copies.append(copy)

    def across(self, slot, src, dst):
        return remote(src, dst, self.across_send.at[slot], self.across_recv.at[slot], self.here.across())

    def hand(self, slot, core):
        block = self.into(self.here.index(self.here.at(self.offsets[slot]), core))
        return remote(block, block, self.hand_send.at[slot], self.hand_recv.at[slot], self.here.sibling())

    def send(self, slot, src):
        self.go(self.across(slot, src, self.out(self.here.chip(self.offsets[slot]))))

    def take(self, slot):
        block = self.into(self.here.chip(self.offsets[slot]))
        self.across(slot, block, block).wait_recv()
        self.go(self.hand(slot, self.here.core))

    def settle(self, slot):
        self.hand(slot, 1 - self.here.core).wait_recv()

    def finish(self):
        for copy in self.copies:
            copy.wait_send()


ATTENTION_STEPS = {
    ("x", 0): (("f", -1),),
    ("x", 1): (("f", 0),),
    ("x", 2): (("f", 1),),
    ("x", 3): (("f", 2), ("c", -1)),
    ("x", 4): (("f", 3),),
    "dots": (("c", 0),),
    "prompt": (("c", 1),),
    "sent": (("c", 2), ("c", 3)),
}


def attention(ep_count, x, weights, small, w_out, cot, table, early, name, collective_id):
    rows, width = x.shape
    kinds, depth, _ = weights.shape
    cols = width // ep_count
    tokens = rows * ep_count
    prompt_len = tokens // 2
    ring = ep_count // 2
    far = ring // 2
    offsets = ring_offsets(ring)
    batches = [[0]] + [[2 * k - 1, 2 * k] for k in range(1, far)] + [[ring - 1]]
    gain_row = depth * ep_count // 128
    block, segment, chunk = 256, 512, 64
    pieces = tokens // segment
    scale = HEAD_DIM ** (-0.5)
    dma = pltpu.SemaphoreType.DMA

    def kernel(*refs):
        ins, outs, scratch = split(refs, 6, 14, len(refs) - 20)
        x_ref, weights_ref, small_ref, w_ref, cot_ref, table_ref = ins
        normed_out, w_final, s_out, full_out, cot_out, cot_other = outs[:6]
        finals, att_out, x_land = outs[6:12], outs[12], outs[13]
        x_s, w_s, s_s, cross, w_ring, cot_ring, w_cross, cot_cross, bufs, loads, dots_s, att_s, held = split(
            scratch, 5, 3, 2, 3, 5, 5, 4, 4, 5, 2, 5, 4, 8
        )
        w_all, q_out, k_out, v_out, nq_out, nk_out, col_out, held_sem = held
        rows_v, normed_v, columns_v, gain_v, lin_v = bufs
        rows_sem, normed_sem = loads
        here = Place(ep_count)
        greet(plane_devices(here) + [here.across()])

        cross_own, cross_send, cross_recv = cross
        first = pltpu.make_async_copy(small_ref, s_out.at[here.grp, here.ep], cross_own)
        first.start()

        def small_over(group):
            return remote(
                small_ref, s_out.at[group, here.ep], cross_send.at[0], cross_recv.at[0], here.across()
            )

        small_over(here.grp).start()
        gather = Gather(here, x_ref, x_land, x_s)
        gather.start()
        columns_of = Exchange(
            here,
            lambda e: weights_ref.at[:, :, pl.ds(pl.multiple_of(e * cols, cols), cols)],
            lambda e: columns_v.at[here.grp, e],
            w_s,
        )
        columns_of.start()
        full = Gather(here, w_ref, full_out.at[here.grp], w_ring)
        full_over = Crossing(
            here, lambda e: full_out.at[here.grp, e], lambda e: full_out.at[1 - here.grp, e], w_cross
        )
        cots = Gather(here, cot_ref, cot_out, cot_ring)
        cots_over = Crossing(here, lambda e: cot_other.at[e], lambda e: cot_other.at[e], cot_cross)
        full_over.send(0, w_ref)
        cots_over.send(0, cot_ref)

        first.wait()
        small_over(1 - here.grp).wait_recv()
        small_over(here.grp).wait_send()
        small_copies = []
        for offset in range(1, here.count):
            mine = s_out.at[:, here.ep]
            copy = remote(mine, mine, s_s[0].at[offset], s_s[1].at[offset], here.peer(offset))
            copy.start()
            small_copies.append(copy)
        for offset in range(1, here.count):
            source = s_out.at[:, here.peer(-offset)[1]]
            remote(source, source, s_s[0].at[offset], s_s[1].at[offset], here.peer(offset)).wait_recv()

        def gains(row, half, owner):
            lines = []
            for i in range(2):
                tile = s_out[(owner + i) // ep_count, (owner + i) % ep_count, pl.ds(0, 16)].astype(F32)
                lines.append(tile[row : row + 1, half * depth : (half + 1) * depth])
            return jnp.concatenate(lines, axis=1)

        for i in range(width // 128):
            gain_v[:, i * 128 : (i + 1) * 128] = gains(gain_row, 0, 2 * i)
        gain_q, gain_k = gains(gain_row, 1, 2 * here.ep), gains(gain_row + 1, 0, 2 * here.ep)

        def chip_of(slot):
            return here.index(here.at(offsets[slot]), 0) // 2

        stores = []

        def leave(src, dst, number):
            stores.append(pltpu.make_async_copy(src, dst, held_sem.at[number]))
            stores[-1].start()


        def norm(batch):
            loaded = []
            for i, slot in enumerate(batch):
                loaded.append(pltpu.make_async_copy(x_land.at[pl.ds(2 * chip_of(slot), 2)], rows_v.at[i], rows_sem.at[i]))
                loaded[-1].start()
            for i, slot in enumerate(batch):
                loaded[i].wait()
                chip = chip_of(slot)
                for core in range(2):

                    def run(j, carry, i=i, core=core, chip=chip):
                        at = pl.ds(pl.multiple_of(j * chunk, chunk), chunk)
                        wide = rows_v[i, core, at].astype(F32)
                        r = lax.rsqrt(jnp.mean(wide * wide, axis=-1, keepdims=True) + eps)
                        normed_v[2 * chip + core, at] = (wide * r * gain_v[...]).astype(BF)
                        return carry

                    lax.fori_loop(0, rows // chunk, run, 0)
                at = pl.ds(2 * chip, 2)
                stores.append(pltpu.make_async_copy(normed_v.at[at], normed_out.at[at], normed_sem.at[slot]))
                stores[-1].start()

        def project(batch):
            for slot in batch:
                chip = chip_of(slot)
                lin = mm(normed_v[pl.ds(2 * chip, 2)].reshape(2 * rows, width), w_all[...])
                at = pl.ds(pl.multiple_of(chip * 2 * rows, 2 * rows), 2 * rows)
                lin_v[0, at] = lin[:, :cols]
                lin_v[1, at] = lin[:, cols : 2 * cols]
                v_out[at] = lin[:, 2 * cols :].astype(BF)

        def poll(point):
            for kind, step in ATTENTION_STEPS.get(point, ()):
                ring_gather, crossing, count = (full, full_over, ring) if kind == "f" else (cots, cots_over, early)
                if step < 0:
                    ring_gather.start()
                    continue
                ring_gather.step(step)
                for slot in batches[step + 1]:
                    if slot < count:
                        crossing.send(slot, ring_gather.dst.at[here.chip(offsets[slot])])

        over = remote(columns_v.at[here.grp], columns_v.at[here.grp], cross_send.at[1], cross_recv.at[1], here.across())
        gather.settle()
        for number, batch in enumerate(batches):
            gather.side(number - 1)
            norm(batch)
            if number < far:
                gather.step(number)
            poll(("x", number))
            if number == 1:
                columns_of.arrive()
                over.start()
            if number == far - 1:
                remote(
                    columns_v.at[1 - here.grp],
                    columns_v.at[1 - here.grp],
                    cross_send.at[1],
                    cross_recv.at[1],
                    here.across(),
                ).wait_recv()
                for owner in range(2 * ep_count):
                    for kind in range(kinds):
                        w_all[owner * depth : (owner + 1) * depth, kind * cols : (kind + 1) * cols] = columns_v[
                            owner // ep_count, owner % ep_count, kind
                        ]
                leave(w_all, w_final, 0)
                for earlier in batches[:number]:
                    project(earlier)
            if number >= far - 1:
                project(batch)

        dots_v, dots_all, dots_sems = dots_s[0], dots_s[1], dots_s[2:]
        stats = []
        for piece in range(pieces):
            at = pl.ds(piece * segment, segment)
            for kind in range(2):
                lin = lin_v[kind, at]
                stats.append(jnp.sum(lin * lin, axis=-1, keepdims=True))
        dots_v[...] = as_rows(stats, dots_v.shape[0])
        spread_dots = Exchange(here, lambda e: dots_v, lambda e: dots_all.at[e], dots_sems)
        spread_dots.start()
        poll("dots")
        spread_dots.arrive()
        total = dots_all[0]
        for e in range(1, ep_count):
            total = total + dots_all[e]
        r_all = as_columns(lax.rsqrt(total / width + eps))
        lane = lax.broadcasted_iota(jnp.int32, (segment, 128), 1)
        for piece in range(pieces):
            at = pl.ds(piece * segment, segment)
            kept = jnp.zeros((segment, 128), F32)
            cosine, sine = turns(table_ref[at])
            for kind, (gain, n_out, out) in enumerate(((gain_q, nq_out, q_out), (gain_k, nk_out, k_out))):
                r = r_all[:, 2 * piece + kind : 2 * piece + kind + 1]
                n = lin_v[kind, at] * r
                n_out[at] = n.astype(BF)
                n = n * gain
                out[at] = (n * cosine + rolled(n) * sine).astype(BF)
                kept = jnp.where(lane == 1 + kind, r, kept)
            col_out[at] = kept

        for number, src in enumerate((q_out, k_out, v_out, nq_out, nk_out)):
            leave(src, finals[number], 1 + number)
        poll("turned")
        att_v, att_sems = att_s[0], att_s[1:]
        per = block // rows
        line = lax.broadcasted_iota(jnp.int32, (block, block), 0)
        column_at = lax.broadcasted_iota(jnp.int32, (block, block), 1)
        causal = line >= column_at
        same = causal & (line // rows == column_at // rows)
        block_lane = lax.broadcasted_iota(jnp.int32, (block, 128), 1)

        def attend(first, spans):
            at = pl.ds(first, block)
            q = q_out[at]
            scores = []
            for begin, length, mask in spans:
                score = mm_nt(q, k_out[pl.ds(begin, length)]) * scale
                scores.append(score if mask is None else jnp.where(mask, score, -1e30))
            top = jnp.max(scores[0], axis=-1, keepdims=True)
            for score in scores[1:]:
                top = jnp.maximum(top, jnp.max(score, axis=-1, keepdims=True))
            powers = [jnp.exp(score - top) for score in scores]
            summed = sum(jnp.sum(power, axis=-1, keepdims=True) for power in powers)
            out = jnp.zeros((block, cols), F32)
            for (begin, length, _), power in zip(spans, powers):
                out = out + mm((power / summed).astype(BF), v_out[pl.ds(begin, length)])
            att_v[pl.ds(first // rows, per)] = out.astype(BF).reshape(per, rows, cols)
            col_out[at] = jnp.where(block_lane == 0, top + jnp.log(summed), col_out[at])

        for number in range(prompt_len // block):
            spans = [(0, number * block, None)] if number else []
            attend(number * block, spans + [(number * block, block, causal)])
        poll("prompt")

        def later(number, carry):
            first = pl.multiple_of(prompt_len + number * block, block)
            attend(first, [(0, prompt_len, None), (first, block, same)])
            return carry

        lax.fori_loop(0, (tokens - prompt_len) // block, later, 0)
        attended = Exchange(here, lambda e: att_v.at[e], lambda e: att_out.at[:, pl.ds(pl.multiple_of(e * cols, cols), cols)], att_sems)
        attended.start()
        leave(col_out, finals[5], 6)
        poll("sent")
        attended.arrive()
        for step in range(-1, far):
            full.side(step)
            cots.side(step)
        for slot in range(ring):
            full_over.take(slot)
            if slot < early:
                cots_over.take(slot)
        for slot in range(ring):
            full_over.settle(slot)
            if slot < early:
                cots_over.settle(slot)
        full.settle()
        cots.settle()
        for part in (gather, full, cots, full_over, cots_over, columns_of, spread_dots, attended):
            part.finish()
        over.wait_send()
        for copy in small_copies:
            copy.wait_send()
        for copy in stores:
            copy.wait()

    hbm = pl.BlockSpec(memory_space=pl.ANY)
    vmem = pl.BlockSpec(memory_space=pltpu.VMEM)

    def low(*shape):
        return jax.ShapeDtypeStruct(shape, BF)

    def wide(*shape):
        return jax.ShapeDtypeStruct(shape, F32)

    outs = pl.pallas_call(
        kernel,
        out_shape=[
            low(ep_count, rows, width),
            low(width, kinds * cols),
            low(2, ep_count, *small.shape),
            low(2, ep_count, *w_out.shape),
            low(ep_count, rows, width),
            low(ep_count, rows, width),
            low(tokens, cols),
            low(tokens, cols),
            low(tokens, cols),
            low(tokens, cols),
            low(tokens, cols),
            wide(tokens, 128),
            low(rows, width),
            low(ep_count, rows, width),
        ],
        in_specs=[hbm, hbm, hbm, hbm, hbm, vmem],
        out_specs=[hbm, hbm, vmem] + [hbm] * 11,
        scratch_shapes=Gather.scratch(ep_count)
        + Exchange.scratch(ep_count)
        + [dma((ep_count,)), dma((ep_count,))]
        + [dma, dma((2,)), dma((2,))]
        + Gather.scratch(ep_count)
        + Gather.scratch(ep_count)
        + Crossing.scratch(ep_count)
        + Crossing.scratch(ep_count)
        + [
            pltpu.VMEM((2, 2, rows, width), BF),
            pltpu.VMEM((ep_count, rows, width), BF),
            pltpu.VMEM((2, ep_count, kinds, depth, cols), BF),
            pltpu.VMEM((1, width), F32),
            pltpu.VMEM((2, tokens, cols), F32),
        ]
        + [dma((2,)), dma((ring,))]
        + [pltpu.VMEM((8, segment), F32), pltpu.VMEM((ep_count, 8, segment), F32)]
        + Exchange.scratch(ep_count)
        + [pltpu.VMEM((ep_count, rows, cols), BF)]
        + Exchange.scratch(ep_count)
        + [pltpu.VMEM((width, kinds * cols), BF)]
        + [pltpu.VMEM((tokens, cols), BF)] * 5
        + [pltpu.VMEM((tokens, 128), F32), dma((7,))],
        compiler_params=pltpu.CompilerParams(
            collective_id=collective_id, has_side_effects=True, vmem_limit_bytes=56 << 20
        ),
        name=name,
    )(x, weights, small, w_out, cot, table)
    return outs[:-1]


def angles_of(position):
    half_dim = HEAD_DIM // 2
    frequency = np.float32(theta_base) ** (-2.0 * np.arange(half_dim, dtype=np.float32) / HEAD_DIM)
    angles = position.astype(np.float32)[:, None] * frequency.astype(np.float32)[None, :]
    return np.concatenate([np.cos(angles), np.sin(angles)], axis=1).astype(np.float32)


def per_device(
    block_input,
    cotangent,
    routes,
    w_query,
    w_key,
    w_value,
    w_output,
    w_router,
    gain_attn,
    gain_query,
    gain_key,
    gain_mlp,
    w_gate,
    w_up,
    w_down,
):
    rows, width = block_input.shape
    top_count = routes.shape[1]
    ep_count = lax.axis_size("ep")
    grp_count = lax.axis_size("grp")
    me = lax.axis_index("ep")
    my_group = lax.axis_index("grp")
    tokens = rows * ep_count
    prompt_len = tokens // 2
    capacity = min(rows, rows * top_count * 33 // (32 * ep_count))
    cols = width // ep_count
    scale = HEAD_DIM ** (-0.5)
    depth = w_query.shape[0]

    chosen = jnp.any(routes[:, :, None] == jnp.arange(ep_count, dtype=jnp.int32), axis=1)
    per_row = 128
    router_rows = depth * ep_count // per_row
    gains = jnp.concatenate([gain_attn, gain_query, gain_key, gain_mlp])
    gain_rows = gains.shape[0] // per_row
    small = jnp.concatenate(
        [
            w_router.reshape(router_rows, per_row),
            gains.reshape(gain_rows, per_row),
            jnp.zeros((16 - router_rows - gain_rows, per_row), BF),
            chosen.T.astype(BF),
        ]
    )
    weights = jnp.stack([w_query, w_key, w_value])
    token = np.arange(tokens)
    table = jnp.asarray(angles_of(np.where(token < prompt_len, token, prompt_len + (token - prompt_len) % rows)))
    early = ep_count // 4
    normed_all, w_all, smalls, full_output, cot_own, cot_other, query, key, value, n_q, n_k, columns, att_loc = attention(
        ep_count, block_input, weights, small, w_output, cotangent, table, early, "attention", 1
    )
    normed_all = normed_all.reshape(tokens, width)
    full_rows = full_output.reshape(grp_count * ep_count, depth, width)
    full_output = full_output.reshape(width, width)
    smalls = smalls.reshape(grp_count * ep_count, small.shape[0], per_row)
    full_router = smalls[:, :router_rows].reshape(width, ep_count)
    gains = smalls[:, router_rows : router_rows + gain_rows].reshape(-1, 4, depth).transpose(1, 0, 2).reshape(4, width)
    gain_first, gain_qnorm, gain_knorm, gain_second = (gains[i].astype(F32) for i in range(4))
    chosen_all = smalls[:, 16:].reshape(grp_count, ep_count, ep_count, rows)

    gain_q = lax.dynamic_slice(gain_qnorm, (me * cols,), (cols,))
    gain_k = lax.dynamic_slice(gain_knorm, (me * cols,), (cols,))

    inputs = block_input.astype(F32)
    residual = inputs + mm(att_loc, full_output)
    r_m = lax.rsqrt(jnp.mean(residual * residual, axis=-1, keepdims=True) + eps)
    n_m = residual * r_m
    normed_mlp = (n_m * gain_second).astype(BF)
    pair = 2 * rows
    slots = -(-2 * capacity // 16) * 16
    chips = ep_count // 2
    mine = lax.dynamic_index_in_dim(chosen_all, me, 2, keepdims=False)
    mine = jnp.where(my_group == 0, mine, mine[::-1]).reshape(2 * chips, pair).astype(F32)
    gate_w, up_w, down_w = w_gate[0], w_up[0], w_down[0]
    _, units, grad_out, hidden, grad_gate_pre, grad_up_pre, _, result_terms, _, d_normed_mlp, gate_grads, _ = experts(
        ep_count, normed_mlp, cot_own, cot_other, early, mine, slots, full_router, gate_w, up_w, down_w, "experts", 4
    )
    gate_grads = gate_grads[:, 0]

    probs = jax.nn.softmax(mm(normed_mlp, full_router), axis=-1)
    d_probs = gate_grads.T
    d_logits = (probs * (d_probs - jnp.sum(probs * d_probs, axis=-1, keepdims=True))).astype(BF)
    local_router = mm_tn(normed_mlp, d_logits)
    d_normed_mlp = d_normed_mlp + mm_nt(d_logits, full_router)
    local_gain_mlp = jnp.sum(d_normed_mlp * n_m, axis=0)
    d_n = d_normed_mlp * gain_second
    d_residual = cotangent.astype(F32) + r_m * (d_n - n_m * jnp.mean(n_m * d_n, axis=-1, keepdims=True))
    d_proj = d_residual.astype(BF)

    gain_rows_own = jnp.stack([gain_q, gain_k])
    owners = grp_count * ep_count
    tiles = jnp.concatenate(
        [
            local_router.reshape(owners, router_rows, per_row),
            jnp.pad(local_gain_mlp.reshape(owners, 1, depth), ((0, 0), (0, 16 - router_rows - 1), (0, per_row - depth))),
        ],
        axis=1,
    )
    d_normed, grad_output, mixture, grad_w, tiles, late, grad_gate, grad_up, grad_down = backward(
        ep_count,
        d_proj,
        att_loc,
        full_rows,
        (query, key, value, n_q, n_k),
        columns,
        table,
        gain_rows_own,
        w_all,
        normed_all,
        result_terms,
        tiles,
        [a.reshape(-1, a.shape[-1]) for a in (units, grad_out, hidden, grad_gate_pre, grad_up_pre)],
        "backward",
        9,
    )[:9]
    block_output = (residual + mixture).astype(BF)
    r_a = lax.rsqrt(jnp.mean(inputs * inputs, axis=-1, keepdims=True) + eps)
    n_a = inputs * r_a
    d_n = d_normed * gain_first
    input_grad = d_residual + r_a * (d_n - n_a * jnp.mean(n_a * d_n, axis=-1, keepdims=True))
    my_rows = my_group * ep_count + me
    grad_w = [grad_w[i].astype(F32) for i in range(3)]
    sums = jnp.sum(tiles, axis=0)
    grad_router = sums[:router_rows].reshape(depth, ep_count)
    gain_part = jnp.sum(late[:, 2, :depth], axis=0) / lax.dynamic_slice(gain_first, (my_rows * depth,), (depth,))
    late = jnp.sum(late.reshape(grp_count, ep_count, 8, cols), axis=0)[:, :2].transpose(1, 0, 2).reshape(2, width)
    late = lax.dynamic_slice(late, (0, my_rows * depth), (2, depth))
    gain_sums = [gain_part, late[0], late[1], sums[router_rows, :depth]]
    grad_gate, grad_up, grad_down = (grad.astype(F32)[None] for grad in (grad_gate, grad_up, grad_down))
    return (
        block_output,
        input_grad,
        grad_w[0],
        grad_w[1],
        grad_w[2],
        grad_output,
        grad_router,
        gain_sums[0],
        gain_sums[1],
        gain_sums[2],
        gain_sums[3],
        grad_gate,
        grad_up,
        grad_down,
    )


def plain_scale(values, gain_vec):
    return values * lax.rsqrt(jnp.mean(values * values, axis=-1, keepdims=True) + eps) * gain_vec


def rotate(values, position):
    token_count = values.shape[0]
    by_head = values.reshape(token_count, -1, HEAD_DIM)
    half_dim = HEAD_DIM // 2
    frequency = theta_base ** (-2.0 * jnp.arange(half_dim, dtype=jnp.float32) / HEAD_DIM)
    angles = position.astype(jnp.float32)[:, None] * frequency[None, :]
    cosine = jnp.cos(angles)[:, None, :]
    sine_part = jnp.sin(angles)[:, None, :]
    former = by_head[..., :half_dim]
    latter = by_head[..., half_dim:]
    turned = jnp.concatenate(
        [former * cosine - latter * sine_part, latter * cosine + former * sine_part], axis=-1
    )
    return turned.reshape(token_count, -1)


def masked_scores(query, keys, allowed, scale):
    raw_scores = jnp.einsum("qhd,khd->hqk", query, keys, preferred_element_type=jnp.float32) * scale
    return jnp.where(allowed[None], raw_scores, -1e30)


def plain_attend(query, keys, values, allowed, scale, head_group):
    outputs = []
    log_totals = []
    for head_start in range(0, query.shape[1], head_group):
        head_slice = slice(head_start, head_start + head_group)
        scores = masked_scores(query[:, head_slice], keys[:, head_slice], allowed, scale)
        largest = jnp.max(scores, axis=-1, keepdims=True)
        exponent = jnp.exp(scores - largest)
        summed = jnp.sum(exponent, axis=-1, keepdims=True)
        weights = (exponent / summed).astype(jnp.bfloat16)
        outputs.append(
            jnp.einsum(
                "hqk,khd->qhd", weights, values[:, head_slice], preferred_element_type=jnp.float32
            )
        )
        log_totals.append(largest + jnp.log(summed))
    return (jnp.concatenate(outputs, axis=1), jnp.concatenate(log_totals, axis=0))


def plain_attend_back(query, keys, values, grad_out, log_totals, allowed, scale, head_group):
    query_grads = []
    key_grads = []
    value_grads = []
    for head_start in range(0, query.shape[1], head_group):
        head_slice = slice(head_start, head_start + head_group)
        query_part = query[:, head_slice]
        keys_part = keys[:, head_slice]
        grad_part = grad_out[:, head_slice]
        scores = masked_scores(query_part, keys_part, allowed, scale)
        weights = jnp.where(allowed[None], jnp.exp(scores - log_totals[head_slice]), 0.0)
        grad_weights = jnp.einsum(
            "qhd,khd->hqk", grad_part, values[:, head_slice], preferred_element_type=jnp.float32
        )
        inner = jnp.sum(weights * grad_weights, axis=-1, keepdims=True)
        grad_scores = (weights * (grad_weights - inner)).astype(jnp.bfloat16)
        query_grads.append(
            jnp.einsum("hqk,khd->qhd", grad_scores, keys_part, preferred_element_type=jnp.float32)
            * scale
        )
        key_grads.append(
            jnp.einsum("hqk,qhd->khd", grad_scores, query_part, preferred_element_type=jnp.float32)
            * scale
        )
        value_grads.append(
            jnp.einsum(
                "hqk,qhd->khd",
                weights.astype(jnp.bfloat16),
                grad_part,
                preferred_element_type=jnp.float32,
            )
        )
    return (
        jnp.concatenate(query_grads, axis=1),
        jnp.concatenate(key_grads, axis=1),
        jnp.concatenate(value_grads, axis=1),
    )


def per_device_plain(
    block_input,
    cotangent,
    routes,
    w_query,
    w_key,
    w_value,
    w_output,
    w_router,
    gain_attn,
    gain_query,
    gain_key,
    gain_mlp,
    w_gate,
    w_up,
    w_down,
):
    row_count, model_width = block_input.shape
    top_count = routes.shape[1]
    ep_count = lax.axis_size("ep")
    my_index = lax.axis_index("ep")
    half_count = ep_count // 2
    prompt_len = row_count * half_count
    capacity = min(row_count, row_count * top_count * 33 // (32 * ep_count))
    head_count = model_width // HEAD_DIM
    head_group = math.gcd(4, head_count)
    scale = HEAD_DIM ** (-0.5)
    gathered = (
        lax.all_gather(w_query, ("grp", "ep"), axis=0, tiled=True),
        lax.all_gather(w_key, ("grp", "ep"), axis=0, tiled=True),
        lax.all_gather(w_value, ("grp", "ep"), axis=0, tiled=True),
        lax.all_gather(w_output, ("grp", "ep"), axis=0, tiled=True),
        lax.all_gather(w_router, ("grp", "ep"), axis=0, tiled=True),
        lax.all_gather(gain_attn, ("grp", "ep"), axis=0, tiled=True),
        lax.all_gather(gain_query, ("grp", "ep"), axis=0, tiled=True),
        lax.all_gather(gain_key, ("grp", "ep"), axis=0, tiled=True),
        lax.all_gather(gain_mlp, ("grp", "ep"), axis=0, tiled=True),
    )
    full_query, full_key, full_value, full_output, full_router = (
        gathered[0],
        gathered[1],
        gathered[2],
        gathered[3],
        gathered[4],
    )
    gain_first = gathered[5].astype(jnp.float32)
    gain_qnorm = gathered[6].astype(jnp.float32)
    gain_knorm = gathered[7].astype(jnp.float32)
    gain_second = gathered[8].astype(jnp.float32)
    offsets = jnp.arange(row_count, dtype=jnp.int32)
    in_prompt = my_index < half_count
    position = jnp.where(in_prompt, my_index * row_count + offsets, prompt_len + offsets)
    key_position = jnp.concatenate([jnp.arange(prompt_len, dtype=jnp.int32), prompt_len + offsets])
    from_prompt = jnp.arange(prompt_len + row_count, dtype=jnp.int32) < prompt_len
    allowed = (key_position[None, :] <= position[:, None]) & (
        from_prompt[None, :] | jnp.logical_not(in_prompt)
    )

    def prepare(linear, gain_vec):
        return rotate(plain_scale(linear, gain_vec), position)

    inputs = block_input.astype(jnp.float32)
    normed = plain_scale(inputs, gain_first).astype(jnp.bfloat16)
    query_lin = jnp.dot(normed, full_query, preferred_element_type=jnp.float32)
    key_lin = jnp.dot(normed, full_key, preferred_element_type=jnp.float32)
    value_lin = jnp.dot(normed, full_value, preferred_element_type=jnp.float32)
    query_low = prepare(query_lin, gain_qnorm).astype(jnp.bfloat16)
    key_low = prepare(key_lin, gain_knorm).astype(jnp.bfloat16)
    value_low = value_lin.astype(jnp.bfloat16)
    shared = (
        lax.all_gather(key_low, "ep", axis=0, tiled=True),
        lax.all_gather(value_low, "ep", axis=0, tiled=True),
    )
    keys = jnp.concatenate([shared[0][:prompt_len], key_low]).reshape(-1, head_count, HEAD_DIM)
    values = jnp.concatenate([shared[1][:prompt_len], value_low]).reshape(-1, head_count, HEAD_DIM)
    query = query_low.reshape(row_count, head_count, HEAD_DIM)
    attn_out, log_totals = plain_attend(query, keys, values, allowed, scale, head_group)
    attended = attn_out.reshape(row_count, model_width).astype(jnp.bfloat16)
    residual = inputs + jnp.dot(attended, full_output, preferred_element_type=jnp.float32)
    normed_mlp = plain_scale(residual, gain_second).astype(jnp.bfloat16)
    logits = jnp.dot(normed_mlp, full_router, preferred_element_type=jnp.float32)
    probs = jax.nn.softmax(logits, axis=-1)
    picks = routes[:, :, None] == jnp.arange(ep_count, dtype=jnp.int32)[None, None, :]
    gates = jnp.sum(jnp.where(picks, probs[:, None, :], 0.0), axis=-1)
    hot_table = picks.reshape(-1, ep_count).astype(jnp.int32)
    before = jnp.cumsum(hot_table, axis=0) - hot_table
    slot_index = jnp.sum(before * hot_table, axis=1)
    target = routes.reshape(-1) * capacity + slot_index
    sentinel = row_count * top_count
    source = (
        jnp.full((ep_count * capacity,), sentinel, jnp.int32)
        .at[target]
        .set(jnp.arange(sentinel, dtype=jnp.int32))
    )
    token_of = source // top_count
    padded_rows = jnp.concatenate([normed_mlp, jnp.zeros((1, model_width), jnp.bfloat16)])
    outgoing = padded_rows[token_of].reshape(ep_count, capacity, model_width)
    arrived = lax.all_to_all(outgoing, "ep", split_axis=0, concat_axis=0, tiled=True)
    units = arrived.reshape(-1, model_width)
    gate_w = w_gate[0]
    up_w = w_up[0]
    down_w = w_down[0]
    gate_pre = jnp.dot(units, gate_w, preferred_element_type=jnp.float32)
    up_pre = jnp.dot(units, up_w, preferred_element_type=jnp.float32)
    hidden = (jax.nn.silu(gate_pre) * up_pre).astype(jnp.bfloat16)
    expert_result = jnp.dot(hidden, down_w, preferred_element_type=jnp.float32).astype(jnp.bfloat16)
    returned = lax.all_to_all(
        expert_result.reshape(ep_count, capacity, model_width),
        "ep",
        split_axis=0,
        concat_axis=0,
        tiled=True,
    )
    picked = (
        returned.reshape(-1, model_width)[target]
        .reshape(row_count, top_count, model_width)
        .astype(jnp.float32)
    )
    output_full = residual + jnp.sum(gates[:, :, None] * picked, axis=1)
    block_output = output_full.astype(jnp.bfloat16)
    back_query, back_key, back_value, back_output, back_router = (
        full_query,
        full_key,
        full_value,
        full_output,
        full_router,
    )
    grad_top = cotangent.astype(jnp.float32)
    grad_gates = jnp.sum(grad_top[:, None, :] * picked, axis=-1)
    grad_expert = (
        (gates[:, :, None] * grad_top[:, None, :]).astype(jnp.bfloat16).reshape(-1, model_width)
    )
    padded_grads = jnp.concatenate([grad_expert, jnp.zeros((1, model_width), jnp.bfloat16)])
    grad_outgoing = padded_grads[source].reshape(ep_count, capacity, model_width)
    grad_arrived = lax.all_to_all(
        grad_outgoing, "ep", split_axis=0, concat_axis=0, tiled=True
    ).reshape(-1, model_width)
    grad_hidden = jnp.einsum("nd,fd->nf", grad_arrived, down_w, preferred_element_type=jnp.float32)
    sigma = jax.nn.sigmoid(gate_pre)
    grad_gate_pre = (grad_hidden * up_pre * sigma * (1.0 + gate_pre * (1.0 - sigma))).astype(
        jnp.bfloat16
    )
    grad_up_pre = (grad_hidden * gate_pre * sigma).astype(jnp.bfloat16)
    local_down = jnp.einsum("nf,nd->fd", hidden, grad_arrived, preferred_element_type=jnp.float32)
    local_gate = jnp.einsum("nd,nf->df", units, grad_gate_pre, preferred_element_type=jnp.float32)
    local_up = jnp.einsum("nd,nf->df", units, grad_up_pre, preferred_element_type=jnp.float32)
    grad_units = jnp.einsum("nf,df->nd", grad_gate_pre, gate_w, preferred_element_type=jnp.float32)
    grad_units = grad_units + jnp.einsum(
        "nf,df->nd", grad_up_pre, up_w, preferred_element_type=jnp.float32
    )
    grad_units = grad_units.astype(jnp.bfloat16).reshape(ep_count, capacity, model_width)
    grad_returned = lax.all_to_all(
        grad_units, "ep", split_axis=0, concat_axis=0, tiled=True
    ).reshape(-1, model_width)
    grad_normed_mlp = jnp.sum(
        grad_returned[target].reshape(row_count, top_count, model_width).astype(jnp.float32), axis=1
    )
    expert_sums = (
        lax.psum(local_gate[None].astype(jnp.bfloat16), "grp").astype(jnp.float32),
        lax.psum(local_up[None].astype(jnp.bfloat16), "grp").astype(jnp.float32),
        lax.psum(local_down[None].astype(jnp.bfloat16), "grp").astype(jnp.float32),
    )
    grad_probs = jnp.sum(jnp.where(picks, grad_gates[:, :, None], 0.0), axis=1)
    grad_logits = (
        probs * (grad_probs - jnp.sum(probs * grad_probs, axis=-1, keepdims=True))
    ).astype(jnp.bfloat16)
    local_router = jnp.einsum(
        "rd,re->de", normed_mlp, grad_logits, preferred_element_type=jnp.float32
    )
    grad_normed_mlp = grad_normed_mlp + jnp.einsum(
        "re,de->rd", grad_logits, back_router, preferred_element_type=jnp.float32
    )
    unused_mlp, second_back = jax.vjp(plain_scale, residual, gain_second)
    grad_from_mlp, local_gain_mlp = second_back(grad_normed_mlp)
    grad_residual = grad_top + grad_from_mlp
    grad_proj = grad_residual.astype(jnp.bfloat16)
    local_output = jnp.einsum("rd,re->de", attended, grad_proj, preferred_element_type=jnp.float32)
    grad_attended = jnp.einsum(
        "re,de->rd", grad_proj, back_output, preferred_element_type=jnp.float32
    )
    grad_attended = grad_attended.astype(jnp.bfloat16).reshape(row_count, head_count, HEAD_DIM)
    grad_query_rot, grad_keys, grad_values = plain_attend_back(
        query, keys, values, grad_attended, log_totals, allowed, scale, head_group
    )
    grad_keys = grad_keys.reshape(-1, model_width)
    grad_values = grad_values.reshape(-1, model_width)
    padding = jnp.zeros((ep_count * row_count - prompt_len, model_width), jnp.float32)
    key_share, value_share = (
        lax.psum_scatter(
            jnp.concatenate([grad_keys[:prompt_len], padding]).astype(jnp.bfloat16),
            "ep",
            scatter_dimension=0,
            tiled=True,
        ).astype(jnp.float32),
        lax.psum_scatter(
            jnp.concatenate([grad_values[:prompt_len], padding]).astype(jnp.bfloat16),
            "ep",
            scatter_dimension=0,
            tiled=True,
        ).astype(jnp.float32),
    )
    grad_key_rot = key_share + grad_keys[prompt_len:]
    grad_value_lin = (value_share + grad_values[prompt_len:]).astype(jnp.bfloat16)
    unused_query, query_back = jax.vjp(prepare, query_lin, gain_qnorm)
    grad_query_lin, local_gain_query = query_back(grad_query_rot.reshape(row_count, model_width))
    unused_key, key_back = jax.vjp(prepare, key_lin, gain_knorm)
    grad_key_lin, local_gain_key = key_back(grad_key_rot)
    grad_query_low = grad_query_lin.astype(jnp.bfloat16)
    grad_key_low = grad_key_lin.astype(jnp.bfloat16)
    local_query = jnp.einsum(
        "rd,re->de", normed, grad_query_low, preferred_element_type=jnp.float32
    )
    local_key = jnp.einsum("rd,re->de", normed, grad_key_low, preferred_element_type=jnp.float32)
    local_value = jnp.einsum(
        "rd,re->de", normed, grad_value_lin, preferred_element_type=jnp.float32
    )
    grad_normed = jnp.einsum(
        "re,de->rd", grad_query_low, back_query, preferred_element_type=jnp.float32
    )
    grad_normed = grad_normed + jnp.einsum(
        "re,de->rd", grad_key_low, back_key, preferred_element_type=jnp.float32
    )
    grad_normed = grad_normed + jnp.einsum(
        "re,de->rd", grad_value_lin, back_value, preferred_element_type=jnp.float32
    )
    unused_first, first_back = jax.vjp(plain_scale, inputs, gain_first)
    grad_from_attn, local_gain_attn = first_back(grad_normed)
    input_grad = grad_residual + grad_from_attn
    summed_grads = (
        lax.psum_scatter(local_query, ("grp", "ep"), scatter_dimension=0, tiled=True),
        lax.psum_scatter(local_key, ("grp", "ep"), scatter_dimension=0, tiled=True),
        lax.psum_scatter(local_value, ("grp", "ep"), scatter_dimension=0, tiled=True),
        lax.psum_scatter(local_output, ("grp", "ep"), scatter_dimension=0, tiled=True),
        lax.psum_scatter(local_router, ("grp", "ep"), scatter_dimension=0, tiled=True),
        lax.psum_scatter(local_gain_attn, ("grp", "ep"), scatter_dimension=0, tiled=True),
        lax.psum_scatter(local_gain_query, ("grp", "ep"), scatter_dimension=0, tiled=True),
        lax.psum_scatter(local_gain_key, ("grp", "ep"), scatter_dimension=0, tiled=True),
        lax.psum_scatter(local_gain_mlp, ("grp", "ep"), scatter_dimension=0, tiled=True),
    )
    return (
        block_output,
        input_grad,
        summed_grads[0],
        summed_grads[1],
        summed_grads[2],
        summed_grads[3],
        summed_grads[4],
        summed_grads[5],
        summed_grads[6],
        summed_grads[7],
        summed_grads[8],
        expert_sums[0],
        expert_sums[1],
        expert_sums[2],
    )


def solution(mesh):
    both = ("grp", "ep")
    return jax.shard_map(
        per_device if mesh.shape["grp"] == 2 else per_device_plain,
        mesh=mesh,
        in_specs=(P(both, None),) * 8 + (P(both),) * 4 + (P("ep", None, None),) * 3,
        out_specs=(P(both, None),) * 7 + (P(both),) * 4 + (P("ep", None, None),) * 3,
        check_vma=False,
    )
```

```python
import math

import jax
import jax.numpy as jnp
import numpy as np
from jax import lax
from jax.experimental import pallas as pl
from jax.experimental.pallas import tpu as pltpu
from jax.sharding import PartitionSpec as P

HEAD_DIM = 128
MESH = pl.DeviceIdType.MESH
BF = jnp.bfloat16
F32 = jnp.float32


eps = 1e-05
theta_base = 10000.0


def mm(a, b):
    return jnp.dot(a, b, preferred_element_type=F32)


def mm_nt(a, b):
    return lax.dot_general(a, b, (((1,), (1,)), ((), ())), preferred_element_type=F32)


def mm_tn(a, b):
    return lax.dot_general(a, b, (((0,), (0,)), ((), ())), preferred_element_type=F32)


class Place:
    def __init__(self, ep_count):
        self.grp = lax.axis_index("grp")
        self.ep = lax.axis_index("ep")
        self.count = ep_count
        self.ring = ep_count // 2
        self.half = self.ring // 2
        self.core = self.ep % 2
        y = (self.ep // 2) % 2
        z = self.ep // 4
        self.place = z + y * (self.ring - 1 - 2 * z)

    def index(self, place, core):
        y = place // self.half
        z = place + y * (self.ring - 1 - 2 * place)
        return (z * 2 + y) * 2 + core

    def at(self, offset):
        return (self.place + offset + self.ring) % self.ring

    def chip(self, offset):
        return self.index(self.at(offset), self.core)

    def right(self):
        return (self.grp, self.chip(1))

    def left(self):
        return (self.grp, self.chip(-1))

    def sibling(self):
        return (self.grp, self.index(self.place, 1 - self.core))

    def across(self):
        return (1 - self.grp, self.ep)

    def peer(self, offset):
        return (self.grp, (self.ep + offset + self.count) % self.count)


def greet(devices):
    barrier = pltpu.get_barrier_semaphore()
    for device in devices:
        pl.semaphore_signal(barrier, inc=1, device_id=device, device_id_type=MESH)
    pl.semaphore_wait(barrier, len(devices))


def remote(src, dst, send, recv, device):
    return pltpu.make_async_remote_copy(
        src_ref=src, dst_ref=dst, send_sem=send, recv_sem=recv, device_id=device, device_id_type=MESH
    )


class Gather:
    def __init__(self, here, src, dst, sems, reach=None):
        self.here, self.src, self.dst, self.reach = here, src, dst, reach
        self.ring_send, self.ring_recv, self.side_send, self.side_recv, self.own_sem = sems
        self.rows = dst.shape[1] // 2
        self.far = here.ring // 2
        self.started = []

    @staticmethod
    def scratch(ep_count):
        far = ep_count // 4
        ring = pltpu.SemaphoreType.DMA((2, far, 2))
        side = pltpu.SemaphoreType.DMA((2, far + 1, 2))
        return [ring, ring, side, side, pltpu.SemaphoreType.DMA]

    def block(self, index, part):
        return self.dst.at[index, pl.ds(part * self.rows, self.rows)]

    def go(self, copy):
        copy.start()
        self.started.append(copy)

    def hops(self, way, part):
        if self.reach is not None:
            return self.reach
        return self.far if way == part else self.far - 1

    def ring_copy(self, way, step, part, src, index):
        device = self.here.right() if way == 0 else self.here.left()
        return remote(
            src, self.block(index, part), self.ring_send.at[way, step, part], self.ring_recv.at[way, step, part], device
        )

    def side_copy(self, way, step, part, src, index):
        return remote(
            src,
            self.block(index, part),
            self.side_send.at[way, step, part],
            self.side_recv.at[way, step, part],
            self.here.sibling(),
        )

    def start(self):
        here = self.here
        for part in range(2):
            src = self.src.at[pl.ds(part * self.rows, self.rows)]
            for way in range(2):
                if self.hops(way, part) > 0:
                    self.go(self.ring_copy(way, 0, part, src, here.ep))
            self.go(self.side_copy(0, 0, part, src, here.ep))
        if self.reach is not None:
            return
        self.own = pltpu.make_async_copy(self.src, self.dst.at[here.ep], self.own_sem)
        self.own.start()

    def step(self, step):
        here = self.here
        for part in range(2):
            for way in range(2):
                if step < self.hops(way, part):
                    index = here.chip(-1 - step if way == 0 else 1 + step)
                    src = self.block(index, part)
                    self.ring_copy(way, step, part, src, index).wait_recv()
                    if step + 1 < self.hops(way, part):
                        self.go(self.ring_copy(way, step + 1, part, src, index))
                    self.go(self.side_copy(way, step + 1, part, src, index))

    def side(self, step):
        here = self.here
        for part in range(2):
            for way in range(2):
                if (step < 0 and way == 0) or (0 <= step < self.hops(way, part)):
                    offset = 0 if step < 0 else (-1 - step if way == 0 else 1 + step)
                    index = here.index(here.at(offset), 1 - here.core)
                    self.side_copy(way, step + 1, part, self.block(index, part), index).wait_recv()

    def settle(self):
        self.own.wait()

    def finish(self):
        for copy in self.started:
            copy.wait_send()


class Exchange:
    def __init__(self, here, src, dst, sems):
        self.here, self.src, self.dst = here, src, dst
        self.send, self.recv, self.own_sem = sems

    @staticmethod
    def scratch(ep_count):
        return [
            pltpu.SemaphoreType.DMA((ep_count,)),
            pltpu.SemaphoreType.DMA((ep_count,)),
            pltpu.SemaphoreType.DMA,
        ]

    def start(self):
        here = self.here
        self.own = pltpu.make_async_copy(self.src(here.ep), self.dst(here.ep), self.own_sem)
        self.own.start()
        self.copies = []
        for offset in range(1, here.count):
            device = here.peer(offset)
            copy = remote(self.src(device[1]), self.dst(here.ep), self.send.at[offset], self.recv.at[offset], device)
            copy.start()
            self.copies.append(copy)

    def arrive(self):
        here = self.here
        self.own.wait()
        for offset in range(1, here.count):
            source = here.peer(-offset)[1]
            remote(
                self.dst(source), self.dst(source), self.send.at[offset], self.recv.at[offset], here.peer(offset)
            ).wait_recv()

    def finish(self):
        for copy in self.copies:
            copy.wait_send()


def far_devices(here):
    return [(1 - here.grp, (here.ep + offset) % here.count) for offset in range(here.count)]


def plane_devices(here):
    return [here.peer(offset) for offset in range(1, here.count)]


def split(refs, *sizes):
    groups, start = [], 0
    for size in sizes:
        groups.append(refs[start : start + size])
        start += size
    return groups


def ring_offsets(ring):
    far = ring // 2
    return [0] + [sign * k for k in range(1, far) for sign in (1, -1)] + [far]


def experts(
    ep_count, block, cot_own, cot_other, early, mine, slots, router, gate_w, up_w, down_w, name, collective_id
):
    rows, width = block.shape
    hidden_width = gate_w.shape[1]
    pair = 2 * rows
    ring = ep_count // 2
    offsets = ring_offsets(ring)
    batches = [[0]] + [[2 * k - 1, 2 * k] for k in range(1, ring // 2)] + [[ring - 1]]
    tile, wide = 512, 1024
    far = ring // 2
    reach = far // 2

    def kernel(*refs):
        ins, outs, scratch = split(refs, 8, 12, len(refs) - 20)
        block_ref, cot_ref, cot_far, mine_ref, router_ref, gate_ref, up_ref, down_ref = ins
        other_ref, u_out, e_out, h_out, g_out, p_out, du_terms, eo_terms, du_joint, sum_out, dot_out, cot_late = outs
        gather_sems, near_sems, cross, cot_cross, bufs, stage, du_s, dot_sems, load_sems = split(scratch, 5, 5, 4, 4, 6, 12, 8, 3, 5)
        across_send, across_recv, hand_send, hand_recv = cross
        gate_v, up_v, down_v, rows_v, cot_v, own_ref = bufs
        u_s, e_s, h_s, g_s, p_s, r_s, dx_s, gate_s, dot_s, line_s, term_v, hot_ref = stage
        dot_send, dot_recv, dot_own = dot_sems
        weight_sem, rows_sem, cot_sem, stage_sem, term_sem = load_sems
        here = Place(ep_count)
        sums = RingSum(here, lambda e: du_terms.at[e], du_joint, du_s[:3], du_s[3:])
        weights = []
        for i, (src, dst) in enumerate(((gate_ref, gate_v), (up_ref, up_v), (down_ref, down_v))):
            copy = pltpu.make_async_copy(src, dst, weight_sem.at[i])
            copy.start()
            weights.append(copy)
        greet(plane_devices(here) + [here.across()])
        gather = Gather(here, block_ref, own_ref, gather_sems)
        gather.start()
        sent = []

        def start(copy):
            copy.start()
            sent.append(copy)

        def cross_copy(slot, src):
            index = here.chip(offsets[slot])
            return remote(src, other_ref.at[index], across_send.at[slot], across_recv.at[slot], here.across())

        def hand_copy(slot, core):
            index = here.index(here.at(offsets[slot]), core)
            return remote(
                other_ref.at[index], other_ref.at[index], hand_send.at[slot], hand_recv.at[slot], here.sibling()
            )

        start(cross_copy(0, block_ref))
        near = Gather(here, other_ref.at[here.ep], other_ref, near_sems, reach)
        straight = 2 * reach + 1
        cot_over = Crossing(here, lambda e: cot_late.at[e], lambda e: cot_late.at[e], cot_cross)
        for slot in range(early, ring):
            cot_over.send(slot, cot_ref.at[here.chip(offsets[slot])])

        def chip_of(slot):
            return here.index(here.at(offsets[slot]), 0) // 2

        def cot_copy(which, slot, buffer):
            src = cot_ref if which == 0 else (cot_far if slot < early else cot_late)
            return pltpu.make_async_copy(src.at[pl.ds(2 * chip_of(slot), 2)], cot_v.at[buffer], cot_sem.at[buffer])

        def rows_copy(src, slot, buffer):
            return pltpu.make_async_copy(
                src.at[pl.ds(2 * chip_of(slot), 2)], rows_v.at[buffer], rows_sem.at[buffer]
            )

        pending = {}
        stages = {"u": (u_s, u_out), "e": (e_s, e_out), "g": (g_s, g_out), "p": (p_s, p_out)}

        def settle(keys):
            for key in keys:
                for copy in pending.pop(key, []):
                    copy.wait()

        def store(key, which, batch):
            src, dst = stages[key]
            sem = list(stages).index(key)
            count = len(batch) * slots
            at = pl.ds(batch[0] * slots, count)
            target = dst.at[which, at]
            pending[key] = [pltpu.make_async_copy(src.at[pl.ds(0, count)], target, stage_sem.at[sem])]
            for copy in pending[key]:
                copy.start()

        def loop(extent, tile, body):
            def run(i, carry):
                body(pl.ds(pl.multiple_of(i * tile, tile), tile))
                return carry

            lax.fori_loop(0, extent // tile, run, 0)

        def prefetch(which, batch, parity):
            for i, slot in enumerate(batch):
                cot_copy(which, slot, 2 * parity + i).start()

        hidden_copies = {}

        def store_hidden(which, batch):
            at = pl.ds(batch[0] * slots, len(batch) * slots)
            sem = weight_sem.at[3 + batches.index(batch)]
            hidden_copies[batch[0]] = pltpu.make_async_copy(h_s.at[at], h_out.at[which, at], sem)
            hidden_copies[batch[0]].start()

        given = []

        def give(src, first, chip, terms):
            buffer = len(given) % 2
            if len(given) > 1:
                given[-2].wait()

            def put(at):
                spread_rows = mm_tn(hot_ref[0, chip], src[pl.ds(first, slots), at]).astype(BF)
                term_v[buffer, :, :, at] = spread_rows.reshape(2, rows, width)

            loop(width, width, put)
            copy = pltpu.make_async_copy(term_v.at[buffer], terms.at[pl.ds(2 * chip, 2)], term_sem.at[buffer])
            copy.start()
            given.append(copy)

        def settle_given():
            for copy in given[-2:]:
                copy.wait()
            given.clear()

        def work(which, batch, parity):
            count = len(batch) * slots
            every = pl.ds(0, count)
            if which == 1:
                for i, slot in enumerate(batch):
                    rows_copy(other_ref, slot, i).start()
                for i, slot in enumerate(batch):
                    rows_copy(other_ref, slot, i).wait()
            for i, slot in enumerate(batch):
                cot_copy(which, slot, 2 * parity + i).wait()
            settle("u")
            for i, slot in enumerate(batch):
                hot = hot_ref[which, chip_of(slot)]

                def pick_rows(at, i=i, hot=hot):
                    if which == 0:
                        taken = own_ref[pl.ds(2 * chip_of(batch[i]), 2), :, at]
                    else:
                        taken = rows_v[i, :, :, at]
                    picked = mm(hot, taken.reshape(pair, width))
                    u_s[pl.ds(i * slots, slots), at] = picked.astype(BF)

                loop(width, width, pick_rows)
            store("u", which, batch)
            logits = mm(u_s[every], router_ref[...])
            lane = lax.broadcasted_iota(jnp.int32, logits.shape, 1)
            powers = jnp.exp(logits - jnp.max(logits, axis=-1, keepdims=True))
            gate = jnp.sum(jnp.where(lane == here.ep, powers, 0.0), axis=-1, keepdims=True)
            gate = gate / jnp.sum(powers, axis=-1, keepdims=True)
            settle("e")
            for i, slot in enumerate(batch):
                hot = hot_ref[which, chip_of(slot)]

                def pick_cots(at, i=i, hot=hot):
                    part = pl.ds(i * slots, slots)
                    picked = mm(hot, cot_v[2 * parity + i, :, :, at].reshape(pair, width))
                    e_s[part, at] = (gate[i * slots : (i + 1) * slots] * picked).astype(BF)
                    if which == 0:
                        r_s[pl.ds((batch[0] + i) * slots, slots), at] = picked.astype(BF)

                loop(width, width, pick_cots)
            store("e", which, batch)
            settle("gp")
            held = pl.ds(batch[0] * slots, count)
            if batch[0] in hidden_copies:
                hidden_copies.pop(batch[0]).wait()
            gate_s[held] = gate

            def inner(at):
                gate_pre = mm(u_s[every], gate_v[:, at])
                up_pre = mm(u_s[every], up_v[:, at])
                grad = mm_nt(e_s[every], down_v[at, :])
                sigma = 1.0 / (1.0 + jnp.exp(-gate_pre))
                swish = gate_pre * sigma
                h_s[held, at] = (swish * up_pre).astype(BF)
                g_s[every, at] = (grad * up_pre * sigma * (1.0 + gate_pre * (1.0 - sigma))).astype(BF)
                p_s[every, at] = (grad * swish).astype(BF)

            loop(hidden_width, tile, inner)
            for key in "gp":
                store(key, which, batch)
            store_hidden(which, batch)
            if which == 1:
                return None
            return lambda: work_back(batch, every)

        def work_back(batch, every):
            def back(at):
                grad = mm_nt(g_s[every], gate_v[at, :]) + mm_nt(p_s[every], up_v[at, :])
                dx_s[every, at] = grad.astype(BF)

            loop(width, wide, back)
            for i, slot in enumerate(batch):
                part = pl.ds(i * slots, slots)
                give(dx_s, i * slots, chip_of(slot), du_terms)

        def results():
            dot_s[...] = jnp.zeros_like(dot_s)

            def outer(at):
                result = mm(h_s[...], down_v[:, at]).astype(BF).astype(F32)
                dot_s[...] += jnp.sum(result * r_s[:, at].astype(F32), axis=-1, keepdims=True)
                r_s[:, at] = (gate_s[...] * result).astype(BF)

            loop(width, tile, outer)
            for slot in range(ring):
                part = pl.ds(slot * slots, slots)
                line = jnp.sum(hot_ref[0, chip_of(slot)].astype(F32) * dot_s[part], axis=0, keepdims=True)
                for core in range(2):
                    line_s[slot, core] = jnp.broadcast_to(line[:, core * rows : (core + 1) * rows], (8, rows))

        prefetch(0, batches[0], 0)
        upto = lax.broadcasted_iota(jnp.int32, (pair, pair), 0) <= lax.broadcasted_iota(jnp.int32, (pair, pair), 1)
        mine_all = mine_ref[...]
        order = mm(mine_all.astype(BF), upto.astype(BF))
        order = jnp.where(mine_all > 0, order - 1.0, -1.0)
        place = lax.broadcasted_iota(jnp.int32, (slots, pair), 0).astype(F32)
        for which in range(2):
            for chip in range(ring):
                line = order[which * ring + chip : which * ring + chip + 1]
                hot_ref[which, chip] = jnp.where(place == line, 1.0, 0.0).astype(BF)
        for copy in weights:
            copy.wait()
        gather.settle()
        for number, batch in enumerate(batches):
            gather.side(number - 1)
            if number + 1 < len(batches):
                prefetch(0, batches[number + 1], (number + 1) % 2)
            else:
                prefetch(1, batches[0], (number + 1) % 2)
            rest = work(0, batch, number % 2)
            if number < far:
                gather.step(number)
                for slot in batches[number + 1]:
                    if slot >= straight:
                        start(cross_copy(slot, own_ref.at[here.chip(offsets[slot])]))
                if number == 1:
                    cross_copy(0, other_ref.at[here.ep]).wait_recv()
                    near.start()
                elif number > 2:
                    near.step(number - 3)
            rest()
        def dot_copy(slot, core, sender_core, source, target):
            return remote(
                line_s.at[slot, core],
                dot_out.at[source],
                dot_send.at[slot, core],
                dot_recv.at[slot, sender_core],
                (here.grp, target),
            )

        settle_given()
        sums.start()
        sums.step(0)
        results()
        own_dots = pltpu.make_async_copy(line_s.at[0, here.core], dot_out.at[here.ep], dot_own)
        own_dots.start()

        start(dot_copy(0, 1 - here.core, here.core, here.ep, here.sibling()[1]))
        for slot in range(1, ring):
            for core in range(2):
                target = here.index(here.at(offsets[slot]), core)
                start(dot_copy(slot, core, here.core, here.ep, target))
        count = len(batches)

        def put(out):
            def keep_sum(at, value):
                out[at] = value

            return keep_sum

        for number, batch in enumerate(batches):
            far_slots = [slot for slot in batch if slot >= straight]
            for slot in far_slots:
                index = here.chip(offsets[slot])
                cross_copy(slot, other_ref.at[index]).wait_recv()
                start(hand_copy(slot, here.core))
            if 0 < number < reach:
                near.step(number)
            if 0 < number < far:
                sums.step(number)
            if number == 1:
                for slot in range(ring):
                    give(r_s, slot * slots, chip_of(slot), eo_terms)
                settle_given()
            if number == far:
                sums.finish(put(sum_out))
            for slot in far_slots:
                hand_copy(slot, 1 - here.core).wait_recv()
            if number <= reach:
                near.side(number - 1)
            parity = (count + number) % 2
            if number + 1 < count:
                late = [slot for slot in batches[number + 1] if slot >= early]
                for slot in late:
                    cot_over.take(slot)
                for slot in late:
                    cot_over.settle(slot)
                prefetch(1, batches[number + 1], 1 - parity)
            work(1, batch, parity)
        own_dots.wait()
        dot_copy(0, 0, 1 - here.core, here.sibling()[1], here.sibling()[1]).wait_recv()
        for slot in range(1, ring):
            for core in range(2):
                source = here.index(here.at(-offsets[slot]), core)
                dot_copy(slot, 0, core, source, source).wait_recv()
        gather.finish()
        near.finish()
        cot_over.finish()
        for copy in sent:
            copy.wait_send()
        settle("uegp")
        for copy in hidden_copies.values():
            copy.wait()

    dma = pltpu.SemaphoreType.DMA
    total = ring * slots
    most = max(len(batch) for batch in batches) * slots
    hbm = pl.BlockSpec(memory_space=pl.ANY)
    vmem = pl.BlockSpec(memory_space=pltpu.VMEM)

    def low(*shape):
        return jax.ShapeDtypeStruct(shape, BF)

    def keep(*shape):
        return pltpu.VMEM(shape, BF)

    return pl.pallas_call(
        kernel,
        out_shape=[
            low(ep_count, rows, width),
            low(2, total, width),
            low(2, total, width),
            low(2, total, hidden_width),
            low(2, total, hidden_width),
            low(2, total, hidden_width),
            low(ep_count, rows, width),
            low(ep_count, rows, width),
            low(ring, rows, width),
            jax.ShapeDtypeStruct((rows, width), F32),
            jax.ShapeDtypeStruct((ep_count, 8, rows), F32),
            low(ep_count, rows, width),
        ],
        in_specs=[hbm, hbm, hbm, vmem, vmem, hbm, hbm, hbm],
        out_specs=[hbm] * 9 + [vmem, hbm, hbm],
        scratch_shapes=Gather.scratch(ep_count)
        + Gather.scratch(ep_count)
        + [dma((ring,))] * 4
        + Crossing.scratch(ep_count)
        + [keep(*gate_w.shape), keep(*up_w.shape), keep(*down_w.shape), keep(2, 2, rows, width), keep(4, 2, rows, width), keep(ep_count, rows, width)]
        + [keep(most, width), keep(most, width), keep(total, hidden_width)]
        + [keep(most, hidden_width)] * 2
        + [keep(total, width), keep(most, width)]
        + [pltpu.VMEM((total, 1), F32), pltpu.VMEM((total, 1), F32), pltpu.VMEM((ring, 2, 8, rows), F32)]
        + [keep(2, 2, rows, width), keep(2, ring, slots, pair)]
        + RingSum.scratch(ep_count, rows, width)
        + [dma((ring, 2)), dma((ring, 2)), dma]
        + [dma((3 + len(batches),)), dma((2,)), dma((4,)), dma((4,)), dma((2,))],
        compiler_params=pltpu.CompilerParams(
            collective_id=collective_id, has_side_effects=True, vmem_limit_bytes=62 << 20
        ),
        name=name,
    )(block, cot_own, cot_other, mine, router, gate_w, up_w, down_w)


class RingSum:
    def __init__(self, here, term, joint, buffers, sems, more=None):
        self.here, self.term, self.joint, self.more = here, term, joint, more
        self.first, self.landed, self.stage = buffers
        self.side_send, self.side_recv, self.ring_send, self.ring_recv, self.stage_sem = sems
        self.far = here.ring // 2
        self.offsets = ring_offsets(here.ring)
        self.part_rows = self.stage.shape[3]
        self.waited, self.copies = set(), []

    @staticmethod
    def scratch(ep_count, rows, width, summands=2, dtype=BF):
        ring, far = ep_count // 2, ep_count // 4
        dma = pltpu.SemaphoreType.DMA
        shapes = [(2, rows, width), (2, far, rows, width), (2, 2, summands, rows // 2, width)]
        buffers = [pltpu.VMEM(shape, dtype) for shape in shapes]
        return buffers + [dma((ring,)), dma((ring,)), dma((2, far, 2)), dma((2, far, 2)), dma((2, 2, summands))]

    def hops(self, way, part):
        return self.far if way == part else self.far - 1

    def rows(self, part):
        return pl.ds(part * self.part_rows, self.part_rows)

    def distance(self, way, part, step):
        distance = max(self.hops(way, part) - step, 0)
        return distance if way == 0 else -distance

    def slot(self, way, part, step):
        offset = self.distance(way, part, step)
        return self.offsets.index(self.far if offset == -self.far else offset)

    def loads(self, way, part, step):
        index = self.here.chip(self.distance(way, part, step))
        sources = [self.term(index), self.joint.at[self.slot(way, part, step)]]
        if self.more is not None:
            sources.append(self.more(index))
        return [
            pltpu.make_async_copy(
                source.at[self.rows(part)], self.stage.at[way, part, i], self.stage_sem.at[way, part, i]
            )
            for i, source in enumerate(sources)
        ]

    def load(self, way, part, step):
        slot = self.slot(way, part, step)
        if slot not in self.waited:
            self.waited.add(slot)
            self.side_copy(slot).wait_recv()
        for copy in self.loads(way, part, step):
            copy.start()

    def side_copy(self, slot):
        here = self.here
        index = here.index(here.at(self.offsets[slot]), 1 - here.core)
        return remote(
            self.term(index), self.joint.at[slot], self.side_send.at[slot], self.side_recv.at[slot], here.sibling()
        )

    def start(self):
        self.trade()
        self.begin()

    def trade(self):
        for slot in reversed(range(len(self.offsets))):
            copy = self.side_copy(slot)
            copy.start()
            self.copies.append(copy)

    def begin(self):
        for part in range(2):
            for way in range(2):
                self.load(way, part, 0)

    def value(self, way, part, step):
        for copy in self.loads(way, part, step):
            copy.wait()
        return sum(self.stage[way, part, i].astype(F32) for i in range(self.stage.shape[2]))

    def ring_copy(self, way, step, part):
        at = self.rows(part)
        src = self.first.at[way, at] if step == 0 else self.landed.at[way, step - 1, at]
        return remote(
            src,
            self.landed.at[way, step, at],
            self.ring_send.at[way, step, part],
            self.ring_recv.at[way, step, part],
            self.here.right() if way == 0 else self.here.left(),
        )

    def step(self, step):
        for part in range(2):
            for way in range(2):
                if step < self.hops(way, part):
                    value = self.value(way, part, step)
                    at = self.rows(part)
                    if step == 0:
                        self.first[way, at] = value.astype(self.first.dtype)
                    else:
                        self.ring_copy(way, step - 1, part).wait_recv()
                        value = value + self.landed[way, step - 1, at].astype(F32)
                        self.landed[way, step - 1, at] = value.astype(self.landed.dtype)
                    copy = self.ring_copy(way, step, part)
                    copy.start()
                    self.copies.append(copy)
                    if step + 1 < self.hops(way, part) or way == 0:
                        self.load(way, part, step + 1)

    def finish(self, put):
        for part in range(2):
            value = self.value(0, part, self.hops(0, part))
            at = self.rows(part)
            for way in range(2):
                count = self.hops(way, part)
                self.ring_copy(way, count - 1, part).wait_recv()
                value = value + self.landed[way, count - 1, at].astype(F32)
            put(at, value)
        for copy in self.copies:
            copy.wait_send()


def rolled(values):
    return pltpu.roll(values, HEAD_DIM // 2, 1)


def turns(table):
    other = rolled(table)
    first = lax.broadcasted_iota(jnp.int32, table.shape, 1) < HEAD_DIM // 2
    return jnp.where(first, table, other), jnp.where(first, -other, table)


def as_rows(columns, count):
    shape = (columns[0].shape[0], 128)
    lane = lax.broadcasted_iota(jnp.int32, shape, 1)
    packed = jnp.zeros(shape, F32)
    for i, column in enumerate(columns):
        packed = jnp.where(lane == i, column, packed)
    return packed.T[:count]


def as_columns(tile):
    padded = jnp.concatenate([tile, jnp.zeros((128 - tile.shape[0], tile.shape[1]), F32)], axis=0)
    return padded.T


BACKWARD_STEPS = {
    "sent": (("x", 0), ("x", 1), ("t", 1)),
    "attended": (("e", 2),),
    "scores": (("e", 3),),
    "dots": (("t", 2),),
    "columns": (("t", 1),),
    "columns_2": (("t", 1),),
    "swap": (
        ("d", 1),
        ("t", 1),
        ("g", 0),
        ("t", 1),
        ("d", 2),
        ("g", 1),
        ("t", 2),
        ("d", 3),
        ("g", 2),
        ("t", 2),
        ("g", 3),
        ("t", 1),
    ),
}


def backward(
    ep_count, d_proj, att_loc, w_out, head, columns, table, gains, w_all, normed, result_terms, tiles, expert_rows, name, collective_id
):
    rows = d_proj.shape[0]
    query, key, value, norm_q, norm_k = head
    tokens, cols = query.shape
    width = w_all.shape[0]
    prompt_len = tokens // 2
    units, grads, hidden, gate_grads, up_grads = expert_rows
    depth_rows, hidden_width = hidden.shape
    ring = ep_count // 2
    far = ring // 2
    out_rows = w_out.shape[1]
    slab, wide, block = 256, 1024, 256
    segment = 512
    pieces = tokens // segment
    scale = HEAD_DIM ** (-0.5)
    dma = pltpu.SemaphoreType.DMA

    def kernel(*refs):
        ins, outs, scratch = split(refs, 20, 16, len(refs) - 36)
        proj_ref, gain_ref = ins[0], ins[9]
        held = ins[1:9] + ins[10:11]
        full_ref, normed_ref, eo_ref, tile_ref, u_ref, e_ref, h_ref, g_ref, p_ref = ins[11:]
        dn_out, go_out, eo_out, gw_out, tile_out, late_out, gate_out, up_out, down_out = outs[:9]
        dn_terms, dn_joint, go_joint, eo_joint, go_mine, go_theirs, x_in = outs[9:]
        dn_s, go_s, eo_s, go_more, gw_s, tile_s, late_s, work_s, att_s, dots_s, own_s, held_s = split(
            scratch, 8, 8, 8, 5, 6, 3, 4, 6, 9, 5, 5, 10
        )
        att_ref, q_ref, k_ref, v_ref, nq_ref, nk_ref, col_ref, table_ref, w_ref = held_s[:9]
        held_copies = [
            pltpu.make_async_copy(src, dst, held_s[9].at[i]) for i, (src, dst) in enumerate(zip(held, held_s[:9]))
        ]
        for copy in held_copies:
            copy.start()
        here = Place(ep_count)
        greet(plane_devices(here) + far_devices(here))
        result = RingSum(here, lambda e: eo_ref.at[e], eo_joint, eo_s[:3], eo_s[3:])
        result.start()
        result.step(0)
        sent = []

        def start(copy):
            copy.start()
            sent.append(copy)

        (att_v, tile_v, dq_s, dk_s, dv_s, lin_s), att_sems = att_s[:6], att_s[6:]
        slab_v, slab_sem, term_v, term_sem, gw_v = own_s

        def full_copy(number):
            return pltpu.make_async_copy(
                full_ref.at[pl.ds(2 * number, 2)], term_v.at[number % 2], term_sem.at[number % 2]
            )

        for number in range(2):
            full_copy(number).start()
        for number in range(ring):
            full_copy(number).wait()
            both = mm_nt(proj_ref[...], term_v[number % 2].reshape(2 * cols, width)).astype(BF)
            for i in range(2):
                tile_v[2 * number + i] = both[:, i * cols : (i + 1) * cols]
            if number + 2 < ring:
                full_copy(number + 2).start()
        attended = Exchange(here, lambda e: tile_v.at[e], lambda e: att_v.at[e], att_sems)
        attended.start()
        result.step(1)

        me = here.grp * ep_count + here.ep

        def tile_copy(turn, offset, source, src, dst, sems):
            group = (here.grp + turn) % 2
            target = (here.ep + offset) % ep_count
            slot = turn * ep_count + offset
            return remote(src(group * ep_count + target), dst.at[source], sems[0].at[slot], sems[1].at[slot], (group, target))

        others = [(turn, offset) for turn in range(2) for offset in range(ep_count) if turn + offset > 0]

        def send_tiles(src, dst, sems):
            own = pltpu.make_async_copy(src(me), dst.at[me], sems[2])
            own.start()
            for turn, offset in others:
                start(tile_copy(turn, offset, me, src, dst, sems))
            return own

        def take_tiles(own, src, dst, sems):
            own.wait()
            for turn, offset in others:
                source = ((here.grp + turn) % 2) * ep_count + (here.ep + ep_count - offset) % ep_count
                tile_copy(turn, offset, source, src, dst, sems).wait_recv()

        x_own, x_joint, go_own_sem, go_send, go_recv = go_more
        go_load = pltpu.make_async_copy(go_theirs.at[:, here.core], x_own, go_own_sem)
        go_side = remote(go_theirs.at[:, 1 - here.core], x_joint, go_send.at[0], go_recv.at[0], here.sibling())

        def go_over(part):
            at = pl.ds(part * (ring // 2), ring // 2)
            return remote(x_own.at[at], x_in.at[at], go_send.at[1 + part], go_recv.at[1 + part], here.across())

        output = RingSum(
            here, lambda e: go_mine.at[e // 2, e % 2], go_joint, go_s[:3], go_s[3:], lambda e: x_in.at[e // 2]
        )

        left, right, sheet, left_sem, right_sem, sheet_sem = work_s
        units = [(u_ref, i) for i in range(width // slab)] + [(h_ref, i) for i in range(hidden_width // slab)]
        turning = width // slab
        done = []

        def right_copies(late):
            if late:
                return [pltpu.make_async_copy(e_ref, right, right_sem.at[0])]
            return [
                pltpu.make_async_copy(src, right.at[:, pl.ds(i * hidden_width, hidden_width)], right_sem.at[i])
                for i, src in enumerate((g_ref, p_ref))
            ]

        def left_copy(number):
            src, i = units[number]
            return pltpu.make_async_copy(src.at[:, pl.ds(i * slab, slab)], left.at[number % 2], left_sem.at[number % 2])

        def sheet_copies(number):
            src, i = units[number]
            at = pl.ds(i * slab, slab)
            if number >= turning:
                return [pltpu.make_async_copy(sheet.at[number % 2], down_out.at[at], sheet_sem.at[number % 2, 0, 0])]
            return [
                pltpu.make_async_copy(
                    sheet.at[number % 2, :, pl.ds(j * hidden_width, hidden_width)], out.at[at], sheet_sem.at[number % 2, 0, j]
                )
                for j, out in enumerate((gate_out, up_out))
            ]

        def unit(number):
            if number in (0, turning):
                for copy in right_copies(number > 0):
                    copy.wait()
            left_copy(number).wait()
            if number + 1 < len(units):
                left_copy(number + 1).start()
            if number >= 2:
                for copy in sheet_copies(number - 2):
                    copy.wait()

            def run(i, carry):
                at = pl.ds(pl.multiple_of(i * wide, wide), wide)
                sheet[number % 2, :, at] = mm_tn(left[number % 2], right[:, at]).astype(sheet.dtype)
                return carry

            lax.fori_loop(0, width // wide, run, 0)
            for copy in sheet_copies(number):
                copy.start()
            if number + 1 == turning:
                for copy in right_copies(True):
                    copy.start()

        def tasks(count):
            for _ in range(min(count, len(units) - len(done))):
                unit(len(done))
                done.append(True)

        for copy in right_copies(False):
            copy.start()
        left_copy(0).start()
        term_copies = []

        def poll(point):
            for kind, number in BACKWARD_STEPS.get(point, ()):
                if kind == "t":
                    tasks(number)
                elif kind == "e":
                    result.step(number)
                elif kind == "d":
                    normed_sum.step(number)
                elif kind == "g":
                    if number == 0:
                        for half in range(2):
                            go_over(half).wait_recv()
                        output.begin()
                    output.step(number)
                elif kind == "x":
                    start(go_over(number))

        for copy in held_copies:
            copy.wait()
        for number in range(ring):
            first = lax.rem((1 - here.grp) * ring + 2 * number, 2 * ring) * cols
            buffer, chip = number % 2, 2 * number % ring
            terms = go_theirs if number < ring // 2 else go_mine
            if number >= 2:
                for copy in term_copies.pop(0):
                    copy.wait()
            if number == ring // 2 + 1:
                go_load.start()
                start(go_side)
            turned = mm_tn(att_ref[:, pl.ds(pl.multiple_of(first, cols), 2 * cols)], proj_ref[...])
            sheet[buffer] = turned.astype(BF)
            copies = [
                pltpu.make_async_copy(
                    sheet.at[buffer, pl.ds((2 * i + j) * out_rows, out_rows)],
                    terms.at[chip + i, j],
                    sheet_sem.at[buffer, i, j],
                )
                for i in range(2)
                for j in range(2)
            ]
            for copy in copies:
                copy.start()
            term_copies.append(copies)
        for copies in term_copies:
            for copy in copies:
                copy.wait()
        go_load.wait()
        go_side.wait_recv()
        for chip in range(ring):
            x_own[chip] = (x_own[chip].astype(F32) + x_joint[chip].astype(F32)).astype(BF)
        poll("sent")
        attended.arrive()
        poll("attended")

        dk_s[...] = jnp.zeros_like(dk_s)
        dv_s[...] = jnp.zeros_like(dv_s)
        per = block // rows
        line = lax.broadcasted_iota(jnp.int32, (block, block), 0)
        column_at = lax.broadcasted_iota(jnp.int32, (block, block), 1)
        causal = line >= column_at
        same = causal & (line // rows == column_at // rows)

        def grads_of(first, spans):
            at = pl.ds(first, block)
            q = q_ref[at]
            g = att_v[pl.ds(first // rows, per)].reshape(block, cols)
            log = col_ref[at, 0:1]
            kept = []
            inner = jnp.zeros((block, 1), F32)
            for begin, length, mask in spans:
                keys = pl.ds(begin, length)
                weight = jnp.exp(mm_nt(q, k_ref[keys]) * scale - log)
                if mask is not None:
                    weight = jnp.where(mask, weight, 0.0)
                d_weight = mm_nt(g, v_ref[keys])
                inner = inner + jnp.sum(weight * d_weight, axis=-1, keepdims=True)
                kept.append((keys, weight, d_weight))
            dq = jnp.zeros((block, cols), F32)
            for keys, weight, d_weight in kept:
                d_score = (weight * (d_weight - inner)).astype(BF)
                dq = dq + mm(d_score, k_ref[keys])
                dk_s[keys] += mm_tn(d_score, q)
                dv_s[keys] += mm_tn(weight.astype(BF), g)
            dq_s[at] = dq * scale

        for number in range(prompt_len // block):
            spans = [(0, number * block, None)] if number else []
            grads_of(number * block, spans + [(number * block, block, causal)])

        def later(number, carry):
            first = pl.multiple_of(prompt_len + number * block, block)
            grads_of(first, [(0, prompt_len, None), (first, block, same)])
            return carry

        poll("prompt")
        lax.fori_loop(0, (tokens - prompt_len) // block, later, 0)
        poll("scores")

        dots_v, dots_all, dots_sems = dots_s[0], dots_s[1], dots_s[2:]
        late_v, late_sems = late_s[0], late_s[1:]
        gain_sums = [jnp.zeros((1, cols), F32), jnp.zeros((1, cols), F32)]
        stats = []
        for piece in range(pieces):
            at = pl.ds(piece * segment, segment)
            cosine, sine = turns(table_ref[at])
            for kind, (ref, n_ref, factor) in enumerate(((dq_s, nq_ref, 1.0), (dk_s, nk_ref, scale))):
                turned = ref[at] * factor
                turned = turned * cosine - rolled(turned) * sine
                gain_sums[kind] = gain_sums[kind] + jnp.sum(turned * n_ref[at].astype(F32), axis=0, keepdims=True)
                turned = turned * gain_ref[kind : kind + 1]
                ref[at] = turned
                stats.append(jnp.sum(turned * n_ref[at].astype(F32), axis=-1, keepdims=True))
        dots_v[...] = as_rows(stats, dots_v.shape[0])
        spread_dots = Exchange(here, lambda e: dots_v, lambda e: dots_all.at[e], dots_sems)
        spread_dots.start()
        gain_tile = jnp.concatenate(gain_sums + [jnp.zeros((6, cols), F32)], axis=0)
        for piece in range(pieces):
            at = pl.ds(piece * segment, segment)
            lin_s[at, 2 * cols : 3 * cols] = dv_s[at].astype(BF)
        slabs = width // slab
        half = slabs // 2

        def slab_at(turn):
            return lax.rem((1 - here.grp) * half + turn, slabs) * slab

        def slab_copy(turn):
            at = pl.ds(pl.multiple_of(slab_at(turn), slab), slab)
            return pltpu.make_async_copy(normed_ref.at[:, at], slab_v.at[turn % 2], slab_sem.at[turn % 2])

        slab_copy(0).start()
        slab_copy(1).start()
        poll("dots")
        spread_dots.arrive()
        total = dots_all[0]
        for e in range(1, ep_count):
            total = total + dots_all[e]
        total = as_columns(total / width)
        for piece in range(pieces):
            at = pl.ds(piece * segment, segment)
            for kind, (ref, n_ref) in enumerate(((dq_s, nq_ref), (dk_s, nk_ref))):
                lane = 2 * piece + kind
                grad = col_ref[at, 1 + kind : 2 + kind] * (ref[at] - n_ref[at].astype(F32) * total[:, lane : lane + 1])
                lin_s[at, kind * cols : (kind + 1) * cols] = grad.astype(BF)

        (gw_x, gw_x_send, gw_x_recv), gw_swap = gw_s[:3], gw_s[3:]
        per_slab = slab // out_rows
        gain_lines = []

        def projections(turn):
            slab_copy(turn).wait()
            first = slab_at(turn)
            grad = mm_tn(slab_v[turn % 2], lin_s[...])
            if turn + 2 < slabs:
                slab_copy(turn + 2).start()
            weight = w_ref[pl.ds(pl.multiple_of(first, slab), slab)].astype(F32)
            line = as_rows([jnp.sum(grad * weight, axis=-1, keepdims=True)], 8)[0:1]
            owner = first // out_rows
            for kind in range(3):
                part = grad[:, kind * cols : (kind + 1) * cols].astype(BF)
                gw_v[pl.ds(owner, per_slab), kind] = part.reshape(per_slab, out_rows, cols)
            for i in range(per_slab):
                part = line[:, i * out_rows : (i + 1) * out_rows]
                part = jnp.concatenate([part, jnp.zeros((1, cols - out_rows), F32)], axis=1)
                late_v[owner + i] = jnp.concatenate([gain_tile[0:2], part, gain_tile[3:]], axis=0)
            return owner

        def over_copy(turn, owner):
            at = pl.ds(owner - (1 - here.grp) * ep_count, per_slab)
            return remote(gw_v.at[pl.ds(owner, per_slab)], gw_x.at[at], gw_x_send.at[turn], gw_x_recv.at[turn], here.across())

        for turn in range(half):
            start(over_copy(turn, projections(turn)))
        poll("columns")
        output.trade()

        normed_sum = RingSum(here, lambda e: dn_terms.at[e], dn_joint, dn_s[:3], dn_s[3:])
        offsets = ring_offsets(ring)
        stores = {}
        for turn, slot in enumerate(reversed(range(ring))):
            chip = here.index(here.at(offsets[slot]), 0) // 2
            if turn >= 2:
                stores.pop(turn - 2).wait()
            at = pl.ds(pl.multiple_of(chip * 2 * rows, 2 * rows), 2 * rows)

            def fill(i, carry, at=at, turn=turn):
                wide_at = pl.ds(pl.multiple_of(i * 1024, 1024), 1024)
                part = mm_nt(lin_s[at], w_ref[wide_at]).astype(BF)
                term_v[turn % 2, :, :, wide_at] = part.reshape(2, rows, 1024)
                return carry

            lax.fori_loop(0, width // 1024, fill, 0)
            stores[turn] = pltpu.make_async_copy(
                term_v.at[turn % 2], dn_terms.at[pl.ds(chip * 2, 2)], term_sem.at[turn % 2]
            )
            stores[turn].start()
        for turn in sorted(stores):
            stores[turn].wait()
        normed_sum.start()
        normed_sum.step(0)
        own_tiles = send_tiles(lambda i: tile_ref.at[i], tile_out, tile_s)
        poll("terms")
        for turn in range(half, slabs):
            projections(turn)
        own_late = send_tiles(lambda i: late_v.at[i], late_out, late_sems)
        poll("columns_2")
        for turn in range(half):
            over_copy(turn, (1 - here.grp) * ep_count + turn * per_slab).wait_recv()
        for e in range(ep_count):
            gw_x[e] = (gw_v[here.grp * ep_count + e].astype(F32) + gw_x[e].astype(F32)).astype(BF)
        swap = Exchange(here, lambda e: gw_x.at[e], lambda e: gw_out.at[:, :, pl.ds(pl.multiple_of(e * cols, cols), cols)], gw_swap)
        swap.start()
        poll("swap")

        def put(out):
            def store(at, value):
                out[at] = value

            return store

        normed_sum.finish(put(dn_out))
        tasks(len(units))
        for number in range(len(units) - 2, len(units)):
            for copy in sheet_copies(number):
                copy.wait()
        result.finish(put(eo_out))
        output.finish(put(go_out))
        take_tiles(own_tiles, lambda i: tile_ref.at[i], tile_out, tile_s)
        take_tiles(own_late, lambda i: late_v.at[i], late_out, late_sems)
        attended.finish()
        spread_dots.finish()
        swap.arrive()
        swap.finish()
        for copy in sent:
            copy.wait_send()

    hbm = pl.BlockSpec(memory_space=pl.ANY)
    vmem = pl.BlockSpec(memory_space=pltpu.VMEM)
    group_rows = 2 * ep_count

    def keep(*shape):
        return pltpu.VMEM(shape, BF)

    def wide_keep(*shape):
        return pltpu.VMEM(shape, F32)

    return pl.pallas_call(
        kernel,
        out_shape=[
            jax.ShapeDtypeStruct((rows, width), F32),
            jax.ShapeDtypeStruct((out_rows, width), F32),
            jax.ShapeDtypeStruct((rows, width), F32),
            jax.ShapeDtypeStruct((3, out_rows, width), BF),
            jax.ShapeDtypeStruct(tiles.shape, F32),
            jax.ShapeDtypeStruct((group_rows, 8, cols), F32),
            jax.ShapeDtypeStruct((width, hidden_width), BF),
            jax.ShapeDtypeStruct((width, hidden_width), BF),
            jax.ShapeDtypeStruct((hidden_width, width), BF),
            jax.ShapeDtypeStruct((ep_count, rows, width), BF),
            jax.ShapeDtypeStruct((ring, rows, width), BF),
            jax.ShapeDtypeStruct((ring, out_rows, width), BF),
            jax.ShapeDtypeStruct((ring, rows, width), BF),
            jax.ShapeDtypeStruct((ring, 2, out_rows, width), BF),
            jax.ShapeDtypeStruct((ring, 2, out_rows, width), BF),
            jax.ShapeDtypeStruct((ring, out_rows, width), BF),
        ],
        in_specs=[vmem] + [hbm] * 8 + [vmem] + [hbm] * 10,
        out_specs=[vmem] * 3 + [hbm] * 13,
        scratch_shapes=RingSum.scratch(ep_count, rows, width)
        + RingSum.scratch(ep_count, out_rows, width, 3)
        + RingSum.scratch(ep_count, rows, width)
        + [keep(ring, out_rows, width)] * 2
        + [dma, dma((3,)), dma((3,))]
        + [keep(ep_count, 3, out_rows, cols)]
        + [dma((ring,)), dma((ring,))]
        + Exchange.scratch(ep_count)
        + [dma((group_rows,)), dma((group_rows,)), dma]
        + [wide_keep(group_rows, 8, cols), dma((group_rows,)), dma((group_rows,)), dma]
        + [keep(2, depth_rows, slab), keep(depth_rows, width), keep(2, slab, width), dma((2,)), dma((2,)), dma((2, 2, 2))]
        + [keep(ep_count, rows, cols)] * 2
        + [wide_keep(tokens, cols)] * 3
        + [keep(tokens, 3 * cols)]
        + Exchange.scratch(ep_count)
        + [wide_keep(8, segment), wide_keep(ep_count, 8, segment)]
        + Exchange.scratch(ep_count)
        + [keep(2, tokens, slab), dma((2,)), keep(2, 2, rows, width), dma((2,))]
        + [keep(group_rows, 3, out_rows, cols)]
        + [keep(rows, width)]
        + [keep(tokens, cols)] * 5
        + [wide_keep(tokens, cols)] * 2
        + [keep(width, 3 * cols), dma((9,))],
        compiler_params=pltpu.CompilerParams(
            collective_id=collective_id, has_side_effects=True, vmem_limit_bytes=63 << 20
        ),
        name=name,
    )(
        d_proj,
        att_loc,
        query,
        key,
        value,
        norm_q,
        norm_k,
        columns,
        table,
        gains,
        w_all,
        w_out.reshape(ep_count, cols, width),
        normed,
        result_terms,
        tiles,
        *expert_rows,
    )


class Crossing:
    def __init__(self, here, out, into, sems):
        self.here, self.out, self.into = here, out, into
        self.across_send, self.across_recv, self.hand_send, self.hand_recv = sems
        self.offsets = ring_offsets(here.ring)
        self.copies = []

    @staticmethod
    def scratch(ep_count):
        return [pltpu.SemaphoreType.DMA((ep_count // 2,))] * 4

    def go(self, copy):
        copy.start()
        self.copies.append(copy)

    def across(self, slot, src, dst):
        return remote(src, dst, self.across_send.at[slot], self.across_recv.at[slot], self.here.across())

    def hand(self, slot, core):
        block = self.into(self.here.index(self.here.at(self.offsets[slot]), core))
        return remote(block, block, self.hand_send.at[slot], self.hand_recv.at[slot], self.here.sibling())

    def send(self, slot, src):
        self.go(self.across(slot, src, self.out(self.here.chip(self.offsets[slot]))))

    def take(self, slot):
        block = self.into(self.here.chip(self.offsets[slot]))
        self.across(slot, block, block).wait_recv()
        self.go(self.hand(slot, self.here.core))

    def settle(self, slot):
        self.hand(slot, 1 - self.here.core).wait_recv()

    def finish(self):
        for copy in self.copies:
            copy.wait_send()


ATTENTION_STEPS = {
    ("x", 0): (("f", -1),),
    ("x", 1): (("f", 0),),
    ("x", 2): (("f", 1),),
    ("x", 3): (("f", 2), ("c", -1)),
    ("x", 4): (("f", 3),),
    "dots": (("c", 0),),
    "prompt": (("c", 1),),
    "sent": (("c", 2), ("c", 3)),
}


def attention(ep_count, x, weights, small, w_out, cot, table, early, name, collective_id):
    rows, width = x.shape
    kinds, depth = len(weights), weights[0].shape[0]
    cols = width // ep_count
    tokens = rows * ep_count
    prompt_len = tokens // 2
    ring = ep_count // 2
    far = ring // 2
    offsets = ring_offsets(ring)
    batches = [[0]] + [[2 * k - 1, 2 * k] for k in range(1, far)] + [[ring - 1]]
    gain_row = depth * ep_count // 128
    block, segment, chunk = 256, 512, 64
    pieces = tokens // segment
    scale = HEAD_DIM ** (-0.5)
    dma = pltpu.SemaphoreType.DMA

    def kernel(*refs):
        ins, outs, scratch = split(refs, 5 + kinds, 14, len(refs) - 19 - kinds)
        x_ref, small_ref, w_ref, cot_ref, table_ref = ins[:5]
        weight_refs = ins[5:]
        normed_out, w_final, s_out, full_out, cot_out, cot_other = outs[:6]
        finals, att_out, x_land = outs[6:12], outs[12], outs[13]
        x_s, w_s, s_s, cross, w_ring, cot_ring, w_cross, cot_cross, bufs, loads, dots_s, att_s, held = split(
            scratch, 5, 3 * kinds, 2, 3, 5, 5, 4, 4, 5, 2, 5, 4, 8
        )
        w_all, q_out, k_out, v_out, nq_out, nk_out, col_out, held_sem = held
        rows_v, normed_v, columns_v, gain_v, lin_v = bufs
        rows_sem, normed_sem = loads
        here = Place(ep_count)
        greet(plane_devices(here) + [here.across()])

        cross_own, cross_send, cross_recv = cross
        first = pltpu.make_async_copy(small_ref, s_out.at[here.grp, here.ep], cross_own)
        first.start()

        def small_over(group):
            return remote(
                small_ref, s_out.at[group, here.ep], cross_send.at[0], cross_recv.at[0], here.across()
            )

        small_over(here.grp).start()
        gather = Gather(here, x_ref, x_land, x_s)
        gather.start()
        columns_of = [
            Exchange(
                here,
                lambda e, ref=ref: ref.at[:, pl.ds(pl.multiple_of(e * cols, cols), cols)],
                lambda e, kind=kind: columns_v.at[here.grp, e, kind],
                w_s[3 * kind : 3 * kind + 3],
            )
            for kind, ref in enumerate(weight_refs)
        ]
        for part in columns_of:
            part.start()
        full = Gather(here, w_ref, full_out.at[here.grp], w_ring)
        full_over = Crossing(
            here, lambda e: full_out.at[here.grp, e], lambda e: full_out.at[1 - here.grp, e], w_cross
        )
        cots = Gather(here, cot_ref, cot_out, cot_ring)
        cots_over = Crossing(here, lambda e: cot_other.at[e], lambda e: cot_other.at[e], cot_cross)
        full_over.send(0, w_ref)
        cots_over.send(0, cot_ref)

        first.wait()
        small_over(1 - here.grp).wait_recv()
        small_over(here.grp).wait_send()
        small_copies = []
        for offset in range(1, here.count):
            mine = s_out.at[:, here.ep]
            copy = remote(mine, mine, s_s[0].at[offset], s_s[1].at[offset], here.peer(offset))
            copy.start()
            small_copies.append(copy)
        for offset in range(1, here.count):
            source = s_out.at[:, here.peer(-offset)[1]]
            remote(source, source, s_s[0].at[offset], s_s[1].at[offset], here.peer(offset)).wait_recv()

        def gains(row, half, owner):
            lines = []
            for i in range(2):
                tile = s_out[(owner + i) // ep_count, (owner + i) % ep_count, pl.ds(0, 16)].astype(F32)
                lines.append(tile[row : row + 1, half * depth : (half + 1) * depth])
            return jnp.concatenate(lines, axis=1)

        for i in range(width // 128):
            gain_v[:, i * 128 : (i + 1) * 128] = gains(gain_row, 0, 2 * i)
        gain_q, gain_k = gains(gain_row, 1, 2 * here.ep), gains(gain_row + 1, 0, 2 * here.ep)

        def chip_of(slot):
            return here.index(here.at(offsets[slot]), 0) // 2

        stores = []

        def leave(src, dst, number):
            stores.append(pltpu.make_async_copy(src, dst, held_sem.at[number]))
            stores[-1].start()


        def norm(batch):
            loaded = []
            for i, slot in enumerate(batch):
                loaded.append(pltpu.make_async_copy(x_land.at[pl.ds(2 * chip_of(slot), 2)], rows_v.at[i], rows_sem.at[i]))
                loaded[-1].start()
            for i, slot in enumerate(batch):
                loaded[i].wait()
                chip = chip_of(slot)
                for core in range(2):

                    def run(j, carry, i=i, core=core, chip=chip):
                        at = pl.ds(pl.multiple_of(j * chunk, chunk), chunk)
                        wide = rows_v[i, core, at].astype(F32)
                        r = lax.rsqrt(jnp.mean(wide * wide, axis=-1, keepdims=True) + eps)
                        normed_v[2 * chip + core, at] = (wide * r * gain_v[...]).astype(BF)
                        return carry

                    lax.fori_loop(0, rows // chunk, run, 0)
                at = pl.ds(2 * chip, 2)
                stores.append(pltpu.make_async_copy(normed_v.at[at], normed_out.at[at], normed_sem.at[slot]))
                stores[-1].start()

        def project(batch):
            for slot in batch:
                chip = chip_of(slot)
                lin = mm(normed_v[pl.ds(2 * chip, 2)].reshape(2 * rows, width), w_all[...])
                at = pl.ds(pl.multiple_of(chip * 2 * rows, 2 * rows), 2 * rows)
                lin_v[0, at] = lin[:, :cols]
                lin_v[1, at] = lin[:, cols : 2 * cols]
                v_out[at] = lin[:, 2 * cols :].astype(BF)

        def poll(point):
            for kind, step in ATTENTION_STEPS.get(point, ()):
                ring_gather, crossing, count = (full, full_over, ring) if kind == "f" else (cots, cots_over, early)
                if step < 0:
                    ring_gather.start()
                    continue
                ring_gather.step(step)
                for slot in batches[step + 1]:
                    if slot < count:
                        crossing.send(slot, ring_gather.dst.at[here.chip(offsets[slot])])

        over = remote(columns_v.at[here.grp], columns_v.at[here.grp], cross_send.at[1], cross_recv.at[1], here.across())
        gather.settle()
        for number, batch in enumerate(batches):
            gather.side(number - 1)
            norm(batch)
            if number < far:
                gather.step(number)
            poll(("x", number))
            if number == 1:
                for part in columns_of:
                    part.arrive()
                over.start()
            if number == far - 1:
                remote(
                    columns_v.at[1 - here.grp],
                    columns_v.at[1 - here.grp],
                    cross_send.at[1],
                    cross_recv.at[1],
                    here.across(),
                ).wait_recv()
                for owner in range(2 * ep_count):
                    for kind in range(kinds):
                        w_all[owner * depth : (owner + 1) * depth, kind * cols : (kind + 1) * cols] = columns_v[
                            owner // ep_count, owner % ep_count, kind
                        ]
                leave(w_all, w_final, 0)
                for earlier in batches[:number]:
                    project(earlier)
            if number >= far - 1:
                project(batch)

        dots_v, dots_all, dots_sems = dots_s[0], dots_s[1], dots_s[2:]
        stats = []
        for piece in range(pieces):
            at = pl.ds(piece * segment, segment)
            for kind in range(2):
                lin = lin_v[kind, at]
                stats.append(jnp.sum(lin * lin, axis=-1, keepdims=True))
        dots_v[...] = as_rows(stats, dots_v.shape[0])
        spread_dots = Exchange(here, lambda e: dots_v, lambda e: dots_all.at[e], dots_sems)
        spread_dots.start()
        poll("dots")
        spread_dots.arrive()
        total = dots_all[0]
        for e in range(1, ep_count):
            total = total + dots_all[e]
        r_all = as_columns(lax.rsqrt(total / width + eps))
        lane = lax.broadcasted_iota(jnp.int32, (segment, 128), 1)
        for piece in range(pieces):
            at = pl.ds(piece * segment, segment)
            kept = jnp.zeros((segment, 128), F32)
            cosine, sine = turns(table_ref[at])
            for kind, (gain, n_out, out) in enumerate(((gain_q, nq_out, q_out), (gain_k, nk_out, k_out))):
                r = r_all[:, 2 * piece + kind : 2 * piece + kind + 1]
                n = lin_v[kind, at] * r
                n_out[at] = n.astype(BF)
                n = n * gain
                out[at] = (n * cosine + rolled(n) * sine).astype(BF)
                kept = jnp.where(lane == 1 + kind, r, kept)
            col_out[at] = kept

        for number, src in enumerate((q_out, k_out, v_out, nq_out, nk_out)):
            leave(src, finals[number], 1 + number)
        poll("turned")
        att_v, att_sems = att_s[0], att_s[1:]
        per = block // rows
        line = lax.broadcasted_iota(jnp.int32, (block, block), 0)
        column_at = lax.broadcasted_iota(jnp.int32, (block, block), 1)
        causal = line >= column_at
        same = causal & (line // rows == column_at // rows)
        block_lane = lax.broadcasted_iota(jnp.int32, (block, 128), 1)

        def attend(first, spans):
            at = pl.ds(first, block)
            q = q_out[at]
            scores = []
            for begin, length, mask in spans:
                score = mm_nt(q, k_out[pl.ds(begin, length)]) * scale
                scores.append(score if mask is None else jnp.where(mask, score, -1e30))
            top = jnp.max(scores[0], axis=-1, keepdims=True)
            for score in scores[1:]:
                top = jnp.maximum(top, jnp.max(score, axis=-1, keepdims=True))
            powers = [jnp.exp(score - top) for score in scores]
            summed = sum(jnp.sum(power, axis=-1, keepdims=True) for power in powers)
            out = jnp.zeros((block, cols), F32)
            for (begin, length, _), power in zip(spans, powers):
                out = out + mm((power / summed).astype(BF), v_out[pl.ds(begin, length)])
            att_v[pl.ds(first // rows, per)] = out.astype(BF).reshape(per, rows, cols)
            col_out[at] = jnp.where(block_lane == 0, top + jnp.log(summed), col_out[at])

        for number in range(prompt_len // block):
            spans = [(0, number * block, None)] if number else []
            attend(number * block, spans + [(number * block, block, causal)])
        poll("prompt")

        def later(number, carry):
            first = pl.multiple_of(prompt_len + number * block, block)
            attend(first, [(0, prompt_len, None), (first, block, same)])
            return carry

        lax.fori_loop(0, (tokens - prompt_len) // block, later, 0)
        attended = Exchange(here, lambda e: att_v.at[e], lambda e: att_out.at[:, pl.ds(pl.multiple_of(e * cols, cols), cols)], att_sems)
        attended.start()
        leave(col_out, finals[5], 6)
        poll("sent")
        attended.arrive()
        for step in range(-1, far):
            full.side(step)
            cots.side(step)
        for slot in range(ring):
            full_over.take(slot)
            if slot < early:
                cots_over.take(slot)
        for slot in range(ring):
            full_over.settle(slot)
            if slot < early:
                cots_over.settle(slot)
        full.settle()
        cots.settle()
        for part in (gather, full, cots, full_over, cots_over, *columns_of, spread_dots, attended):
            part.finish()
        over.wait_send()
        for copy in small_copies:
            copy.wait_send()
        for copy in stores:
            copy.wait()

    hbm = pl.BlockSpec(memory_space=pl.ANY)
    vmem = pl.BlockSpec(memory_space=pltpu.VMEM)

    def low(*shape):
        return jax.ShapeDtypeStruct(shape, BF)

    def wide(*shape):
        return jax.ShapeDtypeStruct(shape, F32)

    outs = pl.pallas_call(
        kernel,
        out_shape=[
            low(ep_count, rows, width),
            low(width, kinds * cols),
            low(2, ep_count, *small.shape),
            low(2, ep_count, *w_out.shape),
            low(ep_count, rows, width),
            low(ep_count, rows, width),
            low(tokens, cols),
            low(tokens, cols),
            low(tokens, cols),
            low(tokens, cols),
            low(tokens, cols),
            wide(tokens, 128),
            low(rows, width),
            low(ep_count, rows, width),
        ],
        in_specs=[hbm, hbm, hbm, hbm, vmem] + [hbm] * kinds,
        out_specs=[hbm, hbm, vmem] + [hbm] * 11,
        scratch_shapes=Gather.scratch(ep_count)
        + Exchange.scratch(ep_count) * kinds
        + [dma((ep_count,)), dma((ep_count,))]
        + [dma, dma((2,)), dma((2,))]
        + Gather.scratch(ep_count)
        + Gather.scratch(ep_count)
        + Crossing.scratch(ep_count)
        + Crossing.scratch(ep_count)
        + [
            pltpu.VMEM((2, 2, rows, width), BF),
            pltpu.VMEM((ep_count, rows, width), BF),
            pltpu.VMEM((2, ep_count, kinds, depth, cols), BF),
            pltpu.VMEM((1, width), F32),
            pltpu.VMEM((2, tokens, cols), F32),
        ]
        + [dma((2,)), dma((ring,))]
        + [pltpu.VMEM((8, segment), F32), pltpu.VMEM((ep_count, 8, segment), F32)]
        + Exchange.scratch(ep_count)
        + [pltpu.VMEM((ep_count, rows, cols), BF)]
        + Exchange.scratch(ep_count)
        + [pltpu.VMEM((width, kinds * cols), BF)]
        + [pltpu.VMEM((tokens, cols), BF)] * 5
        + [pltpu.VMEM((tokens, 128), F32), dma((7,))],
        compiler_params=pltpu.CompilerParams(
            collective_id=collective_id, has_side_effects=True, vmem_limit_bytes=56 << 20
        ),
        name=name,
    )(x, small, w_out, cot, table, *weights)
    return outs[:-1]


def angles_of(position):
    half_dim = HEAD_DIM // 2
    frequency = np.float32(theta_base) ** (-2.0 * np.arange(half_dim, dtype=np.float32) / HEAD_DIM)
    angles = position.astype(np.float32)[:, None] * frequency.astype(np.float32)[None, :]
    return np.concatenate([np.cos(angles), np.sin(angles)], axis=1).astype(np.float32)


def per_device(
    block_input,
    cotangent,
    routes,
    w_query,
    w_key,
    w_value,
    w_output,
    w_router,
    gain_attn,
    gain_query,
    gain_key,
    gain_mlp,
    w_gate,
    w_up,
    w_down,
):
    rows, width = block_input.shape
    top_count = routes.shape[1]
    ep_count = lax.axis_size("ep")
    grp_count = lax.axis_size("grp")
    me = lax.axis_index("ep")
    my_group = lax.axis_index("grp")
    tokens = rows * ep_count
    prompt_len = tokens // 2
    capacity = min(rows, rows * top_count * 33 // (32 * ep_count))
    cols = width // ep_count
    scale = HEAD_DIM ** (-0.5)
    depth = w_query.shape[0]

    chosen = jnp.any(routes[:, :, None] == jnp.arange(ep_count, dtype=jnp.int32), axis=1)
    per_row = 128
    router_rows = depth * ep_count // per_row
    gains = jnp.concatenate([gain_attn, gain_query, gain_key, gain_mlp])
    gain_rows = gains.shape[0] // per_row
    small = jnp.concatenate(
        [
            w_router.reshape(router_rows, per_row),
            gains.reshape(gain_rows, per_row),
            jnp.zeros((16 - router_rows - gain_rows, per_row), BF),
            chosen.T.astype(BF),
        ]
    )
    weights = (w_query, w_key, w_value)
    token = np.arange(tokens)
    table = jnp.asarray(angles_of(np.where(token < prompt_len, token, prompt_len + (token - prompt_len) % rows)))
    early = ep_count // 4
    normed_all, w_all, smalls, full_output, cot_own, cot_other, query, key, value, n_q, n_k, columns, att_loc = attention(
        ep_count, block_input, weights, small, w_output, cotangent, table, early, "attention", 1
    )
    normed_all = normed_all.reshape(tokens, width)
    full_rows = full_output.reshape(grp_count * ep_count, depth, width)
    full_output = full_output.reshape(width, width)
    smalls = smalls.reshape(grp_count * ep_count, small.shape[0], per_row)
    full_router = smalls[:, :router_rows].reshape(width, ep_count)
    gains = smalls[:, router_rows : router_rows + gain_rows].reshape(-1, 4, depth).transpose(1, 0, 2).reshape(4, width)
    gain_first, gain_qnorm, gain_knorm, gain_second = (gains[i].astype(F32) for i in range(4))
    chosen_all = smalls[:, 16:].reshape(grp_count, ep_count, ep_count, rows)

    gain_q = lax.dynamic_slice(gain_qnorm, (me * cols,), (cols,))
    gain_k = lax.dynamic_slice(gain_knorm, (me * cols,), (cols,))

    inputs = block_input.astype(F32)
    residual = inputs + mm(att_loc, full_output)
    r_m = lax.rsqrt(jnp.mean(residual * residual, axis=-1, keepdims=True) + eps)
    n_m = residual * r_m
    normed_mlp = (n_m * gain_second).astype(BF)
    pair = 2 * rows
    slots = -(-2 * capacity // 16) * 16
    chips = ep_count // 2
    mine = lax.dynamic_index_in_dim(chosen_all, me, 2, keepdims=False)
    mine = jnp.where(my_group == 0, mine, mine[::-1]).reshape(2 * chips, pair).astype(F32)
    gate_w, up_w, down_w = w_gate[0], w_up[0], w_down[0]
    _, units, grad_out, hidden, grad_gate_pre, grad_up_pre, _, result_terms, _, d_normed_mlp, gate_grads, _ = experts(
        ep_count, normed_mlp, cot_own, cot_other, early, mine, slots, full_router, gate_w, up_w, down_w, "experts", 4
    )
    gate_grads = gate_grads[:, 0]

    probs = jax.nn.softmax(mm(normed_mlp, full_router), axis=-1)
    d_probs = gate_grads.T
    d_logits = (probs * (d_probs - jnp.sum(probs * d_probs, axis=-1, keepdims=True))).astype(BF)
    local_router = mm_tn(normed_mlp, d_logits)
    d_normed_mlp = d_normed_mlp + mm_nt(d_logits, full_router)
    local_gain_mlp = jnp.sum(d_normed_mlp * n_m, axis=0)
    d_n = d_normed_mlp * gain_second
    d_residual = cotangent.astype(F32) + r_m * (d_n - n_m * jnp.mean(n_m * d_n, axis=-1, keepdims=True))
    d_proj = d_residual.astype(BF)

    gain_rows_own = jnp.stack([gain_q, gain_k])
    owners = grp_count * ep_count
    tiles = jnp.concatenate(
        [
            local_router.reshape(owners, router_rows, per_row),
            jnp.pad(local_gain_mlp.reshape(owners, 1, depth), ((0, 0), (0, 16 - router_rows - 1), (0, per_row - depth))),
        ],
        axis=1,
    )
    d_normed, grad_output, mixture, grad_w, tiles, late, grad_gate, grad_up, grad_down = backward(
        ep_count,
        d_proj,
        att_loc,
        full_rows,
        (query, key, value, n_q, n_k),
        columns,
        table,
        gain_rows_own,
        w_all,
        normed_all,
        result_terms,
        tiles,
        [a.reshape(-1, a.shape[-1]) for a in (units, grad_out, hidden, grad_gate_pre, grad_up_pre)],
        "backward",
        9,
    )[:9]
    block_output = (residual + mixture).astype(BF)
    r_a = lax.rsqrt(jnp.mean(inputs * inputs, axis=-1, keepdims=True) + eps)
    n_a = inputs * r_a
    d_n = d_normed * gain_first
    input_grad = d_residual + r_a * (d_n - n_a * jnp.mean(n_a * d_n, axis=-1, keepdims=True))
    my_rows = my_group * ep_count + me
    grad_w = [grad_w[i].astype(F32) for i in range(3)]
    sums = jnp.sum(tiles, axis=0)
    grad_router = sums[:router_rows].reshape(depth, ep_count)
    gain_part = jnp.sum(late[:, 2, :depth], axis=0) / lax.dynamic_slice(gain_first, (my_rows * depth,), (depth,))
    late = jnp.sum(late.reshape(grp_count, ep_count, 8, cols), axis=0)[:, :2].transpose(1, 0, 2).reshape(2, width)
    late = lax.dynamic_slice(late, (0, my_rows * depth), (2, depth))
    gain_sums = [gain_part, late[0], late[1], sums[router_rows, :depth]]
    grad_gate, grad_up, grad_down = (grad.astype(F32)[None] for grad in (grad_gate, grad_up, grad_down))
    return (
        block_output,
        input_grad,
        grad_w[0],
        grad_w[1],
        grad_w[2],
        grad_output,
        grad_router,
        gain_sums[0],
        gain_sums[1],
        gain_sums[2],
        gain_sums[3],
        grad_gate,
        grad_up,
        grad_down,
    )


def plain_scale(values, gain_vec):
    return values * lax.rsqrt(jnp.mean(values * values, axis=-1, keepdims=True) + eps) * gain_vec


def rotate(values, position):
    token_count = values.shape[0]
    by_head = values.reshape(token_count, -1, HEAD_DIM)
    half_dim = HEAD_DIM // 2
    frequency = theta_base ** (-2.0 * jnp.arange(half_dim, dtype=jnp.float32) / HEAD_DIM)
    angles = position.astype(jnp.float32)[:, None] * frequency[None, :]
    cosine = jnp.cos(angles)[:, None, :]
    sine_part = jnp.sin(angles)[:, None, :]
    former = by_head[..., :half_dim]
    latter = by_head[..., half_dim:]
    turned = jnp.concatenate(
        [former * cosine - latter * sine_part, latter * cosine + former * sine_part], axis=-1
    )
    return turned.reshape(token_count, -1)


def masked_scores(query, keys, allowed, scale):
    raw_scores = jnp.einsum("qhd,khd->hqk", query, keys, preferred_element_type=jnp.float32) * scale
    return jnp.where(allowed[None], raw_scores, -1e30)


def plain_attend(query, keys, values, allowed, scale, head_group):
    outputs = []
    log_totals = []
    for head_start in range(0, query.shape[1], head_group):
        head_slice = slice(head_start, head_start + head_group)
        scores = masked_scores(query[:, head_slice], keys[:, head_slice], allowed, scale)
        largest = jnp.max(scores, axis=-1, keepdims=True)
        exponent = jnp.exp(scores - largest)
        summed = jnp.sum(exponent, axis=-1, keepdims=True)
        weights = (exponent / summed).astype(jnp.bfloat16)
        outputs.append(
            jnp.einsum(
                "hqk,khd->qhd", weights, values[:, head_slice], preferred_element_type=jnp.float32
            )
        )
        log_totals.append(largest + jnp.log(summed))
    return (jnp.concatenate(outputs, axis=1), jnp.concatenate(log_totals, axis=0))


def plain_attend_back(query, keys, values, grad_out, log_totals, allowed, scale, head_group):
    query_grads = []
    key_grads = []
    value_grads = []
    for head_start in range(0, query.shape[1], head_group):
        head_slice = slice(head_start, head_start + head_group)
        query_part = query[:, head_slice]
        keys_part = keys[:, head_slice]
        grad_part = grad_out[:, head_slice]
        scores = masked_scores(query_part, keys_part, allowed, scale)
        weights = jnp.where(allowed[None], jnp.exp(scores - log_totals[head_slice]), 0.0)
        grad_weights = jnp.einsum(
            "qhd,khd->hqk", grad_part, values[:, head_slice], preferred_element_type=jnp.float32
        )
        inner = jnp.sum(weights * grad_weights, axis=-1, keepdims=True)
        grad_scores = (weights * (grad_weights - inner)).astype(jnp.bfloat16)
        query_grads.append(
            jnp.einsum("hqk,khd->qhd", grad_scores, keys_part, preferred_element_type=jnp.float32)
            * scale
        )
        key_grads.append(
            jnp.einsum("hqk,qhd->khd", grad_scores, query_part, preferred_element_type=jnp.float32)
            * scale
        )
        value_grads.append(
            jnp.einsum(
                "hqk,qhd->khd",
                weights.astype(jnp.bfloat16),
                grad_part,
                preferred_element_type=jnp.float32,
            )
        )
    return (
        jnp.concatenate(query_grads, axis=1),
        jnp.concatenate(key_grads, axis=1),
        jnp.concatenate(value_grads, axis=1),
    )


def per_device_plain(
    block_input,
    cotangent,
    routes,
    w_query,
    w_key,
    w_value,
    w_output,
    w_router,
    gain_attn,
    gain_query,
    gain_key,
    gain_mlp,
    w_gate,
    w_up,
    w_down,
):
    row_count, model_width = block_input.shape
    top_count = routes.shape[1]
    ep_count = lax.axis_size("ep")
    my_index = lax.axis_index("ep")
    half_count = ep_count // 2
    prompt_len = row_count * half_count
    capacity = min(row_count, row_count * top_count * 33 // (32 * ep_count))
    head_count = model_width // HEAD_DIM
    head_group = math.gcd(4, head_count)
    scale = HEAD_DIM ** (-0.5)
    gathered = (
        lax.all_gather(w_query, ("grp", "ep"), axis=0, tiled=True),
        lax.all_gather(w_key, ("grp", "ep"), axis=0, tiled=True),
        lax.all_gather(w_value, ("grp", "ep"), axis=0, tiled=True),
        lax.all_gather(w_output, ("grp", "ep"), axis=0, tiled=True),
        lax.all_gather(w_router, ("grp", "ep"), axis=0, tiled=True),
        lax.all_gather(gain_attn, ("grp", "ep"), axis=0, tiled=True),
        lax.all_gather(gain_query, ("grp", "ep"), axis=0, tiled=True),
        lax.all_gather(gain_key, ("grp", "ep"), axis=0, tiled=True),
        lax.all_gather(gain_mlp, ("grp", "ep"), axis=0, tiled=True),
    )
    full_query, full_key, full_value, full_output, full_router = (
        gathered[0],
        gathered[1],
        gathered[2],
        gathered[3],
        gathered[4],
    )
    gain_first = gathered[5].astype(jnp.float32)
    gain_qnorm = gathered[6].astype(jnp.float32)
    gain_knorm = gathered[7].astype(jnp.float32)
    gain_second = gathered[8].astype(jnp.float32)
    offsets = jnp.arange(row_count, dtype=jnp.int32)
    in_prompt = my_index < half_count
    position = jnp.where(in_prompt, my_index * row_count + offsets, prompt_len + offsets)
    key_position = jnp.concatenate([jnp.arange(prompt_len, dtype=jnp.int32), prompt_len + offsets])
    from_prompt = jnp.arange(prompt_len + row_count, dtype=jnp.int32) < prompt_len
    allowed = (key_position[None, :] <= position[:, None]) & (
        from_prompt[None, :] | jnp.logical_not(in_prompt)
    )

    def prepare(linear, gain_vec):
        return rotate(plain_scale(linear, gain_vec), position)

    inputs = block_input.astype(jnp.float32)
    normed = plain_scale(inputs, gain_first).astype(jnp.bfloat16)
    query_lin = jnp.dot(normed, full_query, preferred_element_type=jnp.float32)
    key_lin = jnp.dot(normed, full_key, preferred_element_type=jnp.float32)
    value_lin = jnp.dot(normed, full_value, preferred_element_type=jnp.float32)
    query_low = prepare(query_lin, gain_qnorm).astype(jnp.bfloat16)
    key_low = prepare(key_lin, gain_knorm).astype(jnp.bfloat16)
    value_low = value_lin.astype(jnp.bfloat16)
    shared = (
        lax.all_gather(key_low, "ep", axis=0, tiled=True),
        lax.all_gather(value_low, "ep", axis=0, tiled=True),
    )
    keys = jnp.concatenate([shared[0][:prompt_len], key_low]).reshape(-1, head_count, HEAD_DIM)
    values = jnp.concatenate([shared[1][:prompt_len], value_low]).reshape(-1, head_count, HEAD_DIM)
    query = query_low.reshape(row_count, head_count, HEAD_DIM)
    attn_out, log_totals = plain_attend(query, keys, values, allowed, scale, head_group)
    attended = attn_out.reshape(row_count, model_width).astype(jnp.bfloat16)
    residual = inputs + jnp.dot(attended, full_output, preferred_element_type=jnp.float32)
    normed_mlp = plain_scale(residual, gain_second).astype(jnp.bfloat16)
    logits = jnp.dot(normed_mlp, full_router, preferred_element_type=jnp.float32)
    probs = jax.nn.softmax(logits, axis=-1)
    picks = routes[:, :, None] == jnp.arange(ep_count, dtype=jnp.int32)[None, None, :]
    gates = jnp.sum(jnp.where(picks, probs[:, None, :], 0.0), axis=-1)
    hot_table = picks.reshape(-1, ep_count).astype(jnp.int32)
    before = jnp.cumsum(hot_table, axis=0) - hot_table
    slot_index = jnp.sum(before * hot_table, axis=1)
    target = routes.reshape(-1) * capacity + slot_index
    sentinel = row_count * top_count
    source = (
        jnp.full((ep_count * capacity,), sentinel, jnp.int32)
        .at[target]
        .set(jnp.arange(sentinel, dtype=jnp.int32))
    )
    token_of = source // top_count
    padded_rows = jnp.concatenate([normed_mlp, jnp.zeros((1, model_width), jnp.bfloat16)])
    outgoing = padded_rows[token_of].reshape(ep_count, capacity, model_width)
    arrived = lax.all_to_all(outgoing, "ep", split_axis=0, concat_axis=0, tiled=True)
    units = arrived.reshape(-1, model_width)
    gate_w = w_gate[0]
    up_w = w_up[0]
    down_w = w_down[0]
    gate_pre = jnp.dot(units, gate_w, preferred_element_type=jnp.float32)
    up_pre = jnp.dot(units, up_w, preferred_element_type=jnp.float32)
    hidden = (jax.nn.silu(gate_pre) * up_pre).astype(jnp.bfloat16)
    expert_result = jnp.dot(hidden, down_w, preferred_element_type=jnp.float32).astype(jnp.bfloat16)
    returned = lax.all_to_all(
        expert_result.reshape(ep_count, capacity, model_width),
        "ep",
        split_axis=0,
        concat_axis=0,
        tiled=True,
    )
    picked = (
        returned.reshape(-1, model_width)[target]
        .reshape(row_count, top_count, model_width)
        .astype(jnp.float32)
    )
    output_full = residual + jnp.sum(gates[:, :, None] * picked, axis=1)
    block_output = output_full.astype(jnp.bfloat16)
    back_query, back_key, back_value, back_output, back_router = (
        full_query,
        full_key,
        full_value,
        full_output,
        full_router,
    )
    grad_top = cotangent.astype(jnp.float32)
    grad_gates = jnp.sum(grad_top[:, None, :] * picked, axis=-1)
    grad_expert = (
        (gates[:, :, None] * grad_top[:, None, :]).astype(jnp.bfloat16).reshape(-1, model_width)
    )
    padded_grads = jnp.concatenate([grad_expert, jnp.zeros((1, model_width), jnp.bfloat16)])
    grad_outgoing = padded_grads[source].reshape(ep_count, capacity, model_width)
    grad_arrived = lax.all_to_all(
        grad_outgoing, "ep", split_axis=0, concat_axis=0, tiled=True
    ).reshape(-1, model_width)
    grad_hidden = jnp.einsum("nd,fd->nf", grad_arrived, down_w, preferred_element_type=jnp.float32)
    sigma = jax.nn.sigmoid(gate_pre)
    grad_gate_pre = (grad_hidden * up_pre * sigma * (1.0 + gate_pre * (1.0 - sigma))).astype(
        jnp.bfloat16
    )
    grad_up_pre = (grad_hidden * gate_pre * sigma).astype(jnp.bfloat16)
    local_down = jnp.einsum("nf,nd->fd", hidden, grad_arrived, preferred_element_type=jnp.float32)
    local_gate = jnp.einsum("nd,nf->df", units, grad_gate_pre, preferred_element_type=jnp.float32)
    local_up = jnp.einsum("nd,nf->df", units, grad_up_pre, preferred_element_type=jnp.float32)
    grad_units = jnp.einsum("nf,df->nd", grad_gate_pre, gate_w, preferred_element_type=jnp.float32)
    grad_units = grad_units + jnp.einsum(
        "nf,df->nd", grad_up_pre, up_w, preferred_element_type=jnp.float32
    )
    grad_units = grad_units.astype(jnp.bfloat16).reshape(ep_count, capacity, model_width)
    grad_returned = lax.all_to_all(
        grad_units, "ep", split_axis=0, concat_axis=0, tiled=True
    ).reshape(-1, model_width)
    grad_normed_mlp = jnp.sum(
        grad_returned[target].reshape(row_count, top_count, model_width).astype(jnp.float32), axis=1
    )
    expert_sums = (
        lax.psum(local_gate[None].astype(jnp.bfloat16), "grp").astype(jnp.float32),
        lax.psum(local_up[None].astype(jnp.bfloat16), "grp").astype(jnp.float32),
        lax.psum(local_down[None].astype(jnp.bfloat16), "grp").astype(jnp.float32),
    )
    grad_probs = jnp.sum(jnp.where(picks, grad_gates[:, :, None], 0.0), axis=1)
    grad_logits = (
        probs * (grad_probs - jnp.sum(probs * grad_probs, axis=-1, keepdims=True))
    ).astype(jnp.bfloat16)
    local_router = jnp.einsum(
        "rd,re->de", normed_mlp, grad_logits, preferred_element_type=jnp.float32
    )
    grad_normed_mlp = grad_normed_mlp + jnp.einsum(
        "re,de->rd", grad_logits, back_router, preferred_element_type=jnp.float32
    )
    unused_mlp, second_back = jax.vjp(plain_scale, residual, gain_second)
    grad_from_mlp, local_gain_mlp = second_back(grad_normed_mlp)
    grad_residual = grad_top + grad_from_mlp
    grad_proj = grad_residual.astype(jnp.bfloat16)
    local_output = jnp.einsum("rd,re->de", attended, grad_proj, preferred_element_type=jnp.float32)
    grad_attended = jnp.einsum(
        "re,de->rd", grad_proj, back_output, preferred_element_type=jnp.float32
    )
    grad_attended = grad_attended.astype(jnp.bfloat16).reshape(row_count, head_count, HEAD_DIM)
    grad_query_rot, grad_keys, grad_values = plain_attend_back(
        query, keys, values, grad_attended, log_totals, allowed, scale, head_group
    )
    grad_keys = grad_keys.reshape(-1, model_width)
    grad_values = grad_values.reshape(-1, model_width)
    padding = jnp.zeros((ep_count * row_count - prompt_len, model_width), jnp.float32)
    key_share, value_share = (
        lax.psum_scatter(
            jnp.concatenate([grad_keys[:prompt_len], padding]).astype(jnp.bfloat16),
            "ep",
            scatter_dimension=0,
            tiled=True,
        ).astype(jnp.float32),
        lax.psum_scatter(
            jnp.concatenate([grad_values[:prompt_len], padding]).astype(jnp.bfloat16),
            "ep",
            scatter_dimension=0,
            tiled=True,
        ).astype(jnp.float32),
    )
    grad_key_rot = key_share + grad_keys[prompt_len:]
    grad_value_lin = (value_share + grad_values[prompt_len:]).astype(jnp.bfloat16)
    unused_query, query_back = jax.vjp(prepare, query_lin, gain_qnorm)
    grad_query_lin, local_gain_query = query_back(grad_query_rot.reshape(row_count, model_width))
    unused_key, key_back = jax.vjp(prepare, key_lin, gain_knorm)
    grad_key_lin, local_gain_key = key_back(grad_key_rot)
    grad_query_low = grad_query_lin.astype(jnp.bfloat16)
    grad_key_low = grad_key_lin.astype(jnp.bfloat16)
    local_query = jnp.einsum(
        "rd,re->de", normed, grad_query_low, preferred_element_type=jnp.float32
    )
    local_key = jnp.einsum("rd,re->de", normed, grad_key_low, preferred_element_type=jnp.float32)
    local_value = jnp.einsum(
        "rd,re->de", normed, grad_value_lin, preferred_element_type=jnp.float32
    )
    grad_normed = jnp.einsum(
        "re,de->rd", grad_query_low, back_query, preferred_element_type=jnp.float32
    )
    grad_normed = grad_normed + jnp.einsum(
        "re,de->rd", grad_key_low, back_key, preferred_element_type=jnp.float32
    )
    grad_normed = grad_normed + jnp.einsum(
        "re,de->rd", grad_value_lin, back_value, preferred_element_type=jnp.float32
    )
    unused_first, first_back = jax.vjp(plain_scale, inputs, gain_first)
    grad_from_attn, local_gain_attn = first_back(grad_normed)
    input_grad = grad_residual + grad_from_attn
    summed_grads = (
        lax.psum_scatter(local_query, ("grp", "ep"), scatter_dimension=0, tiled=True),
        lax.psum_scatter(local_key, ("grp", "ep"), scatter_dimension=0, tiled=True),
        lax.psum_scatter(local_value, ("grp", "ep"), scatter_dimension=0, tiled=True),
        lax.psum_scatter(local_output, ("grp", "ep"), scatter_dimension=0, tiled=True),
        lax.psum_scatter(local_router, ("grp", "ep"), scatter_dimension=0, tiled=True),
        lax.psum_scatter(local_gain_attn, ("grp", "ep"), scatter_dimension=0, tiled=True),
        lax.psum_scatter(local_gain_query, ("grp", "ep"), scatter_dimension=0, tiled=True),
        lax.psum_scatter(local_gain_key, ("grp", "ep"), scatter_dimension=0, tiled=True),
        lax.psum_scatter(local_gain_mlp, ("grp", "ep"), scatter_dimension=0, tiled=True),
    )
    return (
        block_output,
        input_grad,
        summed_grads[0],
        summed_grads[1],
        summed_grads[2],
        summed_grads[3],
        summed_grads[4],
        summed_grads[5],
        summed_grads[6],
        summed_grads[7],
        summed_grads[8],
        expert_sums[0],
        expert_sums[1],
        expert_sums[2],
    )


def solution(mesh):
    both = ("grp", "ep")
    return jax.shard_map(
        per_device if mesh.shape["grp"] == 2 else per_device_plain,
        mesh=mesh,
        in_specs=(P(both, None),) * 8 + (P(both),) * 4 + (P("ep", None, None),) * 3,
        out_specs=(P(both, None),) * 7 + (P(both),) * 4 + (P("ep", None, None),) * 3,
        check_vma=False,
    )
```
